256 devices in a mesh: row: 64 (over x, z, core), col: 4 (over y).
Axes of the slice: x: 4, y: 4, z: 8, core: 2. Of those that a mesh axis runs over, the one named last changes fastest.
Arguments:
- blocks: bfloat16 [256, 28, 128, 128], P('row', 'col'), may hold values from -1.5 to 1.5
- nonzero: int32 [256, 28], P('row', 'col'), may hold values 0 or 1
- columns: int32 [256, 28], replicated, may hold values from 0 to 255, as said below
Outputs:
- square: bfloat16 [256, 28, 128, 128], P('row', 'col')
The draws below stay inside these ranges and needn't reach their ends.
Inputs may be any that keep to these rules, and one draw needn't show every extreme that they name: The 28 columns of one block row are distinct. The rows of a slab of 4 consecutive block rows (slab s holds rows s * 4 to s * 4 + 3) all name every row of their own slab, and together name at most 1 distinct block rows of any other slab.
All inputs are finite; a program needn't handle non-finite values. No bound on the sum of `nonzero` on one device may be relied on, other than what follows from the above.
Results may differ from the reference program's by a relative error of at most 0.001.
Values may be sent and summed in bfloat16 or wider, within the bound.
No kernel may reach another device: no remote copies, remote signals or barrier semaphores. Data moves between devices by JAX's collectives and lax.ppermute only.
A program may use at most 192 MiB of HBM per device.

```python
import jax
import jax.numpy as jnp
from jax import lax

B = 128
KB = 28
BR = 4
NB = 256
NPR = 28


def slab_pattern(key, slab_number):
    slab_count = NB // BR
    peer_key, shift_key, row_key = jax.random.split(key, 3)
    others = (slab_number + 1 + jax.random.permutation(peer_key, slab_count - 1)) % slab_count
    position = jnp.arange(NPR, dtype=jnp.int32)
    peer_slot = position % (slab_count - 1)
    depth_level = position // (slab_count - 1)
    shifts = jax.random.randint(shift_key, (slab_count - 1,), 0, BR)
    pool_rows = others[peer_slot] * BR + (depth_level + shifts[peer_slot]) % BR
    own_rows = slab_number * BR + jnp.arange(BR, dtype=jnp.int32)

    def one_row(row_seed):
        pick_key, order_key = jax.random.split(row_seed)
        chosen = pool_rows[jax.random.permutation(pick_key, NPR)[:KB - BR]]
        listed = jnp.concatenate([own_rows, chosen])
        return listed[jax.random.permutation(order_key, KB)]
    return jax.vmap(one_row)(jax.random.split(row_key, BR))


def draw_columns(key, part):
    key = jax.random.fold_in(key, 11)
    slab_count = NB // BR
    slab_seeds = jax.random.split(key, slab_count)
    pattern = jax.vmap(slab_pattern)(slab_seeds, jnp.arange(slab_count, dtype=jnp.int32))
    return pattern.reshape(NB, KB).astype(jnp.int32)


def touch_ends(array, stream_key, low, high):
    index_at = [jax.random.randint(jax.random.fold_in(stream_key, axis), (), 0, length) for axis, length in enumerate(array.shape)]
    main_axis = array.shape.index(max(array.shape))
    neighbour = index_at[:main_axis] + [(index_at[main_axis] + 1) % array.shape[main_axis]] + index_at[main_axis + 1:]
    return array.at[tuple(index_at)].set(low).at[tuple(neighbour)].set(high)


def levels(stream_key, shape, cuts, smallest, largest):
    def one(dim, parts):
        heights = jax.random.uniform(jax.random.fold_in(jax.random.fold_in(stream_key, 6), dim), (parts,), jnp.float32, smallest / len(cuts), largest / len(cuts))
        return jnp.repeat(jnp.exp(heights), shape[dim] // parts).reshape((-1,) + (1,) * (len(shape) - dim - 1))

    loudness = one(*cuts[0])
    for cut in cuts[1:]:
        loudness = loudness * one(*cut)
    return loudness


def noise(stream_key, shape, width, most, cuts=(), held_as=jnp.bfloat16):
    drawn = width * jax.random.normal(stream_key, shape, jnp.float32)
    if cuts:
        drawn = drawn * levels(stream_key, shape, cuts, -0.22, 0.18)
    return jnp.clip(drawn, -most, most).astype(held_as)


def setup_inputs(seed: int = 0) -> dict:
    seeds = jax.random.split(jax.random.key(seed), 4)
    blocks = noise(seeds[0], (NB, KB, B, B), 0.25, 1.5, ((0, 64), (1, 4)))
    nonzero = touch_ends((jax.random.randint(seeds[1], (NB, KB), 0, 4) < 3).astype(jnp.int32), jax.random.fold_in(seeds[1], 1), 0, 1)
    columns = draw_columns(jax.random.fold_in(seeds[3], 71), 0)
    return dict(blocks=blocks, nonzero=nonzero, columns=columns)


def reference(blocks, nonzero, columns):
    masked = blocks * nonzero[:, :, None, None].astype(jnp.bfloat16)
    slot_ids = jnp.arange(KB, dtype=jnp.int32)

    def one_row(inputs):
        row_blocks, row_cols = inputs
        inner_cols = columns[row_cols]
        matches = inner_cols[:, :, None] == row_cols[None, None, :]
        present = jnp.any(matches, axis=1)
        position = jnp.sum(jnp.where(matches, slot_ids[None, :, None], 0), axis=1).astype(jnp.int32)
        picked = masked[row_cols[:, None], position]
        picked = picked * present[:, :, None, None].astype(jnp.bfloat16)
        product_sum = jnp.einsum("tab,tvbc->vac", row_blocks.astype(jnp.float32), picked.astype(jnp.float32))
        return product_sum.astype(jnp.bfloat16)

    return lax.map(one_row, (masked, columns))
```

```python
import functools

import jax
import jax.numpy as jnp
from jax import lax
from jax.experimental import pallas as pl
from jax.experimental.pallas import tpu as pltpu
from jax.sharding import Mesh
from jax.sharding import PartitionSpec as P

BF = jnp.bfloat16
F32 = jnp.float32
I32 = jnp.int32

NX, NZ, NC, NY = 4, 8, 2, 4
ROWS, SLOTS, SIDE = 256, 28, 128
HEIGHT, QUARTER = 4, 7
SLABS = ROWS // HEIGHT
CHIP_ENTRIES = NC * HEIGHT * SLOTS
CUT = SIDE // (NC * NY)
WIDE = SIDE // NY
CAP_Z = 44
CAP_X = 44
LISTED = 48
LIST_FAR = NX * CAP_X
GROUP = 8
FAR_GROUP = 4
ROWS_AT_ONCE = 4
HEIGHT_2 = NC * HEIGHT
OUT_COLS = 72
ZERO_BLOCK = NY * HEIGHT * QUARTER
VMEM_LIMIT = 48 * 1024 * 1024
ROW_AXES = ("x", "z", "core")


def vmem():
    return pl.BlockSpec(memory_space=pltpu.VMEM)


def smem():
    return pl.BlockSpec(memory_space=pltpu.SMEM)


def params():
    return pltpu.CompilerParams(vmem_limit_bytes=VMEM_LIMIT)


def cost(flops, moved):
    return pl.CostEstimate(flops=flops, bytes_accessed=moved, transcendentals=0)


def prepare_kernel(position_ref, keep_ref, blocks_ref, whole_ref, cuts_ref):
    part = position_ref[3]
    for row in range(HEIGHT):
        for slot in range(QUARTER):
            block = blocks_ref[row, slot]
            turned = jnp.where(keep_ref[row, slot] != 0, block, jnp.zeros_like(block)).T
            whole_ref[row, slot] = turned
            chip = (row + slot + part * QUARTER) & (NX - 1)
            for piece in range(NC * NY):
                cuts_ref[chip * (NC * NY) + piece, slot] = turned[piece * CUT : (piece + 1) * CUT]
    rows = iota((CUT, SIDE), 0) - position_ref[2] * HEIGHT
    lanes = iota((CUT, SIDE), 1) - position_ref[0] * SLOTS - part * QUARTER
    flags = jnp.zeros((CUT, SIDE), F32)
    for row in range(HEIGHT):
        for slot in range(QUARTER):
            here = (rows == row) & (lanes == slot)
            flags = jnp.where(here & (keep_ref[row, slot] != 0), 1.0, flags)
    for peer in range(NX * NC * NY):
        cuts_ref[peer, QUARTER] = flags.astype(BF)


def prepare(position, nonzero, blocks):
    return pl.pallas_call(
        prepare_kernel,
        out_shape=(
            jax.ShapeDtypeStruct((HEIGHT, QUARTER, SIDE, SIDE), BF),
            jax.ShapeDtypeStruct((NX * NC * NY, QUARTER + 1, CUT, SIDE), BF),
        ),
        in_specs=[smem(), smem(), vmem()],
        out_specs=(vmem(), vmem()),
        compiler_params=params(),
        name="prepare",
    )(position, nonzero, blocks)


def pack_kernel(unroll, index_ref, source_ref, *refs):
    out_ref = refs[-1]
    peers, count = out_ref.shape[0], out_ref.shape[1] // unroll * unroll
    for peer in range(peers):

        def step(i, carry):
            for j in range(unroll):
                at = i * unroll + j
                out_ref[peer, at] = source_ref[index_ref[0, peer * LISTED + at]]
            return carry

        lax.fori_loop(0, count // unroll, step, 0)
        if len(refs) > 1:
            out_ref[peer, count] = refs[0][peer]


def pack(index, source, peers, count, *notes):
    return pl.pallas_call(
        functools.partial(pack_kernel, 4),
        out_shape=jax.ShapeDtypeStruct((peers, count, CUT, SIDE), BF),
        in_specs=[smem(), vmem()] + [vmem()] * len(notes),
        out_specs=vmem(),
        compiler_params=params(),
        name="pack",
    )(index, source, *notes)


def own_block(whole_ref, place, rows):
    value = whole_ref[jnp.minimum(place, ZERO_BLOCK - 1), rows, :]
    return jnp.where(place < ZERO_BLOCK, value, jnp.zeros_like(value))


def out_place(place):
    return (place // QUARTER) % HEIGHT, place // (QUARTER * HEIGHT) * QUARTER + place % QUARTER


def own_kernel(
    plan_ref,
    whole_ref,
    out_ref,
    total,
    panel,
    near,
):
    first = pl.multiple_of(plan_ref[15, 0] * WIDE, WIDE)
    for inner in range(HEIGHT):
        for member in range(HEIGHT):
            panel[pl.ds(inner * SIDE, SIDE), pl.ds(member * SIDE, SIDE)] = own_block(
                whole_ref, plan_ref[9 + member, inner], pl.ds(0, SIDE)
            )

    def step(group, carry):
        for at in range(GROUP):
            for inner in range(HEIGHT):
                near[pl.ds(at * WIDE, WIDE), pl.ds(inner * SIDE, SIDE)] = own_block(
                    whole_ref, plan_ref[4 + inner, group * GROUP + at], pl.ds(first, WIDE)
                )
        value = jnp.dot(near[...], panel[...], preferred_element_type=F32)
        total[pl.ds(group * GROUP, GROUP)] = value.reshape(GROUP, WIDE, HEIGHT * SIDE)
        return carry

    lax.fori_loop(0, plan_ref[15, 1], step, 0)
    for place in range(ZERO_BLOCK):
        member, slot = out_place(place)
        column = plan_ref[8, member * (128 // HEIGHT) + slot]
        out_ref[place] = total[column, :, pl.ds(member * SIDE, SIDE)]


def own_sums(lists, whole):
    flops = 2 * 32 * WIDE * (HEIGHT * SIDE) ** 2
    return pl.pallas_call(
        own_kernel,
        out_shape=jax.ShapeDtypeStruct((ZERO_BLOCK, WIDE, SIDE), F32),
        in_specs=[smem(), vmem()],
        out_specs=vmem(),
        scratch_shapes=[
            pltpu.VMEM((OUT_COLS, WIDE, HEIGHT * SIDE), F32),
            pltpu.VMEM((HEIGHT * SIDE, HEIGHT * SIDE), BF),
            pltpu.VMEM((GROUP * WIDE, HEIGHT * SIDE), BF),
        ],
        compiler_params=params(),
        cost_estimate=cost(flops, 3 * ZERO_BLOCK * SIDE * SIDE),
        name="own_sums",
    )(lists, whole)


def far_kernel(
    own_ref,
    plan_ref,
    whole_ref,
    far_ref,
    near_ref,
    out_ref,
    total,
):
    def clear(group, carry):
        total[pl.ds(group * GROUP, GROUP)] = jnp.zeros((GROUP, WIDE, HEIGHT * SIDE), F32)
        return carry

    lax.fori_loop(0, own_ref[15, 1], clear, 0)

    def product(named, offset):
        begin = plan_ref[2, named]
        length = plan_ref[3, named]
        right = jnp.concatenate(
            [
                own_block(whole_ref, own_ref[member, named], pl.ds(0, SIDE))
                for member in range(HEIGHT)
            ],
            axis=1,
        )
        pieces, columns = [], []
        for at in range(FAR_GROUP):
            place = jnp.minimum(begin + offset + at, LIST_FAR - 1)
            index = plan_ref[0, place]
            for half in range(NC):
                pieces.append(far_ref[index + half * CAP_X])
            columns.append(jnp.where(offset + at < length, plan_ref[1, place], OUT_COLS))
        value = jnp.dot(jnp.concatenate(pieces, axis=0), right, preferred_element_type=F32)
        return value, columns

    def add(value, columns):
        for at, column in enumerate(columns):
            total[column] = total[column] + value[at * WIDE : (at + 1) * WIDE]

    def first_step(step, carry):
        done = [product(step * ROWS_AT_ONCE + at, 0) for at in range(ROWS_AT_ONCE)]
        for value, columns in done:
            add(value, columns)
        return carry

    named_rows = own_ref[15, 2]
    lax.fori_loop(0, (named_rows + ROWS_AT_ONCE - 1) // ROWS_AT_ONCE, first_step, 0)

    def rest(named, carry):
        def rest_step(step, inner_carry):
            add(*product(named, step * FAR_GROUP))
            return inner_carry

        lax.fori_loop(1, (plan_ref[3, named] + FAR_GROUP - 1) // FAR_GROUP, rest_step, 0)
        return carry

    lax.fori_loop(0, named_rows, rest, 0)

    for place in range(ZERO_BLOCK):
        member, slot = out_place(place)
        column = own_ref[8, member * (128 // HEIGHT) + slot]
        value = total[column, :, pl.ds(member * SIDE, SIDE)] + near_ref[place]
        out_ref[place] = value.astype(BF)


def far_sums(own_lists, far_lists, whole, far, near):
    return pl.pallas_call(
        far_kernel,
        out_shape=jax.ShapeDtypeStruct((ZERO_BLOCK, WIDE, SIDE), BF),
        in_specs=[smem(), smem(), vmem(), vmem(), vmem()],
        out_specs=vmem(),
        scratch_shapes=[pltpu.VMEM((OUT_COLS + 1, WIDE, HEIGHT * SIDE), F32)],
        compiler_params=params(),
        name="far_sums",
    )(own_lists, far_lists, whole, far, near)


def finish_kernel(cuts_ref, out_ref):
    for row in range(HEIGHT):
        for slot in range(QUARTER):
            turned = jnp.concatenate([cuts_ref[part, row, slot] for part in range(NY)], axis=0)
            out_ref[row, slot] = turned.T


def finish(cuts):
    return pl.pallas_call(
        finish_kernel,
        out_shape=jax.ShapeDtypeStruct((HEIGHT, QUARTER, SIDE, SIDE), BF),
        in_specs=[vmem()],
        out_specs=vmem(),
        compiler_params=params(),
        name="finish",
    )(cuts)


def iota(shape, axis):
    return lax.broadcasted_iota(I32, shape, axis)


def dot(a, b):
    return jnp.dot(a.astype(BF), b.astype(BF), preferred_element_type=F32)


def dot_rows(a, b):
    return lax.dot_general(
        a.astype(BF), b.astype(BF), (((1,), (1,)), ((), ())), preferred_element_type=F32
    )


def earlier(size, lower, group=None, key=None):
    row, column = iota((size, size), 0), iota((size, size), 1)
    first, second = (row, column) if key is None else (key(row), key(column))
    pairs = first > second if lower else first < second
    if group is not None:
        pairs = pairs & (group(row) == group(column))
    return pairs.astype(F32)


def places(need, order, group=None, key=None):
    lower = earlier(need.shape[0], True, group, key)
    return dot(need, order) + jnp.sum(dot(lower, need), axis=1, keepdims=True)


def select(need, groups, group, capacity, order):
    size, lanes = need.shape
    place = places(need, order, group)
    held = dot_rows(jnp.ones((8, lanes), F32), need)
    first = dot(held, earlier(size, False, group))[0:1]
    last = first + held[0:1]
    index = iota((groups * capacity, 1), 0)
    number = jnp.zeros_like(index)
    for boundary in range(1, groups):
        number = number + (index >= boundary * capacity).astype(I32)
    slot = (index - number * capacity).astype(F32)
    chosen = (first <= slot) & (slot < last)
    if group is not None:
        chosen = chosen & (number == group(iota((groups * capacity, size), 1)))
    chosen = chosen.astype(F32)
    code = jnp.where((need > 0) & (place < capacity), place, 250.0)
    return chosen, dot(chosen, code) == slot


def values_of(chosen, hit, value):
    value = jnp.where(hit, dot(chosen, value), 0.0)
    return dot_rows(jnp.ones((8, value.shape[1]), F32), value)


def quarter_of(slot):
    return sum((slot >= bound * QUARTER).astype(I32) for bound in range(1, NY))


def kept_blocks(slot, flags, begin):
    kept = jnp.zeros(slot.shape, F32)
    for number in range(SLOTS):
        at = begin + number
        kept = jnp.where(slot == number, flags[:, at : at + 1], kept)
    return kept


def plane_of(row):
    return (row // HEIGHT_2) % NZ


def pattern_kernel(columns_ref, slots_ref, union_ref, far_ref):
    step = 64
    for begin in range(0, ROWS, step):
        column = iota((step, ROWS), 1)
        found = jnp.full((step, ROWS), -1, I32)
        for slot in range(SLOTS):
            at = columns_ref[begin : begin + step, slot : slot + 1]
            found = jnp.where(at == column, slot, found)
        slots_ref[begin : begin + step, :] = found
    names = (slots_ref[...] >= 0).astype(F32)
    mine = iota((128, ROWS), 1) // HEIGHT == iota((128, ROWS), 0)
    union = (dot(mine.astype(F32), names) > 0).astype(F32)
    union_ref[...] = union
    far_ref[...] = jnp.where(mine, 0.0, union).T


def pattern(columns):
    return pl.pallas_call(
        pattern_kernel,
        out_shape=(
            jax.ShapeDtypeStruct((ROWS, ROWS), I32),
            jax.ShapeDtypeStruct((128, ROWS), F32),
            jax.ShapeDtypeStruct((ROWS, 128), F32),
        ),
        in_specs=[vmem()],
        out_specs=(vmem(), vmem(), vmem()),
        compiler_params=params(),
        cost_estimate=cost(2 * SLOTS * ROWS**3 // 4, 8 * ROWS**2),
        name="pattern",
    )(columns)


def send_kernel(position_ref, slots_ref, union_ref, far_ref, near_ref, send_ref, notes_ref):
    x, z = position_ref[0], position_ref[1]
    flags = functools.reduce(
        jnp.add,
        [near_ref[peer * (QUARTER + 1) + QUARTER].astype(F32) for peer in range(NX * NC * NY)],
    )[0:HEIGHT_2]
    plane = NX * HEIGHT_2
    slots, named_by, kept = [], [], []
    for number in range(NX):
        rows = pl.ds(pl.multiple_of((number * NZ + z) * HEIGHT_2, HEIGHT_2), HEIGHT_2)
        slots.append(slots_ref[rows, :])
        named_by.append(far_ref[rows, :])
        kept.append(kept_blocks(slots[-1], flags, number * SLOTS))
    slot = jnp.concatenate(slots, axis=0)
    row = iota(slot.shape, 0)
    mine = jnp.where(((row + slot) & (NX - 1)) == x, jnp.concatenate(kept, axis=0), 0.0)
    quarter = quarter_of(slot)
    held = ((row // HEIGHT_2 * NY + quarter) * NC + (row // HEIGHT) % NC) * (QUARTER + 1)
    held = (held + slot - quarter * QUARTER).astype(F32) * mine

    order = earlier(ROWS, False)
    union = union_ref[...]
    shape = (NZ * plane, 128)
    to = (iota(shape, 1) // NC) % NZ == iota(shape, 0) // plane
    named_by = jnp.concatenate(named_by * NZ, axis=0)
    wanted = dot(jnp.where(to, named_by, 0.0), union) > 0
    need = jnp.where(wanted, jnp.concatenate([mine] * NZ, axis=0), 0.0)
    chosen, hit = select(need, NZ, lambda index: index // plane, LISTED, order)
    held = jnp.concatenate([held] * NZ, axis=0)
    send_ref[...] = values_of(chosen, hit, held)[0:1].astype(I32)
    asked = dot(chosen, named_by) * dot_rows(hit.astype(F32), union)
    place = iota((8, LISTED), 1)
    for number in range(NZ):
        target = iota((NX * NC, 128), 0)
        slab = (target // NC * NZ + number) * NC + target % NC
        choice = (iota((NX * NC, 128), 1) == slab).astype(F32)
        part = dot_rows(choice, asked[number * LISTED : (number + 1) * LISTED])
        part = jnp.where(place < CAP_Z, part, 0.0)
        part = jnp.concatenate([part, jnp.zeros((8, SIDE - LISTED), F32)], axis=1)
        notes_ref[number] = jnp.concatenate([flags, part], axis=0).astype(BF)


def send_lists(position, slots, union, far, near):
    return pl.pallas_call(
        send_kernel,
        out_shape=(
            jax.ShapeDtypeStruct((1, NZ * LISTED), I32),
            jax.ShapeDtypeStruct((NZ, CUT, SIDE), BF),
        ),
        in_specs=[smem()] + [vmem()] * 4,
        out_specs=(vmem(), vmem()),
        compiler_params=params(),
        name="send_lists",
    )(position, slots, union, far, near)


def route_kernel(along_ref, out_ref):
    asked = jnp.concatenate(
        [along_ref[plane, CAP_Z].astype(F32)[CUT // 2 :] for plane in range(NZ)], axis=0
    )
    shape = asked.shape
    chosen, hit = select(asked, 8, lambda index: index & 7, LISTED, earlier(SIDE, False))
    source = values_of(chosen, hit, (iota(shape, 0) // 8).astype(F32))
    place = values_of(chosen, hit, iota(shape, 1).astype(F32))
    out_ref[...] = (source * (CAP_Z + 1) + place)[0:1].astype(I32)


def route(along):
    return pl.pallas_call(
        route_kernel,
        out_shape=jax.ShapeDtypeStruct((1, NX * NC * LISTED), I32),
        in_specs=[vmem()],
        out_specs=vmem(),
        compiler_params=params(),
        name="route",
    )(along)


def own_plan_kernel(position_ref, slots_ref, union_ref, out_ref):
    x, z, core, part = (position_ref[i] for i in range(4))
    chip = x * NZ + z
    slab = chip * NC + core
    order = earlier(ROWS, False)
    out_ref[...] = jnp.zeros_like(out_ref)
    mine = union_ref[pl.ds(slab, 1), :]
    rank = dot(jnp.broadcast_to(mine, (8, ROWS)), order)

    both = slots_ref[pl.ds(pl.multiple_of(chip * HEIGHT_2, HEIGHT_2), HEIGHT_2), :]
    swapped = jnp.concatenate([both[HEIGHT:], both[:HEIGHT]], axis=0)
    slot = jnp.where(core == 0, both, swapped)
    quarter = quarter_of(slot)
    held = (quarter * HEIGHT + iota(slot.shape, 0)) * QUARTER + slot - quarter * QUARTER
    held = jnp.where(slot >= 0, held - ZERO_BLOCK, 0).astype(F32)

    every = iota((1, ROWS), 1)
    named = jnp.where(every // HEIGHT == slab, 0.0, mine)
    position = dot(jnp.broadcast_to(named, (8, ROWS)), order)[0:1]
    number = iota((SLABS, ROWS), 0).astype(F32)
    chosen = ((position == number) & (named > 0)).astype(F32)
    out_ref[0:4, 0:SLABS] = dot_rows(held, chosen)[0:HEIGHT].astype(I32) + ZERO_BLOCK

    number = iota((OUT_COLS, ROWS), 0).astype(F32)
    chosen = ((rank[0:1] == number) & (mine > 0)).astype(F32)
    out_ref[4:8, 0:OUT_COLS] = dot_rows(held, chosen)[0:HEIGHT].astype(I32) + ZERO_BLOCK
    wide = 128 // HEIGHT
    chosen = jnp.concatenate(
        [slot[i : i + 1] == iota((wide, ROWS), 0) for i in range(HEIGHT)], axis=0
    )
    out_ref[8:9, 0:128] = dot_rows(rank, chosen.astype(F32))[0:1].astype(I32)
    chosen = (iota((8, ROWS), 1) == iota((8, ROWS), 0) + slab * HEIGHT).astype(F32)
    out_ref[9:13, 0:8] = dot_rows(held, chosen)[0:HEIGHT].astype(I32) + ZERO_BLOCK
    groups = ((jnp.sum(mine) + (GROUP - 1)) * (1.0 / GROUP)).astype(I32)
    lane = iota((1, 128), 1)
    scalars = jnp.where(lane == 0, part, 0)
    scalars = jnp.where(lane == 1, groups, scalars)
    out_ref[15:16, :] = jnp.where(lane == 2, jnp.sum(named).astype(I32), scalars)


def own_plan(position, slots, union):
    return pl.pallas_call(
        own_plan_kernel,
        out_shape=jax.ShapeDtypeStruct((16, 128), I32),
        in_specs=[smem(), vmem(), vmem()],
        out_specs=vmem(),
        compiler_params=params(),
        cost_estimate=cost(ROWS**3, 4 * ROWS**2),
        name="own_plan",
    )(position, slots, union)


def far_plan_kernel(position_ref, slots_ref, union_ref, far_ref, along_ref, out_ref, kept_ref):
    x, z, core = (position_ref[i] for i in range(3))
    slab = (x * NZ + z) * NC + core
    order = earlier(ROWS, False)
    out_ref[...] = jnp.zeros_like(out_ref)
    for plane in range(NZ):
        flags = along_ref[plane, CAP_Z].astype(F32)[0:HEIGHT_2]
        for number in range(NX):
            begin = (number * NZ + plane) * HEIGHT_2
            rows = slice(begin, begin + HEIGHT_2)
            kept_ref[rows, :] = kept_blocks(slots_ref[rows, :], flags, number * SLOTS)
    kept = kept_ref[...]
    far, union = far_ref[...], union_ref[...]
    dealt = (iota(kept.shape, 0) + slots_ref[...]) & (NX - 1)

    mine = union_ref[pl.ds(slab, 1), :]
    rank = dot(jnp.broadcast_to(mine, (8, ROWS)), order)[0:1]
    named = jnp.sum(jnp.where(iota(far.shape, 1) == slab, far, 0.0), axis=1, keepdims=True)
    need = kept * named * mine
    place = jnp.zeros((ROWS, ROWS), F32)
    for number in range(NX):
        inside = places(
            jnp.where(dealt == number, need, 0.0),
            order,
            key=lambda row: plane_of(row) * ROWS + row,
        )
        inside = jnp.minimum(inside, CAP_X - 1.0) + number * CAP_X
        place = jnp.where(dealt == number, inside, place)
    chosen, hit = select(need, 1, None, LIST_FAR, order)
    place = values_of(chosen, hit, place)[0:1].astype(I32)
    skipped = sum((place >= bound * CAP_X).astype(I32) for bound in range(1, NX))
    out_ref[0:1, 0:LIST_FAR] = place + skipped * ((NC - 1) * CAP_X)
    column = values_of(chosen, hit, jnp.broadcast_to(rank, (ROWS, ROWS)))
    out_ref[1:2, 0:LIST_FAR] = column[0:1].astype(I32)

    count = dot_rows(jnp.ones((8, ROWS), F32), need)
    start = jnp.minimum(dot(count, order), 250.0)
    row = jnp.where(iota((1, ROWS), 1) // HEIGHT == slab, 0.0, mine)
    position = dot(jnp.broadcast_to(row, (8, ROWS)), order)[0:1]
    number = iota((SLABS, ROWS), 0).astype(F32)
    chosen = ((position == number) & (row > 0)).astype(F32)
    out_ref[2:3, 0:SLABS] = dot_rows(start, chosen)[0:1].astype(I32)
    out_ref[3:4, 0:SLABS] = dot_rows(count, chosen)[0:1].astype(I32)

    in_plane = (plane_of(iota((8, ROWS), 1)) == iota((8, ROWS), 0)).astype(F32)
    sharing = [jnp.where(dealt == number, kept, 0.0) for number in range(NX)]
    most_x = jnp.float32(0)
    for names in sharing:
        most_x = jnp.maximum(most_x, jnp.max(jnp.sum(dot_rows(names, union) * far, axis=0)))
    most_z = jnp.float32(0)
    for to in range(NZ):
        part_of = (iota((ROWS, 128), 1) // NC) % NZ == to
        wanted = dot(jnp.where(part_of, far, 0.0), union) > 0
        for names in sharing:
            need = jnp.where(wanted, names, 0.0)
            most_z = jnp.maximum(most_z, jnp.max(jnp.sum(dot(in_plane, need), axis=1)))
    fits = (most_x <= CAP_X) & (most_z <= CAP_Z)
    out_ref[4:5, :] = jnp.zeros((1, 256), I32) + fits.astype(I32)


def far_plan(position, slots, union, far, along):
    return pl.pallas_call(
        far_plan_kernel,
        out_shape=jax.ShapeDtypeStruct((8, 256), I32),
        in_specs=[smem()] + [vmem()] * 4,
        out_specs=vmem(),
        scratch_shapes=[pltpu.VMEM((ROWS, ROWS), F32)],
        compiler_params=params(),
        cost_estimate=cost(2 * 60 * ROWS**3, 8 * ROWS**2),
        name="far_plan",
    )(position, slots, union, far, along)


def dense(blocks, nonzero, columns):
    slab = lax.axis_index(ROW_AXES)
    part = lax.axis_index("col")
    masked = blocks * nonzero[:, :, None, None].astype(BF)
    slab_ids = jnp.arange(SLABS, dtype=I32)
    local_rows = jnp.arange(HEIGHT, dtype=I32)
    grouped = columns.reshape(SLABS, HEIGHT * SLOTS)
    targets = slab * HEIGHT + local_rows
    wanted = jnp.any(grouped[:, :, None] == targets[None, None, :], axis=1)
    wanted = wanted & (slab_ids != slab)[:, None]
    picked = jnp.sum(jnp.where(wanted, local_rows, 0), axis=1)
    filled = jnp.any(wanted, axis=1)
    outgoing = jnp.where(filled[:, None, None, None], masked[picked], jnp.zeros((), BF))
    incoming = lax.all_to_all(outgoing, ROW_AXES, split_axis=0, concat_axis=0, tiled=True)
    row_table = jnp.concatenate([incoming, masked], axis=0)
    own_cols = lax.dynamic_slice_in_dim(columns, slab * HEIGHT, HEIGHT, 0)
    source = own_cols // HEIGHT
    row_index = jnp.where(source == slab, SLABS + own_cols % HEIGHT, source)
    far_cols = columns[own_cols]
    far_quarter = lax.dynamic_slice_in_dim(far_cols, part * QUARTER, QUARTER, 2)
    whole = lax.all_gather(masked, "col", axis=1, tiled=True)
    results = []
    for member in range(HEIGHT):
        match = far_quarter[member][:, :, None] == own_cols[member][None, None, :]
        products = jnp.einsum(
            "tab,tubc->tuac", whole[member], row_table[row_index[member]],
            preferred_element_type=F32,
        )
        summed = lax.dot_general(
            match.astype(F32).reshape(SLOTS * QUARTER, SLOTS),
            products.reshape(SLOTS * QUARTER, SIDE * SIDE),
            (((0,), (0,)), ((), ())),
            precision=lax.Precision.HIGHEST,
            preferred_element_type=F32,
        )
        results.append(summed.reshape(SLOTS, SIDE, SIDE))
    square = lax.psum_scatter(jnp.stack(results), "col", scatter_dimension=1, tiled=True)
    return square.astype(BF)


def shards(blocks, nonzero, columns):
    position = jnp.stack([lax.axis_index(name) for name in ROW_AXES + ("col",)])
    turned, cuts = prepare(position, nonzero, blocks)
    cuts, names = lax.optimization_barrier((cuts, columns))
    slots, union, named_by = pattern(names)
    near = lax.all_to_all(cuts, ("x", "col", "core"), split_axis=0, concat_axis=0, tiled=True)
    near, turned = lax.optimization_barrier((near, turned))
    whole = lax.all_gather(turned, "col", axis=0, tiled=False)
    whole = whole.reshape(ZERO_BLOCK, SIDE, SIDE)
    near = near.reshape(NX * NC * NY * (QUARTER + 1), CUT, SIDE)
    send, notes = send_lists(position, slots, union, named_by, near)
    packed = pack(send, near, NZ, CAP_Z + 1, notes)
    packed, slots = lax.optimization_barrier((packed, slots))
    along = lax.all_to_all(packed, "z", split_axis=0, concat_axis=0, tiled=True)
    own_lists = own_plan(position, slots, union)
    packed = pack(route(along), along.reshape(-1, CUT, SIDE), NX * NC, CAP_X)
    packed, notes = lax.optimization_barrier((packed, along))
    far = lax.all_to_all(packed, ("x", "core"), split_axis=0, concat_axis=0, tiled=True)
    far = far.reshape(NX * NC * CAP_X, CUT, SIDE)
    far_lists = far_plan(position, slots, union, named_by, notes)
    result = far_sums(own_lists, far_lists, whole, far, own_sums(own_lists, whole))
    result = result.reshape(NY, HEIGHT, QUARTER, WIDE, SIDE)
    result = lax.all_to_all(result, "col", split_axis=0, concat_axis=0, tiled=True)
    square = finish(result)
    return lax.cond(
        far_lists[4, 0] != 0,
        lambda value, *_: value,
        lambda _, *inputs: dense(*inputs),
        square,
        blocks,
        nonzero,
        columns,
    )


def solution(mesh):
    fine = Mesh(mesh.devices.reshape(NX, NZ, NC, NY), ROW_AXES + ("col",))
    spec = P(ROW_AXES, "col", None, None)
    return jax.shard_map(
        shards,
        mesh=fine,
        in_specs=(spec, P(ROW_AXES, "col"), P()),
        out_specs=spec,
        check_vma=False,
    )
```

```python
import functools

import jax
import jax.numpy as jnp
from jax import lax
from jax.experimental import pallas as pl
from jax.experimental.pallas import tpu as pltpu
from jax.sharding import Mesh
from jax.sharding import PartitionSpec as P

BF = jnp.bfloat16
F32 = jnp.float32
I32 = jnp.int32

NX, NZ, NC, NY = 4, 8, 2, 4
ROWS, SLOTS, SIDE = 256, 28, 128
HEIGHT, QUARTER = 4, 7
SLABS = ROWS // HEIGHT
PEERS = NX * NC * NY
HELD = 32
ENTRIES = PEERS * HELD
PIECE = SIDE * SIDE // PEERS
WIDE = SIDE // NY
TARGETS = NX * NC
CAP_Z = 124
ROWS_Z = 128
CAP_X = 120
GROUP = 8
FAR_GROUP = 4
ROWS_AT_ONCE = 4
HEIGHT_2 = NC * HEIGHT
OUT_COLS = 72
ZERO_BLOCK = NY * HEIGHT * QUARTER
VMEM_LIMIT = 48 * 1024 * 1024
ROW_AXES = ("x", "z", "core")


def vmem():
    return pl.BlockSpec(memory_space=pltpu.VMEM)


def smem():
    return pl.BlockSpec(memory_space=pltpu.SMEM)


def params():
    return pltpu.CompilerParams(vmem_limit_bytes=VMEM_LIMIT)


def cost(flops, moved):
    return pl.CostEstimate(flops=flops, bytes_accessed=moved, transcendentals=0)


def prepare_kernel(position_ref, keep_ref, blocks_ref, whole_ref, cuts_ref, rows_ref):
    x, core, part = position_ref[0], position_ref[2], position_ref[3]
    lanes = iota((8, ENTRIES), 1) - ((part * NX + x) * NC + core) * HELD
    flags = jnp.zeros((8, ENTRIES), F32)
    for row in range(HEIGHT):
        for slot in range(QUARTER):
            number = row * QUARTER + slot
            keep = keep_ref[row, slot] != 0
            flags = jnp.where((lanes == number) & keep, 1.0, flags)
            block = blocks_ref[row, slot].astype(F32)
            turned = jnp.where(keep, block, jnp.zeros_like(block)).T
            whole_ref[row, slot] = turned.astype(BF)
            for quarter in range(NY):
                for part_of in range(NY):
                    begin = quarter * WIDE + part_of * TARGETS
                    rows = pl.ds(quarter * TARGETS * HELD + number, TARGETS, stride=HELD)
                    rows_ref[part_of, rows, :] = turned[begin : begin + TARGETS]
    for begin in range(0, PEERS, 8):
        for part_of in range(NY):
            for extra in range(HELD - SLOTS):
                rows = pl.ds(begin * HELD + SLOTS + extra, 8, stride=HELD)
                at = extra * PIECE + part_of * SIDE
                value = flags[:, at : at + SIDE] if extra < 2 else jnp.zeros((8, SIDE), F32)
                rows_ref[part_of, rows, :] = value
    for peer in range(PEERS):
        rows = pl.ds(peer * HELD, HELD)
        cuts_ref[peer] = jnp.concatenate(
            [rows_ref[part_of, rows, :] for part_of in range(NY)], axis=1
        ).astype(BF)


def prepare(position, nonzero, blocks):
    return pl.pallas_call(
        prepare_kernel,
        out_shape=(
            jax.ShapeDtypeStruct((HEIGHT, QUARTER, SIDE, SIDE), BF),
            jax.ShapeDtypeStruct((PEERS, HELD, PIECE), BF),
        ),
        in_specs=[smem(), smem(), vmem()],
        out_specs=(vmem(), vmem()),
        scratch_shapes=[pltpu.VMEM((NY, ENTRIES, SIDE), F32)],
        compiler_params=params(),
        name="prepare",
    )(position, nonzero, blocks)


def own_block(whole_ref, place, rows):
    value = whole_ref[jnp.minimum(place, ZERO_BLOCK - 1), rows, :]
    return jnp.where(place < ZERO_BLOCK, value, jnp.zeros_like(value))


def out_place(place):
    return (place // QUARTER) % HEIGHT, place // (QUARTER * HEIGHT) * QUARTER + place % QUARTER


def own_kernel(
    plan_ref,
    whole_ref,
    out_ref,
    total,
    panel,
    near,
):
    first = pl.multiple_of(plan_ref[15, 0] * WIDE, WIDE)
    for inner in range(HEIGHT):
        for member in range(HEIGHT):
            panel[pl.ds(inner * SIDE, SIDE), pl.ds(member * SIDE, SIDE)] = own_block(
                whole_ref, plan_ref[9 + member, inner], pl.ds(0, SIDE)
            )

    def step(group, carry):
        for at in range(GROUP):
            for inner in range(HEIGHT):
                near[pl.ds(at * WIDE, WIDE), pl.ds(inner * SIDE, SIDE)] = own_block(
                    whole_ref, plan_ref[4 + inner, group * GROUP + at], pl.ds(first, WIDE)
                )
        value = jnp.dot(near[...], panel[...], preferred_element_type=F32)
        total[pl.ds(group * GROUP, GROUP)] = value.reshape(GROUP, WIDE, HEIGHT * SIDE)
        return carry

    lax.fori_loop(0, plan_ref[15, 1], step, 0)
    for place in range(ZERO_BLOCK):
        member, slot = out_place(place)
        column = plan_ref[8, member * (128 // HEIGHT) + slot]
        out_ref[place] = total[column, :, pl.ds(member * SIDE, SIDE)]


def own_sums(lists, whole):
    flops = 2 * 32 * WIDE * (HEIGHT * SIDE) ** 2
    return pl.pallas_call(
        own_kernel,
        out_shape=jax.ShapeDtypeStruct((ZERO_BLOCK, WIDE, SIDE), F32),
        in_specs=[smem(), vmem()],
        out_specs=vmem(),
        scratch_shapes=[
            pltpu.VMEM((OUT_COLS, WIDE, HEIGHT * SIDE), F32),
            pltpu.VMEM((HEIGHT * SIDE, HEIGHT * SIDE), BF),
            pltpu.VMEM((GROUP * WIDE, HEIGHT * SIDE), BF),
        ],
        compiler_params=params(),
        cost_estimate=cost(flops, 3 * ZERO_BLOCK * SIDE * SIDE),
        name="own_sums",
    )(lists, whole)


def far_kernel(
    own_ref,
    plan_ref,
    whole_ref,
    far_ref,
    near_ref,
    out_ref,
    total,
    pieces_ref,
):
    for sender in range(TARGETS):
        rows = pl.ds(sender * CAP_X, CAP_X)
        for part in range(NY):
            lanes = slice(part * SIDE, (part + 1) * SIDE)
            pieces_ref[part, rows, :] = far_ref[rows, lanes].astype(F32)

    def clear(group, carry):
        total[pl.ds(group * GROUP, GROUP)] = jnp.zeros((GROUP, WIDE, HEIGHT * SIDE), F32)
        return carry

    lax.fori_loop(0, own_ref[15, 1], clear, 0)

    def product(named, offset):
        begin = plan_ref[2, named]
        length = plan_ref[3, named]
        right = jnp.concatenate(
            [
                own_block(whole_ref, own_ref[member, named], pl.ds(0, SIDE))
                for member in range(HEIGHT)
            ],
            axis=1,
        )
        pieces, columns = [], []
        for at in range(FAR_GROUP):
            place = jnp.minimum(begin + offset + at, CAP_X - 1)
            rows = pl.ds(plan_ref[0, place], TARGETS, stride=CAP_X)
            for part in range(NY):
                pieces.append(pieces_ref[part, rows, :])
            columns.append(jnp.where(offset + at < length, plan_ref[1, place], OUT_COLS))
        left = jnp.concatenate(pieces, axis=0).astype(BF)
        return jnp.dot(left, right, preferred_element_type=F32), columns

    def add(value, columns):
        for at, column in enumerate(columns):
            total[column] = total[column] + value[at * WIDE : (at + 1) * WIDE]

    def first_step(step, carry):
        done = [product(step * ROWS_AT_ONCE + at, 0) for at in range(ROWS_AT_ONCE)]
        for value, columns in done:
            add(value, columns)
        return carry

    named_rows = own_ref[15, 2]
    lax.fori_loop(0, (named_rows + ROWS_AT_ONCE - 1) // ROWS_AT_ONCE, first_step, 0)

    def rest(named, carry):
        def rest_step(step, inner_carry):
            add(*product(named, step * FAR_GROUP))
            return inner_carry

        lax.fori_loop(1, (plan_ref[3, named] + FAR_GROUP - 1) // FAR_GROUP, rest_step, 0)
        return carry

    lax.fori_loop(0, named_rows, rest, 0)

    for place in range(ZERO_BLOCK):
        member, slot = out_place(place)
        column = own_ref[8, member * (128 // HEIGHT) + slot]
        value = total[column, :, pl.ds(member * SIDE, SIDE)] + near_ref[place]
        out_ref[place] = value.astype(BF)


def far_sums(own_lists, far_lists, whole, far, near):
    return pl.pallas_call(
        far_kernel,
        out_shape=jax.ShapeDtypeStruct((ZERO_BLOCK, WIDE, SIDE), BF),
        in_specs=[smem(), smem(), vmem(), vmem(), vmem()],
        out_specs=vmem(),
        scratch_shapes=[
            pltpu.VMEM((OUT_COLS + 1, WIDE, HEIGHT * SIDE), F32),
            pltpu.VMEM((NY, TARGETS * CAP_X, SIDE), F32),
        ],
        compiler_params=params(),
        name="far_sums",
    )(own_lists, far_lists, whole, far, near)


def finish_kernel(cuts_ref, out_ref):
    for row in range(HEIGHT):
        for slot in range(QUARTER):
            turned = jnp.concatenate([cuts_ref[part, row, slot] for part in range(NY)], axis=0)
            out_ref[row, slot] = turned.T


def finish(cuts):
    return pl.pallas_call(
        finish_kernel,
        out_shape=jax.ShapeDtypeStruct((HEIGHT, QUARTER, SIDE, SIDE), BF),
        in_specs=[vmem()],
        out_specs=vmem(),
        compiler_params=params(),
        name="finish",
    )(cuts)


def iota(shape, axis):
    return lax.broadcasted_iota(I32, shape, axis)


def dot(a, b):
    return jnp.dot(a.astype(BF), b.astype(BF), preferred_element_type=F32)


def dot_rows(a, b):
    return lax.dot_general(
        a.astype(BF), b.astype(BF), (((1,), (1,)), ((), ())), preferred_element_type=F32
    )


def earlier(size):
    return (iota((size, size), 0) < iota((size, size), 1)).astype(F32)


def places(need):
    order = earlier(SIDE)
    parts = []
    before = jnp.zeros((need.shape[0], 1), F32)
    for begin in range(0, need.shape[1], SIDE):
        part = need[:, begin : begin + SIDE]
        parts.append(dot(part, order) + before)
        before = before + jnp.sum(part, axis=1, keepdims=True)
    return jnp.concatenate(parts, axis=1)


def codes(need, capacity):
    place = places(need)
    return jnp.where((need > 0) & (place < capacity), place, -1.0)


def one_hot(code, rows):
    return (iota((rows, code.shape[1]), 0).astype(F32) == code).astype(F32)


def quarter_of(slot):
    return sum((slot >= bound * QUARTER).astype(I32) for bound in range(1, NY))


def pattern_kernel(position_ref, columns_ref, entries_ref, slots_ref, union_ref, need_ref, kq_ref):
    step = 64
    for begin in range(0, ROWS, step):
        column = iota((step, ROWS), 1)
        found = jnp.full((step, ROWS), -1, I32)
        for slot in range(SLOTS):
            at = columns_ref[begin : begin + step, slot : slot + 1]
            found = jnp.where(at == column, slot, found)
        slots_ref[begin : begin + step, :] = found
    names = (slots_ref[...] >= 0).astype(F32)
    mine = iota((128, ROWS), 1) // HEIGHT == iota((128, ROWS), 0)
    union = (dot(mine.astype(F32), names) > 0).astype(F32)
    union_ref[...] = union

    entry = iota((1, ENTRIES), 1)
    peer, number = entry // HELD, entry % HELD
    x, core = (peer // NC) % NX, peer % NC
    row = ((x * NZ + position_ref[1]) * NC + core) * HEIGHT + quarter_of(number)
    column = entries_ref[...]
    every = iota((ROWS, ENTRIES), 0)
    named = dot(jnp.where(mine, 0.0, union), (every == row).astype(F32))
    need_ref[...] = named * dot(union, (every == column).astype(F32))
    kind = iota((8, ENTRIES), 0)
    both = jnp.where(kind == 1, jnp.maximum(column, 0), 0)
    kq_ref[...] = jnp.where(kind == 0, row, both).astype(F32)


def pattern(position, columns, entries):
    return pl.pallas_call(
        pattern_kernel,
        out_shape=(
            jax.ShapeDtypeStruct((ROWS, ROWS), I32),
            jax.ShapeDtypeStruct((128, ROWS), F32),
            jax.ShapeDtypeStruct((128, ENTRIES), F32),
            jax.ShapeDtypeStruct((8, ENTRIES), F32),
        ),
        in_specs=[smem(), vmem(), vmem()],
        out_specs=(vmem(), vmem(), vmem(), vmem()),
        compiler_params=params(),
        cost_estimate=cost(2 * SLOTS * ROWS**3 // 4, 8 * ROWS**2),
        name="pattern",
    )(position, columns, entries)


def send_kernel(need_ref, kq_ref, near_ref, out_ref, chosen_ref):
    near = near_ref[...]
    kind = iota((8, ENTRIES), 0)
    pick = (iota((8, ENTRIES), 1) % HELD == SLOTS + kind) & (kind < 2)
    flags = dot(pick.astype(F32), near)
    flags = jnp.concatenate([flags[0:1], flags[1:2]], axis=1)
    need = need_ref[...] * flags
    slab = iota((8, 128), 1)
    plane = (slab // NC) % NZ == iota((8, 128), 0)
    wanted = (dot(plane.astype(F32), need) > 0).astype(F32)
    code = codes(wanted, CAP_Z)
    most = jnp.max(jnp.sum(wanted, axis=1, keepdims=True), axis=0, keepdims=True)
    most = jnp.broadcast_to(jnp.minimum(most, 250.0), (1, 128))
    totals = jnp.minimum(dot_rows(jnp.ones((8, ENTRIES), F32), need)[0:1], 250.0)
    for to in range(NZ):
        chosen_ref[to * ROWS_Z : (to + 1) * ROWS_Z, :] = one_hot(code[to : to + 1], ROWS_Z).astype(BF)
    packed = jnp.dot(chosen_ref[...], near, preferred_element_type=F32)
    tail = iota((16, PIECE), 0)
    kq = kq_ref[...]
    for to in range(NZ):
        target = iota((8, 128), 0)
        choice = slab == (target // NC * NZ + to) * NC + target % NC
        asked = jnp.concatenate([dot(choice.astype(F32), need), kq], axis=0)
        notes = dot_rows(asked, chosen_ref[to * ROWS_Z : (to + 1) * ROWS_Z, :])
        first = jnp.concatenate([notes[i : i + 1] for i in range(4)], axis=1)
        second = jnp.concatenate([notes[i : i + 1] for i in range(4, 8)], axis=1)
        third = jnp.concatenate([notes[8:9], notes[9:10], totals, most], axis=1)
        begin = to * ROWS_Z
        out_ref[to, 0 : ROWS_Z - 16] = packed[begin : begin + ROWS_Z - 16].astype(BF)
        value = packed[begin + ROWS_Z - 16 : begin + ROWS_Z]
        value = jnp.where(tail == 12, first, value)
        value = jnp.where(tail == 13, second, value)
        value = jnp.where(tail == 14, third, value)
        out_ref[to, ROWS_Z - 16 : ROWS_Z] = value.astype(BF)


def send(need, kq, near):
    return pl.pallas_call(
        send_kernel,
        out_shape=jax.ShapeDtypeStruct((NZ, ROWS_Z, PIECE), BF),
        in_specs=[vmem()] * 3,
        out_specs=vmem(),
        scratch_shapes=[pltpu.VMEM((NZ * ROWS_Z, ENTRIES), BF)],
        compiler_params=params(),
        name="send",
    )(need, kq, near)


def notes_of(along_ref):
    asked, third = [], []
    for plane in range(NZ):
        rows = pl.ds(plane * ROWS_Z + ROWS_Z - 16, 16)
        notes = along_ref[rows, :].astype(F32)
        asked.append(
            jnp.concatenate(
                [
                    notes[12 + i // 4 : 13 + i // 4, i % 4 * SIDE : (i % 4 + 1) * SIDE]
                    for i in range(TARGETS)
                ],
                axis=0,
            )
        )
        third.append(notes[14:15])
    return jnp.concatenate(asked, axis=1), third


def route_kernel(along_ref, out_ref, chosen_ref):
    asked, _ = notes_of(along_ref)
    code = codes(asked, CAP_X)
    for to in range(TARGETS):
        chosen_ref[to * SIDE : (to + 1) * SIDE, :] = one_hot(code[to : to + 1], SIDE).astype(BF)
    packed = jnp.dot(chosen_ref[...], along_ref[...], preferred_element_type=F32)
    for to in range(TARGETS):
        out_ref[to] = packed[to * SIDE : to * SIDE + CAP_X].astype(BF)


def route(along):
    return pl.pallas_call(
        route_kernel,
        out_shape=jax.ShapeDtypeStruct((TARGETS, CAP_X, PIECE), BF),
        in_specs=[vmem()],
        out_specs=vmem(),
        scratch_shapes=[pltpu.VMEM((TARGETS * SIDE, NZ * ROWS_Z), BF)],
        compiler_params=params(),
        name="route",
    )(along)


def own_plan_kernel(position_ref, slots_ref, union_ref, out_ref):
    x, z, core, part = (position_ref[i] for i in range(4))
    chip = x * NZ + z
    slab = chip * NC + core
    order = earlier(ROWS)
    out_ref[...] = jnp.zeros_like(out_ref)
    mine = union_ref[pl.ds(slab, 1), :]
    rank = dot(jnp.broadcast_to(mine, (8, ROWS)), order)

    both = slots_ref[pl.ds(pl.multiple_of(chip * HEIGHT_2, HEIGHT_2), HEIGHT_2), :]
    swapped = jnp.concatenate([both[HEIGHT:], both[:HEIGHT]], axis=0)
    slot = jnp.where(core == 0, both, swapped)
    quarter = quarter_of(slot)
    held = (quarter * HEIGHT + iota(slot.shape, 0)) * QUARTER + slot - quarter * QUARTER
    held = jnp.where(slot >= 0, held - ZERO_BLOCK, 0).astype(F32)

    every = iota((1, ROWS), 1)
    named = jnp.where(every // HEIGHT == slab, 0.0, mine)
    position = dot(jnp.broadcast_to(named, (8, ROWS)), order)[0:1]
    number = iota((SLABS, ROWS), 0).astype(F32)
    chosen = ((position == number) & (named > 0)).astype(F32)
    out_ref[0:4, 0:SLABS] = dot_rows(held, chosen)[0:HEIGHT].astype(I32) + ZERO_BLOCK

    number = iota((OUT_COLS, ROWS), 0).astype(F32)
    chosen = ((rank[0:1] == number) & (mine > 0)).astype(F32)
    out_ref[4:8, 0:OUT_COLS] = dot_rows(held, chosen)[0:HEIGHT].astype(I32) + ZERO_BLOCK
    wide = 128 // HEIGHT
    chosen = jnp.concatenate(
        [slot[i : i + 1] == iota((wide, ROWS), 0) for i in range(HEIGHT)], axis=0
    )
    out_ref[8:9, 0:128] = dot_rows(rank, chosen.astype(F32))[0:1].astype(I32)
    chosen = (iota((8, ROWS), 1) == iota((8, ROWS), 0) + slab * HEIGHT).astype(F32)
    out_ref[9:13, 0:8] = dot_rows(held, chosen)[0:HEIGHT].astype(I32) + ZERO_BLOCK
    groups = ((jnp.sum(mine) + (GROUP - 1)) * (1.0 / GROUP)).astype(I32)
    lane = iota((1, 128), 1)
    scalars = jnp.where(lane == 0, part, 0)
    scalars = jnp.where(lane == 1, groups, scalars)
    out_ref[15:16, :] = jnp.where(lane == 2, jnp.sum(named).astype(I32), scalars)


def own_plan(position, slots, union):
    return pl.pallas_call(
        own_plan_kernel,
        out_shape=jax.ShapeDtypeStruct((16, 128), I32),
        in_specs=[smem(), vmem(), vmem()],
        out_specs=vmem(),
        compiler_params=params(),
        cost_estimate=cost(ROWS**3, 4 * ROWS**2),
        name="own_plan",
    )(position, slots, union)


def far_plan_kernel(position_ref, union_ref, along_ref, out_ref):
    x, z, core = (position_ref[i] for i in range(3))
    slab = (x * NZ + z) * NC + core
    out_ref[...] = jnp.zeros_like(out_ref)
    asked, third = notes_of(along_ref)
    mine = iota(asked.shape, 0) == x * NC + core
    asked = jnp.sum(jnp.where(mine, asked, 0.0), axis=0, keepdims=True)
    number = jnp.sum(asked).astype(I32)
    code = codes(jnp.broadcast_to(asked, (8, asked.shape[1])), CAP_X)[0:1]
    chosen = one_hot(code, SIDE)
    row = jnp.concatenate([part[:, :SIDE] for part in third], axis=1)
    column = jnp.concatenate([part[:, SIDE : 2 * SIDE] for part in third], axis=1)
    row_down = jnp.sum(chosen * row, axis=1, keepdims=True).astype(I32)
    column_down = jnp.sum(chosen * column, axis=1, keepdims=True).astype(I32)
    row_along = dot_rows(jnp.broadcast_to(row, (8, row.shape[1])), chosen)[0:1].astype(I32)

    down, along = iota((SIDE, SIDE), 0), iota((SIDE, SIDE), 1)
    less = (row_down < row_along) | ((row_down == row_along) & (down < along))
    order = jnp.sum((less & (down < number)).astype(F32), axis=0, keepdims=True)
    ordered = ((order == down.astype(F32)) & (along < number)).astype(F32)
    position = iota((8, SIDE), 1).astype(F32)
    out_ref[0:1, 0:SIDE] = dot_rows(position, ordered)[0:1].astype(I32)
    names = union_ref[pl.ds(slab, 1), :]
    order = earlier(ROWS)
    rank = dot(jnp.broadcast_to(names, (8, ROWS)), order)
    every = iota((SIDE, ROWS), 1)
    rank = dot_rows(rank, (every == column_down).astype(F32))
    out_ref[1:2, 0:SIDE] = dot_rows(rank, ordered)[0:1].astype(I32)

    valid = iota((SIDE, ROWS), 0) < number
    count = dot(jnp.ones((8, SIDE), F32), ((every == row_down) & valid).astype(F32))
    start = jnp.minimum(dot(count, order), 250.0)
    row = jnp.where(iota((1, ROWS), 1) // HEIGHT == slab, 0.0, names)
    position = dot(jnp.broadcast_to(row, (8, ROWS)), order)[0:1]
    chosen = ((position == iota((SLABS, ROWS), 0).astype(F32)) & (row > 0)).astype(F32)
    out_ref[2:3, 0:SLABS] = dot_rows(start, chosen)[0:1].astype(I32)
    out_ref[3:4, 0:SLABS] = dot_rows(count, chosen)[0:1].astype(I32)

    third = functools.reduce(jnp.maximum, third), functools.reduce(jnp.add, third)
    most_z = jnp.max(third[0][:, 3 * SIDE :])
    most_x = jnp.max(third[1][:, 2 * SIDE : 3 * SIDE])
    fits = (most_x <= CAP_X) & (most_z <= CAP_Z)
    out_ref[4:5, :] = jnp.zeros((1, SIDE), I32) + fits.astype(I32)


def far_plan(position, union, along):
    return pl.pallas_call(
        far_plan_kernel,
        out_shape=jax.ShapeDtypeStruct((8, 128), I32),
        in_specs=[smem(), vmem(), vmem()],
        out_specs=vmem(),
        compiler_params=params(),
        cost_estimate=cost(2 * 20 * ROWS**3, 8 * ROWS**2),
        name="far_plan",
    )(position, union, along)


def dense(blocks, nonzero, columns):
    slab = lax.axis_index(ROW_AXES)
    part = lax.axis_index("col")
    masked = blocks * nonzero[:, :, None, None].astype(BF)
    slab_ids = jnp.arange(SLABS, dtype=I32)
    local_rows = jnp.arange(HEIGHT, dtype=I32)
    grouped = columns.reshape(SLABS, HEIGHT * SLOTS)
    targets = slab * HEIGHT + local_rows
    wanted = jnp.any(grouped[:, :, None] == targets[None, None, :], axis=1)
    wanted = wanted & (slab_ids != slab)[:, None]
    picked = jnp.sum(jnp.where(wanted, local_rows, 0), axis=1)
    filled = jnp.any(wanted, axis=1)
    outgoing = jnp.where(filled[:, None, None, None], masked[picked], jnp.zeros((), BF))
    incoming = lax.all_to_all(outgoing, ROW_AXES, split_axis=0, concat_axis=0, tiled=True)
    row_table = jnp.concatenate([incoming, masked], axis=0)
    own_cols = lax.dynamic_slice_in_dim(columns, slab * HEIGHT, HEIGHT, 0)
    source = own_cols // HEIGHT
    row_index = jnp.where(source == slab, SLABS + own_cols % HEIGHT, source)
    far_cols = columns[own_cols]
    far_quarter = lax.dynamic_slice_in_dim(far_cols, part * QUARTER, QUARTER, 2)
    whole = lax.all_gather(masked, "col", axis=1, tiled=True)
    results = []
    for member in range(HEIGHT):
        match = far_quarter[member][:, :, None] == own_cols[member][None, None, :]
        products = jnp.einsum(
            "tab,tubc->tuac", whole[member], row_table[row_index[member]],
            preferred_element_type=F32,
        )
        summed = lax.dot_general(
            match.astype(F32).reshape(SLOTS * QUARTER, SLOTS),
            products.reshape(SLOTS * QUARTER, SIDE * SIDE),
            (((0,), (0,)), ((), ())),
            precision=lax.Precision.HIGHEST,
            preferred_element_type=F32,
        )
        results.append(summed.reshape(SLOTS, SIDE, SIDE))
    square = lax.psum_scatter(jnp.stack(results), "col", scatter_dimension=1, tiled=True)
    return square.astype(BF)


def plane_columns(columns):
    split = columns.reshape(NX, NZ, NC, HEIGHT, NY, QUARTER)
    mine = lax.dynamic_index_in_dim(split, lax.axis_index("z"), 1, keepdims=False)
    mine = mine.transpose(3, 0, 1, 2, 4).reshape(PEERS, SLOTS)
    return jnp.pad(mine, ((0, 0), (0, HELD - SLOTS)), constant_values=-1).reshape(1, ENTRIES)


def shards(blocks, nonzero, columns):
    position = jnp.stack([lax.axis_index(name) for name in ROW_AXES + ("col",)])
    turned, cuts = prepare(position, nonzero, blocks)
    cuts, names = lax.optimization_barrier((cuts, columns))
    slots, union, need, kq = pattern(position, names, plane_columns(columns))
    near = lax.all_to_all(cuts, ("col", "x", "core"), split_axis=0, concat_axis=0, tiled=True)
    near, turned, need = lax.optimization_barrier((near, turned, need))
    whole = lax.all_gather(turned, "col", axis=0, tiled=False)
    whole = whole.reshape(ZERO_BLOCK, SIDE, SIDE)
    packed = send(need, kq, near.reshape(ENTRIES, PIECE))
    packed, slots = lax.optimization_barrier((packed, slots))
    along = lax.all_to_all(packed, "z", split_axis=0, concat_axis=0, tiled=True)
    along = along.reshape(NZ * ROWS_Z, PIECE)
    own_lists = own_plan(position, slots, union)
    packed, notes = lax.optimization_barrier((route(along), along))
    far = lax.all_to_all(packed, ("x", "core"), split_axis=0, concat_axis=0, tiled=True)
    far_lists = far_plan(position, union, notes)
    far = far.reshape(TARGETS * CAP_X, PIECE)
    far, fits = lax.optimization_barrier((far, far_lists[4, 0] != 0))
    result = far_sums(own_lists, far_lists, whole, far, own_sums(own_lists, whole))
    result = result.reshape(NY, HEIGHT, QUARTER, WIDE, SIDE)
    result = lax.all_to_all(result, "col", split_axis=0, concat_axis=0, tiled=True)
    square = finish(result)
    return lax.cond(
        fits,
        lambda value, *_: value,
        lambda _, *inputs: dense(*inputs),
        square,
        blocks,
        nonzero,
        columns,
    )


def solution(mesh):
    fine = Mesh(mesh.devices.reshape(NX, NZ, NC, NY), ROW_AXES + ("col",))
    spec = P(ROW_AXES, "col", None, None)
    return jax.shard_map(
        shards,
        mesh=fine,
        in_specs=(spec, P(ROW_AXES, "col"), P()),
        out_specs=spec,
        check_vma=False,
    )
```

```python
import functools

import jax
import jax.numpy as jnp
from jax import lax
from jax.experimental import pallas as pl
from jax.experimental.pallas import tpu as pltpu
from jax.sharding import Mesh
from jax.sharding import PartitionSpec as P

BF = jnp.bfloat16
F32 = jnp.float32
I32 = jnp.int32

NX, NZ, NC, NY = 4, 8, 2, 4
ROWS, SLOTS, SIDE = 256, 28, 128
HEIGHT, QUARTER = 4, 7
SLABS = ROWS // HEIGHT
PEERS = NX * NC * NY
HELD = 32
ENTRIES = PEERS * HELD
PIECE = SIDE * SIDE // PEERS
WIDE = SIDE // NY
TARGETS = NX * NC
CAP_Z = 124
ROWS_Z = 128
CAP_X = 120
GROUP = 8
FAR_GROUP = 4
ROWS_AT_ONCE = 4
HEIGHT_2 = NC * HEIGHT
OUT_COLS = 72
ZERO_BLOCK = NY * HEIGHT * QUARTER
VMEM_LIMIT = 48 * 1024 * 1024
ROW_AXES = ("x", "z", "core")


def vmem():
    return pl.BlockSpec(memory_space=pltpu.VMEM)


def smem():
    return pl.BlockSpec(memory_space=pltpu.SMEM)


def params():
    return pltpu.CompilerParams(vmem_limit_bytes=VMEM_LIMIT)


def cost(flops, moved):
    return pl.CostEstimate(flops=flops, bytes_accessed=moved, transcendentals=0)


def prepare_kernel(position_ref, keep_ref, blocks_ref, cuts_ref, rows_ref):
    x, core, part = position_ref[0], position_ref[2], position_ref[3]
    lanes = iota((8, ENTRIES), 1) - ((part * NX + x) * NC + core) * HELD
    flags = jnp.zeros((8, ENTRIES), F32)
    for row in range(HEIGHT):
        for slot in range(QUARTER):
            number = row * QUARTER + slot
            keep = keep_ref[row, slot] != 0
            flags = jnp.where((lanes == number) & keep, 1.0, flags)
            block = blocks_ref[row, slot].astype(F32)
            turned = jnp.where(keep, block, jnp.zeros_like(block)).T
            for quarter in range(NY):
                for part_of in range(NY):
                    begin = quarter * WIDE + part_of * TARGETS
                    rows = pl.ds(quarter * TARGETS * HELD + number, TARGETS, stride=HELD)
                    rows_ref[part_of, rows, :] = turned[begin : begin + TARGETS]
    for begin in range(0, PEERS, 8):
        for part_of in range(NY):
            for extra in range(HELD - SLOTS):
                rows = pl.ds(begin * HELD + SLOTS + extra, 8, stride=HELD)
                at = extra * PIECE + part_of * SIDE
                value = flags[:, at : at + SIDE] if extra < 2 else jnp.zeros((8, SIDE), F32)
                rows_ref[part_of, rows, :] = value
    for peer in range(PEERS):
        rows = pl.ds(peer * HELD, HELD)
        cuts_ref[peer] = jnp.concatenate(
            [rows_ref[part_of, rows, :] for part_of in range(NY)], axis=1
        ).astype(BF)


def prepare(position, nonzero, blocks):
    return pl.pallas_call(
        prepare_kernel,
        out_shape=jax.ShapeDtypeStruct((PEERS, HELD, PIECE), BF),
        in_specs=[smem(), smem(), vmem()],
        out_specs=vmem(),
        scratch_shapes=[pltpu.VMEM((NY, ENTRIES, SIDE), F32)],
        compiler_params=params(),
        name="prepare",
    )(position, nonzero, blocks)


def turn_kernel(keep_ref, blocks_ref, out_ref):
    for row in range(HEIGHT):
        for slot in range(QUARTER):
            block = blocks_ref[row, slot]
            out_ref[row, slot] = jnp.where(
                keep_ref[row, slot] != 0, block, jnp.zeros_like(block)
            ).T


def turn(nonzero, blocks):
    return pl.pallas_call(
        turn_kernel,
        out_shape=jax.ShapeDtypeStruct((HEIGHT, QUARTER, SIDE, SIDE), BF),
        in_specs=[smem(), vmem()],
        out_specs=vmem(),
        compiler_params=params(),
        cost_estimate=cost(2 * SLOTS * SIDE**3, 4 * SLOTS * SIDE**2),
        name="turn",
    )(nonzero, blocks)


def own_block(whole_ref, place, rows):
    value = whole_ref[jnp.minimum(place, ZERO_BLOCK - 1), rows, :]
    return jnp.where(place < ZERO_BLOCK, value, jnp.zeros_like(value))


def out_place(place):
    return (place // QUARTER) % HEIGHT, place // (QUARTER * HEIGHT) * QUARTER + place % QUARTER


def own_kernel(
    plan_ref,
    whole_ref,
    out_ref,
    total,
    panel,
    near,
):
    first = pl.multiple_of(plan_ref[15, 0] * WIDE, WIDE)
    for inner in range(HEIGHT):
        for member in range(HEIGHT):
            panel[pl.ds(inner * SIDE, SIDE), pl.ds(member * SIDE, SIDE)] = own_block(
                whole_ref, plan_ref[9 + member, inner], pl.ds(0, SIDE)
            )

    def step(group, carry):
        for at in range(GROUP):
            for inner in range(HEIGHT):
                near[pl.ds(at * WIDE, WIDE), pl.ds(inner * SIDE, SIDE)] = own_block(
                    whole_ref, plan_ref[4 + inner, group * GROUP + at], pl.ds(first, WIDE)
                )
        value = jnp.dot(near[...], panel[...], preferred_element_type=F32)
        total[pl.ds(group * GROUP, GROUP)] = value.reshape(GROUP, WIDE, HEIGHT * SIDE)
        return carry

    lax.fori_loop(0, plan_ref[15, 1], step, 0)
    for place in range(ZERO_BLOCK):
        member, slot = out_place(place)
        column = plan_ref[8, member * (128 // HEIGHT) + slot]
        out_ref[place] = total[column, :, pl.ds(member * SIDE, SIDE)]


def own_sums(lists, whole):
    flops = 2 * 32 * WIDE * (HEIGHT * SIDE) ** 2
    return pl.pallas_call(
        own_kernel,
        out_shape=jax.ShapeDtypeStruct((ZERO_BLOCK, WIDE, SIDE), F32),
        in_specs=[smem(), vmem()],
        out_specs=vmem(),
        scratch_shapes=[
            pltpu.VMEM((OUT_COLS, WIDE, HEIGHT * SIDE), F32),
            pltpu.VMEM((HEIGHT * SIDE, HEIGHT * SIDE), BF),
            pltpu.VMEM((GROUP * WIDE, HEIGHT * SIDE), BF),
        ],
        compiler_params=params(),
        cost_estimate=cost(flops, 3 * ZERO_BLOCK * SIDE * SIDE),
        name="own_sums",
    )(lists, whole)


def far_kernel(
    own_ref,
    plan_ref,
    whole_ref,
    far_ref,
    near_ref,
    out_ref,
    total,
    pieces_ref,
):
    for sender in range(TARGETS):
        rows = pl.ds(sender * CAP_X, CAP_X)
        for part in range(NY):
            lanes = slice(part * SIDE, (part + 1) * SIDE)
            pieces_ref[part, rows, :] = far_ref[rows, lanes].astype(F32)

    def clear(group, carry):
        total[pl.ds(group * GROUP, GROUP)] = jnp.zeros((GROUP, WIDE, HEIGHT * SIDE), F32)
        return carry

    lax.fori_loop(0, own_ref[15, 1], clear, 0)

    def product(named, offset):
        begin = plan_ref[2, named]
        length = plan_ref[3, named]
        right = jnp.concatenate(
            [
                own_block(whole_ref, own_ref[member, named], pl.ds(0, SIDE))
                for member in range(HEIGHT)
            ],
            axis=1,
        )
        pieces, columns = [], []
        for at in range(FAR_GROUP):
            place = jnp.minimum(begin + offset + at, CAP_X - 1)
            rows = pl.ds(plan_ref[0, place], TARGETS, stride=CAP_X)
            for part in range(NY):
                pieces.append(pieces_ref[part, rows, :])
            columns.append(jnp.where(offset + at < length, plan_ref[1, place], OUT_COLS))
        left = jnp.concatenate(pieces, axis=0).astype(BF)
        return jnp.dot(left, right, preferred_element_type=F32), columns

    def add(value, columns):
        for at, column in enumerate(columns):
            total[column] = total[column] + value[at * WIDE : (at + 1) * WIDE]

    def first_step(step, carry):
        done = [product(step * ROWS_AT_ONCE + at, 0) for at in range(ROWS_AT_ONCE)]
        for value, columns in done:
            add(value, columns)
        return carry

    named_rows = own_ref[15, 2]
    lax.fori_loop(0, (named_rows + ROWS_AT_ONCE - 1) // ROWS_AT_ONCE, first_step, 0)

    def rest(named, carry):
        def rest_step(step, inner_carry):
            add(*product(named, step * FAR_GROUP))
            return inner_carry

        lax.fori_loop(1, (plan_ref[3, named] + FAR_GROUP - 1) // FAR_GROUP, rest_step, 0)
        return carry

    lax.fori_loop(0, named_rows, rest, 0)

    for place in range(ZERO_BLOCK):
        member, slot = out_place(place)
        column = own_ref[8, member * (128 // HEIGHT) + slot]
        value = total[column, :, pl.ds(member * SIDE, SIDE)] + near_ref[place]
        out_ref[place] = value.astype(BF)


def far_sums(own_lists, far_lists, whole, far, near):
    return pl.pallas_call(
        far_kernel,
        out_shape=jax.ShapeDtypeStruct((ZERO_BLOCK, WIDE, SIDE), BF),
        in_specs=[smem(), smem(), vmem(), vmem(), vmem()],
        out_specs=vmem(),
        scratch_shapes=[
            pltpu.VMEM((OUT_COLS + 1, WIDE, HEIGHT * SIDE), F32),
            pltpu.VMEM((NY, TARGETS * CAP_X, SIDE), F32),
        ],
        compiler_params=params(),
        name="far_sums",
    )(own_lists, far_lists, whole, far, near)


def finish_kernel(cuts_ref, out_ref):
    for row in range(HEIGHT):
        for slot in range(QUARTER):
            turned = jnp.concatenate([cuts_ref[part, row, slot] for part in range(NY)], axis=0)
            out_ref[row, slot] = turned.T


def finish(cuts):
    return pl.pallas_call(
        finish_kernel,
        out_shape=jax.ShapeDtypeStruct((HEIGHT, QUARTER, SIDE, SIDE), BF),
        in_specs=[vmem()],
        out_specs=vmem(),
        compiler_params=params(),
        name="finish",
    )(cuts)


def iota(shape, axis):
    return lax.broadcasted_iota(I32, shape, axis)


def dot(a, b):
    return jnp.dot(a.astype(BF), b.astype(BF), preferred_element_type=F32)


def dot_rows(a, b):
    return lax.dot_general(
        a.astype(BF), b.astype(BF), (((1,), (1,)), ((), ())), preferred_element_type=F32
    )


def earlier(size):
    return (iota((size, size), 0) < iota((size, size), 1)).astype(F32)


def places(need):
    order = earlier(SIDE)
    parts = []
    before = jnp.zeros((need.shape[0], 1), F32)
    for begin in range(0, need.shape[1], SIDE):
        part = need[:, begin : begin + SIDE]
        parts.append(dot(part, order) + before)
        before = before + jnp.sum(part, axis=1, keepdims=True)
    return jnp.concatenate(parts, axis=1)


def codes(need, capacity):
    place = places(need)
    return jnp.where((need > 0) & (place < capacity), place, -1.0)


def one_hot(code, rows):
    return (iota((rows, code.shape[1]), 0).astype(F32) == code).astype(F32)


def quarter_of(slot):
    return sum((slot >= bound * QUARTER).astype(I32) for bound in range(1, NY))


def pattern_kernel(position_ref, columns_ref, entries_ref, slots_ref, union_ref, need_ref, kq_ref):
    step = 64
    for begin in range(0, ROWS, step):
        column = iota((step, ROWS), 1)
        found = jnp.full((step, ROWS), -1, I32)
        for slot in range(SLOTS):
            at = columns_ref[begin : begin + step, slot : slot + 1]
            found = jnp.where(at == column, slot, found)
        slots_ref[begin : begin + step, :] = found
    names = (slots_ref[...] >= 0).astype(F32)
    mine = iota((128, ROWS), 1) // HEIGHT == iota((128, ROWS), 0)
    union = (dot(mine.astype(F32), names) > 0).astype(F32)
    union_ref[...] = union

    entry = iota((1, ENTRIES), 1)
    peer, number = entry // HELD, entry % HELD
    x, core = (peer // NC) % NX, peer % NC
    row = ((x * NZ + position_ref[1]) * NC + core) * HEIGHT + quarter_of(number)
    column = entries_ref[...]
    every = iota((ROWS, ENTRIES), 0)
    named = dot(jnp.where(mine, 0.0, union), (every == row).astype(F32))
    need_ref[...] = named * dot(union, (every == column).astype(F32))
    kind = iota((8, ENTRIES), 0)
    both = jnp.where(kind == 1, jnp.maximum(column, 0), 0)
    kq_ref[...] = jnp.where(kind == 0, row, both).astype(F32)


def pattern(position, columns, entries):
    return pl.pallas_call(
        pattern_kernel,
        out_shape=(
            jax.ShapeDtypeStruct((ROWS, ROWS), I32),
            jax.ShapeDtypeStruct((128, ROWS), F32),
            jax.ShapeDtypeStruct((128, ENTRIES), F32),
            jax.ShapeDtypeStruct((8, ENTRIES), F32),
        ),
        in_specs=[smem(), vmem(), vmem()],
        out_specs=(vmem(), vmem(), vmem(), vmem()),
        compiler_params=params(),
        cost_estimate=cost(2 * SLOTS * ROWS**3 // 4, 8 * ROWS**2),
        name="pattern",
    )(position, columns, entries)


def send_kernel(need_ref, kq_ref, near_ref, out_ref, chosen_ref):
    near = near_ref[...]
    kind = iota((8, ENTRIES), 0)
    pick = (iota((8, ENTRIES), 1) % HELD == SLOTS + kind) & (kind < 2)
    flags = dot(pick.astype(F32), near)
    flags = jnp.concatenate([flags[0:1], flags[1:2]], axis=1)
    need = need_ref[...] * flags
    slab = iota((8, 128), 1)
    plane = (slab // NC) % NZ == iota((8, 128), 0)
    wanted = (dot(plane.astype(F32), need) > 0).astype(F32)
    code = codes(wanted, CAP_Z)
    most = jnp.max(jnp.sum(wanted, axis=1, keepdims=True), axis=0, keepdims=True)
    most = jnp.broadcast_to(jnp.minimum(most, 250.0), (1, 128))
    totals = jnp.minimum(dot_rows(jnp.ones((8, ENTRIES), F32), need)[0:1], 250.0)
    for to in range(NZ):
        chosen_ref[to * ROWS_Z : (to + 1) * ROWS_Z, :] = one_hot(code[to : to + 1], ROWS_Z).astype(BF)
    packed = jnp.dot(chosen_ref[...], near, preferred_element_type=F32)
    tail = iota((16, PIECE), 0)
    kq = kq_ref[...]
    for to in range(NZ):
        target = iota((8, 128), 0)
        choice = slab == (target // NC * NZ + to) * NC + target % NC
        asked = jnp.concatenate([dot(choice.astype(F32), need), kq], axis=0)
        notes = dot_rows(asked, chosen_ref[to * ROWS_Z : (to + 1) * ROWS_Z, :])
        first = jnp.concatenate([notes[i : i + 1] for i in range(4)], axis=1)
        second = jnp.concatenate([notes[i : i + 1] for i in range(4, 8)], axis=1)
        third = jnp.concatenate([notes[8:9], notes[9:10], totals, most], axis=1)
        begin = to * ROWS_Z
        out_ref[to, 0 : ROWS_Z - 16] = packed[begin : begin + ROWS_Z - 16].astype(BF)
        value = packed[begin + ROWS_Z - 16 : begin + ROWS_Z]
        value = jnp.where(tail == 12, first, value)
        value = jnp.where(tail == 13, second, value)
        value = jnp.where(tail == 14, third, value)
        out_ref[to, ROWS_Z - 16 : ROWS_Z] = value.astype(BF)


def send(need, kq, near):
    return pl.pallas_call(
        send_kernel,
        out_shape=jax.ShapeDtypeStruct((NZ, ROWS_Z, PIECE), BF),
        in_specs=[vmem()] * 3,
        out_specs=vmem(),
        scratch_shapes=[pltpu.VMEM((NZ * ROWS_Z, ENTRIES), BF)],
        compiler_params=params(),
        name="send",
    )(need, kq, near)


def notes_of(along_ref):
    asked, third = [], []
    for plane in range(NZ):
        rows = pl.ds(plane * ROWS_Z + ROWS_Z - 16, 16)
        notes = along_ref[rows, :].astype(F32)
        asked.append(
            jnp.concatenate(
                [
                    notes[12 + i // 4 : 13 + i // 4, i % 4 * SIDE : (i % 4 + 1) * SIDE]
                    for i in range(TARGETS)
                ],
                axis=0,
            )
        )
        third.append(notes[14:15])
    return jnp.concatenate(asked, axis=1), third


def route_kernel(along_ref, out_ref, chosen_ref):
    asked, _ = notes_of(along_ref)
    code = codes(asked, CAP_X)
    for to in range(TARGETS):
        chosen_ref[to * SIDE : (to + 1) * SIDE, :] = one_hot(code[to : to + 1], SIDE).astype(BF)
    packed = jnp.dot(chosen_ref[...], along_ref[...], preferred_element_type=F32)
    for to in range(TARGETS):
        out_ref[to] = packed[to * SIDE : to * SIDE + CAP_X].astype(BF)


def route(along):
    return pl.pallas_call(
        route_kernel,
        out_shape=jax.ShapeDtypeStruct((TARGETS, CAP_X, PIECE), BF),
        in_specs=[vmem()],
        out_specs=vmem(),
        scratch_shapes=[pltpu.VMEM((TARGETS * SIDE, NZ * ROWS_Z), BF)],
        compiler_params=params(),
        name="route",
    )(along)


def own_plan_kernel(position_ref, slots_ref, union_ref, out_ref):
    x, z, core, part = (position_ref[i] for i in range(4))
    chip = x * NZ + z
    slab = chip * NC + core
    order = earlier(ROWS)
    out_ref[...] = jnp.zeros_like(out_ref)
    mine = union_ref[pl.ds(slab, 1), :]
    rank = dot(jnp.broadcast_to(mine, (8, ROWS)), order)

    both = slots_ref[pl.ds(pl.multiple_of(chip * HEIGHT_2, HEIGHT_2), HEIGHT_2), :]
    swapped = jnp.concatenate([both[HEIGHT:], both[:HEIGHT]], axis=0)
    slot = jnp.where(core == 0, both, swapped)
    quarter = quarter_of(slot)
    held = (quarter * HEIGHT + iota(slot.shape, 0)) * QUARTER + slot - quarter * QUARTER
    held = jnp.where(slot >= 0, held - ZERO_BLOCK, 0).astype(F32)

    every = iota((1, ROWS), 1)
    named = jnp.where(every // HEIGHT == slab, 0.0, mine)
    position = dot(jnp.broadcast_to(named, (8, ROWS)), order)[0:1]
    number = iota((SLABS, ROWS), 0).astype(F32)
    chosen = ((position == number) & (named > 0)).astype(F32)
    out_ref[0:4, 0:SLABS] = dot_rows(held, chosen)[0:HEIGHT].astype(I32) + ZERO_BLOCK

    number = iota((OUT_COLS, ROWS), 0).astype(F32)
    chosen = ((rank[0:1] == number) & (mine > 0)).astype(F32)
    out_ref[4:8, 0:OUT_COLS] = dot_rows(held, chosen)[0:HEIGHT].astype(I32) + ZERO_BLOCK
    wide = 128 // HEIGHT
    chosen = jnp.concatenate(
        [slot[i : i + 1] == iota((wide, ROWS), 0) for i in range(HEIGHT)], axis=0
    )
    out_ref[8:9, 0:128] = dot_rows(rank, chosen.astype(F32))[0:1].astype(I32)
    chosen = (iota((8, ROWS), 1) == iota((8, ROWS), 0) + slab * HEIGHT).astype(F32)
    out_ref[9:13, 0:8] = dot_rows(held, chosen)[0:HEIGHT].astype(I32) + ZERO_BLOCK
    groups = ((jnp.sum(mine) + (GROUP - 1)) * (1.0 / GROUP)).astype(I32)
    lane = iota((1, 128), 1)
    scalars = jnp.where(lane == 0, part, 0)
    scalars = jnp.where(lane == 1, groups, scalars)
    out_ref[15:16, :] = jnp.where(lane == 2, jnp.sum(named).astype(I32), scalars)


def own_plan(position, slots, union):
    return pl.pallas_call(
        own_plan_kernel,
        out_shape=jax.ShapeDtypeStruct((16, 128), I32),
        in_specs=[smem(), vmem(), vmem()],
        out_specs=vmem(),
        compiler_params=params(),
        cost_estimate=cost(ROWS**3, 4 * ROWS**2),
        name="own_plan",
    )(position, slots, union)


def far_plan_kernel(position_ref, union_ref, along_ref, out_ref):
    x, z, core = (position_ref[i] for i in range(3))
    slab = (x * NZ + z) * NC + core
    out_ref[...] = jnp.zeros_like(out_ref)
    asked, third = notes_of(along_ref)
    mine = iota(asked.shape, 0) == x * NC + core
    asked = jnp.sum(jnp.where(mine, asked, 0.0), axis=0, keepdims=True)
    number = jnp.sum(asked).astype(I32)
    code = codes(jnp.broadcast_to(asked, (8, asked.shape[1])), CAP_X)[0:1]
    chosen = one_hot(code, SIDE)
    row = jnp.concatenate([part[:, :SIDE] for part in third], axis=1)
    column = jnp.concatenate([part[:, SIDE : 2 * SIDE] for part in third], axis=1)
    row_down = jnp.sum(chosen * row, axis=1, keepdims=True).astype(I32)
    column_down = jnp.sum(chosen * column, axis=1, keepdims=True).astype(I32)
    row_along = dot_rows(jnp.broadcast_to(row, (8, row.shape[1])), chosen)[0:1].astype(I32)

    down, along = iota((SIDE, SIDE), 0), iota((SIDE, SIDE), 1)
    less = (row_down < row_along) | ((row_down == row_along) & (down < along))
    order = jnp.sum((less & (down < number)).astype(F32), axis=0, keepdims=True)
    ordered = ((order == down.astype(F32)) & (along < number)).astype(F32)
    position = iota((8, SIDE), 1).astype(F32)
    out_ref[0:1, 0:SIDE] = dot_rows(position, ordered)[0:1].astype(I32)
    names = union_ref[pl.ds(slab, 1), :]
    order = earlier(ROWS)
    rank = dot(jnp.broadcast_to(names, (8, ROWS)), order)
    every = iota((SIDE, ROWS), 1)
    rank = dot_rows(rank, (every == column_down).astype(F32))
    out_ref[1:2, 0:SIDE] = dot_rows(rank, ordered)[0:1].astype(I32)

    valid = iota((SIDE, ROWS), 0) < number
    count = dot(jnp.ones((8, SIDE), F32), ((every == row_down) & valid).astype(F32))
    start = jnp.minimum(dot(count, order), 250.0)
    row = jnp.where(iota((1, ROWS), 1) // HEIGHT == slab, 0.0, names)
    position = dot(jnp.broadcast_to(row, (8, ROWS)), order)[0:1]
    chosen = ((position == iota((SLABS, ROWS), 0).astype(F32)) & (row > 0)).astype(F32)
    out_ref[2:3, 0:SLABS] = dot_rows(start, chosen)[0:1].astype(I32)
    out_ref[3:4, 0:SLABS] = dot_rows(count, chosen)[0:1].astype(I32)

    third = functools.reduce(jnp.maximum, third), functools.reduce(jnp.add, third)
    most_z = jnp.max(third[0][:, 3 * SIDE :])
    most_x = jnp.max(third[1][:, 2 * SIDE : 3 * SIDE])
    fits = (most_x <= CAP_X) & (most_z <= CAP_Z)
    out_ref[4:5, :] = jnp.zeros((1, SIDE), I32) + fits.astype(I32)


def far_plan(position, union, along):
    return pl.pallas_call(
        far_plan_kernel,
        out_shape=jax.ShapeDtypeStruct((8, 128), I32),
        in_specs=[smem(), vmem(), vmem()],
        out_specs=vmem(),
        compiler_params=params(),
        cost_estimate=cost(2 * 20 * ROWS**3, 8 * ROWS**2),
        name="far_plan",
    )(position, union, along)


def dense(blocks, nonzero, columns):
    slab = lax.axis_index(ROW_AXES)
    part = lax.axis_index("col")
    masked = blocks * nonzero[:, :, None, None].astype(BF)
    slab_ids = jnp.arange(SLABS, dtype=I32)
    local_rows = jnp.arange(HEIGHT, dtype=I32)
    grouped = columns.reshape(SLABS, HEIGHT * SLOTS)
    targets = slab * HEIGHT + local_rows
    wanted = jnp.any(grouped[:, :, None] == targets[None, None, :], axis=1)
    wanted = wanted & (slab_ids != slab)[:, None]
    picked = jnp.sum(jnp.where(wanted, local_rows, 0), axis=1)
    filled = jnp.any(wanted, axis=1)
    outgoing = jnp.where(filled[:, None, None, None], masked[picked], jnp.zeros((), BF))
    incoming = lax.all_to_all(outgoing, ROW_AXES, split_axis=0, concat_axis=0, tiled=True)
    row_table = jnp.concatenate([incoming, masked], axis=0)
    own_cols = lax.dynamic_slice_in_dim(columns, slab * HEIGHT, HEIGHT, 0)
    source = own_cols // HEIGHT
    row_index = jnp.where(source == slab, SLABS + own_cols % HEIGHT, source)
    far_cols = columns[own_cols]
    far_quarter = lax.dynamic_slice_in_dim(far_cols, part * QUARTER, QUARTER, 2)
    whole = lax.all_gather(masked, "col", axis=1, tiled=True)
    results = []
    for member in range(HEIGHT):
        match = far_quarter[member][:, :, None] == own_cols[member][None, None, :]
        products = jnp.einsum(
            "tab,tubc->tuac", whole[member], row_table[row_index[member]],
            preferred_element_type=F32,
        )
        summed = lax.dot_general(
            match.astype(F32).reshape(SLOTS * QUARTER, SLOTS),
            products.reshape(SLOTS * QUARTER, SIDE * SIDE),
            (((0,), (0,)), ((), ())),
            precision=lax.Precision.HIGHEST,
            preferred_element_type=F32,
        )
        results.append(summed.reshape(SLOTS, SIDE, SIDE))
    square = lax.psum_scatter(jnp.stack(results), "col", scatter_dimension=1, tiled=True)
    return square.astype(BF)


def plane_columns(columns):
    split = columns.reshape(NX, NZ, NC, HEIGHT, NY, QUARTER)
    mine = lax.dynamic_index_in_dim(split, lax.axis_index("z"), 1, keepdims=False)
    mine = mine.transpose(3, 0, 1, 2, 4).reshape(PEERS, SLOTS)
    return jnp.pad(mine, ((0, 0), (0, HELD - SLOTS)), constant_values=-1).reshape(1, ENTRIES)


def shards(blocks, nonzero, columns):
    position = jnp.stack([lax.axis_index(name) for name in ROW_AXES + ("col",)])
    cuts = prepare(position, nonzero, blocks)
    cuts, names, same = lax.optimization_barrier((cuts, columns, blocks))
    turned = turn(nonzero, same)
    slots, union, need, kq = pattern(position, names, plane_columns(columns))
    near = lax.all_to_all(cuts, ("col", "x", "core"), split_axis=0, concat_axis=0, tiled=True)
    near, turned, need = lax.optimization_barrier((near, turned, need))
    whole = lax.all_gather(turned, "col", axis=0, tiled=False)
    whole = whole.reshape(ZERO_BLOCK, SIDE, SIDE)
    packed = send(need, kq, near.reshape(ENTRIES, PIECE))
    packed, slots = lax.optimization_barrier((packed, slots))
    along = lax.all_to_all(packed, "z", split_axis=0, concat_axis=0, tiled=True)
    along = along.reshape(NZ * ROWS_Z, PIECE)
    own_lists = own_plan(position, slots, union)
    packed, notes = lax.optimization_barrier((route(along), along))
    far = lax.all_to_all(packed, ("x", "core"), split_axis=0, concat_axis=0, tiled=True)
    far_lists = far_plan(position, union, notes)
    far = far.reshape(TARGETS * CAP_X, PIECE)
    own = own_sums(own_lists, whole)
    far, fits, own = lax.optimization_barrier((far, far_lists[4, 0] != 0, own))
    result = far_sums(own_lists, far_lists, whole, far, own)
    result = result.reshape(NY, HEIGHT, QUARTER, WIDE, SIDE)
    result = lax.all_to_all(result, "col", split_axis=0, concat_axis=0, tiled=True)
    square = finish(result)
    return lax.cond(
        fits,
        lambda value, *_: value,
        lambda _, *inputs: dense(*inputs),
        square,
        blocks,
        nonzero,
        columns,
    )


def solution(mesh):
    fine = Mesh(mesh.devices.reshape(NX, NZ, NC, NY), ROW_AXES + ("col",))
    spec = P(ROW_AXES, "col", None, None)
    return jax.shard_map(
        shards,
        mesh=fine,
        in_specs=(spec, P(ROW_AXES, "col"), P()),
        out_specs=spec,
        check_vma=False,
    )
```

```python
import functools

import jax
import jax.numpy as jnp
from jax import lax
from jax.experimental import pallas as pl
from jax.experimental.pallas import tpu as pltpu
from jax.sharding import Mesh
from jax.sharding import PartitionSpec as P

BF = jnp.bfloat16
F32 = jnp.float32
I32 = jnp.int32

NX, NZ, NC, NY = 4, 8, 2, 4
ROWS, SLOTS, SIDE = 256, 28, 128
HEIGHT, QUARTER = 4, 7
SLABS = ROWS // HEIGHT
PEERS = NX * NC * NY
HELD = 32
ENTRIES = PEERS * HELD
PIECE = SIDE * SIDE // PEERS
WIDE = SIDE // NY
TARGETS = NX * NC
CAP_Z = 124
ROWS_Z = 128
CAP_X = 120
GROUP = 8
FAR_GROUP = 4
ROWS_AT_ONCE = 4
HEIGHT_2 = NC * HEIGHT
OUT_COLS = 72
ZERO_BLOCK = NY * HEIGHT * QUARTER
VMEM_LIMIT = 48 * 1024 * 1024
ROW_AXES = ("x", "z", "core")


def vmem():
    return pl.BlockSpec(memory_space=pltpu.VMEM)


def smem():
    return pl.BlockSpec(memory_space=pltpu.SMEM)


def params():
    return pltpu.CompilerParams(vmem_limit_bytes=VMEM_LIMIT)


def cost(flops, moved):
    return pl.CostEstimate(flops=flops, bytes_accessed=moved, transcendentals=0)


def prepare_kernel(position_ref, keep_ref, blocks_ref, cuts_ref, rows_ref):
    x, core, part = position_ref[0], position_ref[2], position_ref[3]
    lanes = iota((8, ENTRIES), 1) - ((part * NX + x) * NC + core) * HELD
    flags = jnp.zeros((8, ENTRIES), F32)
    for row in range(HEIGHT):
        for slot in range(QUARTER):
            number = row * QUARTER + slot
            keep = keep_ref[row, slot] != 0
            flags = jnp.where((lanes == number) & keep, 1.0, flags)
            block = blocks_ref[row, slot].astype(F32)
            turned = jnp.where(keep, block, jnp.zeros_like(block)).T
            for quarter in range(NY):
                for part_of in range(NY):
                    begin = quarter * WIDE + part_of * TARGETS
                    rows = pl.ds(quarter * TARGETS * HELD + number, TARGETS, stride=HELD)
                    rows_ref[part_of, rows, :] = turned[begin : begin + TARGETS]
    for begin in range(0, PEERS, 8):
        for part_of in range(NY):
            for extra in range(HELD - SLOTS):
                rows = pl.ds(begin * HELD + SLOTS + extra, 8, stride=HELD)
                at = extra * PIECE + part_of * SIDE
                value = flags[:, at : at + SIDE] if extra < 2 else jnp.zeros((8, SIDE), F32)
                rows_ref[part_of, rows, :] = value
    for peer in range(PEERS):
        rows = pl.ds(peer * HELD, HELD)
        cuts_ref[peer] = jnp.concatenate(
            [rows_ref[part_of, rows, :] for part_of in range(NY)], axis=1
        ).astype(BF)


def prepare(position, nonzero, blocks):
    return pl.pallas_call(
        prepare_kernel,
        out_shape=jax.ShapeDtypeStruct((PEERS, HELD, PIECE), BF),
        in_specs=[smem(), smem(), vmem()],
        out_specs=vmem(),
        scratch_shapes=[pltpu.VMEM((NY, ENTRIES, SIDE), F32)],
        compiler_params=params(),
        name="prepare",
    )(position, nonzero, blocks)


def turn_kernel(keep_ref, blocks_ref, out_ref):
    for row in range(HEIGHT):
        for slot in range(QUARTER):
            block = blocks_ref[row, slot]
            out_ref[row, slot] = jnp.where(
                keep_ref[row, slot] != 0, block, jnp.zeros_like(block)
            ).T


def turn(nonzero, blocks):
    return pl.pallas_call(
        turn_kernel,
        out_shape=jax.ShapeDtypeStruct((HEIGHT, QUARTER, SIDE, SIDE), BF),
        in_specs=[smem(), vmem()],
        out_specs=vmem(),
        compiler_params=params(),
        cost_estimate=cost(2 * SLOTS * SIDE**3, 4 * SLOTS * SIDE**2),
        name="turn",
    )(nonzero, blocks)


def own_block(whole_ref, place, rows):
    value = whole_ref[jnp.minimum(place, ZERO_BLOCK - 1), rows, :]
    return jnp.where(place < ZERO_BLOCK, value, jnp.zeros_like(value))


def out_place(place):
    return (place // QUARTER) % HEIGHT, place // (QUARTER * HEIGHT) * QUARTER + place % QUARTER


def own_kernel(
    plan_ref,
    whole_ref,
    out_ref,
    total,
    panel,
    near,
):
    first = pl.multiple_of(plan_ref[15, 0] * WIDE, WIDE)
    for inner in range(HEIGHT):
        for member in range(HEIGHT):
            panel[pl.ds(inner * SIDE, SIDE), pl.ds(member * SIDE, SIDE)] = own_block(
                whole_ref, plan_ref[9 + member, inner], pl.ds(0, SIDE)
            )

    def step(group, carry):
        for at in range(GROUP):
            for inner in range(HEIGHT):
                near[pl.ds(at * WIDE, WIDE), pl.ds(inner * SIDE, SIDE)] = own_block(
                    whole_ref, plan_ref[4 + inner, group * GROUP + at], pl.ds(first, WIDE)
                )
        value = jnp.dot(near[...], panel[...], preferred_element_type=F32)
        total[pl.ds(group * GROUP, GROUP)] = value.reshape(GROUP, WIDE, HEIGHT * SIDE)
        return carry

    lax.fori_loop(0, plan_ref[15, 1], step, 0)
    for place in range(ZERO_BLOCK):
        member, slot = out_place(place)
        column = plan_ref[8, member * (128 // HEIGHT) + slot]
        out_ref[place] = total[column, :, pl.ds(member * SIDE, SIDE)]


def own_sums(lists, whole):
    flops = 2 * 32 * WIDE * (HEIGHT * SIDE) ** 2
    return pl.pallas_call(
        own_kernel,
        out_shape=jax.ShapeDtypeStruct((ZERO_BLOCK, WIDE, SIDE), F32),
        in_specs=[smem(), vmem()],
        out_specs=vmem(),
        scratch_shapes=[
            pltpu.VMEM((OUT_COLS, WIDE, HEIGHT * SIDE), F32),
            pltpu.VMEM((HEIGHT * SIDE, HEIGHT * SIDE), BF),
            pltpu.VMEM((GROUP * WIDE, HEIGHT * SIDE), BF),
        ],
        compiler_params=params(),
        cost_estimate=cost(flops, 3 * ZERO_BLOCK * SIDE * SIDE),
        name="own_sums",
    )(lists, whole)


def far_kernel(
    own_ref,
    plan_ref,
    whole_ref,
    far_ref,
    near_ref,
    out_ref,
    total,
    pieces_ref,
):
    for sender in range(TARGETS):
        rows = pl.ds(sender * CAP_X, CAP_X)
        for part in range(NY):
            lanes = slice(part * SIDE, (part + 1) * SIDE)
            pieces_ref[part, rows, :] = far_ref[rows, lanes].astype(F32)

    def clear(group, carry):
        total[pl.ds(group * GROUP, GROUP)] = jnp.zeros((GROUP, WIDE, HEIGHT * SIDE), F32)
        return carry

    lax.fori_loop(0, own_ref[15, 1], clear, 0)

    def product(named, offset):
        begin = plan_ref[2, named]
        length = plan_ref[3, named]
        right = jnp.concatenate(
            [
                own_block(whole_ref, own_ref[member, named], pl.ds(0, SIDE))
                for member in range(HEIGHT)
            ],
            axis=1,
        )
        pieces, columns = [], []
        for at in range(FAR_GROUP):
            place = jnp.minimum(begin + offset + at, CAP_X - 1)
            rows = pl.ds(plan_ref[0, place], TARGETS, stride=CAP_X)
            for part in range(NY):
                pieces.append(pieces_ref[part, rows, :])
            columns.append(jnp.where(offset + at < length, plan_ref[1, place], OUT_COLS))
        left = jnp.concatenate(pieces, axis=0).astype(BF)
        return jnp.dot(left, right, preferred_element_type=F32), columns

    def add(value, columns):
        for at, column in enumerate(columns):
            total[column] = total[column] + value[at * WIDE : (at + 1) * WIDE]

    def first_step(step, carry):
        done = [product(step * ROWS_AT_ONCE + at, 0) for at in range(ROWS_AT_ONCE)]
        for value, columns in done:
            add(value, columns)
        return carry

    named_rows = own_ref[15, 2]
    lax.fori_loop(0, (named_rows + ROWS_AT_ONCE - 1) // ROWS_AT_ONCE, first_step, 0)

    def rest(named, carry):
        def rest_step(step, inner_carry):
            add(*product(named, step * FAR_GROUP))
            return inner_carry

        lax.fori_loop(1, (plan_ref[3, named] + FAR_GROUP - 1) // FAR_GROUP, rest_step, 0)
        return carry

    lax.fori_loop(0, named_rows, rest, 0)

    for place in range(ZERO_BLOCK):
        member, slot = out_place(place)
        column = own_ref[8, member * (128 // HEIGHT) + slot]
        value = total[column, :, pl.ds(member * SIDE, SIDE)] + near_ref[place]
        out_ref[place] = value.astype(BF)


def far_sums(own_lists, far_lists, whole, far, near):
    return pl.pallas_call(
        far_kernel,
        out_shape=jax.ShapeDtypeStruct((ZERO_BLOCK, WIDE, SIDE), BF),
        in_specs=[smem(), smem(), vmem(), vmem(), vmem()],
        out_specs=vmem(),
        scratch_shapes=[
            pltpu.VMEM((OUT_COLS + 1, WIDE, HEIGHT * SIDE), F32),
            pltpu.VMEM((NY, TARGETS * CAP_X, SIDE), F32),
        ],
        compiler_params=params(),
        name="far_sums",
    )(own_lists, far_lists, whole, far, near)


def finish_kernel(cuts_ref, out_ref):
    for row in range(HEIGHT):
        for slot in range(QUARTER):
            turned = jnp.concatenate([cuts_ref[part, row, slot] for part in range(NY)], axis=0)
            out_ref[row, slot] = turned.T


def finish(cuts):
    return pl.pallas_call(
        finish_kernel,
        out_shape=jax.ShapeDtypeStruct((HEIGHT, QUARTER, SIDE, SIDE), BF),
        in_specs=[vmem()],
        out_specs=vmem(),
        compiler_params=params(),
        name="finish",
    )(cuts)


def iota(shape, axis):
    return lax.broadcasted_iota(I32, shape, axis)


def dot(a, b):
    return jnp.dot(a.astype(BF), b.astype(BF), preferred_element_type=F32)


def dot_rows(a, b):
    return lax.dot_general(
        a.astype(BF), b.astype(BF), (((1,), (1,)), ((), ())), preferred_element_type=F32
    )


def earlier(size):
    return (iota((size, size), 0) < iota((size, size), 1)).astype(F32)


def places(need):
    order = earlier(SIDE)
    parts = []
    before = jnp.zeros((need.shape[0], 1), F32)
    for begin in range(0, need.shape[1], SIDE):
        part = need[:, begin : begin + SIDE]
        parts.append(dot(part, order) + before)
        before = before + jnp.sum(part, axis=1, keepdims=True)
    return jnp.concatenate(parts, axis=1)


def codes(need, capacity):
    place = places(need)
    return jnp.where((need > 0) & (place < capacity), place, -1.0)


def one_hot(code, rows):
    return (iota((rows, code.shape[1]), 0).astype(F32) == code).astype(F32)


def quarter_of(slot):
    return sum((slot >= bound * QUARTER).astype(I32) for bound in range(1, NY))


def pattern_kernel(position_ref, columns_ref, entries_ref, slots_ref, union_ref, need_ref, kq_ref):
    step = 64
    for begin in range(0, ROWS, step):
        column = iota((step, ROWS), 1)
        found = jnp.full((step, ROWS), -1, I32)
        for slot in range(SLOTS):
            at = columns_ref[begin : begin + step, slot : slot + 1]
            found = jnp.where(at == column, slot, found)
        slots_ref[begin : begin + step, :] = found
    names = (slots_ref[...] >= 0).astype(F32)
    mine = iota((128, ROWS), 1) // HEIGHT == iota((128, ROWS), 0)
    union = (dot(mine.astype(F32), names) > 0).astype(F32)
    union_ref[...] = union

    entry = iota((1, ENTRIES), 1)
    peer, number = entry // HELD, entry % HELD
    x, core = (peer // NC) % NX, peer % NC
    row = ((x * NZ + position_ref[1]) * NC + core) * HEIGHT + quarter_of(number)
    column = entries_ref[...]
    every = iota((ROWS, ENTRIES), 0)
    named = dot(jnp.where(mine, 0.0, union), (every == row).astype(F32))
    need_ref[...] = named * dot(union, (every == column).astype(F32))
    kind = iota((8, ENTRIES), 0)
    both = jnp.where(kind == 1, jnp.maximum(column, 0), 0)
    kq_ref[...] = jnp.where(kind == 0, row, both).astype(F32)


def pattern(position, columns, entries):
    return pl.pallas_call(
        pattern_kernel,
        out_shape=(
            jax.ShapeDtypeStruct((ROWS, ROWS), I32),
            jax.ShapeDtypeStruct((128, ROWS), F32),
            jax.ShapeDtypeStruct((128, ENTRIES), F32),
            jax.ShapeDtypeStruct((8, ENTRIES), F32),
        ),
        in_specs=[smem(), vmem(), vmem()],
        out_specs=(vmem(), vmem(), vmem(), vmem()),
        compiler_params=params(),
        cost_estimate=cost(2 * SLOTS * ROWS**3 // 4, 8 * ROWS**2),
        name="pattern",
    )(position, columns, entries)


def send_kernel(position_ref, need_ref, kq_ref, near_ref, *refs):
    *out_refs, chosen_ref = refs
    z = position_ref[1]
    near = near_ref[...]
    kind = iota((8, ENTRIES), 0)
    pick = (iota((8, ENTRIES), 1) % HELD == SLOTS + kind) & (kind < 2)
    flags = dot(pick.astype(F32), near)
    flags = jnp.concatenate([flags[0:1], flags[1:2]], axis=1)
    need = need_ref[...] * flags
    slab = iota((8, 128), 1)
    plane = (slab // NC) % NZ == (iota((8, 128), 0) + z) & (NZ - 1)
    wanted = (dot(plane.astype(F32), need) > 0).astype(F32)
    code = codes(wanted, CAP_Z)
    most = jnp.max(jnp.sum(wanted, axis=1, keepdims=True), axis=0, keepdims=True)
    most = jnp.broadcast_to(jnp.minimum(most, 250.0), (1, 128))
    totals = jnp.minimum(dot_rows(jnp.ones((8, ENTRIES), F32), need)[0:1], 250.0)
    for to in range(NZ):
        chosen_ref[to * ROWS_Z : (to + 1) * ROWS_Z, :] = one_hot(code[to : to + 1], ROWS_Z).astype(BF)
    packed = jnp.dot(chosen_ref[...], near, preferred_element_type=F32)
    tail = iota((16, PIECE), 0)
    kq = kq_ref[...]
    for to in range(NZ):
        target = iota((8, 128), 0)
        choice = slab == (target // NC * NZ + ((z + to) & (NZ - 1))) * NC + target % NC
        asked = jnp.concatenate([dot(choice.astype(F32), need), kq], axis=0)
        notes = dot_rows(asked, chosen_ref[to * ROWS_Z : (to + 1) * ROWS_Z, :])
        first = jnp.concatenate([notes[i : i + 1] for i in range(4)], axis=1)
        second = jnp.concatenate([notes[i : i + 1] for i in range(4, 8)], axis=1)
        third = jnp.concatenate([notes[8:9], notes[9:10], totals, most], axis=1)
        begin = to * ROWS_Z
        out_refs[to][0 : ROWS_Z - 16] = packed[begin : begin + ROWS_Z - 16].astype(BF)
        value = packed[begin + ROWS_Z - 16 : begin + ROWS_Z]
        value = jnp.where(tail == 12, first, value)
        value = jnp.where(tail == 13, second, value)
        value = jnp.where(tail == 14, third, value)
        out_refs[to][ROWS_Z - 16 : ROWS_Z] = value.astype(BF)


def send(position, need, kq, near):
    return pl.pallas_call(
        send_kernel,
        out_shape=[jax.ShapeDtypeStruct((ROWS_Z, PIECE), BF)] * NZ,
        in_specs=[smem()] + [vmem()] * 3,
        out_specs=[vmem()] * NZ,
        scratch_shapes=[pltpu.VMEM((NZ * ROWS_Z, ENTRIES), BF)],
        compiler_params=params(),
        name="send",
    )(position, need, kq, near)


def notes_of(along_refs):
    asked, third = [], []
    for along_ref in along_refs:
        notes = along_ref[ROWS_Z - 16 : ROWS_Z].astype(F32)
        asked.append(
            jnp.concatenate(
                [
                    notes[12 + i // 4 : 13 + i // 4, i % 4 * SIDE : (i % 4 + 1) * SIDE]
                    for i in range(TARGETS)
                ],
                axis=0,
            )
        )
        third.append(notes[14:15])
    return jnp.concatenate(asked, axis=1), third


def route_kernel(*refs):
    *along_refs, out_ref, chosen_ref, along_ref = refs
    asked, _ = notes_of(along_refs)
    for number, ref in enumerate(along_refs):
        along_ref[number * ROWS_Z : (number + 1) * ROWS_Z] = ref[...]
    code = codes(asked, CAP_X)
    for to in range(TARGETS):
        chosen_ref[to * SIDE : (to + 1) * SIDE, :] = one_hot(code[to : to + 1], SIDE).astype(BF)
    packed = jnp.dot(chosen_ref[...], along_ref[...], preferred_element_type=F32)
    for to in range(TARGETS):
        out_ref[to] = packed[to * SIDE : to * SIDE + CAP_X].astype(BF)


def route(along):
    return pl.pallas_call(
        route_kernel,
        out_shape=jax.ShapeDtypeStruct((TARGETS, CAP_X, PIECE), BF),
        in_specs=[vmem()] * NZ,
        out_specs=vmem(),
        scratch_shapes=[
            pltpu.VMEM((TARGETS * SIDE, NZ * ROWS_Z), BF),
            pltpu.VMEM((NZ * ROWS_Z, PIECE), BF),
        ],
        compiler_params=params(),
        name="route",
    )(*along)


def own_plan_kernel(position_ref, slots_ref, union_ref, out_ref):
    x, z, core, part = (position_ref[i] for i in range(4))
    chip = x * NZ + z
    slab = chip * NC + core
    order = earlier(ROWS)
    out_ref[...] = jnp.zeros_like(out_ref)
    mine = union_ref[pl.ds(slab, 1), :]
    rank = dot(jnp.broadcast_to(mine, (8, ROWS)), order)

    both = slots_ref[pl.ds(pl.multiple_of(chip * HEIGHT_2, HEIGHT_2), HEIGHT_2), :]
    swapped = jnp.concatenate([both[HEIGHT:], both[:HEIGHT]], axis=0)
    slot = jnp.where(core == 0, both, swapped)
    quarter = quarter_of(slot)
    held = (quarter * HEIGHT + iota(slot.shape, 0)) * QUARTER + slot - quarter * QUARTER
    held = jnp.where(slot >= 0, held - ZERO_BLOCK, 0).astype(F32)

    every = iota((1, ROWS), 1)
    named = jnp.where(every // HEIGHT == slab, 0.0, mine)
    position = dot(jnp.broadcast_to(named, (8, ROWS)), order)[0:1]
    number = iota((SLABS, ROWS), 0).astype(F32)
    chosen = ((position == number) & (named > 0)).astype(F32)
    out_ref[0:4, 0:SLABS] = dot_rows(held, chosen)[0:HEIGHT].astype(I32) + ZERO_BLOCK

    number = iota((OUT_COLS, ROWS), 0).astype(F32)
    chosen = ((rank[0:1] == number) & (mine > 0)).astype(F32)
    out_ref[4:8, 0:OUT_COLS] = dot_rows(held, chosen)[0:HEIGHT].astype(I32) + ZERO_BLOCK
    wide = 128 // HEIGHT
    chosen = jnp.concatenate(
        [slot[i : i + 1] == iota((wide, ROWS), 0) for i in range(HEIGHT)], axis=0
    )
    out_ref[8:9, 0:128] = dot_rows(rank, chosen.astype(F32))[0:1].astype(I32)
    chosen = (iota((8, ROWS), 1) == iota((8, ROWS), 0) + slab * HEIGHT).astype(F32)
    out_ref[9:13, 0:8] = dot_rows(held, chosen)[0:HEIGHT].astype(I32) + ZERO_BLOCK
    groups = ((jnp.sum(mine) + (GROUP - 1)) * (1.0 / GROUP)).astype(I32)
    lane = iota((1, 128), 1)
    scalars = jnp.where(lane == 0, part, 0)
    scalars = jnp.where(lane == 1, groups, scalars)
    out_ref[15:16, :] = jnp.where(lane == 2, jnp.sum(named).astype(I32), scalars)


def own_plan(position, slots, union):
    return pl.pallas_call(
        own_plan_kernel,
        out_shape=jax.ShapeDtypeStruct((16, 128), I32),
        in_specs=[smem(), vmem(), vmem()],
        out_specs=vmem(),
        compiler_params=params(),
        cost_estimate=cost(ROWS**3, 4 * ROWS**2),
        name="own_plan",
    )(position, slots, union)


def far_plan_kernel(position_ref, union_ref, *refs):
    *along_refs, out_ref = refs
    x, z, core = (position_ref[i] for i in range(3))
    slab = (x * NZ + z) * NC + core
    out_ref[...] = jnp.zeros_like(out_ref)
    asked, third = notes_of(along_refs)
    mine = iota(asked.shape, 0) == x * NC + core
    asked = jnp.sum(jnp.where(mine, asked, 0.0), axis=0, keepdims=True)
    number = jnp.sum(asked).astype(I32)
    code = codes(jnp.broadcast_to(asked, (8, asked.shape[1])), CAP_X)[0:1]
    chosen = one_hot(code, SIDE)
    row = jnp.concatenate([part[:, :SIDE] for part in third], axis=1)
    column = jnp.concatenate([part[:, SIDE : 2 * SIDE] for part in third], axis=1)
    row_down = jnp.sum(chosen * row, axis=1, keepdims=True).astype(I32)
    column_down = jnp.sum(chosen * column, axis=1, keepdims=True).astype(I32)
    row_along = dot_rows(jnp.broadcast_to(row, (8, row.shape[1])), chosen)[0:1].astype(I32)

    down, along = iota((SIDE, SIDE), 0), iota((SIDE, SIDE), 1)
    less = (row_down < row_along) | ((row_down == row_along) & (down < along))
    order = jnp.sum((less & (down < number)).astype(F32), axis=0, keepdims=True)
    ordered = ((order == down.astype(F32)) & (along < number)).astype(F32)
    position = iota((8, SIDE), 1).astype(F32)
    out_ref[0:1, 0:SIDE] = dot_rows(position, ordered)[0:1].astype(I32)
    names = union_ref[pl.ds(slab, 1), :]
    order = earlier(ROWS)
    rank = dot(jnp.broadcast_to(names, (8, ROWS)), order)
    every = iota((SIDE, ROWS), 1)
    rank = dot_rows(rank, (every == column_down).astype(F32))
    out_ref[1:2, 0:SIDE] = dot_rows(rank, ordered)[0:1].astype(I32)

    valid = iota((SIDE, ROWS), 0) < number
    count = dot(jnp.ones((8, SIDE), F32), ((every == row_down) & valid).astype(F32))
    start = jnp.minimum(dot(count, order), 250.0)
    row = jnp.where(iota((1, ROWS), 1) // HEIGHT == slab, 0.0, names)
    position = dot(jnp.broadcast_to(row, (8, ROWS)), order)[0:1]
    chosen = ((position == iota((SLABS, ROWS), 0).astype(F32)) & (row > 0)).astype(F32)
    out_ref[2:3, 0:SLABS] = dot_rows(start, chosen)[0:1].astype(I32)
    out_ref[3:4, 0:SLABS] = dot_rows(count, chosen)[0:1].astype(I32)

    third = functools.reduce(jnp.maximum, third), functools.reduce(jnp.add, third)
    most_z = jnp.max(third[0][:, 3 * SIDE :])
    most_x = jnp.max(third[1][:, 2 * SIDE : 3 * SIDE])
    fits = (most_x <= CAP_X) & (most_z <= CAP_Z)
    out_ref[4:5, :] = jnp.zeros((1, SIDE), I32) + fits.astype(I32)


def far_plan(position, union, along):
    return pl.pallas_call(
        far_plan_kernel,
        out_shape=jax.ShapeDtypeStruct((8, 128), I32),
        in_specs=[smem()] + [vmem()] * (1 + NZ),
        out_specs=vmem(),
        compiler_params=params(),
        cost_estimate=cost(2 * 20 * ROWS**3, 8 * ROWS**2),
        name="far_plan",
    )(position, union, *along)


def dense(blocks, nonzero, columns):
    slab = lax.axis_index(ROW_AXES)
    part = lax.axis_index("col")
    masked = blocks * nonzero[:, :, None, None].astype(BF)
    slab_ids = jnp.arange(SLABS, dtype=I32)
    local_rows = jnp.arange(HEIGHT, dtype=I32)
    grouped = columns.reshape(SLABS, HEIGHT * SLOTS)
    targets = slab * HEIGHT + local_rows
    wanted = jnp.any(grouped[:, :, None] == targets[None, None, :], axis=1)
    wanted = wanted & (slab_ids != slab)[:, None]
    picked = jnp.sum(jnp.where(wanted, local_rows, 0), axis=1)
    filled = jnp.any(wanted, axis=1)
    outgoing = jnp.where(filled[:, None, None, None], masked[picked], jnp.zeros((), BF))
    incoming = lax.all_to_all(outgoing, ROW_AXES, split_axis=0, concat_axis=0, tiled=True)
    row_table = jnp.concatenate([incoming, masked], axis=0)
    own_cols = lax.dynamic_slice_in_dim(columns, slab * HEIGHT, HEIGHT, 0)
    source = own_cols // HEIGHT
    row_index = jnp.where(source == slab, SLABS + own_cols % HEIGHT, source)
    far_cols = columns[own_cols]
    far_quarter = lax.dynamic_slice_in_dim(far_cols, part * QUARTER, QUARTER, 2)
    whole = lax.all_gather(masked, "col", axis=1, tiled=True)
    results = []
    for member in range(HEIGHT):
        match = far_quarter[member][:, :, None] == own_cols[member][None, None, :]
        products = jnp.einsum(
            "tab,tubc->tuac", whole[member], row_table[row_index[member]],
            preferred_element_type=F32,
        )
        summed = lax.dot_general(
            match.astype(F32).reshape(SLOTS * QUARTER, SLOTS),
            products.reshape(SLOTS * QUARTER, SIDE * SIDE),
            (((0,), (0,)), ((), ())),
            precision=lax.Precision.HIGHEST,
            preferred_element_type=F32,
        )
        results.append(summed.reshape(SLOTS, SIDE, SIDE))
    square = lax.psum_scatter(jnp.stack(results), "col", scatter_dimension=1, tiled=True)
    return square.astype(BF)


def plane_columns(columns):
    split = columns.reshape(NX, NZ, NC, HEIGHT, NY, QUARTER)
    mine = lax.dynamic_index_in_dim(split, lax.axis_index("z"), 1, keepdims=False)
    mine = mine.transpose(3, 0, 1, 2, 4).reshape(PEERS, SLOTS)
    return jnp.pad(mine, ((0, 0), (0, HELD - SLOTS)), constant_values=-1).reshape(1, ENTRIES)


def shards(blocks, nonzero, columns):
    position = jnp.stack([lax.axis_index(name) for name in ROW_AXES + ("col",)])
    cuts = prepare(position, nonzero, blocks)
    cuts, names, same = lax.optimization_barrier((cuts, columns, blocks))
    turned = turn(nonzero, same)
    slots, union, need, kq = pattern(position, names, plane_columns(columns))
    near = lax.all_to_all(cuts, ("col", "x", "core"), split_axis=0, concat_axis=0, tiled=True)
    near, turned, need = lax.optimization_barrier((near, turned, need))
    whole = lax.all_gather(turned, "col", axis=0, tiled=False)
    whole = whole.reshape(ZERO_BLOCK, SIDE, SIDE)
    packed = send(position, need, kq, near.reshape(ENTRIES, PIECE))
    packed, slots = lax.optimization_barrier((packed, slots))
    along = [packed[0]] + [
        lax.ppermute(packed[step], "z", [(i, (i + step) % NZ) for i in range(NZ)])
        for step in range(1, NZ)
    ]
    own_lists = own_plan(position, slots, union)
    packed, notes = lax.optimization_barrier((route(along), along))
    far = lax.all_to_all(packed, ("x", "core"), split_axis=0, concat_axis=0, tiled=True)
    far_lists = far_plan(position, union, notes)
    far = far.reshape(TARGETS * CAP_X, PIECE)
    own = own_sums(own_lists, whole)
    far, fits, own = lax.optimization_barrier((far, far_lists[4, 0] != 0, own))
    result = far_sums(own_lists, far_lists, whole, far, own)
    result = result.reshape(NY, HEIGHT, QUARTER, WIDE, SIDE)
    result = lax.all_to_all(result, "col", split_axis=0, concat_axis=0, tiled=True)
    square = finish(result)
    return lax.cond(
        fits,
        lambda value, *_: value,
        lambda _, *inputs: dense(*inputs),
        square,
        blocks,
        nonzero,
        columns,
    )


def solution(mesh):
    fine = Mesh(mesh.devices.reshape(NX, NZ, NC, NY), ROW_AXES + ("col",))
    spec = P(ROW_AXES, "col", None, None)
    return jax.shard_map(
        shards,
        mesh=fine,
        in_specs=(spec, P(ROW_AXES, "col"), P()),
        out_specs=spec,
        check_vma=False,
    )
```

```python
import functools

import jax
import jax.numpy as jnp
from jax import lax
from jax.experimental import pallas as pl
from jax.experimental.pallas import tpu as pltpu
from jax.sharding import Mesh
from jax.sharding import PartitionSpec as P

BF = jnp.bfloat16
F32 = jnp.float32
I32 = jnp.int32

NX, NZ, NC, NY = 4, 8, 2, 4
ROWS, SLOTS, SIDE = 256, 28, 128
HEIGHT, QUARTER = 4, 7
SLABS = ROWS // HEIGHT
PEERS = NX * NC * NY
HELD = 32
ENTRIES = PEERS * HELD
PIECE = SIDE * SIDE // PEERS
WIDE = SIDE // NY
TARGETS = NX * NC
CAP_Z = 124
ROWS_Z = 128
CAP_X = 120
ORDER_Z = (3, 5, 4, 2, 6, 1, 7)
ORDER_Y = (1, 3, 2)
GROUP = 8
FAR_GROUP = 4
ROWS_AT_ONCE = 4
HEIGHT_2 = NC * HEIGHT
OUT_COLS = 72
ZERO_BLOCK = NY * HEIGHT * QUARTER
VMEM_LIMIT = 48 * 1024 * 1024
ROW_AXES = ("x", "z", "core")


def vmem():
    return pl.BlockSpec(memory_space=pltpu.VMEM)


def smem():
    return pl.BlockSpec(memory_space=pltpu.SMEM)


def params():
    return pltpu.CompilerParams(vmem_limit_bytes=VMEM_LIMIT)


def cost(flops, moved):
    return pl.CostEstimate(flops=flops, bytes_accessed=moved, transcendentals=0)


def prepare_kernel(position_ref, keep_ref, blocks_ref, cuts_ref, rows_ref):
    x, core, part = position_ref[0], position_ref[2], position_ref[3]
    lanes = iota((8, ENTRIES), 1) - ((part * NX + x) * NC + core) * HELD
    flags = jnp.zeros((8, ENTRIES), F32)
    for row in range(HEIGHT):
        for slot in range(QUARTER):
            number = row * QUARTER + slot
            keep = keep_ref[row, slot] != 0
            flags = jnp.where((lanes == number) & keep, 1.0, flags)
            block = blocks_ref[row, slot]
            turned = jnp.where(keep, block, jnp.zeros_like(block)).T.astype(F32)
            for quarter in range(NY):
                for part_of in range(NY):
                    begin = quarter * WIDE + part_of * TARGETS
                    rows = pl.ds(quarter * TARGETS * HELD + number, TARGETS, stride=HELD)
                    rows_ref[part_of, rows, :] = turned[begin : begin + TARGETS]
    for begin in range(0, PEERS, 8):
        for part_of in range(NY):
            for extra in range(HELD - SLOTS):
                rows = pl.ds(begin * HELD + SLOTS + extra, 8, stride=HELD)
                at = extra * PIECE + part_of * SIDE
                value = flags[:, at : at + SIDE] if extra < 2 else jnp.zeros((8, SIDE), F32)
                rows_ref[part_of, rows, :] = value
    for peer in range(PEERS):
        rows = pl.ds(peer * HELD, HELD)
        cuts_ref[peer] = jnp.concatenate(
            [rows_ref[part_of, rows, :] for part_of in range(NY)], axis=1
        ).astype(BF)


def prepare(position, nonzero, blocks):
    return pl.pallas_call(
        prepare_kernel,
        out_shape=jax.ShapeDtypeStruct((PEERS, HELD, PIECE), BF),
        in_specs=[smem(), smem(), vmem()],
        out_specs=vmem(),
        scratch_shapes=[pltpu.VMEM((NY, ENTRIES, SIDE), F32)],
        compiler_params=params(),
        name="prepare",
    )(position, nonzero, blocks)


def turn_kernel(keep_ref, blocks_ref, out_ref):
    for row in range(HEIGHT):
        for slot in range(QUARTER):
            block = blocks_ref[row, slot]
            out_ref[row, slot] = jnp.where(
                keep_ref[row, slot] != 0, block, jnp.zeros_like(block)
            ).T


def turn(nonzero, blocks):
    return pl.pallas_call(
        turn_kernel,
        out_shape=jax.ShapeDtypeStruct((HEIGHT, QUARTER, SIDE, SIDE), BF),
        in_specs=[smem(), vmem()],
        out_specs=vmem(),
        compiler_params=params(),
        cost_estimate=cost(2 * SLOTS * SIDE**3, 4 * SLOTS * SIDE**2),
        name="turn",
    )(nonzero, blocks)


def own_block(whole_ref, place, rows):
    value = whole_ref[jnp.minimum(place, ZERO_BLOCK - 1), rows, :]
    return jnp.where(place < ZERO_BLOCK, value, jnp.zeros_like(value))


def out_place(place):
    return (place // QUARTER) % HEIGHT, place // (QUARTER * HEIGHT) * QUARTER + place % QUARTER


def own_kernel(
    plan_ref,
    whole_ref,
    out_ref,
    total,
    panel,
    near,
):
    first = pl.multiple_of(plan_ref[15, 0] * WIDE, WIDE)
    for inner in range(HEIGHT):
        for member in range(HEIGHT):
            panel[pl.ds(inner * SIDE, SIDE), pl.ds(member * SIDE, SIDE)] = own_block(
                whole_ref, plan_ref[9 + member, inner], pl.ds(0, SIDE)
            )

    def step(group, carry):
        for at in range(GROUP):
            for inner in range(HEIGHT):
                near[pl.ds(at * WIDE, WIDE), pl.ds(inner * SIDE, SIDE)] = own_block(
                    whole_ref, plan_ref[4 + inner, group * GROUP + at], pl.ds(first, WIDE)
                )
        value = jnp.dot(near[...], panel[...], preferred_element_type=F32)
        total[pl.ds(group * GROUP, GROUP)] = value.reshape(GROUP, WIDE, HEIGHT * SIDE)
        return carry

    lax.fori_loop(0, plan_ref[15, 1], step, 0)
    for place in range(ZERO_BLOCK):
        member, slot = out_place(place)
        column = plan_ref[8, member * (128 // HEIGHT) + slot]
        out_ref[place] = total[column, :, pl.ds(member * SIDE, SIDE)]


def own_sums(lists, whole):
    flops = 2 * 32 * WIDE * (HEIGHT * SIDE) ** 2
    return pl.pallas_call(
        own_kernel,
        out_shape=jax.ShapeDtypeStruct((ZERO_BLOCK, WIDE, SIDE), F32),
        in_specs=[smem(), vmem()],
        out_specs=vmem(),
        scratch_shapes=[
            pltpu.VMEM((OUT_COLS, WIDE, HEIGHT * SIDE), F32),
            pltpu.VMEM((HEIGHT * SIDE, HEIGHT * SIDE), BF),
            pltpu.VMEM((GROUP * WIDE, HEIGHT * SIDE), BF),
        ],
        compiler_params=params(),
        cost_estimate=cost(flops, 3 * ZERO_BLOCK * SIDE * SIDE),
        name="own_sums",
    )(lists, whole)


def far_kernel(
    own_ref,
    plan_ref,
    whole_ref,
    far_ref,
    near_ref,
    *refs,
):
    *out_refs, total, pieces_ref = refs
    for sender in range(TARGETS):
        rows = pl.ds(sender * CAP_X, CAP_X)
        for part in range(NY):
            lanes = slice(part * SIDE, (part + 1) * SIDE)
            pieces_ref[part, rows, :] = far_ref[rows, lanes].astype(F32)

    def clear(group, carry):
        total[pl.ds(group * GROUP, GROUP)] = jnp.zeros((GROUP, WIDE, HEIGHT * SIDE), F32)
        return carry

    lax.fori_loop(0, own_ref[15, 1], clear, 0)

    def product(named, offset):
        begin = plan_ref[2, named]
        length = plan_ref[3, named]
        right = jnp.concatenate(
            [
                own_block(whole_ref, own_ref[member, named], pl.ds(0, SIDE))
                for member in range(HEIGHT)
            ],
            axis=1,
        )
        pieces, columns = [], []
        for at in range(FAR_GROUP):
            place = jnp.minimum(begin + offset + at, CAP_X - 1)
            rows = pl.ds(plan_ref[0, place], TARGETS, stride=CAP_X)
            for part in range(NY):
                pieces.append(pieces_ref[part, rows, :])
            columns.append(jnp.where(offset + at < length, plan_ref[1, place], OUT_COLS))
        left = jnp.concatenate(pieces, axis=0).astype(BF)
        return jnp.dot(left, right, preferred_element_type=F32), columns

    def add(value, columns):
        for at, column in enumerate(columns):
            total[column] = total[column] + value[at * WIDE : (at + 1) * WIDE]

    def first_step(step, carry):
        done = [product(step * ROWS_AT_ONCE + at, 0) for at in range(ROWS_AT_ONCE)]
        for value, columns in done:
            add(value, columns)
        return carry

    named_rows = own_ref[15, 2]
    lax.fori_loop(0, (named_rows + ROWS_AT_ONCE - 1) // ROWS_AT_ONCE, first_step, 0)

    def rest(named, carry):
        def rest_step(step, inner_carry):
            add(*product(named, step * FAR_GROUP))
            return inner_carry

        lax.fori_loop(1, (plan_ref[3, named] + FAR_GROUP - 1) // FAR_GROUP, rest_step, 0)
        return carry

    lax.fori_loop(0, named_rows, rest, 0)

    for step, out_ref in enumerate(out_refs):
        part = (own_ref[15, 0] + step) & (NY - 1)
        for place in range(HEIGHT * QUARTER):
            member, slot = place // QUARTER, part * QUARTER + place % QUARTER
            column = own_ref[8, member * (128 // HEIGHT) + slot]
            value = total[column, :, pl.ds(member * SIDE, SIDE)]
            value = value + near_ref[part * (HEIGHT * QUARTER) + place]
            out_ref[place] = value.astype(BF)


def far_sums(own_lists, far_lists, whole, far, near):
    return pl.pallas_call(
        far_kernel,
        out_shape=[jax.ShapeDtypeStruct((HEIGHT * QUARTER, WIDE, SIDE), BF)] * NY,
        in_specs=[smem(), smem(), vmem(), vmem(), vmem()],
        out_specs=[vmem()] * NY,
        scratch_shapes=[
            pltpu.VMEM((OUT_COLS + 1, WIDE, HEIGHT * SIDE), F32),
            pltpu.VMEM((NY, TARGETS * CAP_X, SIDE), F32),
        ],
        compiler_params=params(),
        name="far_sums",
    )(own_lists, far_lists, whole, far, near)


def finish_kernel(position_ref, *refs):
    *cut_refs, out_ref, turned_ref = refs
    for step, cut_ref in zip((0,) + ORDER_Y, cut_refs):
        part = (position_ref[3] - step) & (NY - 1)
        rows = pl.ds(pl.multiple_of(part * WIDE, WIDE), WIDE)
        for place in range(HEIGHT * QUARTER):
            turned_ref[place, rows, :] = cut_ref[place]
    for row in range(HEIGHT):
        for slot in range(QUARTER):
            out_ref[row, slot] = turned_ref[row * QUARTER + slot].T


def finish(position, cuts):
    return pl.pallas_call(
        finish_kernel,
        out_shape=jax.ShapeDtypeStruct((HEIGHT, QUARTER, SIDE, SIDE), BF),
        in_specs=[smem()] + [vmem()] * NY,
        out_specs=vmem(),
        scratch_shapes=[pltpu.VMEM((HEIGHT * QUARTER, SIDE, SIDE), BF)],
        compiler_params=params(),
        name="finish",
    )(position, *cuts)


def iota(shape, axis):
    return lax.broadcasted_iota(I32, shape, axis)


def dot(a, b):
    return jnp.dot(a.astype(BF), b.astype(BF), preferred_element_type=F32)


def dot_rows(a, b):
    return lax.dot_general(
        a.astype(BF), b.astype(BF), (((1,), (1,)), ((), ())), preferred_element_type=F32
    )


def earlier(size):
    return (iota((size, size), 0) < iota((size, size), 1)).astype(F32)


def places(need):
    order = earlier(SIDE)
    parts = []
    before = jnp.zeros((need.shape[0], 1), F32)
    for begin in range(0, need.shape[1], SIDE):
        part = need[:, begin : begin + SIDE]
        parts.append(dot(part, order) + before)
        before = before + jnp.sum(part, axis=1, keepdims=True)
    return jnp.concatenate(parts, axis=1)


def codes(need, capacity):
    place = places(need)
    return jnp.where((need > 0) & (place < capacity), place, -1.0)


def one_hot(code, rows):
    return (iota((rows, code.shape[1]), 0).astype(F32) == code).astype(F32)


def quarter_of(slot):
    return sum((slot >= bound * QUARTER).astype(I32) for bound in range(1, NY))


def pattern_kernel(position_ref, columns_ref, entries_ref, slots_ref, union_ref, need_ref, kq_ref):
    step = 64
    for begin in range(0, ROWS, step):
        column = iota((step, ROWS), 1)
        found = jnp.full((step, ROWS), -1, I32)
        for slot in range(SLOTS):
            at = columns_ref[begin : begin + step, slot : slot + 1]
            found = jnp.where(at == column, slot, found)
        slots_ref[begin : begin + step, :] = found
    names = (slots_ref[...] >= 0).astype(F32)
    mine = iota((128, ROWS), 1) // HEIGHT == iota((128, ROWS), 0)
    union = (dot(mine.astype(F32), names) > 0).astype(F32)
    union_ref[...] = union

    entry = iota((1, ENTRIES), 1)
    peer, number = entry // HELD, entry % HELD
    x, core = (peer // NC) % NX, peer % NC
    row = ((x * NZ + position_ref[1]) * NC + core) * HEIGHT + quarter_of(number)
    column = entries_ref[...]
    every = iota((ROWS, ENTRIES), 0)
    named = dot(jnp.where(mine, 0.0, union), (every == row).astype(F32))
    need_ref[...] = named * dot(union, (every == column).astype(F32))
    kind = iota((8, ENTRIES), 0)
    both = jnp.where(kind == 1, jnp.maximum(column, 0), 0)
    kq_ref[...] = jnp.where(kind == 0, row, both).astype(F32)


def pattern(position, columns, entries):
    return pl.pallas_call(
        pattern_kernel,
        out_shape=(
            jax.ShapeDtypeStruct((ROWS, ROWS), I32),
            jax.ShapeDtypeStruct((128, ROWS), F32),
            jax.ShapeDtypeStruct((128, ENTRIES), F32),
            jax.ShapeDtypeStruct((8, ENTRIES), F32),
        ),
        in_specs=[smem(), vmem(), vmem()],
        out_specs=(vmem(), vmem(), vmem(), vmem()),
        compiler_params=params(),
        cost_estimate=cost(2 * SLOTS * ROWS**3 // 4, 8 * ROWS**2),
        name="pattern",
    )(position, columns, entries)


def send_kernel(position_ref, need_ref, kq_ref, near_ref, *refs):
    *out_refs, chosen_ref = refs
    z = position_ref[1]
    near = near_ref[...]
    kind = iota((8, ENTRIES), 0)
    pick = (iota((8, ENTRIES), 1) % HELD == SLOTS + kind) & (kind < 2)
    flags = dot(pick.astype(F32), near)
    flags = jnp.concatenate([flags[0:1], flags[1:2]], axis=1)
    need = need_ref[...] * flags
    slab = iota((8, 128), 1)
    plane = (slab // NC) % NZ == (iota((8, 128), 0) + z) & (NZ - 1)
    wanted = (dot(plane.astype(F32), need) > 0).astype(F32)
    code = codes(wanted, CAP_Z)
    most = jnp.max(jnp.sum(wanted, axis=1, keepdims=True), axis=0, keepdims=True)
    most = jnp.broadcast_to(jnp.minimum(most, 250.0), (1, 128))
    totals = jnp.minimum(dot_rows(jnp.ones((8, ENTRIES), F32), need)[0:1], 250.0)
    for to in range(NZ):
        chosen_ref[to * ROWS_Z : (to + 1) * ROWS_Z, :] = one_hot(code[to : to + 1], ROWS_Z).astype(BF)
    packed = jnp.dot(chosen_ref[...], near, preferred_element_type=F32)
    tail = iota((16, PIECE), 0)
    kq = kq_ref[...]
    for to in range(NZ):
        target = iota((8, 128), 0)
        choice = slab == (target // NC * NZ + ((z + to) & (NZ - 1))) * NC + target % NC
        asked = jnp.concatenate([dot(choice.astype(F32), need), kq], axis=0)
        notes = dot_rows(asked, chosen_ref[to * ROWS_Z : (to + 1) * ROWS_Z, :])
        first = jnp.concatenate([notes[i : i + 1] for i in range(4)], axis=1)
        second = jnp.concatenate([notes[i : i + 1] for i in range(4, 8)], axis=1)
        third = jnp.concatenate([notes[8:9], notes[9:10], totals, most], axis=1)
        begin = to * ROWS_Z
        out_refs[to][0 : ROWS_Z - 16] = packed[begin : begin + ROWS_Z - 16].astype(BF)
        value = packed[begin + ROWS_Z - 16 : begin + ROWS_Z]
        value = jnp.where(tail == 12, first, value)
        value = jnp.where(tail == 13, second, value)
        value = jnp.where(tail == 14, third, value)
        out_refs[to][ROWS_Z - 16 : ROWS_Z] = value.astype(BF)


def send(position, need, kq, near):
    return pl.pallas_call(
        send_kernel,
        out_shape=[jax.ShapeDtypeStruct((ROWS_Z, PIECE), BF)] * NZ,
        in_specs=[smem()] + [vmem()] * 3,
        out_specs=[vmem()] * NZ,
        scratch_shapes=[pltpu.VMEM((NZ * ROWS_Z, ENTRIES), BF)],
        compiler_params=params(),
        name="send",
    )(position, need, kq, near)


def notes_of(along_refs):
    asked, third = [], []
    for along_ref in along_refs:
        notes = along_ref[ROWS_Z - 16 : ROWS_Z].astype(F32)
        asked.append(
            jnp.concatenate(
                [
                    notes[12 + i // 4 : 13 + i // 4, i % 4 * SIDE : (i % 4 + 1) * SIDE]
                    for i in range(TARGETS)
                ],
                axis=0,
            )
        )
        third.append(notes[14:15])
    return jnp.concatenate(asked, axis=1), third


def route_kernel(*refs):
    *along_refs, out_ref, chosen_ref, along_ref = refs
    asked, _ = notes_of(along_refs)
    for number, ref in enumerate(along_refs):
        along_ref[number * ROWS_Z : (number + 1) * ROWS_Z] = ref[...]
    code = codes(asked, CAP_X)
    for to in range(TARGETS):
        chosen_ref[to * SIDE : (to + 1) * SIDE, :] = one_hot(code[to : to + 1], SIDE).astype(BF)
    packed = jnp.dot(chosen_ref[...], along_ref[...], preferred_element_type=F32)
    for to in range(TARGETS):
        out_ref[to] = packed[to * SIDE : to * SIDE + CAP_X].astype(BF)


def route(along):
    return pl.pallas_call(
        route_kernel,
        out_shape=jax.ShapeDtypeStruct((TARGETS, CAP_X, PIECE), BF),
        in_specs=[vmem()] * NZ,
        out_specs=vmem(),
        scratch_shapes=[
            pltpu.VMEM((TARGETS * SIDE, NZ * ROWS_Z), BF),
            pltpu.VMEM((NZ * ROWS_Z, PIECE), BF),
        ],
        compiler_params=params(),
        name="route",
    )(*along)


def own_plan_kernel(position_ref, slots_ref, union_ref, out_ref):
    x, z, core, part = (position_ref[i] for i in range(4))
    chip = x * NZ + z
    slab = chip * NC + core
    order = earlier(ROWS)
    out_ref[...] = jnp.zeros_like(out_ref)
    mine = union_ref[pl.ds(slab, 1), :]
    rank = dot(jnp.broadcast_to(mine, (8, ROWS)), order)

    both = slots_ref[pl.ds(pl.multiple_of(chip * HEIGHT_2, HEIGHT_2), HEIGHT_2), :]
    swapped = jnp.concatenate([both[HEIGHT:], both[:HEIGHT]], axis=0)
    slot = jnp.where(core == 0, both, swapped)
    quarter = quarter_of(slot)
    held = (quarter * HEIGHT + iota(slot.shape, 0)) * QUARTER + slot - quarter * QUARTER
    held = jnp.where(slot >= 0, held - ZERO_BLOCK, 0).astype(F32)

    every = iota((1, ROWS), 1)
    named = jnp.where(every // HEIGHT == slab, 0.0, mine)
    position = dot(jnp.broadcast_to(named, (8, ROWS)), order)[0:1]
    number = iota((SLABS, ROWS), 0).astype(F32)
    chosen = ((position == number) & (named > 0)).astype(F32)
    out_ref[0:4, 0:SLABS] = dot_rows(held, chosen)[0:HEIGHT].astype(I32) + ZERO_BLOCK

    number = iota((OUT_COLS, ROWS), 0).astype(F32)
    chosen = ((rank[0:1] == number) & (mine > 0)).astype(F32)
    out_ref[4:8, 0:OUT_COLS] = dot_rows(held, chosen)[0:HEIGHT].astype(I32) + ZERO_BLOCK
    wide = 128 // HEIGHT
    chosen = jnp.concatenate(
        [slot[i : i + 1] == iota((wide, ROWS), 0) for i in range(HEIGHT)], axis=0
    )
    out_ref[8:9, 0:128] = dot_rows(rank, chosen.astype(F32))[0:1].astype(I32)
    chosen = (iota((8, ROWS), 1) == iota((8, ROWS), 0) + slab * HEIGHT).astype(F32)
    out_ref[9:13, 0:8] = dot_rows(held, chosen)[0:HEIGHT].astype(I32) + ZERO_BLOCK
    groups = ((jnp.sum(mine) + (GROUP - 1)) * (1.0 / GROUP)).astype(I32)
    lane = iota((1, 128), 1)
    scalars = jnp.where(lane == 0, part, 0)
    scalars = jnp.where(lane == 1, groups, scalars)
    out_ref[15:16, :] = jnp.where(lane == 2, jnp.sum(named).astype(I32), scalars)


def own_plan(position, slots, union):
    return pl.pallas_call(
        own_plan_kernel,
        out_shape=jax.ShapeDtypeStruct((16, 128), I32),
        in_specs=[smem(), vmem(), vmem()],
        out_specs=vmem(),
        compiler_params=params(),
        cost_estimate=cost(ROWS**3, 4 * ROWS**2),
        name="own_plan",
    )(position, slots, union)


def far_plan_kernel(position_ref, union_ref, *refs):
    *along_refs, out_ref = refs
    x, z, core = (position_ref[i] for i in range(3))
    slab = (x * NZ + z) * NC + core
    out_ref[...] = jnp.zeros_like(out_ref)
    asked, third = notes_of(along_refs)
    mine = iota(asked.shape, 0) == x * NC + core
    asked = jnp.sum(jnp.where(mine, asked, 0.0), axis=0, keepdims=True)
    number = jnp.sum(asked).astype(I32)
    code = codes(jnp.broadcast_to(asked, (8, asked.shape[1])), CAP_X)[0:1]
    chosen = one_hot(code, SIDE)
    row = jnp.concatenate([part[:, :SIDE] for part in third], axis=1)
    column = jnp.concatenate([part[:, SIDE : 2 * SIDE] for part in third], axis=1)
    row_down = jnp.sum(chosen * row, axis=1, keepdims=True).astype(I32)
    column_down = jnp.sum(chosen * column, axis=1, keepdims=True).astype(I32)
    row_along = dot_rows(jnp.broadcast_to(row, (8, row.shape[1])), chosen)[0:1].astype(I32)

    down, along = iota((SIDE, SIDE), 0), iota((SIDE, SIDE), 1)
    less = (row_down < row_along) | ((row_down == row_along) & (down < along))
    order = jnp.sum((less & (down < number)).astype(F32), axis=0, keepdims=True)
    ordered = ((order == down.astype(F32)) & (along < number)).astype(F32)
    position = iota((8, SIDE), 1).astype(F32)
    out_ref[0:1, 0:SIDE] = dot_rows(position, ordered)[0:1].astype(I32)
    names = union_ref[pl.ds(slab, 1), :]
    order = earlier(ROWS)
    rank = dot(jnp.broadcast_to(names, (8, ROWS)), order)
    every = iota((SIDE, ROWS), 1)
    rank = dot_rows(rank, (every == column_down).astype(F32))
    out_ref[1:2, 0:SIDE] = dot_rows(rank, ordered)[0:1].astype(I32)

    valid = iota((SIDE, ROWS), 0) < number
    count = dot(jnp.ones((8, SIDE), F32), ((every == row_down) & valid).astype(F32))
    start = jnp.minimum(dot(count, order), 250.0)
    row = jnp.where(iota((1, ROWS), 1) // HEIGHT == slab, 0.0, names)
    position = dot(jnp.broadcast_to(row, (8, ROWS)), order)[0:1]
    chosen = ((position == iota((SLABS, ROWS), 0).astype(F32)) & (row > 0)).astype(F32)
    out_ref[2:3, 0:SLABS] = dot_rows(start, chosen)[0:1].astype(I32)
    out_ref[3:4, 0:SLABS] = dot_rows(count, chosen)[0:1].astype(I32)

    third = functools.reduce(jnp.maximum, third), functools.reduce(jnp.add, third)
    most_z = jnp.max(third[0][:, 3 * SIDE :])
    most_x = jnp.max(third[1][:, 2 * SIDE : 3 * SIDE])
    fits = (most_x <= CAP_X) & (most_z <= CAP_Z)
    out_ref[4:5, :] = jnp.zeros((1, SIDE), I32) + fits.astype(I32)


def far_plan(position, union, along):
    return pl.pallas_call(
        far_plan_kernel,
        out_shape=jax.ShapeDtypeStruct((8, 128), I32),
        in_specs=[smem()] + [vmem()] * (1 + NZ),
        out_specs=vmem(),
        compiler_params=params(),
        cost_estimate=cost(2 * 20 * ROWS**3, 8 * ROWS**2),
        name="far_plan",
    )(position, union, *along)


def dense(blocks, nonzero, columns):
    slab = lax.axis_index(ROW_AXES)
    part = lax.axis_index("col")
    masked = blocks * nonzero[:, :, None, None].astype(BF)
    slab_ids = jnp.arange(SLABS, dtype=I32)
    local_rows = jnp.arange(HEIGHT, dtype=I32)
    grouped = columns.reshape(SLABS, HEIGHT * SLOTS)
    targets = slab * HEIGHT + local_rows
    wanted = jnp.any(grouped[:, :, None] == targets[None, None, :], axis=1)
    wanted = wanted & (slab_ids != slab)[:, None]
    picked = jnp.sum(jnp.where(wanted, local_rows, 0), axis=1)
    filled = jnp.any(wanted, axis=1)
    outgoing = jnp.where(filled[:, None, None, None], masked[picked], jnp.zeros((), BF))
    incoming = lax.all_to_all(outgoing, ROW_AXES, split_axis=0, concat_axis=0, tiled=True)
    row_table = jnp.concatenate([incoming, masked], axis=0)
    own_cols = lax.dynamic_slice_in_dim(columns, slab * HEIGHT, HEIGHT, 0)
    source = own_cols // HEIGHT
    row_index = jnp.where(source == slab, SLABS + own_cols % HEIGHT, source)
    far_cols = columns[own_cols]
    far_quarter = lax.dynamic_slice_in_dim(far_cols, part * QUARTER, QUARTER, 2)
    whole = lax.all_gather(masked, "col", axis=1, tiled=True)
    results = []
    for member in range(HEIGHT):
        match = far_quarter[member][:, :, None] == own_cols[member][None, None, :]
        products = jnp.einsum(
            "tab,tubc->tuac", whole[member], row_table[row_index[member]],
            preferred_element_type=F32,
        )
        summed = lax.dot_general(
            match.astype(F32).reshape(SLOTS * QUARTER, SLOTS),
            products.reshape(SLOTS * QUARTER, SIDE * SIDE),
            (((0,), (0,)), ((), ())),
            precision=lax.Precision.HIGHEST,
            preferred_element_type=F32,
        )
        results.append(summed.reshape(SLOTS, SIDE, SIDE))
    square = lax.psum_scatter(jnp.stack(results), "col", scatter_dimension=1, tiled=True)
    return square.astype(BF)


def plane_columns(columns):
    split = columns.reshape(NX, NZ, NC, HEIGHT, NY, QUARTER)
    mine = lax.dynamic_index_in_dim(split, lax.axis_index("z"), 1, keepdims=False)
    mine = mine.transpose(3, 0, 1, 2, 4).reshape(PEERS, SLOTS)
    return jnp.pad(mine, ((0, 0), (0, HELD - SLOTS)), constant_values=-1).reshape(1, ENTRIES)


def shards(blocks, nonzero, columns):
    position = jnp.stack([lax.axis_index(name) for name in ROW_AXES + ("col",)])
    cuts = prepare(position, nonzero, blocks)
    cuts, names, same = lax.optimization_barrier((cuts, columns, blocks))
    turned = turn(nonzero, same)
    slots, union, need, kq = pattern(position, names, plane_columns(columns))
    near = lax.all_to_all(cuts, ("col", "x", "core"), split_axis=0, concat_axis=0, tiled=True)
    near, turned, need = lax.optimization_barrier((near, turned, need))
    whole = lax.all_gather(turned, "col", axis=0, tiled=False)
    whole = whole.reshape(ZERO_BLOCK, SIDE, SIDE)
    packed = send(position, need, kq, near.reshape(ENTRIES, PIECE))
    packed, slots = lax.optimization_barrier((packed, slots))
    along = [packed[0]] + [
        lax.ppermute(packed[step], "z", [(i, (i + step) % NZ) for i in range(NZ)])
        for step in ORDER_Z
    ]
    own_lists = own_plan(position, slots, union)
    packed, notes = lax.optimization_barrier((route(along), along))
    far = lax.all_to_all(packed, ("x", "core"), split_axis=0, concat_axis=0, tiled=True)
    far_lists = far_plan(position, union, notes)
    far = far.reshape(TARGETS * CAP_X, PIECE)
    own = own_sums(own_lists, whole)
    far, fits, own = lax.optimization_barrier((far, far_lists[4, 0] != 0, own))
    result = far_sums(own_lists, far_lists, whole, far, own)
    cuts = [result[0]]
    for step in ORDER_Y:
        pairs = [(i, (i + step) % NY) for i in range(NY)]
        cuts.append(lax.ppermute(result[step], "col", pairs))
    square = finish(position, cuts)
    return lax.cond(
        fits,
        lambda value, *_: value,
        lambda _, *inputs: dense(*inputs),
        square,
        blocks,
        nonzero,
        columns,
    )


def solution(mesh):
    fine = Mesh(mesh.devices.reshape(NX, NZ, NC, NY), ROW_AXES + ("col",))
    spec = P(ROW_AXES, "col", None, None)
    return jax.shard_map(
        shards,
        mesh=fine,
        in_specs=(spec, P(ROW_AXES, "col"), P()),
        out_specs=spec,
        check_vma=False,
    )
```

```python
import functools

import jax
import jax.numpy as jnp
from jax import lax
from jax.experimental import pallas as pl
from jax.experimental.pallas import tpu as pltpu
from jax.sharding import Mesh
from jax.sharding import PartitionSpec as P

BF = jnp.bfloat16
F32 = jnp.float32
I32 = jnp.int32

NX, NZ, NC, NY = 4, 8, 2, 4
ROWS, SLOTS, SIDE = 256, 28, 128
HEIGHT, QUARTER = 4, 7
SLABS = ROWS // HEIGHT
PEERS = NX * NC * NY
HELD = 32
ENTRIES = PEERS * HELD
PIECE = SIDE * SIDE // PEERS
WIDE = SIDE // NY
TARGETS = NX * NC
CAP_Z = 124
ROWS_Z = 128
CAP_X = 120
ORDER_Z = (3, 5, 4, 2, 6, 1, 7)
ORDER_Y = (1, 3, 2)
GROUP = 8
FAR_GROUP = 4
ROWS_AT_ONCE = 4
HEIGHT_2 = NC * HEIGHT
OUT_COLS = 72
ZERO_BLOCK = NY * HEIGHT * QUARTER
VMEM_LIMIT = 48 * 1024 * 1024
ROW_AXES = ("x", "z", "core")


def vmem():
    return pl.BlockSpec(memory_space=pltpu.VMEM)


def smem():
    return pl.BlockSpec(memory_space=pltpu.SMEM)


def params():
    return pltpu.CompilerParams(vmem_limit_bytes=VMEM_LIMIT)


def cost(flops, moved):
    return pl.CostEstimate(flops=flops, bytes_accessed=moved, transcendentals=0)


def prepare_kernel(position_ref, keep_ref, blocks_ref, cuts_ref, rows_ref):
    x, core, part = position_ref[0], position_ref[2], position_ref[3]
    lanes = iota((8, ENTRIES), 1) - ((part * NX + x) * NC + core) * HELD
    flags = jnp.zeros((8, ENTRIES), F32)
    for row in range(HEIGHT):
        for slot in range(QUARTER):
            number = row * QUARTER + slot
            keep = keep_ref[row, slot] != 0
            flags = jnp.where((lanes == number) & keep, 1.0, flags)
            block = blocks_ref[row, slot].astype(F32)
            rows_ref[number] = jnp.where(keep, block, jnp.zeros_like(block)).T
    for part_of in range(NY):
        for extra in range(HELD - SLOTS):
            at = extra * PIECE + part_of * SIDE
            value = flags[:, at : at + SIDE] if extra < 2 else jnp.zeros((8, SIDE), F32)
            for quarter in range(NY):
                begin = quarter * WIDE + part_of * TARGETS
                rows_ref[SLOTS + extra, begin : begin + TARGETS] = value
    for quarter in range(NY):
        peers = slice(quarter * TARGETS, (quarter + 1) * TARGETS)
        for part_of in range(NY):
            begin = quarter * WIDE + part_of * TARGETS
            for half in range(0, HELD, 16):
                rows = rows_ref[half : half + 16, begin : begin + TARGETS]
                cuts_ref[peers, half : half + 16, part_of * SIDE : (part_of + 1) * SIDE] = (
                    jnp.swapaxes(rows, 0, 1).astype(BF)
                )


def prepare(position, nonzero, blocks):
    return pl.pallas_call(
        prepare_kernel,
        out_shape=jax.ShapeDtypeStruct((PEERS, HELD, PIECE), BF),
        in_specs=[smem(), smem(), vmem()],
        out_specs=vmem(),
        scratch_shapes=[pltpu.VMEM((HELD, SIDE, SIDE), F32)],
        compiler_params=params(),
        name="prepare",
    )(position, nonzero, blocks)


def turn_kernel(keep_ref, blocks_ref, out_ref):
    for row in range(HEIGHT):
        for slot in range(QUARTER):
            block = blocks_ref[row, slot]
            out_ref[row, slot] = jnp.where(
                keep_ref[row, slot] != 0, block, jnp.zeros_like(block)
            ).T


def turn(nonzero, blocks):
    return pl.pallas_call(
        turn_kernel,
        out_shape=jax.ShapeDtypeStruct((HEIGHT, QUARTER, SIDE, SIDE), BF),
        in_specs=[smem(), vmem()],
        out_specs=vmem(),
        compiler_params=params(),
        cost_estimate=cost(2 * SLOTS * SIDE**3, 4 * SLOTS * SIDE**2),
        name="turn",
    )(nonzero, blocks)


def own_block(whole_ref, place, rows):
    value = whole_ref[jnp.minimum(place, ZERO_BLOCK - 1), rows, :]
    return jnp.where(place < ZERO_BLOCK, value, jnp.zeros_like(value))


def out_place(place):
    return (place // QUARTER) % HEIGHT, place // (QUARTER * HEIGHT) * QUARTER + place % QUARTER


def own_kernel(
    plan_ref,
    whole_ref,
    out_ref,
    total,
    panel,
    near,
):
    first = pl.multiple_of(plan_ref[15, 0] * WIDE, WIDE)
    for inner in range(HEIGHT):
        for member in range(HEIGHT):
            panel[pl.ds(inner * SIDE, SIDE), pl.ds(member * SIDE, SIDE)] = own_block(
                whole_ref, plan_ref[9 + member, inner], pl.ds(0, SIDE)
            )

    def step(group, carry):
        for at in range(GROUP):
            for inner in range(HEIGHT):
                near[pl.ds(at * WIDE, WIDE), pl.ds(inner * SIDE, SIDE)] = own_block(
                    whole_ref, plan_ref[4 + inner, group * GROUP + at], pl.ds(first, WIDE)
                )
        value = jnp.dot(near[...], panel[...], preferred_element_type=F32)
        total[pl.ds(group * GROUP, GROUP)] = value.reshape(GROUP, WIDE, HEIGHT * SIDE)
        return carry

    lax.fori_loop(0, plan_ref[15, 1], step, 0)
    for place in range(ZERO_BLOCK):
        member, slot = out_place(place)
        column = plan_ref[8, member * (128 // HEIGHT) + slot]
        out_ref[place] = total[column, :, pl.ds(member * SIDE, SIDE)]


def own_sums(lists, whole):
    flops = 2 * 32 * WIDE * (HEIGHT * SIDE) ** 2
    return pl.pallas_call(
        own_kernel,
        out_shape=jax.ShapeDtypeStruct((ZERO_BLOCK, WIDE, SIDE), F32),
        in_specs=[smem(), vmem()],
        out_specs=vmem(),
        scratch_shapes=[
            pltpu.VMEM((OUT_COLS, WIDE, HEIGHT * SIDE), F32),
            pltpu.VMEM((HEIGHT * SIDE, HEIGHT * SIDE), BF),
            pltpu.VMEM((GROUP * WIDE, HEIGHT * SIDE), BF),
        ],
        compiler_params=params(),
        cost_estimate=cost(flops, 3 * ZERO_BLOCK * SIDE * SIDE),
        name="own_sums",
    )(lists, whole)


def far_kernel(
    own_ref,
    plan_ref,
    whole_ref,
    far_ref,
    near_ref,
    *refs,
):
    *out_refs, total, pieces_ref = refs
    for sender in range(TARGETS):
        rows = pl.ds(sender * CAP_X, CAP_X)
        for part in range(NY):
            lanes = slice(part * SIDE, (part + 1) * SIDE)
            pieces_ref[part, rows, :] = far_ref[rows, lanes].astype(F32)

    def clear(group, carry):
        total[pl.ds(group * GROUP, GROUP)] = jnp.zeros((GROUP, WIDE, HEIGHT * SIDE), F32)
        return carry

    lax.fori_loop(0, own_ref[15, 1], clear, 0)

    def product(step):
        begin = plan_ref[2, step]
        length = plan_ref[3, step]
        right = jnp.concatenate(
            [
                own_block(whole_ref, plan_ref[4 + member, step], pl.ds(0, SIDE))
                for member in range(HEIGHT)
            ],
            axis=1,
        )
        pieces, columns = [], []
        for at in range(FAR_GROUP):
            place = jnp.minimum(begin + at, CAP_X - 1)
            rows = pl.ds(plan_ref[0, place], TARGETS, stride=CAP_X)
            for part in range(NY):
                pieces.append(pieces_ref[part, rows, :])
            columns.append(jnp.where(at < length, plan_ref[1, place], OUT_COLS))
        left = jnp.concatenate(pieces, axis=0).astype(BF)
        return jnp.dot(left, right, preferred_element_type=F32), columns

    def add(value, columns):
        for at, column in enumerate(columns):
            total[column] = total[column] + value[at * WIDE : (at + 1) * WIDE]

    def steps(number, carry):
        done = [product(number * ROWS_AT_ONCE + at) for at in range(ROWS_AT_ONCE)]
        for value, columns in done:
            add(value, columns)
        return carry

    lax.fori_loop(0, (plan_ref[8, 0] + ROWS_AT_ONCE - 1) // ROWS_AT_ONCE, steps, 0)

    for step, out_ref in enumerate(out_refs):
        part = (own_ref[15, 0] + step) & (NY - 1)
        for place in range(HEIGHT * QUARTER):
            member, slot = place // QUARTER, part * QUARTER + place % QUARTER
            column = own_ref[8, member * (128 // HEIGHT) + slot]
            value = total[column, :, pl.ds(member * SIDE, SIDE)]
            value = value + near_ref[part * (HEIGHT * QUARTER) + place]
            out_ref[place] = value.astype(BF)


def far_sums(own_lists, far_lists, whole, far, near):
    return pl.pallas_call(
        far_kernel,
        out_shape=[jax.ShapeDtypeStruct((HEIGHT * QUARTER, WIDE, SIDE), BF)] * NY,
        in_specs=[smem(), smem(), vmem(), vmem(), vmem()],
        out_specs=[vmem()] * NY,
        scratch_shapes=[
            pltpu.VMEM((OUT_COLS + 1, WIDE, HEIGHT * SIDE), F32),
            pltpu.VMEM((NY, TARGETS * CAP_X, SIDE), F32),
        ],
        compiler_params=params(),
        name="far_sums",
    )(own_lists, far_lists, whole, far, near)


def finish_kernel(position_ref, *refs):
    *cut_refs, out_ref, turned_ref = refs
    for step, cut_ref in zip((0,) + ORDER_Y, cut_refs):
        part = (position_ref[3] - step) & (NY - 1)
        rows = pl.ds(pl.multiple_of(part * WIDE, WIDE), WIDE)
        for place in range(HEIGHT * QUARTER):
            turned_ref[place, rows, :] = cut_ref[place]
    for row in range(HEIGHT):
        for slot in range(QUARTER):
            out_ref[row, slot] = turned_ref[row * QUARTER + slot].T


def finish(position, cuts):
    return pl.pallas_call(
        finish_kernel,
        out_shape=jax.ShapeDtypeStruct((HEIGHT, QUARTER, SIDE, SIDE), BF),
        in_specs=[smem()] + [vmem()] * NY,
        out_specs=vmem(),
        scratch_shapes=[pltpu.VMEM((HEIGHT * QUARTER, SIDE, SIDE), BF)],
        compiler_params=params(),
        name="finish",
    )(position, *cuts)


def iota(shape, axis):
    return lax.broadcasted_iota(I32, shape, axis)


def dot(a, b):
    return jnp.dot(a.astype(BF), b.astype(BF), preferred_element_type=F32)


def dot_rows(a, b):
    return lax.dot_general(
        a.astype(BF), b.astype(BF), (((1,), (1,)), ((), ())), preferred_element_type=F32
    )


def earlier(size):
    return (iota((size, size), 0) < iota((size, size), 1)).astype(F32)


def places(need):
    order = earlier(SIDE)
    parts = []
    before = jnp.zeros((need.shape[0], 1), F32)
    for begin in range(0, need.shape[1], SIDE):
        part = need[:, begin : begin + SIDE]
        parts.append(dot(part, order) + before)
        before = before + jnp.sum(part, axis=1, keepdims=True)
    return jnp.concatenate(parts, axis=1)


def codes(need, capacity):
    place = places(need)
    return jnp.where((need > 0) & (place < capacity), place, -1.0)


def one_hot(code, rows):
    return (iota((rows, code.shape[1]), 0).astype(F32) == code).astype(F32)


def quarter_of(slot):
    return sum((slot >= bound * QUARTER).astype(I32) for bound in range(1, NY))


def pattern_kernel(position_ref, columns_ref, entries_ref, slots_ref, union_ref, need_ref, kq_ref):
    step = 64
    for begin in range(0, ROWS, step):
        column = iota((step, ROWS), 1)
        found = jnp.full((step, ROWS), -1, I32)
        for slot in range(SLOTS):
            at = columns_ref[begin : begin + step, slot : slot + 1]
            found = jnp.where(at == column, slot, found)
        slots_ref[begin : begin + step, :] = found
    names = (slots_ref[...] >= 0).astype(F32)
    mine = iota((128, ROWS), 1) // HEIGHT == iota((128, ROWS), 0)
    union = (dot(mine.astype(F32), names) > 0).astype(F32)
    union_ref[...] = union

    entry = iota((1, ENTRIES), 1)
    peer, number = entry // HELD, entry % HELD
    x, core = (peer // NC) % NX, peer % NC
    row = ((x * NZ + position_ref[1]) * NC + core) * HEIGHT + quarter_of(number)
    column = entries_ref[...]
    every = iota((ROWS, ENTRIES), 0)
    named = dot(jnp.where(mine, 0.0, union), (every == row).astype(F32))
    need_ref[...] = named * dot(union, (every == column).astype(F32))
    kind = iota((8, ENTRIES), 0)
    both = jnp.where(kind == 1, jnp.maximum(column, 0), 0)
    kq_ref[...] = jnp.where(kind == 0, row, both).astype(F32)


def pattern(position, columns, entries):
    return pl.pallas_call(
        pattern_kernel,
        out_shape=(
            jax.ShapeDtypeStruct((ROWS, ROWS), I32),
            jax.ShapeDtypeStruct((128, ROWS), F32),
            jax.ShapeDtypeStruct((128, ENTRIES), F32),
            jax.ShapeDtypeStruct((8, ENTRIES), F32),
        ),
        in_specs=[smem(), vmem(), vmem()],
        out_specs=(vmem(), vmem(), vmem(), vmem()),
        compiler_params=params(),
        cost_estimate=cost(2 * SLOTS * ROWS**3 // 4, 8 * ROWS**2),
        name="pattern",
    )(position, columns, entries)


def send_kernel(position_ref, need_ref, kq_ref, near_ref, *refs):
    *out_refs, chosen_ref = refs
    z = position_ref[1]
    near = near_ref[...]
    kind = iota((8, ENTRIES), 0)
    pick = (iota((8, ENTRIES), 1) % HELD == SLOTS + kind) & (kind < 2)
    flags = dot(pick.astype(F32), near)
    flags = jnp.concatenate([flags[0:1], flags[1:2]], axis=1)
    need = need_ref[...] * flags
    slab = iota((8, 128), 1)
    plane = (slab // NC) % NZ == (iota((8, 128), 0) + z) & (NZ - 1)
    wanted = (dot(plane.astype(F32), need) > 0).astype(F32)
    code = codes(wanted, CAP_Z)
    most = jnp.max(jnp.sum(wanted, axis=1, keepdims=True), axis=0, keepdims=True)
    most = jnp.broadcast_to(jnp.minimum(most, 250.0), (1, 128))
    totals = jnp.minimum(dot_rows(jnp.ones((8, ENTRIES), F32), need)[0:1], 250.0)
    for to in range(NZ):
        chosen_ref[to * ROWS_Z : (to + 1) * ROWS_Z, :] = one_hot(code[to : to + 1], ROWS_Z).astype(BF)
    packed = jnp.dot(chosen_ref[...], near, preferred_element_type=F32)
    tail = iota((16, PIECE), 0)
    kq = kq_ref[...]
    for to in range(NZ):
        target = iota((8, 128), 0)
        choice = slab == (target // NC * NZ + ((z + to) & (NZ - 1))) * NC + target % NC
        asked = jnp.concatenate([dot(choice.astype(F32), need), kq], axis=0)
        notes = dot_rows(asked, chosen_ref[to * ROWS_Z : (to + 1) * ROWS_Z, :])
        first = jnp.concatenate([notes[i : i + 1] for i in range(4)], axis=1)
        second = jnp.concatenate([notes[i : i + 1] for i in range(4, 8)], axis=1)
        third = jnp.concatenate([notes[8:9], notes[9:10], totals, most], axis=1)
        begin = to * ROWS_Z
        out_refs[to][0 : ROWS_Z - 16] = packed[begin : begin + ROWS_Z - 16].astype(BF)
        value = packed[begin + ROWS_Z - 16 : begin + ROWS_Z]
        value = jnp.where(tail == 12, first, value)
        value = jnp.where(tail == 13, second, value)
        value = jnp.where(tail == 14, third, value)
        out_refs[to][ROWS_Z - 16 : ROWS_Z] = value.astype(BF)


def send(position, need, kq, near):
    return pl.pallas_call(
        send_kernel,
        out_shape=[jax.ShapeDtypeStruct((ROWS_Z, PIECE), BF)] * NZ,
        in_specs=[smem()] + [vmem()] * 3,
        out_specs=[vmem()] * NZ,
        scratch_shapes=[pltpu.VMEM((NZ * ROWS_Z, ENTRIES), BF)],
        compiler_params=params(),
        name="send",
    )(position, need, kq, near)


def notes_of(along_refs):
    asked, third = [], []
    for along_ref in along_refs:
        notes = along_ref[ROWS_Z - 16 : ROWS_Z].astype(F32)
        asked.append(
            jnp.concatenate(
                [
                    notes[12 + i // 4 : 13 + i // 4, i % 4 * SIDE : (i % 4 + 1) * SIDE]
                    for i in range(TARGETS)
                ],
                axis=0,
            )
        )
        third.append(notes[14:15])
    return jnp.concatenate(asked, axis=1), third


def route_kernel(*refs):
    *along_refs, out_ref, chosen_ref, along_ref = refs
    asked, _ = notes_of(along_refs)
    for number, ref in enumerate(along_refs):
        along_ref[number * ROWS_Z : (number + 1) * ROWS_Z] = ref[...]
    code = codes(asked, CAP_X)
    for to in range(TARGETS):
        chosen_ref[to * SIDE : (to + 1) * SIDE, :] = one_hot(code[to : to + 1], SIDE).astype(BF)
    packed = jnp.dot(chosen_ref[...], along_ref[...], preferred_element_type=F32)
    for to in range(TARGETS):
        out_ref[to] = packed[to * SIDE : to * SIDE + CAP_X].astype(BF)


def route(along):
    return pl.pallas_call(
        route_kernel,
        out_shape=jax.ShapeDtypeStruct((TARGETS, CAP_X, PIECE), BF),
        in_specs=[vmem()] * NZ,
        out_specs=vmem(),
        scratch_shapes=[
            pltpu.VMEM((TARGETS * SIDE, NZ * ROWS_Z), BF),
            pltpu.VMEM((NZ * ROWS_Z, PIECE), BF),
        ],
        compiler_params=params(),
        name="route",
    )(*along)


def own_places(position_ref, slots_ref):
    chip = position_ref[0] * NZ + position_ref[1]
    both = slots_ref[pl.ds(pl.multiple_of(chip * HEIGHT_2, HEIGHT_2), HEIGHT_2), :]
    swapped = jnp.concatenate([both[HEIGHT:], both[:HEIGHT]], axis=0)
    slot = jnp.where(position_ref[2] == 0, both, swapped)
    quarter = quarter_of(slot)
    held = (quarter * HEIGHT + iota(slot.shape, 0)) * QUARTER + slot - quarter * QUARTER
    return slot, jnp.where(slot >= 0, held - ZERO_BLOCK, 0).astype(F32)


def own_plan_kernel(position_ref, slots_ref, union_ref, out_ref):
    x, z, core, part = (position_ref[i] for i in range(4))
    slab = (x * NZ + z) * NC + core
    order = earlier(ROWS)
    out_ref[...] = jnp.zeros_like(out_ref)
    mine = union_ref[pl.ds(slab, 1), :]
    rank = dot(jnp.broadcast_to(mine, (8, ROWS)), order)

    slot, held = own_places(position_ref, slots_ref)
    number = iota((OUT_COLS, ROWS), 0).astype(F32)
    chosen = ((rank[0:1] == number) & (mine > 0)).astype(F32)
    out_ref[4:8, 0:OUT_COLS] = dot_rows(held, chosen)[0:HEIGHT].astype(I32) + ZERO_BLOCK
    wide = 128 // HEIGHT
    chosen = jnp.concatenate(
        [slot[i : i + 1] == iota((wide, ROWS), 0) for i in range(HEIGHT)], axis=0
    )
    out_ref[8:9, 0:128] = dot_rows(rank, chosen.astype(F32))[0:1].astype(I32)
    chosen = (iota((8, ROWS), 1) == iota((8, ROWS), 0) + slab * HEIGHT).astype(F32)
    out_ref[9:13, 0:8] = dot_rows(held, chosen)[0:HEIGHT].astype(I32) + ZERO_BLOCK
    groups = ((jnp.sum(mine) + (GROUP - 1)) * (1.0 / GROUP)).astype(I32)
    lane = iota((1, 128), 1)
    scalars = jnp.where(lane == 0, part, 0)
    out_ref[15:16, :] = jnp.where(lane == 1, groups, scalars)


def own_plan(position, slots, union):
    return pl.pallas_call(
        own_plan_kernel,
        out_shape=jax.ShapeDtypeStruct((16, 128), I32),
        in_specs=[smem(), vmem(), vmem()],
        out_specs=vmem(),
        compiler_params=params(),
        cost_estimate=cost(ROWS**3, 4 * ROWS**2),
        name="own_plan",
    )(position, slots, union)


def far_plan_kernel(position_ref, slots_ref, union_ref, *refs):
    *along_refs, out_ref = refs
    x, z, core = (position_ref[i] for i in range(3))
    slab = (x * NZ + z) * NC + core
    out_ref[...] = jnp.zeros_like(out_ref)
    asked, third = notes_of(along_refs)
    mine = iota(asked.shape, 0) == x * NC + core
    asked = jnp.sum(jnp.where(mine, asked, 0.0), axis=0, keepdims=True)
    number = jnp.sum(asked).astype(I32)
    code = codes(jnp.broadcast_to(asked, (8, asked.shape[1])), CAP_X)[0:1]
    chosen = one_hot(code, SIDE)
    row = jnp.concatenate([part[:, :SIDE] for part in third], axis=1)
    column = jnp.concatenate([part[:, SIDE : 2 * SIDE] for part in third], axis=1)
    row_down = jnp.sum(chosen * row, axis=1, keepdims=True).astype(I32)
    column_down = jnp.sum(chosen * column, axis=1, keepdims=True).astype(I32)
    row_along = dot_rows(jnp.broadcast_to(row, (8, row.shape[1])), chosen)[0:1].astype(I32)

    down, along = iota((SIDE, SIDE), 0), iota((SIDE, SIDE), 1)
    less = (row_down < row_along) | ((row_down == row_along) & (down < along))
    order = jnp.sum((less & (down < number)).astype(F32), axis=0, keepdims=True)
    ordered = ((order == down.astype(F32)) & (along < number)).astype(F32)
    position = iota((8, SIDE), 1).astype(F32)
    out_ref[0:1, 0:SIDE] = dot_rows(position, ordered)[0:1].astype(I32)
    names = union_ref[pl.ds(slab, 1), :]
    order = earlier(ROWS)
    rank = dot(jnp.broadcast_to(names, (8, ROWS)), order)
    every = iota((SIDE, ROWS), 1)
    rank = dot_rows(rank, (every == column_down).astype(F32))
    out_ref[1:2, 0:SIDE] = dot_rows(rank, ordered)[0:1].astype(I32)

    valid = iota((SIDE, ROWS), 0) < number
    count = dot(jnp.ones((8, SIDE), F32), ((every == row_down) & valid).astype(F32))
    start = jnp.minimum(dot(count, order), 250.0)[0:1]
    _, held = own_places(position_ref, slots_ref)
    needed = ((count + (FAR_GROUP - 1)) * (1.0 / FAR_GROUP)).astype(I32).astype(F32)
    first = dot(needed, order)[0:1]
    number = iota((SIDE, ROWS), 0).astype(F32)
    chosen = ((first <= number) & (number < first + needed[0:1])).astype(F32)
    kind = iota((8, ROWS), 0)
    values = jnp.where(kind == 0, start, jnp.where(kind == 1, first, count))
    values = dot_rows(values, chosen).astype(I32)
    done = (iota((1, SIDE), 1) - values[1:2]) * FAR_GROUP
    steps = jnp.sum(needed[0:1]).astype(I32)
    valid = iota((1, SIDE), 1) < steps
    out_ref[2:3, :] = jnp.where(valid, values[0:1] + done, 0)
    out_ref[3:4, :] = jnp.where(valid, values[2:3] - done, 0)
    out_ref[4:8, :] = dot_rows(held, chosen)[0:HEIGHT].astype(I32) + ZERO_BLOCK
    out_ref[8:9, :] = jnp.zeros((1, SIDE), I32) + jnp.minimum(steps, SIDE)

    third = functools.reduce(jnp.maximum, third), functools.reduce(jnp.add, third)
    most_z = jnp.max(third[0][:, 3 * SIDE :])
    most_x = jnp.max(third[1][:, 2 * SIDE : 3 * SIDE])
    fits = (most_x <= CAP_X) & (most_z <= CAP_Z)
    out_ref[9:10, :] = jnp.zeros((1, SIDE), I32) + fits.astype(I32)


def far_plan(position, slots, union, along):
    return pl.pallas_call(
        far_plan_kernel,
        out_shape=jax.ShapeDtypeStruct((16, 128), I32),
        in_specs=[smem()] + [vmem()] * (2 + NZ),
        out_specs=vmem(),
        compiler_params=params(),
        cost_estimate=cost(2 * 20 * ROWS**3, 8 * ROWS**2),
        name="far_plan",
    )(position, slots, union, *along)


def dense(blocks, nonzero, columns):
    slab = lax.axis_index(ROW_AXES)
    part = lax.axis_index("col")
    masked = blocks * nonzero[:, :, None, None].astype(BF)
    slab_ids = jnp.arange(SLABS, dtype=I32)
    local_rows = jnp.arange(HEIGHT, dtype=I32)
    grouped = columns.reshape(SLABS, HEIGHT * SLOTS)
    targets = slab * HEIGHT + local_rows
    wanted = jnp.any(grouped[:, :, None] == targets[None, None, :], axis=1)
    wanted = wanted & (slab_ids != slab)[:, None]
    picked = jnp.sum(jnp.where(wanted, local_rows, 0), axis=1)
    filled = jnp.any(wanted, axis=1)
    outgoing = jnp.where(filled[:, None, None, None], masked[picked], jnp.zeros((), BF))
    incoming = lax.all_to_all(outgoing, ROW_AXES, split_axis=0, concat_axis=0, tiled=True)
    row_table = jnp.concatenate([incoming, masked], axis=0)
    own_cols = lax.dynamic_slice_in_dim(columns, slab * HEIGHT, HEIGHT, 0)
    source = own_cols // HEIGHT
    row_index = jnp.where(source == slab, SLABS + own_cols % HEIGHT, source)
    far_cols = columns[own_cols]
    far_quarter = lax.dynamic_slice_in_dim(far_cols, part * QUARTER, QUARTER, 2)
    whole = lax.all_gather(masked, "col", axis=1, tiled=True)
    results = []
    for member in range(HEIGHT):
        match = far_quarter[member][:, :, None] == own_cols[member][None, None, :]
        products = jnp.einsum(
            "tab,tubc->tuac", whole[member], row_table[row_index[member]],
            preferred_element_type=F32,
        )
        summed = lax.dot_general(
            match.astype(F32).reshape(SLOTS * QUARTER, SLOTS),
            products.reshape(SLOTS * QUARTER, SIDE * SIDE),
            (((0,), (0,)), ((), ())),
            precision=lax.Precision.HIGHEST,
            preferred_element_type=F32,
        )
        results.append(summed.reshape(SLOTS, SIDE, SIDE))
    square = lax.psum_scatter(jnp.stack(results), "col", scatter_dimension=1, tiled=True)
    return square.astype(BF)


def plane_columns(columns):
    split = columns.reshape(NX, NZ, NC, HEIGHT, NY, QUARTER)
    mine = lax.dynamic_index_in_dim(split, lax.axis_index("z"), 1, keepdims=False)
    mine = mine.transpose(3, 0, 1, 2, 4).reshape(PEERS, SLOTS)
    return jnp.pad(mine, ((0, 0), (0, HELD - SLOTS)), constant_values=-1).reshape(1, ENTRIES)


def shards(blocks, nonzero, columns):
    position = jnp.stack([lax.axis_index(name) for name in ROW_AXES + ("col",)])
    cuts = prepare(position, nonzero, blocks)
    cuts, names, same = lax.optimization_barrier((cuts, columns, blocks))
    turned = turn(nonzero, same)
    slots, union, need, kq = pattern(position, names, plane_columns(columns))
    near = lax.all_to_all(cuts, ("col", "x", "core"), split_axis=0, concat_axis=0, tiled=True)
    whole = lax.all_gather(turned, "col", axis=0, tiled=False)
    whole = whole.reshape(ZERO_BLOCK, SIDE, SIDE)
    packed = send(position, need, kq, near.reshape(ENTRIES, PIECE))
    packed, slots = lax.optimization_barrier((packed, slots))
    along = [packed[0]] + [
        lax.ppermute(packed[step], "z", [(i, (i + step) % NZ) for i in range(NZ)])
        for step in ORDER_Z
    ]
    own_lists = own_plan(position, slots, union)
    packed, notes = lax.optimization_barrier((route(along), along))
    far = lax.all_to_all(packed, ("x", "core"), split_axis=0, concat_axis=0, tiled=True)
    far_lists = far_plan(position, slots, union, notes)
    far = far.reshape(TARGETS * CAP_X, PIECE)
    own = own_sums(own_lists, whole)
    far, fits, own = lax.optimization_barrier((far, far_lists[9, 0] != 0, own))
    result = far_sums(own_lists, far_lists, whole, far, own)
    cuts = [result[0]]
    for step in ORDER_Y:
        pairs = [(i, (i + step) % NY) for i in range(NY)]
        cuts.append(lax.ppermute(result[step], "col", pairs))
    square = finish(position, cuts)
    return lax.cond(
        fits,
        lambda value, *_: value,
        lambda _, *inputs: dense(*inputs),
        square,
        blocks,
        nonzero,
        columns,
    )


def solution(mesh):
    fine = Mesh(mesh.devices.reshape(NX, NZ, NC, NY), ROW_AXES + ("col",))
    spec = P(ROW_AXES, "col", None, None)
    return jax.shard_map(
        shards,
        mesh=fine,
        in_specs=(spec, P(ROW_AXES, "col"), P()),
        out_specs=spec,
        check_vma=False,
    )
```

```python
import functools

import jax
import jax.numpy as jnp
from jax import lax
from jax.experimental import pallas as pl
from jax.experimental.pallas import tpu as pltpu
from jax.sharding import Mesh
from jax.sharding import PartitionSpec as P

BF = jnp.bfloat16
F32 = jnp.float32
I32 = jnp.int32

NX, NZ, NC, NY = 4, 8, 2, 4
ROWS, SLOTS, SIDE = 256, 28, 128
HEIGHT, QUARTER = 4, 7
SLABS = ROWS // HEIGHT
PEERS = NX * NC * NY
HELD = 32
ENTRIES = PEERS * HELD
PIECE = SIDE * SIDE // PEERS
WIDE = SIDE // NY
TARGETS = NX * NC
CAP_Z = 124
ROWS_Z = 128
CAP_X = 120
ORDER_Z = (3, 5, 4, 2, 6, 1, 7)
ORDER_Y = (1, 3, 2)
GROUP = 8
FAR_GROUP = 3
ROWS_AT_ONCE = 4
HEIGHT_2 = NC * HEIGHT
OUT_COLS = 72
ZERO_BLOCK = NY * HEIGHT * QUARTER
VMEM_LIMIT = 48 * 1024 * 1024
ROW_AXES = ("x", "z", "core")


def vmem():
    return pl.BlockSpec(memory_space=pltpu.VMEM)


def smem():
    return pl.BlockSpec(memory_space=pltpu.SMEM)


def params():
    return pltpu.CompilerParams(vmem_limit_bytes=VMEM_LIMIT)


def cost(flops, moved):
    return pl.CostEstimate(flops=flops, bytes_accessed=moved, transcendentals=0)


def prepare_kernel(position_ref, keep_ref, blocks_ref, cuts_ref, rows_ref):
    x, core, part = position_ref[0], position_ref[2], position_ref[3]
    lanes = iota((8, ENTRIES), 1) - ((part * NX + x) * NC + core) * HELD
    flags = jnp.zeros((8, ENTRIES), F32)
    for row in range(HEIGHT):
        for slot in range(QUARTER):
            number = row * QUARTER + slot
            keep = keep_ref[row, slot] != 0
            flags = jnp.where((lanes == number) & keep, 1.0, flags)
            block = blocks_ref[row, slot].astype(F32)
            rows_ref[number] = jnp.where(keep, block, jnp.zeros_like(block)).T
    for part_of in range(NY):
        for extra in range(HELD - SLOTS):
            at = extra * PIECE + part_of * SIDE
            value = flags[:, at : at + SIDE] if extra < 2 else jnp.zeros((8, SIDE), F32)
            for quarter in range(NY):
                begin = quarter * WIDE + part_of * TARGETS
                rows_ref[SLOTS + extra, begin : begin + TARGETS] = value
    for quarter in range(NY):
        peers = slice(quarter * TARGETS, (quarter + 1) * TARGETS)
        for part_of in range(NY):
            begin = quarter * WIDE + part_of * TARGETS
            for half in range(0, HELD, 16):
                rows = rows_ref[half : half + 16, begin : begin + TARGETS]
                cuts_ref[peers, half : half + 16, part_of * SIDE : (part_of + 1) * SIDE] = (
                    jnp.swapaxes(rows, 0, 1).astype(BF)
                )


def prepare(position, nonzero, blocks):
    return pl.pallas_call(
        prepare_kernel,
        out_shape=jax.ShapeDtypeStruct((PEERS, HELD, PIECE), BF),
        in_specs=[smem(), smem(), vmem()],
        out_specs=vmem(),
        scratch_shapes=[pltpu.VMEM((HELD, SIDE, SIDE), F32)],
        compiler_params=params(),
        name="prepare",
    )(position, nonzero, blocks)


def turn_kernel(keep_ref, blocks_ref, out_ref):
    for row in range(HEIGHT):
        for slot in range(QUARTER):
            block = blocks_ref[row, slot]
            out_ref[row, slot] = jnp.where(
                keep_ref[row, slot] != 0, block, jnp.zeros_like(block)
            ).T


def turn(nonzero, blocks):
    return pl.pallas_call(
        turn_kernel,
        out_shape=jax.ShapeDtypeStruct((HEIGHT, QUARTER, SIDE, SIDE), BF),
        in_specs=[smem(), vmem()],
        out_specs=vmem(),
        compiler_params=params(),
        cost_estimate=cost(2 * SLOTS * SIDE**3, 4 * SLOTS * SIDE**2),
        name="turn",
    )(nonzero, blocks)


def own_block(whole_ref, place, rows):
    value = whole_ref[jnp.minimum(place, ZERO_BLOCK - 1), rows, :]
    return jnp.where(place < ZERO_BLOCK, value, jnp.zeros_like(value))


def out_place(place):
    return (place // QUARTER) % HEIGHT, place // (QUARTER * HEIGHT) * QUARTER + place % QUARTER


def own_kernel(
    plan_ref,
    whole_ref,
    out_ref,
    total,
    panel,
    near,
):
    first = pl.multiple_of(plan_ref[15, 0] * WIDE, WIDE)
    for inner in range(HEIGHT):
        for member in range(HEIGHT):
            panel[pl.ds(inner * SIDE, SIDE), pl.ds(member * SIDE, SIDE)] = own_block(
                whole_ref, plan_ref[9 + member, inner], pl.ds(0, SIDE)
            )

    def step(group, carry):
        for at in range(GROUP):
            for inner in range(HEIGHT):
                near[pl.ds(at * WIDE, WIDE), pl.ds(inner * SIDE, SIDE)] = own_block(
                    whole_ref, plan_ref[4 + inner, group * GROUP + at], pl.ds(first, WIDE)
                )
        value = jnp.dot(near[...], panel[...], preferred_element_type=F32)
        total[pl.ds(group * GROUP, GROUP)] = value.reshape(GROUP, WIDE, HEIGHT * SIDE)
        return carry

    lax.fori_loop(0, plan_ref[15, 1], step, 0)
    for place in range(ZERO_BLOCK):
        member, slot = out_place(place)
        column = plan_ref[8, member * (128 // HEIGHT) + slot]
        out_ref[place] = total[column, :, pl.ds(member * SIDE, SIDE)]


def own_sums(lists, whole):
    flops = 2 * 32 * WIDE * (HEIGHT * SIDE) ** 2
    return pl.pallas_call(
        own_kernel,
        out_shape=jax.ShapeDtypeStruct((ZERO_BLOCK, WIDE, SIDE), F32),
        in_specs=[smem(), vmem()],
        out_specs=vmem(),
        scratch_shapes=[
            pltpu.VMEM((OUT_COLS, WIDE, HEIGHT * SIDE), F32),
            pltpu.VMEM((HEIGHT * SIDE, HEIGHT * SIDE), BF),
            pltpu.VMEM((GROUP * WIDE, HEIGHT * SIDE), BF),
        ],
        compiler_params=params(),
        cost_estimate=cost(flops, 3 * ZERO_BLOCK * SIDE * SIDE),
        name="own_sums",
    )(lists, whole)


def far_kernel(
    own_ref,
    plan_ref,
    whole_ref,
    far_ref,
    near_ref,
    *refs,
):
    *out_refs, total, pieces_ref = refs
    for sender in range(TARGETS):
        rows = pl.ds(sender * CAP_X, CAP_X)
        for part in range(NY):
            lanes = slice(part * SIDE, (part + 1) * SIDE)
            pieces_ref[part, rows, :] = far_ref[rows, lanes].astype(F32)

    def clear(group, carry):
        total[pl.ds(group * GROUP, GROUP)] = jnp.zeros((GROUP, WIDE, HEIGHT * SIDE), F32)
        return carry

    lax.fori_loop(0, own_ref[15, 1], clear, 0)

    def product(step):
        begin = plan_ref[2, step]
        length = plan_ref[3, step]
        right = jnp.concatenate(
            [
                own_block(whole_ref, plan_ref[4 + member, step], pl.ds(0, SIDE))
                for member in range(HEIGHT)
            ],
            axis=1,
        )
        pieces, columns = [], []
        for at in range(FAR_GROUP):
            place = jnp.minimum(begin + at, CAP_X - 1)
            rows = pl.ds(plan_ref[0, place], TARGETS, stride=CAP_X)
            for part in range(NY):
                pieces.append(pieces_ref[part, rows, :])
            columns.append(jnp.where(at < length, plan_ref[1, place], OUT_COLS))
        left = jnp.concatenate(pieces, axis=0).astype(BF)
        return jnp.dot(left, right, preferred_element_type=F32), columns

    def add(value, columns):
        for at, column in enumerate(columns):
            total[column] = total[column] + value[at * WIDE : (at + 1) * WIDE]

    def steps(number, carry):
        done = [product(number * ROWS_AT_ONCE + at) for at in range(ROWS_AT_ONCE)]
        for value, columns in done:
            add(value, columns)
        return carry

    lax.fori_loop(0, (plan_ref[8, 0] + ROWS_AT_ONCE - 1) // ROWS_AT_ONCE, steps, 0)

    for step, out_ref in enumerate(out_refs):
        part = (own_ref[15, 0] + step) & (NY - 1)
        for place in range(HEIGHT * QUARTER):
            member, slot = place // QUARTER, part * QUARTER + place % QUARTER
            column = own_ref[8, member * (128 // HEIGHT) + slot]
            value = total[column, :, pl.ds(member * SIDE, SIDE)]
            value = value + near_ref[part * (HEIGHT * QUARTER) + place]
            out_ref[place] = value.astype(BF)


def far_sums(own_lists, far_lists, whole, far, near):
    return pl.pallas_call(
        far_kernel,
        out_shape=[jax.ShapeDtypeStruct((HEIGHT * QUARTER, WIDE, SIDE), BF)] * NY,
        in_specs=[smem(), smem(), vmem(), vmem(), vmem()],
        out_specs=[vmem()] * NY,
        scratch_shapes=[
            pltpu.VMEM((OUT_COLS + 1, WIDE, HEIGHT * SIDE), F32),
            pltpu.VMEM((NY, TARGETS * CAP_X, SIDE), F32),
        ],
        compiler_params=params(),
        name="far_sums",
    )(own_lists, far_lists, whole, far, near)


def finish_kernel(position_ref, *refs):
    *cut_refs, out_ref = refs
    at = dict(zip((0,) + ORDER_Y, cut_refs))
    for part in range(NY):

        @pl.when(position_ref[3] == part)
        def _():
            order = [at[(part - sender) % NY] for sender in range(NY)]
            for row in range(HEIGHT):
                for slot in range(QUARTER):
                    cuts = [ref[row * QUARTER + slot] for ref in order]
                    out_ref[row, slot] = jnp.concatenate(cuts, axis=0).T


def finish(position, cuts):
    return pl.pallas_call(
        finish_kernel,
        out_shape=jax.ShapeDtypeStruct((HEIGHT, QUARTER, SIDE, SIDE), BF),
        in_specs=[smem()] + [vmem()] * NY,
        out_specs=vmem(),
        compiler_params=params(),
        name="finish",
    )(position, *cuts)


def iota(shape, axis):
    return lax.broadcasted_iota(I32, shape, axis)


def dot(a, b):
    return jnp.dot(a.astype(BF), b.astype(BF), preferred_element_type=F32)


def dot_rows(a, b):
    return lax.dot_general(
        a.astype(BF), b.astype(BF), (((1,), (1,)), ((), ())), preferred_element_type=F32
    )


def earlier(size):
    return (iota((size, size), 0) < iota((size, size), 1)).astype(F32)


def places(need):
    order = earlier(SIDE)
    parts = []
    before = jnp.zeros((need.shape[0], 1), F32)
    for begin in range(0, need.shape[1], SIDE):
        part = need[:, begin : begin + SIDE]
        parts.append(dot(part, order) + before)
        before = before + jnp.sum(part, axis=1, keepdims=True)
    return jnp.concatenate(parts, axis=1)


def codes(need, capacity):
    place = places(need)
    return jnp.where((need > 0) & (place < capacity), place, -1.0)


def one_hot(code, rows):
    number = iota((rows, code.shape[1]), 0).astype(F32).astype(BF)
    return jnp.where(number == code.astype(BF), jnp.ones((), BF), jnp.zeros((), BF))


def quarter_of(slot):
    return sum((slot >= bound * QUARTER).astype(I32) for bound in range(1, NY))


def pattern_kernel(position_ref, columns_ref, entries_ref, slots_ref, union_ref, need_ref, kq_ref):
    step = 64
    for begin in range(0, ROWS, step):
        column = iota((step, ROWS), 1)
        found = jnp.full((step, ROWS), -1, I32)
        for slot in range(SLOTS):
            at = columns_ref[begin : begin + step, slot : slot + 1]
            found = jnp.where(at == column, slot, found)
        slots_ref[begin : begin + step, :] = found
    names = (slots_ref[...] >= 0).astype(F32)
    mine = iota((128, ROWS), 1) // HEIGHT == iota((128, ROWS), 0)
    union = (dot(mine.astype(F32), names) > 0).astype(F32)
    union_ref[...] = union

    entry = iota((1, ENTRIES), 1)
    peer, number = entry // HELD, entry % HELD
    x, core = (peer // NC) % NX, peer % NC
    row = ((x * NZ + position_ref[1]) * NC + core) * HEIGHT + quarter_of(number)
    column = entries_ref[...]
    every = iota((ROWS, ENTRIES), 0)
    named = dot(jnp.where(mine, 0.0, union), (every == row).astype(F32))
    need_ref[...] = named * dot(union, (every == column).astype(F32))
    kind = iota((8, ENTRIES), 0)
    both = jnp.where(kind == 1, jnp.maximum(column, 0), 0)
    kq_ref[...] = jnp.where(kind == 0, row, both).astype(F32)


def pattern(position, columns, entries):
    return pl.pallas_call(
        pattern_kernel,
        out_shape=(
            jax.ShapeDtypeStruct((ROWS, ROWS), I32),
            jax.ShapeDtypeStruct((128, ROWS), F32),
            jax.ShapeDtypeStruct((128, ENTRIES), F32),
            jax.ShapeDtypeStruct((8, ENTRIES), F32),
        ),
        in_specs=[smem(), vmem(), vmem()],
        out_specs=(vmem(), vmem(), vmem(), vmem()),
        compiler_params=params(),
        cost_estimate=cost(2 * SLOTS * ROWS**3 // 4, 8 * ROWS**2),
        name="pattern",
    )(position, columns, entries)


def send_kernel(position_ref, need_ref, kq_ref, near_ref, *refs):
    *out_refs, chosen_ref = refs
    z = position_ref[1]
    near = near_ref[...]
    kind = iota((8, ENTRIES), 0)
    pick = (iota((8, ENTRIES), 1) % HELD == SLOTS + kind) & (kind < 2)
    flags = dot(pick.astype(F32), near)
    flags = jnp.concatenate([flags[0:1], flags[1:2]], axis=1)
    need = need_ref[...] * flags
    slab = iota((8, 128), 1)
    plane = (slab // NC) % NZ == (iota((8, 128), 0) + z) & (NZ - 1)
    wanted = (dot(plane.astype(F32), need) > 0).astype(F32)
    code = codes(wanted, CAP_Z)
    most = jnp.max(jnp.sum(wanted, axis=1, keepdims=True), axis=0, keepdims=True)
    most = jnp.broadcast_to(jnp.minimum(most, 250.0), (1, 128))
    totals = jnp.minimum(dot_rows(jnp.ones((8, ENTRIES), F32), need)[0:1], 250.0)
    for to in range(NZ):
        chosen_ref[to * ROWS_Z : (to + 1) * ROWS_Z, :] = one_hot(code[to : to + 1], ROWS_Z)
    packed = jnp.dot(chosen_ref[...], near, preferred_element_type=F32)
    tail = iota((16, PIECE), 0)
    kq = kq_ref[...]
    for to in range(NZ):
        target = iota((8, 128), 0)
        choice = slab == (target // NC * NZ + ((z + to) & (NZ - 1))) * NC + target % NC
        asked = jnp.concatenate([dot(choice.astype(F32), need), kq], axis=0)
        notes = dot_rows(asked, chosen_ref[to * ROWS_Z : (to + 1) * ROWS_Z, :])
        first = jnp.concatenate([notes[i : i + 1] for i in range(4)], axis=1)
        second = jnp.concatenate([notes[i : i + 1] for i in range(4, 8)], axis=1)
        third = jnp.concatenate([notes[8:9], notes[9:10], totals, most], axis=1)
        begin = to * ROWS_Z
        out_refs[to][0 : ROWS_Z - 16] = packed[begin : begin + ROWS_Z - 16].astype(BF)
        value = packed[begin + ROWS_Z - 16 : begin + ROWS_Z]
        value = jnp.where(tail == 12, first, value)
        value = jnp.where(tail == 13, second, value)
        value = jnp.where(tail == 14, third, value)
        out_refs[to][ROWS_Z - 16 : ROWS_Z] = value.astype(BF)


def send(position, need, kq, near):
    return pl.pallas_call(
        send_kernel,
        out_shape=[jax.ShapeDtypeStruct((ROWS_Z, PIECE), BF)] * NZ,
        in_specs=[smem()] + [vmem()] * 3,
        out_specs=[vmem()] * NZ,
        scratch_shapes=[pltpu.VMEM((NZ * ROWS_Z, ENTRIES), BF)],
        compiler_params=params(),
        name="send",
    )(position, need, kq, near)


def notes_of(along_refs):
    asked, third = [], []
    for along_ref in along_refs:
        notes = along_ref[ROWS_Z - 16 : ROWS_Z].astype(F32)
        asked.append(
            jnp.concatenate(
                [
                    notes[12 + i // 4 : 13 + i // 4, i % 4 * SIDE : (i % 4 + 1) * SIDE]
                    for i in range(TARGETS)
                ],
                axis=0,
            )
        )
        third.append(notes[14:15])
    return jnp.concatenate(asked, axis=1), third


def route_kernel(*refs):
    *along_refs, out_ref, chosen_ref, along_ref = refs
    asked, _ = notes_of(along_refs)
    for number, ref in enumerate(along_refs):
        along_ref[number * ROWS_Z : (number + 1) * ROWS_Z] = ref[...]
    code = codes(asked, CAP_X)
    for to in range(TARGETS):
        chosen_ref[to * SIDE : (to + 1) * SIDE, :] = one_hot(code[to : to + 1], SIDE)
    packed = jnp.dot(chosen_ref[...], along_ref[...], preferred_element_type=F32)
    for to in range(TARGETS):
        out_ref[to] = packed[to * SIDE : to * SIDE + CAP_X].astype(BF)


def route(along):
    return pl.pallas_call(
        route_kernel,
        out_shape=jax.ShapeDtypeStruct((TARGETS, CAP_X, PIECE), BF),
        in_specs=[vmem()] * NZ,
        out_specs=vmem(),
        scratch_shapes=[
            pltpu.VMEM((TARGETS * SIDE, NZ * ROWS_Z), BF),
            pltpu.VMEM((NZ * ROWS_Z, PIECE), BF),
        ],
        compiler_params=params(),
        name="route",
    )(*along)


def own_places(position_ref, slots_ref):
    chip = position_ref[0] * NZ + position_ref[1]
    both = slots_ref[pl.ds(pl.multiple_of(chip * HEIGHT_2, HEIGHT_2), HEIGHT_2), :]
    swapped = jnp.concatenate([both[HEIGHT:], both[:HEIGHT]], axis=0)
    slot = jnp.where(position_ref[2] == 0, both, swapped)
    quarter = quarter_of(slot)
    held = (quarter * HEIGHT + iota(slot.shape, 0)) * QUARTER + slot - quarter * QUARTER
    return slot, jnp.where(slot >= 0, held - ZERO_BLOCK, 0).astype(F32)


def own_plan_kernel(position_ref, slots_ref, union_ref, out_ref):
    x, z, core, part = (position_ref[i] for i in range(4))
    slab = (x * NZ + z) * NC + core
    order = earlier(ROWS)
    out_ref[...] = jnp.zeros_like(out_ref)
    mine = union_ref[pl.ds(slab, 1), :]
    rank = dot(jnp.broadcast_to(mine, (8, ROWS)), order)

    slot, held = own_places(position_ref, slots_ref)
    number = iota((OUT_COLS, ROWS), 0).astype(F32)
    chosen = ((rank[0:1] == number) & (mine > 0)).astype(F32)
    out_ref[4:8, 0:OUT_COLS] = dot_rows(held, chosen)[0:HEIGHT].astype(I32) + ZERO_BLOCK
    wide = 128 // HEIGHT
    chosen = jnp.concatenate(
        [slot[i : i + 1] == iota((wide, ROWS), 0) for i in range(HEIGHT)], axis=0
    )
    out_ref[8:9, 0:128] = dot_rows(rank, chosen.astype(F32))[0:1].astype(I32)
    chosen = (iota((8, ROWS), 1) == iota((8, ROWS), 0) + slab * HEIGHT).astype(F32)
    out_ref[9:13, 0:8] = dot_rows(held, chosen)[0:HEIGHT].astype(I32) + ZERO_BLOCK
    groups = ((jnp.sum(mine) + (GROUP - 1)) * (1.0 / GROUP)).astype(I32)
    lane = iota((1, 128), 1)
    scalars = jnp.where(lane == 0, part, 0)
    out_ref[15:16, :] = jnp.where(lane == 1, groups, scalars)


def own_plan(position, slots, union):
    return pl.pallas_call(
        own_plan_kernel,
        out_shape=jax.ShapeDtypeStruct((16, 128), I32),
        in_specs=[smem(), vmem(), vmem()],
        out_specs=vmem(),
        compiler_params=params(),
        cost_estimate=cost(ROWS**3, 4 * ROWS**2),
        name="own_plan",
    )(position, slots, union)


def far_plan_kernel(position_ref, slots_ref, union_ref, *refs):
    *along_refs, out_ref = refs
    x, z, core = (position_ref[i] for i in range(3))
    slab = (x * NZ + z) * NC + core
    out_ref[...] = jnp.zeros_like(out_ref)
    asked, third = notes_of(along_refs)
    mine = iota(asked.shape, 0) == x * NC + core
    asked = jnp.sum(jnp.where(mine, asked, 0.0), axis=0, keepdims=True)
    number = jnp.sum(asked).astype(I32)
    code = codes(jnp.broadcast_to(asked, (8, asked.shape[1])), CAP_X)[0:1]
    chosen = one_hot(code, SIDE).astype(F32)
    row = jnp.concatenate([part[:, :SIDE] for part in third], axis=1)
    column = jnp.concatenate([part[:, SIDE : 2 * SIDE] for part in third], axis=1)
    row_down = jnp.sum(chosen * row, axis=1, keepdims=True).astype(I32)
    column_down = jnp.sum(chosen * column, axis=1, keepdims=True).astype(I32)
    row_along = dot_rows(jnp.broadcast_to(row, (8, row.shape[1])), chosen)[0:1].astype(I32)

    down, along = iota((SIDE, SIDE), 0), iota((SIDE, SIDE), 1)
    less = (row_down < row_along) | ((row_down == row_along) & (down < along))
    order = jnp.sum((less & (down < number)).astype(F32), axis=0, keepdims=True)
    ordered = ((order == down.astype(F32)) & (along < number)).astype(F32)
    position = iota((8, SIDE), 1).astype(F32)
    out_ref[0:1, 0:SIDE] = dot_rows(position, ordered)[0:1].astype(I32)
    names = union_ref[pl.ds(slab, 1), :]
    order = earlier(ROWS)
    rank = dot(jnp.broadcast_to(names, (8, ROWS)), order)
    every = iota((SIDE, ROWS), 1)
    rank = dot_rows(rank, (every == column_down).astype(F32))
    out_ref[1:2, 0:SIDE] = dot_rows(rank, ordered)[0:1].astype(I32)

    valid = iota((SIDE, ROWS), 0) < number
    count = dot(jnp.ones((8, SIDE), F32), ((every == row_down) & valid).astype(F32))
    start = jnp.minimum(dot(count, order), 250.0)[0:1]
    _, held = own_places(position_ref, slots_ref)
    needed = ((count + (FAR_GROUP - 1)) * (1.0 / FAR_GROUP)).astype(I32).astype(F32)
    first = dot(needed, order)[0:1]
    number = iota((SIDE, ROWS), 0).astype(F32)
    chosen = ((first <= number) & (number < first + needed[0:1])).astype(F32)
    kind = iota((8, ROWS), 0)
    values = jnp.where(kind == 0, start, jnp.where(kind == 1, first, count))
    values = dot_rows(values, chosen).astype(I32)
    done = (iota((1, SIDE), 1) - values[1:2]) * FAR_GROUP
    steps = jnp.sum(needed[0:1]).astype(I32)
    valid = iota((1, SIDE), 1) < steps
    out_ref[2:3, :] = jnp.where(valid, values[0:1] + done, 0)
    out_ref[3:4, :] = jnp.where(valid, values[2:3] - done, 0)
    out_ref[4:8, :] = dot_rows(held, chosen)[0:HEIGHT].astype(I32) + ZERO_BLOCK
    out_ref[8:9, :] = jnp.zeros((1, SIDE), I32) + jnp.minimum(steps, SIDE)

    third = functools.reduce(jnp.maximum, third), functools.reduce(jnp.add, third)
    most_z = jnp.max(third[0][:, 3 * SIDE :])
    most_x = jnp.max(third[1][:, 2 * SIDE : 3 * SIDE])
    fits = (most_x <= CAP_X) & (most_z <= CAP_Z)
    out_ref[9:10, :] = jnp.zeros((1, SIDE), I32) + fits.astype(I32)


def far_plan(position, slots, union, along):
    return pl.pallas_call(
        far_plan_kernel,
        out_shape=jax.ShapeDtypeStruct((16, 128), I32),
        in_specs=[smem()] + [vmem()] * (2 + NZ),
        out_specs=vmem(),
        compiler_params=params(),
        cost_estimate=cost(2 * 20 * ROWS**3, 8 * ROWS**2),
        name="far_plan",
    )(position, slots, union, *along)


def dense(blocks, nonzero, columns):
    slab = lax.axis_index(ROW_AXES)
    part = lax.axis_index("col")
    masked = blocks * nonzero[:, :, None, None].astype(BF)
    slab_ids = jnp.arange(SLABS, dtype=I32)
    local_rows = jnp.arange(HEIGHT, dtype=I32)
    grouped = columns.reshape(SLABS, HEIGHT * SLOTS)
    targets = slab * HEIGHT + local_rows
    wanted = jnp.any(grouped[:, :, None] == targets[None, None, :], axis=1)
    wanted = wanted & (slab_ids != slab)[:, None]
    picked = jnp.sum(jnp.where(wanted, local_rows, 0), axis=1)
    filled = jnp.any(wanted, axis=1)
    outgoing = jnp.where(filled[:, None, None, None], masked[picked], jnp.zeros((), BF))
    incoming = lax.all_to_all(outgoing, ROW_AXES, split_axis=0, concat_axis=0, tiled=True)
    row_table = jnp.concatenate([incoming, masked], axis=0)
    own_cols = lax.dynamic_slice_in_dim(columns, slab * HEIGHT, HEIGHT, 0)
    source = own_cols // HEIGHT
    row_index = jnp.where(source == slab, SLABS + own_cols % HEIGHT, source)
    far_cols = columns[own_cols]
    far_quarter = lax.dynamic_slice_in_dim(far_cols, part * QUARTER, QUARTER, 2)
    whole = lax.all_gather(masked, "col", axis=1, tiled=True)
    results = []
    for member in range(HEIGHT):
        match = far_quarter[member][:, :, None] == own_cols[member][None, None, :]
        products = jnp.einsum(
            "tab,tubc->tuac", whole[member], row_table[row_index[member]],
            preferred_element_type=F32,
        )
        summed = lax.dot_general(
            match.astype(F32).reshape(SLOTS * QUARTER, SLOTS),
            products.reshape(SLOTS * QUARTER, SIDE * SIDE),
            (((0,), (0,)), ((), ())),
            precision=lax.Precision.HIGHEST,
            preferred_element_type=F32,
        )
        results.append(summed.reshape(SLOTS, SIDE, SIDE))
    square = lax.psum_scatter(jnp.stack(results), "col", scatter_dimension=1, tiled=True)
    return square.astype(BF)


def plane_columns(columns):
    split = columns.reshape(NX, NZ, NC, HEIGHT, NY, QUARTER)
    mine = lax.dynamic_index_in_dim(split, lax.axis_index("z"), 1, keepdims=False)
    mine = mine.transpose(3, 0, 1, 2, 4).reshape(PEERS, SLOTS)
    return jnp.pad(mine, ((0, 0), (0, HELD - SLOTS)), constant_values=-1).reshape(1, ENTRIES)


def shards(blocks, nonzero, columns):
    position = jnp.stack([lax.axis_index(name) for name in ROW_AXES + ("col",)])
    cuts = prepare(position, nonzero, blocks)
    cuts, names, same = lax.optimization_barrier((cuts, columns, blocks))
    turned = turn(nonzero, same)
    slots, union, need, kq = pattern(position, names, plane_columns(columns))
    near = lax.all_to_all(cuts, ("col", "x", "core"), split_axis=0, concat_axis=0, tiled=True)
    near, turned, need = lax.optimization_barrier((near, turned, need))
    whole = lax.all_gather(turned, "col", axis=0, tiled=False)
    whole = whole.reshape(ZERO_BLOCK, SIDE, SIDE)
    packed = send(position, need, kq, near.reshape(ENTRIES, PIECE))
    packed, slots = lax.optimization_barrier((packed, slots))
    along = [packed[0]] + [
        lax.ppermute(packed[step], "z", [(i, (i + step) % NZ) for i in range(NZ)])
        for step in ORDER_Z
    ]
    own_lists = own_plan(position, slots, union)
    packed, notes = lax.optimization_barrier((route(along), along))
    far = lax.all_to_all(packed, ("x", "core"), split_axis=0, concat_axis=0, tiled=True)
    far_lists = far_plan(position, slots, union, notes)
    far = far.reshape(TARGETS * CAP_X, PIECE)
    own = own_sums(own_lists, whole)
    far, fits, own = lax.optimization_barrier((far, far_lists[9, 0] != 0, own))
    result = far_sums(own_lists, far_lists, whole, far, own)
    cuts = [result[0]]
    for step in ORDER_Y:
        pairs = [(i, (i + step) % NY) for i in range(NY)]
        cuts.append(lax.ppermute(result[step], "col", pairs))
    square = finish(position, cuts)
    return lax.cond(
        fits,
        lambda value, *_: value,
        lambda _, *inputs: dense(*inputs),
        square,
        blocks,
        nonzero,
        columns,
    )


def solution(mesh):
    fine = Mesh(mesh.devices.reshape(NX, NZ, NC, NY), ROW_AXES + ("col",))
    spec = P(ROW_AXES, "col", None, None)
    return jax.shard_map(
        shards,
        mesh=fine,
        in_specs=(spec, P(ROW_AXES, "col"), P()),
        out_specs=spec,
        check_vma=False,
    )
```

```python
import functools

import jax
import jax.numpy as jnp
from jax import lax
from jax.experimental import pallas as pl
from jax.experimental.pallas import tpu as pltpu
from jax.sharding import Mesh
from jax.sharding import PartitionSpec as P

BF = jnp.bfloat16
F32 = jnp.float32
I32 = jnp.int32

NX, NZ, NC, NY = 4, 8, 2, 4
ROWS, SLOTS, SIDE = 256, 28, 128
HEIGHT, QUARTER = 4, 7
SLABS = ROWS // HEIGHT
PEERS = NX * NC * NY
HELD = 32
ENTRIES = PEERS * HELD
PIECE = SIDE * SIDE // PEERS
WIDE = SIDE // NY
TARGETS = NX * NC
CAP_Z = 124
ROWS_Z = 128
CAP_X = 120
ORDER_Z = (4, 3, 5, 2, 6, 1, 7)
ORDER_Y = (2, 1, 3)
GROUP = 8
FAR_GROUP = 3
STEPS_AT_ONCE = 8
HEIGHT_2 = NC * HEIGHT
OUT_COLS = 72
ZERO_BLOCK = NY * HEIGHT * QUARTER
VMEM_LIMIT = 48 * 1024 * 1024
ROW_AXES = ("x", "z", "core")


def vmem():
    return pl.BlockSpec(memory_space=pltpu.VMEM)


def smem():
    return pl.BlockSpec(memory_space=pltpu.SMEM)


def params():
    return pltpu.CompilerParams(vmem_limit_bytes=VMEM_LIMIT)


def cost(flops, moved):
    return pl.CostEstimate(flops=flops, bytes_accessed=moved, transcendentals=0)


def prepare_kernel(position_ref, keep_ref, blocks_ref, cuts_ref, rows_ref):
    x, core, part = position_ref[0], position_ref[2], position_ref[3]
    lanes = iota((8, ENTRIES), 1) - ((part * NX + x) * NC + core) * HELD
    flags = jnp.zeros((8, ENTRIES), F32)
    for row in range(HEIGHT):
        for slot in range(QUARTER):
            number = row * QUARTER + slot
            keep = keep_ref[row, slot] != 0
            flags = jnp.where((lanes == number) & keep, 1.0, flags)
            block = blocks_ref[row, slot].astype(F32)
            rows_ref[number] = jnp.where(keep, block, jnp.zeros_like(block)).T
    for part_of in range(NY):
        for extra in range(HELD - SLOTS):
            at = extra * PIECE + part_of * SIDE
            value = flags[:, at : at + SIDE] if extra < 2 else jnp.zeros((8, SIDE), F32)
            for quarter in range(NY):
                begin = quarter * WIDE + part_of * TARGETS
                rows_ref[SLOTS + extra, begin : begin + TARGETS] = value
    for quarter in range(NY):
        peers = slice(quarter * TARGETS, (quarter + 1) * TARGETS)
        for part_of in range(NY):
            begin = quarter * WIDE + part_of * TARGETS
            for half in range(0, HELD, 16):
                rows = rows_ref[half : half + 16, begin : begin + TARGETS]
                cuts_ref[peers, half : half + 16, part_of * SIDE : (part_of + 1) * SIDE] = (
                    jnp.swapaxes(rows, 0, 1).astype(BF)
                )


def prepare(position, nonzero, blocks):
    return pl.pallas_call(
        prepare_kernel,
        out_shape=jax.ShapeDtypeStruct((PEERS, HELD, PIECE), BF),
        in_specs=[smem(), smem(), vmem()],
        out_specs=vmem(),
        scratch_shapes=[pltpu.VMEM((HELD, SIDE, SIDE), F32)],
        compiler_params=params(),
        name="prepare",
    )(position, nonzero, blocks)


def turn_kernel(keep_ref, blocks_ref, out_ref):
    for row in range(HEIGHT):
        for slot in range(QUARTER):
            block = blocks_ref[row, slot]
            out_ref[row, slot] = jnp.where(
                keep_ref[row, slot] != 0, block, jnp.zeros_like(block)
            ).T


def turn(nonzero, blocks):
    return pl.pallas_call(
        turn_kernel,
        out_shape=jax.ShapeDtypeStruct((HEIGHT, QUARTER, SIDE, SIDE), BF),
        in_specs=[smem(), vmem()],
        out_specs=vmem(),
        compiler_params=params(),
        cost_estimate=cost(2 * SLOTS * SIDE**3, 4 * SLOTS * SIDE**2),
        name="turn",
    )(nonzero, blocks)


def own_block(whole_ref, place, rows):
    value = whole_ref[jnp.minimum(place, ZERO_BLOCK - 1), rows, :]
    return jnp.where(place < ZERO_BLOCK, value, jnp.zeros_like(value))


def out_place(place):
    return (place // QUARTER) % HEIGHT, place // (QUARTER * HEIGHT) * QUARTER + place % QUARTER


def own_kernel(
    plan_ref,
    whole_ref,
    out_ref,
    total,
    panel,
    near,
):
    first = pl.multiple_of(plan_ref[15, 0] * WIDE, WIDE)
    for inner in range(HEIGHT):
        for member in range(HEIGHT):
            panel[pl.ds(inner * SIDE, SIDE), pl.ds(member * SIDE, SIDE)] = own_block(
                whole_ref, plan_ref[9 + member, inner], pl.ds(0, SIDE)
            )

    def step(group, carry):
        for at in range(GROUP):
            for inner in range(HEIGHT):
                near[pl.ds(at * WIDE, WIDE), pl.ds(inner * SIDE, SIDE)] = own_block(
                    whole_ref, plan_ref[4 + inner, group * GROUP + at], pl.ds(first, WIDE)
                )
        value = jnp.dot(near[...], panel[...], preferred_element_type=F32)
        total[pl.ds(group * GROUP, GROUP)] = value.reshape(GROUP, WIDE, HEIGHT * SIDE)
        return carry

    lax.fori_loop(0, plan_ref[15, 1], step, 0)
    for place in range(ZERO_BLOCK):
        member, slot = out_place(place)
        column = plan_ref[8, member * (128 // HEIGHT) + slot]
        out_ref[place] = total[column, :, pl.ds(member * SIDE, SIDE)]


def own_sums(lists, whole):
    flops = 2 * 32 * WIDE * (HEIGHT * SIDE) ** 2
    return pl.pallas_call(
        own_kernel,
        out_shape=jax.ShapeDtypeStruct((ZERO_BLOCK, WIDE, SIDE), F32),
        in_specs=[smem(), vmem()],
        out_specs=vmem(),
        scratch_shapes=[
            pltpu.VMEM((OUT_COLS, WIDE, HEIGHT * SIDE), F32),
            pltpu.VMEM((HEIGHT * SIDE, HEIGHT * SIDE), BF),
            pltpu.VMEM((GROUP * WIDE, HEIGHT * SIDE), BF),
        ],
        compiler_params=params(),
        cost_estimate=cost(flops, 3 * ZERO_BLOCK * SIDE * SIDE),
        name="own_sums",
    )(lists, whole)


def far_kernel(
    own_ref,
    plan_ref,
    whole_ref,
    far_ref,
    near_ref,
    *refs,
):
    *out_refs, total, pieces_ref = refs
    for sender in range(TARGETS):
        rows = pl.ds(sender * CAP_X, CAP_X)
        for part in range(NY):
            lanes = slice(part * SIDE, (part + 1) * SIDE)
            pieces_ref[part, rows, :] = far_ref[rows, lanes].astype(F32)

    def clear(group, carry):
        total[pl.ds(group * GROUP, GROUP)] = jnp.zeros((GROUP, WIDE, HEIGHT * SIDE), F32)
        return carry

    lax.fori_loop(0, own_ref[15, 1], clear, 0)

    def add_product(step):
        begin = plan_ref[2, step]
        length = plan_ref[3, step]
        pieces, columns = [], []
        for at in range(FAR_GROUP):
            place = jnp.minimum(begin + at, CAP_X - 1)
            rows = pl.ds(plan_ref[0, place], TARGETS, stride=CAP_X)
            for part in range(NY):
                pieces.append(pieces_ref[part, rows, :])
            columns.append(jnp.where(at < length, plan_ref[1, place], OUT_COLS))
        left = jnp.concatenate(pieces, axis=0).astype(BF)
        for member in range(0, HEIGHT, 2):
            right = jnp.concatenate(
                [
                    own_block(whole_ref, plan_ref[4 + member + at, step], pl.ds(0, SIDE))
                    for at in range(2)
                ],
                axis=1,
            )
            value = jnp.dot(left, right, preferred_element_type=F32)
            lanes = pl.ds(member * SIDE, 2 * SIDE)
            for at, column in enumerate(columns):
                rows = slice(at * WIDE, (at + 1) * WIDE)
                total[column, :, lanes] = total[column, :, lanes] + value[rows]

    def steps(number, carry):
        for at in range(STEPS_AT_ONCE):
            add_product(number * STEPS_AT_ONCE + at)
        return carry

    lax.fori_loop(0, (plan_ref[8, 0] + STEPS_AT_ONCE - 1) // STEPS_AT_ONCE, steps, 0)

    for step, out_ref in enumerate(out_refs):
        part = (own_ref[15, 0] + step) & (NY - 1)
        for place in range(HEIGHT * QUARTER):
            member, slot = place // QUARTER, part * QUARTER + place % QUARTER
            column = own_ref[8, member * (128 // HEIGHT) + slot]
            value = total[column, :, pl.ds(member * SIDE, SIDE)]
            value = value + near_ref[part * (HEIGHT * QUARTER) + place]
            out_ref[place] = value.astype(BF)


def far_sums(own_lists, far_lists, whole, far, near):
    return pl.pallas_call(
        far_kernel,
        out_shape=[jax.ShapeDtypeStruct((HEIGHT * QUARTER, WIDE, SIDE), BF)] * NY,
        in_specs=[smem(), smem(), vmem(), vmem(), vmem()],
        out_specs=[vmem()] * NY,
        scratch_shapes=[
            pltpu.VMEM((OUT_COLS + 1, WIDE, HEIGHT * SIDE), F32),
            pltpu.VMEM((NY, TARGETS * CAP_X, SIDE), F32),
        ],
        compiler_params=params(),
        name="far_sums",
    )(own_lists, far_lists, whole, far, near)


def finish_kernel(position_ref, *refs):
    *cut_refs, out_ref = refs
    at = dict(zip((0,) + ORDER_Y, cut_refs))
    for part in range(NY):

        @pl.when(position_ref[3] == part)
        def _():
            order = [at[(part - sender) % NY] for sender in range(NY)]
            for row in range(HEIGHT):
                for slot in range(QUARTER):
                    cuts = [ref[row * QUARTER + slot] for ref in order]
                    out_ref[row, slot] = jnp.concatenate(cuts, axis=0).T


def finish(position, cuts):
    return pl.pallas_call(
        finish_kernel,
        out_shape=jax.ShapeDtypeStruct((HEIGHT, QUARTER, SIDE, SIDE), BF),
        in_specs=[smem()] + [vmem()] * NY,
        out_specs=vmem(),
        compiler_params=params(),
        name="finish",
    )(position, *cuts)


def iota(shape, axis):
    return lax.broadcasted_iota(I32, shape, axis)


def dot(a, b):
    return jnp.dot(a.astype(BF), b.astype(BF), preferred_element_type=F32)


def dot_rows(a, b):
    return lax.dot_general(
        a.astype(BF), b.astype(BF), (((1,), (1,)), ((), ())), preferred_element_type=F32
    )


def earlier(size):
    return (iota((size, size), 0) < iota((size, size), 1)).astype(F32)


def places(need):
    order = earlier(SIDE)
    parts = []
    before = jnp.zeros((need.shape[0], 1), F32)
    for begin in range(0, need.shape[1], SIDE):
        part = need[:, begin : begin + SIDE]
        parts.append(dot(part, order) + before)
        before = before + jnp.sum(part, axis=1, keepdims=True)
    return jnp.concatenate(parts, axis=1)


def codes(need, capacity):
    place = places(need)
    return jnp.where((need > 0) & (place < capacity), place, -1.0)


def one_hot(code, rows):
    number = iota((rows, code.shape[1]), 0).astype(F32).astype(BF)
    return jnp.where(number == code.astype(BF), jnp.ones((), BF), jnp.zeros((), BF))


def quarter_of(slot):
    return sum((slot >= bound * QUARTER).astype(I32) for bound in range(1, NY))


def pattern_kernel(position_ref, columns_ref, entries_ref, slots_ref, union_ref, need_ref, kq_ref):
    step = 64
    for begin in range(0, ROWS, step):
        column = iota((step, ROWS), 1)
        found = jnp.full((step, ROWS), -1, I32)
        for slot in range(SLOTS):
            at = columns_ref[begin : begin + step, slot : slot + 1]
            found = jnp.where(at == column, slot, found)
        slots_ref[begin : begin + step, :] = found
    names = (slots_ref[...] >= 0).astype(F32)
    mine = iota((128, ROWS), 1) // HEIGHT == iota((128, ROWS), 0)
    union = (dot(mine.astype(F32), names) > 0).astype(F32)
    union_ref[...] = union

    entry = iota((1, ENTRIES), 1)
    peer, number = entry // HELD, entry % HELD
    x, core = (peer // NC) % NX, peer % NC
    row = ((x * NZ + position_ref[1]) * NC + core) * HEIGHT + quarter_of(number)
    column = entries_ref[...]
    every = iota((ROWS, ENTRIES), 0)
    named = dot(jnp.where(mine, 0.0, union), (every == row).astype(F32))
    need_ref[...] = named * dot(union, (every == column).astype(F32))
    kind = iota((8, ENTRIES), 0)
    both = jnp.where(kind == 1, jnp.maximum(column, 0), 0)
    kq_ref[...] = jnp.where(kind == 0, row, both).astype(F32)


def pattern(position, columns, entries):
    return pl.pallas_call(
        pattern_kernel,
        out_shape=(
            jax.ShapeDtypeStruct((ROWS, ROWS), I32),
            jax.ShapeDtypeStruct((128, ROWS), F32),
            jax.ShapeDtypeStruct((128, ENTRIES), F32),
            jax.ShapeDtypeStruct((8, ENTRIES), F32),
        ),
        in_specs=[smem(), vmem(), vmem()],
        out_specs=(vmem(), vmem(), vmem(), vmem()),
        compiler_params=params(),
        cost_estimate=cost(2 * SLOTS * ROWS**3 // 4, 8 * ROWS**2),
        name="pattern",
    )(position, columns, entries)


def send_kernel(position_ref, need_ref, kq_ref, near_ref, *refs):
    *out_refs, chosen_ref = refs
    z = position_ref[1]
    near = near_ref[...]
    kind = iota((8, ENTRIES), 0)
    pick = (iota((8, ENTRIES), 1) % HELD == SLOTS + kind) & (kind < 2)
    flags = dot(pick.astype(F32), near)
    flags = jnp.concatenate([flags[0:1], flags[1:2]], axis=1)
    need = need_ref[...] * flags
    slab = iota((8, 128), 1)
    plane = (slab // NC) % NZ == (iota((8, 128), 0) + z) & (NZ - 1)
    wanted = (dot(plane.astype(F32), need) > 0).astype(F32)
    code = codes(wanted, CAP_Z)
    most = jnp.max(jnp.sum(wanted, axis=1, keepdims=True), axis=0, keepdims=True)
    most = jnp.broadcast_to(jnp.minimum(most, 250.0), (1, 128))
    totals = jnp.minimum(dot_rows(jnp.ones((8, ENTRIES), F32), need)[0:1], 250.0)
    for to in range(NZ):
        chosen_ref[to * ROWS_Z : (to + 1) * ROWS_Z, :] = one_hot(code[to : to + 1], ROWS_Z)
    packed = jnp.dot(chosen_ref[...], near, preferred_element_type=F32)
    tail = iota((16, PIECE), 0)
    kq = kq_ref[...]
    for to in range(NZ):
        target = iota((8, 128), 0)
        choice = slab == (target // NC * NZ + ((z + to) & (NZ - 1))) * NC + target % NC
        asked = jnp.concatenate([dot(choice.astype(F32), need), kq], axis=0)
        notes = dot_rows(asked, chosen_ref[to * ROWS_Z : (to + 1) * ROWS_Z, :])
        first = jnp.concatenate([notes[i : i + 1] for i in range(4)], axis=1)
        second = jnp.concatenate([notes[i : i + 1] for i in range(4, 8)], axis=1)
        third = jnp.concatenate([notes[8:9], notes[9:10], totals, most], axis=1)
        begin = to * ROWS_Z
        out_refs[to][0 : ROWS_Z - 16] = packed[begin : begin + ROWS_Z - 16].astype(BF)
        value = packed[begin + ROWS_Z - 16 : begin + ROWS_Z]
        value = jnp.where(tail == 12, first, value)
        value = jnp.where(tail == 13, second, value)
        value = jnp.where(tail == 14, third, value)
        out_refs[to][ROWS_Z - 16 : ROWS_Z] = value.astype(BF)


def send(position, need, kq, near):
    return pl.pallas_call(
        send_kernel,
        out_shape=[jax.ShapeDtypeStruct((ROWS_Z, PIECE), BF)] * NZ,
        in_specs=[smem()] + [vmem()] * 3,
        out_specs=[vmem()] * NZ,
        scratch_shapes=[pltpu.VMEM((NZ * ROWS_Z, ENTRIES), BF)],
        compiler_params=params(),
        name="send",
    )(position, need, kq, near)


def notes_of(along_refs):
    asked, third = [], []
    for along_ref in along_refs:
        notes = along_ref[ROWS_Z - 16 : ROWS_Z].astype(F32)
        asked.append(
            jnp.concatenate(
                [
                    notes[12 + i // 4 : 13 + i // 4, i % 4 * SIDE : (i % 4 + 1) * SIDE]
                    for i in range(TARGETS)
                ],
                axis=0,
            )
        )
        third.append(notes[14:15])
    return jnp.concatenate(asked, axis=1), third


def route_kernel(*refs):
    *along_refs, out_ref, chosen_ref, along_ref = refs
    asked, _ = notes_of(along_refs)
    for number, ref in enumerate(along_refs):
        along_ref[number * ROWS_Z : (number + 1) * ROWS_Z] = ref[...]
    code = codes(asked, CAP_X)
    for to in range(TARGETS):
        chosen_ref[to * SIDE : (to + 1) * SIDE, :] = one_hot(code[to : to + 1], SIDE)
    packed = jnp.dot(chosen_ref[...], along_ref[...], preferred_element_type=F32)
    for to in range(TARGETS):
        out_ref[to] = packed[to * SIDE : to * SIDE + CAP_X].astype(BF)


def route(along):
    return pl.pallas_call(
        route_kernel,
        out_shape=jax.ShapeDtypeStruct((TARGETS, CAP_X, PIECE), BF),
        in_specs=[vmem()] * NZ,
        out_specs=vmem(),
        scratch_shapes=[
            pltpu.VMEM((TARGETS * SIDE, NZ * ROWS_Z), BF),
            pltpu.VMEM((NZ * ROWS_Z, PIECE), BF),
        ],
        compiler_params=params(),
        name="route",
    )(*along)


def own_places(position_ref, slots_ref):
    chip = position_ref[0] * NZ + position_ref[1]
    both = slots_ref[pl.ds(pl.multiple_of(chip * HEIGHT_2, HEIGHT_2), HEIGHT_2), :]
    swapped = jnp.concatenate([both[HEIGHT:], both[:HEIGHT]], axis=0)
    slot = jnp.where(position_ref[2] == 0, both, swapped)
    quarter = quarter_of(slot)
    held = (quarter * HEIGHT + iota(slot.shape, 0)) * QUARTER + slot - quarter * QUARTER
    return slot, jnp.where(slot >= 0, held - ZERO_BLOCK, 0).astype(F32)


def own_plan_kernel(position_ref, slots_ref, union_ref, out_ref):
    x, z, core, part = (position_ref[i] for i in range(4))
    slab = (x * NZ + z) * NC + core
    order = earlier(ROWS)
    out_ref[...] = jnp.zeros_like(out_ref)
    mine = union_ref[pl.ds(slab, 1), :]
    rank = dot(jnp.broadcast_to(mine, (8, ROWS)), order)

    slot, held = own_places(position_ref, slots_ref)
    number = iota((OUT_COLS, ROWS), 0).astype(F32)
    chosen = ((rank[0:1] == number) & (mine > 0)).astype(F32)
    out_ref[4:8, 0:OUT_COLS] = dot_rows(held, chosen)[0:HEIGHT].astype(I32) + ZERO_BLOCK
    wide = 128 // HEIGHT
    chosen = jnp.concatenate(
        [slot[i : i + 1] == iota((wide, ROWS), 0) for i in range(HEIGHT)], axis=0
    )
    out_ref[8:9, 0:128] = dot_rows(rank, chosen.astype(F32))[0:1].astype(I32)
    chosen = (iota((8, ROWS), 1) == iota((8, ROWS), 0) + slab * HEIGHT).astype(F32)
    out_ref[9:13, 0:8] = dot_rows(held, chosen)[0:HEIGHT].astype(I32) + ZERO_BLOCK
    groups = ((jnp.sum(mine) + (GROUP - 1)) * (1.0 / GROUP)).astype(I32)
    lane = iota((1, 128), 1)
    scalars = jnp.where(lane == 0, part, 0)
    out_ref[15:16, :] = jnp.where(lane == 1, groups, scalars)


def own_plan(position, slots, union):
    return pl.pallas_call(
        own_plan_kernel,
        out_shape=jax.ShapeDtypeStruct((16, 128), I32),
        in_specs=[smem(), vmem(), vmem()],
        out_specs=vmem(),
        compiler_params=params(),
        cost_estimate=cost(ROWS**3, 4 * ROWS**2),
        name="own_plan",
    )(position, slots, union)


def far_plan_kernel(position_ref, slots_ref, union_ref, *refs):
    *along_refs, out_ref = refs
    x, z, core = (position_ref[i] for i in range(3))
    slab = (x * NZ + z) * NC + core
    out_ref[...] = jnp.zeros_like(out_ref)
    asked, third = notes_of(along_refs)
    mine = iota(asked.shape, 0) == x * NC + core
    asked = jnp.sum(jnp.where(mine, asked, 0.0), axis=0, keepdims=True)
    number = jnp.sum(asked).astype(I32)
    code = codes(jnp.broadcast_to(asked, (8, asked.shape[1])), CAP_X)[0:1]
    chosen = one_hot(code, SIDE).astype(F32)
    row = jnp.concatenate([part[:, :SIDE] for part in third], axis=1)
    column = jnp.concatenate([part[:, SIDE : 2 * SIDE] for part in third], axis=1)
    row_down = jnp.sum(chosen * row, axis=1, keepdims=True).astype(I32)
    column_down = jnp.sum(chosen * column, axis=1, keepdims=True).astype(I32)
    row_along = dot_rows(jnp.broadcast_to(row, (8, row.shape[1])), chosen)[0:1].astype(I32)

    down, along = iota((SIDE, SIDE), 0), iota((SIDE, SIDE), 1)
    less = (row_down < row_along) | ((row_down == row_along) & (down < along))
    order = jnp.sum((less & (down < number)).astype(F32), axis=0, keepdims=True)
    ordered = ((order == down.astype(F32)) & (along < number)).astype(F32)
    position = iota((8, SIDE), 1).astype(F32)
    out_ref[0:1, 0:SIDE] = dot_rows(position, ordered)[0:1].astype(I32)
    names = union_ref[pl.ds(slab, 1), :]
    order = earlier(ROWS)
    rank = dot(jnp.broadcast_to(names, (8, ROWS)), order)
    every = iota((SIDE, ROWS), 1)
    rank = dot_rows(rank, (every == column_down).astype(F32))
    out_ref[1:2, 0:SIDE] = dot_rows(rank, ordered)[0:1].astype(I32)

    valid = iota((SIDE, ROWS), 0) < number
    count = dot(jnp.ones((8, SIDE), F32), ((every == row_down) & valid).astype(F32))
    start = jnp.minimum(dot(count, order), 250.0)[0:1]
    _, held = own_places(position_ref, slots_ref)
    needed = ((count + (FAR_GROUP - 1)) * (1.0 / FAR_GROUP)).astype(I32).astype(F32)
    first = dot(needed, order)[0:1]
    number = iota((SIDE, ROWS), 0).astype(F32)
    chosen = ((first <= number) & (number < first + needed[0:1])).astype(F32)
    kind = iota((8, ROWS), 0)
    values = jnp.where(kind == 0, start, jnp.where(kind == 1, first, count))
    values = dot_rows(values, chosen).astype(I32)
    done = (iota((1, SIDE), 1) - values[1:2]) * FAR_GROUP
    steps = jnp.sum(needed[0:1]).astype(I32)
    valid = iota((1, SIDE), 1) < steps
    out_ref[2:3, :] = jnp.where(valid, values[0:1] + done, 0)
    out_ref[3:4, :] = jnp.where(valid, values[2:3] - done, 0)
    out_ref[4:8, :] = dot_rows(held, chosen)[0:HEIGHT].astype(I32) + ZERO_BLOCK
    out_ref[8:9, :] = jnp.zeros((1, SIDE), I32) + jnp.minimum(steps, SIDE)

    third = functools.reduce(jnp.maximum, third), functools.reduce(jnp.add, third)
    most_z = jnp.max(third[0][:, 3 * SIDE :])
    most_x = jnp.max(third[1][:, 2 * SIDE : 3 * SIDE])
    fits = (most_x <= CAP_X) & (most_z <= CAP_Z)
    out_ref[9:10, :] = jnp.zeros((1, SIDE), I32) + fits.astype(I32)


def far_plan(position, slots, union, along):
    return pl.pallas_call(
        far_plan_kernel,
        out_shape=jax.ShapeDtypeStruct((16, 128), I32),
        in_specs=[smem()] + [vmem()] * (2 + NZ),
        out_specs=vmem(),
        compiler_params=params(),
        cost_estimate=cost(2 * 20 * ROWS**3, 8 * ROWS**2),
        name="far_plan",
    )(position, slots, union, *along)


def dense(blocks, nonzero, columns):
    slab = lax.axis_index(ROW_AXES)
    part = lax.axis_index("col")
    masked = blocks * nonzero[:, :, None, None].astype(BF)
    slab_ids = jnp.arange(SLABS, dtype=I32)
    local_rows = jnp.arange(HEIGHT, dtype=I32)
    grouped = columns.reshape(SLABS, HEIGHT * SLOTS)
    targets = slab * HEIGHT + local_rows
    wanted = jnp.any(grouped[:, :, None] == targets[None, None, :], axis=1)
    wanted = wanted & (slab_ids != slab)[:, None]
    picked = jnp.sum(jnp.where(wanted, local_rows, 0), axis=1)
    filled = jnp.any(wanted, axis=1)
    outgoing = jnp.where(filled[:, None, None, None], masked[picked], jnp.zeros((), BF))
    incoming = lax.all_to_all(outgoing, ROW_AXES, split_axis=0, concat_axis=0, tiled=True)
    row_table = jnp.concatenate([incoming, masked], axis=0)
    own_cols = lax.dynamic_slice_in_dim(columns, slab * HEIGHT, HEIGHT, 0)
    source = own_cols // HEIGHT
    row_index = jnp.where(source == slab, SLABS + own_cols % HEIGHT, source)
    far_cols = columns[own_cols]
    far_quarter = lax.dynamic_slice_in_dim(far_cols, part * QUARTER, QUARTER, 2)
    whole = lax.all_gather(masked, "col", axis=1, tiled=True)
    results = []
    for member in range(HEIGHT):
        match = far_quarter[member][:, :, None] == own_cols[member][None, None, :]
        products = jnp.einsum(
            "tab,tubc->tuac", whole[member], row_table[row_index[member]],
            preferred_element_type=F32,
        )
        summed = lax.dot_general(
            match.astype(F32).reshape(SLOTS * QUARTER, SLOTS),
            products.reshape(SLOTS * QUARTER, SIDE * SIDE),
            (((0,), (0,)), ((), ())),
            precision=lax.Precision.HIGHEST,
            preferred_element_type=F32,
        )
        results.append(summed.reshape(SLOTS, SIDE, SIDE))
    square = lax.psum_scatter(jnp.stack(results), "col", scatter_dimension=1, tiled=True)
    return square.astype(BF)


def plane_columns(columns):
    split = columns.reshape(NX, NZ, NC, HEIGHT, NY, QUARTER)
    mine = lax.dynamic_index_in_dim(split, lax.axis_index("z"), 1, keepdims=False)
    mine = mine.transpose(3, 0, 1, 2, 4).reshape(PEERS, SLOTS)
    return jnp.pad(mine, ((0, 0), (0, HELD - SLOTS)), constant_values=-1).reshape(1, ENTRIES)


def shards(blocks, nonzero, columns):
    position = jnp.stack([lax.axis_index(name) for name in ROW_AXES + ("col",)])
    cuts = prepare(position, nonzero, blocks)
    cuts, names, same = lax.optimization_barrier((cuts, columns, blocks))
    turned = turn(nonzero, same)
    slots, union, need, kq = pattern(position, names, plane_columns(columns))
    near = lax.all_to_all(cuts, ("col", "x", "core"), split_axis=0, concat_axis=0, tiled=True)
    near, turned, need = lax.optimization_barrier((near, turned, need))
    whole = lax.all_gather(turned, "col", axis=0, tiled=False)
    whole = whole.reshape(ZERO_BLOCK, SIDE, SIDE)
    packed = send(position, need, kq, near.reshape(ENTRIES, PIECE))
    packed, slots = lax.optimization_barrier((packed, slots))
    along = [packed[0]] + [
        lax.ppermute(packed[step], "z", [(i, (i + step) % NZ) for i in range(NZ)])
        for step in ORDER_Z
    ]
    own_lists = own_plan(position, slots, union)
    packed, notes = lax.optimization_barrier((route(along), along))
    far = lax.all_to_all(packed, ("x", "core"), split_axis=0, concat_axis=0, tiled=True)
    far_lists = far_plan(position, slots, union, notes)
    far = far.reshape(TARGETS * CAP_X, PIECE)
    own = own_sums(own_lists, whole)
    far, fits, own = lax.optimization_barrier((far, far_lists[9, 0] != 0, own))
    result = far_sums(own_lists, far_lists, whole, far, own)
    cuts = [result[0]]
    for step in ORDER_Y:
        pairs = [(i, (i + step) % NY) for i in range(NY)]
        cuts.append(lax.ppermute(result[step], "col", pairs))
    square = finish(position, cuts)
    return lax.cond(
        fits,
        lambda value, *_: value,
        lambda _, *inputs: dense(*inputs),
        square,
        blocks,
        nonzero,
        columns,
    )


def solution(mesh):
    fine = Mesh(mesh.devices.reshape(NX, NZ, NC, NY), ROW_AXES + ("col",))
    spec = P(ROW_AXES, "col", None, None)
    return jax.shard_map(
        shards,
        mesh=fine,
        in_specs=(spec, P(ROW_AXES, "col"), P()),
        out_specs=spec,
        check_vma=False,
    )
```

```python
import functools

import jax
import jax.numpy as jnp
from jax import lax
from jax.experimental import pallas as pl
from jax.experimental.pallas import tpu as pltpu
from jax.sharding import Mesh
from jax.sharding import PartitionSpec as P

BF = jnp.bfloat16
F32 = jnp.float32
I32 = jnp.int32

NX, NZ, NC, NY = 4, 8, 2, 4
ROWS, SLOTS, SIDE = 256, 28, 128
HEIGHT, QUARTER = 4, 7
SLABS = ROWS // HEIGHT
PEERS = NX * NC * NY
HELD = 32
ENTRIES = PEERS * HELD
PIECE = SIDE * SIDE // PEERS
WIDE = SIDE // NY
TARGETS = NX * NC
CAP_Z = 124
ROWS_Z = 128
CAP_X = 120
ORDER_Z = (4, 3, 5, 2, 6, 1, 7)
ORDER_Y = (2, 1, 3)
GROUP = 8
FAR_GROUP = 3
STEPS_AT_ONCE = 8
HEIGHT_2 = NC * HEIGHT
OUT_COLS = 72
ZERO_BLOCK = NY * HEIGHT * QUARTER
VMEM_LIMIT = 48 * 1024 * 1024
ROW_AXES = ("x", "z", "core")


def vmem():
    return pl.BlockSpec(memory_space=pltpu.VMEM)


def smem():
    return pl.BlockSpec(memory_space=pltpu.SMEM)


def params():
    return pltpu.CompilerParams(vmem_limit_bytes=VMEM_LIMIT)


def cost(flops, moved):
    return pl.CostEstimate(flops=flops, bytes_accessed=moved, transcendentals=0)


def prepare_kernel(position_ref, keep_ref, blocks_ref, cuts_ref, rows_ref):
    x, core, part = position_ref[0], position_ref[2], position_ref[3]
    lanes = iota((8, ENTRIES), 1) - ((part * NX + x) * NC + core) * HELD
    flags = jnp.zeros((8, ENTRIES), F32)
    for row in range(HEIGHT):
        for slot in range(QUARTER):
            number = row * QUARTER + slot
            keep = keep_ref[row, slot] != 0
            flags = jnp.where((lanes == number) & keep, 1.0, flags)
            block = blocks_ref[row, slot].astype(F32)
            rows_ref[number] = jnp.where(keep, block, jnp.zeros_like(block)).T
    for part_of in range(NY):
        for extra in range(HELD - SLOTS):
            at = extra * PIECE + part_of * SIDE
            value = flags[:, at : at + SIDE] if extra < 2 else jnp.zeros((8, SIDE), F32)
            for quarter in range(NY):
                begin = quarter * WIDE + part_of * TARGETS
                rows_ref[SLOTS + extra, begin : begin + TARGETS] = value
    for quarter in range(NY):
        peers = slice(quarter * TARGETS, (quarter + 1) * TARGETS)
        for part_of in range(NY):
            begin = quarter * WIDE + part_of * TARGETS
            for half in range(0, HELD, 16):
                rows = rows_ref[half : half + 16, begin : begin + TARGETS]
                cuts_ref[peers, half : half + 16, part_of * SIDE : (part_of + 1) * SIDE] = (
                    jnp.swapaxes(rows, 0, 1).astype(BF)
                )


def prepare(position, nonzero, blocks):
    return pl.pallas_call(
        prepare_kernel,
        out_shape=jax.ShapeDtypeStruct((PEERS, HELD, PIECE), BF),
        in_specs=[smem(), smem(), vmem()],
        out_specs=vmem(),
        scratch_shapes=[pltpu.VMEM((HELD, SIDE, SIDE), F32)],
        compiler_params=params(),
        name="prepare",
    )(position, nonzero, blocks)


def turn_kernel(keep_ref, blocks_ref, out_ref):
    for row in range(HEIGHT):
        for slot in range(QUARTER):
            block = blocks_ref[row, slot]
            out_ref[row, slot] = jnp.where(
                keep_ref[row, slot] != 0, block, jnp.zeros_like(block)
            ).T


def turn(nonzero, blocks):
    return pl.pallas_call(
        turn_kernel,
        out_shape=jax.ShapeDtypeStruct((HEIGHT, QUARTER, SIDE, SIDE), BF),
        in_specs=[smem(), vmem()],
        out_specs=vmem(),
        compiler_params=params(),
        cost_estimate=cost(2 * SLOTS * SIDE**3, 4 * SLOTS * SIDE**2),
        name="turn",
    )(nonzero, blocks)


def own_block(whole_ref, place, rows):
    value = whole_ref[jnp.minimum(place, ZERO_BLOCK - 1), rows, :]
    return jnp.where(place < ZERO_BLOCK, value, jnp.zeros_like(value))


def out_place(place):
    return (place // QUARTER) % HEIGHT, place // (QUARTER * HEIGHT) * QUARTER + place % QUARTER


def own_kernel(
    plan_ref,
    whole_ref,
    out_ref,
    total,
    panel,
    near,
):
    first = pl.multiple_of(plan_ref[15, 0] * WIDE, WIDE)
    for inner in range(HEIGHT):
        for member in range(HEIGHT):
            panel[pl.ds(inner * SIDE, SIDE), pl.ds(member * SIDE, SIDE)] = own_block(
                whole_ref, plan_ref[9 + member, inner], pl.ds(0, SIDE)
            )

    def step(group, carry):
        for at in range(GROUP):
            for inner in range(HEIGHT):
                near[pl.ds(at * WIDE, WIDE), pl.ds(inner * SIDE, SIDE)] = own_block(
                    whole_ref, plan_ref[4 + inner, group * GROUP + at], pl.ds(first, WIDE)
                )
        value = jnp.dot(near[...], panel[...], preferred_element_type=F32)
        total[pl.ds(group * GROUP, GROUP)] = value.reshape(GROUP, WIDE, HEIGHT * SIDE)
        return carry

    lax.fori_loop(0, plan_ref[15, 1], step, 0)
    for place in range(ZERO_BLOCK):
        member, slot = out_place(place)
        column = plan_ref[8, member * (128 // HEIGHT) + slot]
        out_ref[place] = total[column, :, pl.ds(member * SIDE, SIDE)]


def own_sums(lists, whole):
    flops = 2 * 32 * WIDE * (HEIGHT * SIDE) ** 2
    return pl.pallas_call(
        own_kernel,
        out_shape=jax.ShapeDtypeStruct((ZERO_BLOCK, WIDE, SIDE), F32),
        in_specs=[smem(), vmem()],
        out_specs=vmem(),
        scratch_shapes=[
            pltpu.VMEM((OUT_COLS, WIDE, HEIGHT * SIDE), F32),
            pltpu.VMEM((HEIGHT * SIDE, HEIGHT * SIDE), BF),
            pltpu.VMEM((GROUP * WIDE, HEIGHT * SIDE), BF),
        ],
        compiler_params=params(),
        cost_estimate=cost(flops, 3 * ZERO_BLOCK * SIDE * SIDE),
        name="own_sums",
    )(lists, whole)


def far_kernel(
    own_ref,
    plan_ref,
    whole_ref,
    far_ref,
    near_ref,
    *refs,
):
    *out_refs, low, high, pieces_ref = refs
    halves = (low, high)
    for sender in range(TARGETS):
        rows = pl.ds(sender * CAP_X, CAP_X)
        for part in range(NY):
            lanes = slice(part * SIDE, (part + 1) * SIDE)
            pieces_ref[part, rows, :] = far_ref[rows, lanes].astype(F32)

    def clear(group, carry):
        for total in halves:
            total[pl.ds(group * GROUP, GROUP)] = jnp.zeros((GROUP, WIDE, 2 * SIDE), F32)
        return carry

    lax.fori_loop(0, own_ref[15, 1], clear, 0)

    def add_product(step):
        begin = plan_ref[2, step]
        length = plan_ref[3, step]
        pieces, columns = [], []
        for at in range(FAR_GROUP):
            place = jnp.minimum(begin + at, CAP_X - 1)
            rows = pl.ds(plan_ref[0, place], TARGETS, stride=CAP_X)
            for part in range(NY):
                pieces.append(pieces_ref[part, rows, :])
            columns.append(jnp.where(at < length, plan_ref[1, place], OUT_COLS))
        left = jnp.concatenate(pieces, axis=0).astype(BF)
        for half, total in enumerate(halves):
            right = jnp.concatenate(
                [
                    own_block(whole_ref, plan_ref[4 + 2 * half + at, step], pl.ds(0, SIDE))
                    for at in range(2)
                ],
                axis=1,
            )
            value = jnp.dot(left, right, preferred_element_type=F32)
            before = [total[column] for column in columns]
            for at, column in enumerate(columns):
                total[column] = before[at] + value[at * WIDE : (at + 1) * WIDE]

    def steps(number, carry):
        for at in range(STEPS_AT_ONCE):
            add_product(number * STEPS_AT_ONCE + at)
        return carry

    lax.fori_loop(0, (plan_ref[8, 0] + STEPS_AT_ONCE - 1) // STEPS_AT_ONCE, steps, 0)

    for step, out_ref in enumerate(out_refs):
        part = (own_ref[15, 0] + step) & (NY - 1)
        for place in range(HEIGHT * QUARTER):
            member, slot = place // QUARTER, part * QUARTER + place % QUARTER
            column = own_ref[8, member * (128 // HEIGHT) + slot]
            value = halves[member // 2][column, :, pl.ds(member % 2 * SIDE, SIDE)]
            value = value + near_ref[part * (HEIGHT * QUARTER) + place]
            out_ref[place] = value.astype(BF)


def far_sums(own_lists, far_lists, whole, far, near):
    return pl.pallas_call(
        far_kernel,
        out_shape=[jax.ShapeDtypeStruct((HEIGHT * QUARTER, WIDE, SIDE), BF)] * NY,
        in_specs=[smem(), smem(), vmem(), vmem(), vmem()],
        out_specs=[vmem()] * NY,
        scratch_shapes=[
            pltpu.VMEM((OUT_COLS + 1, WIDE, 2 * SIDE), F32),
            pltpu.VMEM((OUT_COLS + 1, WIDE, 2 * SIDE), F32),
            pltpu.VMEM((NY, TARGETS * CAP_X, SIDE), F32),
        ],
        compiler_params=params(),
        name="far_sums",
    )(own_lists, far_lists, whole, far, near)


def finish_kernel(position_ref, *refs):
    *cut_refs, out_ref = refs
    at = dict(zip((0,) + ORDER_Y, cut_refs))
    for part in range(NY):

        @pl.when(position_ref[3] == part)
        def _():
            order = [at[(part - sender) % NY] for sender in range(NY)]
            for row in range(HEIGHT):
                for slot in range(QUARTER):
                    cuts = [ref[row * QUARTER + slot] for ref in order]
                    out_ref[row, slot] = jnp.concatenate(cuts, axis=0).T


def finish(position, cuts):
    return pl.pallas_call(
        finish_kernel,
        out_shape=jax.ShapeDtypeStruct((HEIGHT, QUARTER, SIDE, SIDE), BF),
        in_specs=[smem()] + [vmem()] * NY,
        out_specs=vmem(),
        compiler_params=params(),
        name="finish",
    )(position, *cuts)


def iota(shape, axis):
    return lax.broadcasted_iota(I32, shape, axis)


def dot(a, b):
    return jnp.dot(a.astype(BF), b.astype(BF), preferred_element_type=F32)


def dot_rows(a, b):
    return lax.dot_general(
        a.astype(BF), b.astype(BF), (((1,), (1,)), ((), ())), preferred_element_type=F32
    )


def earlier(size):
    return (iota((size, size), 0) < iota((size, size), 1)).astype(F32)


def places(need):
    order = earlier(SIDE)
    parts = []
    before = jnp.zeros((need.shape[0], 1), F32)
    for begin in range(0, need.shape[1], SIDE):
        part = need[:, begin : begin + SIDE]
        parts.append(dot(part, order) + before)
        before = before + jnp.sum(part, axis=1, keepdims=True)
    return jnp.concatenate(parts, axis=1)


def codes(need, capacity):
    place = places(need)
    return jnp.where((need > 0) & (place < capacity), place, -1.0)


def one_hot(code, rows):
    number = iota((rows, code.shape[1]), 0).astype(F32).astype(BF)
    return jnp.where(number == code.astype(BF), jnp.ones((), BF), jnp.zeros((), BF))


def quarter_of(slot):
    return sum((slot >= bound * QUARTER).astype(I32) for bound in range(1, NY))


def pattern_kernel(position_ref, columns_ref, entries_ref, slots_ref, union_ref, need_ref, kq_ref):
    step = 64
    for begin in range(0, ROWS, step):
        column = iota((step, ROWS), 1)
        found = jnp.full((step, ROWS), -1, I32)
        for slot in range(SLOTS):
            at = columns_ref[begin : begin + step, slot : slot + 1]
            found = jnp.where(at == column, slot, found)
        slots_ref[begin : begin + step, :] = found
    names = (slots_ref[...] >= 0).astype(F32)
    mine = iota((128, ROWS), 1) // HEIGHT == iota((128, ROWS), 0)
    union = (dot(mine.astype(F32), names) > 0).astype(F32)
    union_ref[...] = union

    entry = iota((1, ENTRIES), 1)
    peer, number = entry // HELD, entry % HELD
    x, core = (peer // NC) % NX, peer % NC
    row = ((x * NZ + position_ref[1]) * NC + core) * HEIGHT + quarter_of(number)
    column = entries_ref[...]
    every = iota((ROWS, ENTRIES), 0)
    named = dot(jnp.where(mine, 0.0, union), (every == row).astype(F32))
    need_ref[...] = named * dot(union, (every == column).astype(F32))
    kind = iota((8, ENTRIES), 0)
    both = jnp.where(kind == 1, jnp.maximum(column, 0), 0)
    kq_ref[...] = jnp.where(kind == 0, row, both).astype(F32)


def pattern(position, columns, entries):
    return pl.pallas_call(
        pattern_kernel,
        out_shape=(
            jax.ShapeDtypeStruct((ROWS, ROWS), I32),
            jax.ShapeDtypeStruct((128, ROWS), F32),
            jax.ShapeDtypeStruct((128, ENTRIES), F32),
            jax.ShapeDtypeStruct((8, ENTRIES), F32),
        ),
        in_specs=[smem(), vmem(), vmem()],
        out_specs=(vmem(), vmem(), vmem(), vmem()),
        compiler_params=params(),
        cost_estimate=cost(2 * SLOTS * ROWS**3 // 4, 8 * ROWS**2),
        name="pattern",
    )(position, columns, entries)


def send_kernel(position_ref, need_ref, kq_ref, near_ref, *refs):
    *out_refs, chosen_ref = refs
    z = position_ref[1]
    near = near_ref[...]
    kind = iota((8, ENTRIES), 0)
    pick = (iota((8, ENTRIES), 1) % HELD == SLOTS + kind) & (kind < 2)
    flags = dot(pick.astype(F32), near)
    flags = jnp.concatenate([flags[0:1], flags[1:2]], axis=1)
    need = need_ref[...] * flags
    slab = iota((8, 128), 1)
    plane = (slab // NC) % NZ == (iota((8, 128), 0) + z) & (NZ - 1)
    wanted = (dot(plane.astype(F32), need) > 0).astype(F32)
    code = codes(wanted, CAP_Z)
    most = jnp.max(jnp.sum(wanted, axis=1, keepdims=True), axis=0, keepdims=True)
    most = jnp.broadcast_to(jnp.minimum(most, 250.0), (1, 128))
    totals = jnp.minimum(dot_rows(jnp.ones((8, ENTRIES), F32), need)[0:1], 250.0)
    for to in range(NZ):
        chosen_ref[to * ROWS_Z : (to + 1) * ROWS_Z, :] = one_hot(code[to : to + 1], ROWS_Z)
    packed = jnp.dot(chosen_ref[...], near, preferred_element_type=F32)
    kq = kq_ref[...]
    line = iota((128, ENTRIES), 0)
    facts = jnp.where(line == SLABS, kq[0:1], jnp.where(line == SLABS + 1, kq[1:2], need))
    facts = jnp.dot(chosen_ref[...], facts.T.astype(BF), preferred_element_type=F32)
    tail = iota((16, PIECE), 0)
    slab = iota((16, 128), 1)
    target = iota((16, 128), 0)
    for to in range(NZ):
        choice = (target // NC * NZ + ((z + to) & (NZ - 1))) * NC + target % NC
        choice = slab == jnp.where(target < TARGETS, choice, SLABS - TARGETS + target)
        notes = dot_rows(choice, facts[to * ROWS_Z : (to + 1) * ROWS_Z])
        first = jnp.concatenate([notes[i : i + 1] for i in range(4)], axis=1)
        second = jnp.concatenate([notes[i : i + 1] for i in range(4, 8)], axis=1)
        third = jnp.concatenate([notes[8:9], notes[9:10], totals, most], axis=1)
        begin = to * ROWS_Z
        out_refs[to][0 : ROWS_Z - 16] = packed[begin : begin + ROWS_Z - 16].astype(BF)
        value = packed[begin + ROWS_Z - 16 : begin + ROWS_Z]
        value = jnp.where(tail == 12, first, value)
        value = jnp.where(tail == 13, second, value)
        value = jnp.where(tail == 14, third, value)
        out_refs[to][ROWS_Z - 16 : ROWS_Z] = value.astype(BF)


def send(position, need, kq, near):
    return pl.pallas_call(
        send_kernel,
        out_shape=[jax.ShapeDtypeStruct((ROWS_Z, PIECE), BF)] * NZ,
        in_specs=[smem()] + [vmem()] * 3,
        out_specs=[vmem()] * NZ,
        scratch_shapes=[pltpu.VMEM((NZ * ROWS_Z, ENTRIES), BF)],
        compiler_params=params(),
        name="send",
    )(position, need, kq, near)


def notes_of(along_refs):
    asked, third = [], []
    for along_ref in along_refs:
        notes = along_ref[ROWS_Z - 16 : ROWS_Z].astype(F32)
        asked.append(
            jnp.concatenate(
                [
                    notes[12 + i // 4 : 13 + i // 4, i % 4 * SIDE : (i % 4 + 1) * SIDE]
                    for i in range(TARGETS)
                ],
                axis=0,
            )
        )
        third.append(notes[14:15])
    return jnp.concatenate(asked, axis=1), third


def route_kernel(*refs):
    *along_refs, out_ref, chosen_ref, along_ref = refs
    asked, _ = notes_of(along_refs)
    for number, ref in enumerate(along_refs):
        along_ref[number * ROWS_Z : (number + 1) * ROWS_Z] = ref[...]
    code = codes(asked, CAP_X)
    for to in range(TARGETS):
        chosen_ref[to * SIDE : (to + 1) * SIDE, :] = one_hot(code[to : to + 1], SIDE)
    packed = jnp.dot(chosen_ref[...], along_ref[...], preferred_element_type=F32)
    for to in range(TARGETS):
        out_ref[to] = packed[to * SIDE : to * SIDE + CAP_X].astype(BF)


def route(along):
    return pl.pallas_call(
        route_kernel,
        out_shape=jax.ShapeDtypeStruct((TARGETS, CAP_X, PIECE), BF),
        in_specs=[vmem()] * NZ,
        out_specs=vmem(),
        scratch_shapes=[
            pltpu.VMEM((TARGETS * SIDE, NZ * ROWS_Z), BF),
            pltpu.VMEM((NZ * ROWS_Z, PIECE), BF),
        ],
        compiler_params=params(),
        name="route",
    )(*along)


def own_places(position_ref, slots_ref):
    chip = position_ref[0] * NZ + position_ref[1]
    both = slots_ref[pl.ds(pl.multiple_of(chip * HEIGHT_2, HEIGHT_2), HEIGHT_2), :]
    swapped = jnp.concatenate([both[HEIGHT:], both[:HEIGHT]], axis=0)
    slot = jnp.where(position_ref[2] == 0, both, swapped)
    quarter = quarter_of(slot)
    held = (quarter * HEIGHT + iota(slot.shape, 0)) * QUARTER + slot - quarter * QUARTER
    return slot, jnp.where(slot >= 0, held - ZERO_BLOCK, 0).astype(F32)


def own_plan_kernel(position_ref, slots_ref, union_ref, out_ref):
    x, z, core, part = (position_ref[i] for i in range(4))
    slab = (x * NZ + z) * NC + core
    order = earlier(ROWS)
    out_ref[...] = jnp.zeros_like(out_ref)
    mine = union_ref[pl.ds(slab, 1), :]
    rank = dot(jnp.broadcast_to(mine, (8, ROWS)), order)

    slot, held = own_places(position_ref, slots_ref)
    number = iota((OUT_COLS, ROWS), 0).astype(F32)
    chosen = ((rank[0:1] == number) & (mine > 0)).astype(F32)
    out_ref[4:8, 0:OUT_COLS] = dot_rows(held, chosen)[0:HEIGHT].astype(I32) + ZERO_BLOCK
    wide = 128 // HEIGHT
    chosen = jnp.concatenate(
        [slot[i : i + 1] == iota((wide, ROWS), 0) for i in range(HEIGHT)], axis=0
    )
    out_ref[8:9, 0:128] = dot_rows(rank, chosen.astype(F32))[0:1].astype(I32)
    chosen = (iota((8, ROWS), 1) == iota((8, ROWS), 0) + slab * HEIGHT).astype(F32)
    out_ref[9:13, 0:8] = dot_rows(held, chosen)[0:HEIGHT].astype(I32) + ZERO_BLOCK
    groups = ((jnp.sum(mine) + (GROUP - 1)) * (1.0 / GROUP)).astype(I32)
    lane = iota((1, 128), 1)
    scalars = jnp.where(lane == 0, part, 0)
    out_ref[15:16, :] = jnp.where(lane == 1, groups, scalars)


def own_plan(position, slots, union):
    return pl.pallas_call(
        own_plan_kernel,
        out_shape=jax.ShapeDtypeStruct((16, 128), I32),
        in_specs=[smem(), vmem(), vmem()],
        out_specs=vmem(),
        compiler_params=params(),
        cost_estimate=cost(ROWS**3, 4 * ROWS**2),
        name="own_plan",
    )(position, slots, union)


def far_plan_kernel(position_ref, slots_ref, union_ref, *refs):
    *along_refs, out_ref = refs
    x, z, core = (position_ref[i] for i in range(3))
    slab = (x * NZ + z) * NC + core
    out_ref[...] = jnp.zeros_like(out_ref)
    asked, third = notes_of(along_refs)
    mine = iota(asked.shape, 0) == x * NC + core
    asked = jnp.sum(jnp.where(mine, asked, 0.0), axis=0, keepdims=True)
    number = jnp.sum(asked).astype(I32)
    code = codes(jnp.broadcast_to(asked, (8, asked.shape[1])), CAP_X)[0:1]
    chosen = one_hot(code, SIDE).astype(F32)
    row = jnp.concatenate([part[:, :SIDE] for part in third], axis=1)
    column = jnp.concatenate([part[:, SIDE : 2 * SIDE] for part in third], axis=1)
    row_down = jnp.sum(chosen * row, axis=1, keepdims=True).astype(I32)
    column_down = jnp.sum(chosen * column, axis=1, keepdims=True).astype(I32)
    row_along = dot_rows(jnp.broadcast_to(row, (8, row.shape[1])), chosen)[0:1].astype(I32)

    down, along = iota((SIDE, SIDE), 0), iota((SIDE, SIDE), 1)
    less = (row_down < row_along) | ((row_down == row_along) & (down < along))
    order = jnp.sum((less & (down < number)).astype(F32), axis=0, keepdims=True)
    ordered = ((order == down.astype(F32)) & (along < number)).astype(F32)
    position = iota((8, SIDE), 1).astype(F32)
    out_ref[0:1, 0:SIDE] = dot_rows(position, ordered)[0:1].astype(I32)
    names = union_ref[pl.ds(slab, 1), :]
    order = earlier(ROWS)
    rank = dot(jnp.broadcast_to(names, (8, ROWS)), order)
    every = iota((SIDE, ROWS), 1)
    rank = dot_rows(rank, (every == column_down).astype(F32))
    out_ref[1:2, 0:SIDE] = dot_rows(rank, ordered)[0:1].astype(I32)

    valid = iota((SIDE, ROWS), 0) < number
    count = dot(jnp.ones((8, SIDE), F32), ((every == row_down) & valid).astype(F32))
    start = jnp.minimum(dot(count, order), 250.0)[0:1]
    _, held = own_places(position_ref, slots_ref)
    needed = ((count + (FAR_GROUP - 1)) * (1.0 / FAR_GROUP)).astype(I32).astype(F32)
    first = dot(needed, order)[0:1]
    number = iota((SIDE, ROWS), 0).astype(F32)
    chosen = ((first <= number) & (number < first + needed[0:1])).astype(F32)
    kind = iota((8, ROWS), 0)
    values = jnp.where(kind == 0, start, jnp.where(kind == 1, first, count))
    values = dot_rows(values, chosen).astype(I32)
    done = (iota((1, SIDE), 1) - values[1:2]) * FAR_GROUP
    steps = jnp.sum(needed[0:1]).astype(I32)
    valid = iota((1, SIDE), 1) < steps
    out_ref[2:3, :] = jnp.where(valid, values[0:1] + done, 0)
    out_ref[3:4, :] = jnp.where(valid, values[2:3] - done, 0)
    out_ref[4:8, :] = dot_rows(held, chosen)[0:HEIGHT].astype(I32) + ZERO_BLOCK
    out_ref[8:9, :] = jnp.zeros((1, SIDE), I32) + jnp.minimum(steps, SIDE)

    third = functools.reduce(jnp.maximum, third), functools.reduce(jnp.add, third)
    most_z = jnp.max(third[0][:, 3 * SIDE :])
    most_x = jnp.max(third[1][:, 2 * SIDE : 3 * SIDE])
    fits = (most_x <= CAP_X) & (most_z <= CAP_Z)
    out_ref[9:10, :] = jnp.zeros((1, SIDE), I32) + fits.astype(I32)


def far_plan(position, slots, union, along):
    return pl.pallas_call(
        far_plan_kernel,
        out_shape=jax.ShapeDtypeStruct((16, 128), I32),
        in_specs=[smem()] + [vmem()] * (2 + NZ),
        out_specs=vmem(),
        compiler_params=params(),
        cost_estimate=cost(2 * 20 * ROWS**3, 8 * ROWS**2),
        name="far_plan",
    )(position, slots, union, *along)


def dense(blocks, nonzero, columns):
    slab = lax.axis_index(ROW_AXES)
    part = lax.axis_index("col")
    masked = blocks * nonzero[:, :, None, None].astype(BF)
    slab_ids = jnp.arange(SLABS, dtype=I32)
    local_rows = jnp.arange(HEIGHT, dtype=I32)
    grouped = columns.reshape(SLABS, HEIGHT * SLOTS)
    targets = slab * HEIGHT + local_rows
    wanted = jnp.any(grouped[:, :, None] == targets[None, None, :], axis=1)
    wanted = wanted & (slab_ids != slab)[:, None]
    picked = jnp.sum(jnp.where(wanted, local_rows, 0), axis=1)
    filled = jnp.any(wanted, axis=1)
    outgoing = jnp.where(filled[:, None, None, None], masked[picked], jnp.zeros((), BF))
    incoming = lax.all_to_all(outgoing, ROW_AXES, split_axis=0, concat_axis=0, tiled=True)
    row_table = jnp.concatenate([incoming, masked], axis=0)
    own_cols = lax.dynamic_slice_in_dim(columns, slab * HEIGHT, HEIGHT, 0)
    source = own_cols // HEIGHT
    row_index = jnp.where(source == slab, SLABS + own_cols % HEIGHT, source)
    far_cols = columns[own_cols]
    far_quarter = lax.dynamic_slice_in_dim(far_cols, part * QUARTER, QUARTER, 2)
    whole = lax.all_gather(masked, "col", axis=1, tiled=True)
    results = []
    for member in range(HEIGHT):
        match = far_quarter[member][:, :, None] == own_cols[member][None, None, :]
        products = jnp.einsum(
            "tab,tubc->tuac", whole[member], row_table[row_index[member]],
            preferred_element_type=F32,
        )
        summed = lax.dot_general(
            match.astype(F32).reshape(SLOTS * QUARTER, SLOTS),
            products.reshape(SLOTS * QUARTER, SIDE * SIDE),
            (((0,), (0,)), ((), ())),
            precision=lax.Precision.HIGHEST,
            preferred_element_type=F32,
        )
        results.append(summed.reshape(SLOTS, SIDE, SIDE))
    square = lax.psum_scatter(jnp.stack(results), "col", scatter_dimension=1, tiled=True)
    return square.astype(BF)


def plane_columns(columns):
    split = columns.reshape(NX, NZ, NC, HEIGHT, NY, QUARTER)
    mine = lax.dynamic_index_in_dim(split, lax.axis_index("z"), 1, keepdims=False)
    mine = mine.transpose(3, 0, 1, 2, 4).reshape(PEERS, SLOTS)
    return jnp.pad(mine, ((0, 0), (0, HELD - SLOTS)), constant_values=-1).reshape(1, ENTRIES)


def shards(blocks, nonzero, columns):
    position = jnp.stack([lax.axis_index(name) for name in ROW_AXES + ("col",)])
    cuts = prepare(position, nonzero, blocks)
    cuts, names, same = lax.optimization_barrier((cuts, columns, blocks))
    turned = turn(nonzero, same)
    slots, union, need, kq = pattern(position, names, plane_columns(columns))
    near = lax.all_to_all(cuts, ("col", "x", "core"), split_axis=0, concat_axis=0, tiled=True)
    near, turned, need = lax.optimization_barrier((near, turned, need))
    whole = lax.all_gather(turned, "col", axis=0, tiled=False)
    whole = whole.reshape(ZERO_BLOCK, SIDE, SIDE)
    packed = send(position, need, kq, near.reshape(ENTRIES, PIECE))
    packed, slots = lax.optimization_barrier((packed, slots))
    along = [packed[0]] + [
        lax.ppermute(packed[step], "z", [(i, (i + step) % NZ) for i in range(NZ)])
        for step in ORDER_Z
    ]
    own_lists = own_plan(position, slots, union)
    packed, notes = lax.optimization_barrier((route(along), along))
    far = lax.all_to_all(packed, ("x", "core"), split_axis=0, concat_axis=0, tiled=True)
    far_lists = far_plan(position, slots, union, notes)
    far = far.reshape(TARGETS * CAP_X, PIECE)
    own = own_sums(own_lists, whole)
    far, fits, own = lax.optimization_barrier((far, far_lists[9, 0] != 0, own))
    result = far_sums(own_lists, far_lists, whole, far, own)
    cuts = [result[0]]
    for step in ORDER_Y:
        pairs = [(i, (i + step) % NY) for i in range(NY)]
        cuts.append(lax.ppermute(result[step], "col", pairs))
    square = finish(position, cuts)
    return lax.cond(
        fits,
        lambda value, *_: value,
        lambda _, *inputs: dense(*inputs),
        square,
        blocks,
        nonzero,
        columns,
    )


def solution(mesh):
    fine = Mesh(mesh.devices.reshape(NX, NZ, NC, NY), ROW_AXES + ("col",))
    spec = P(ROW_AXES, "col", None, None)
    return jax.shard_map(
        shards,
        mesh=fine,
        in_specs=(spec, P(ROW_AXES, "col"), P()),
        out_specs=spec,
        check_vma=False,
    )
```

```python
import functools

import jax
import jax.numpy as jnp
from jax import lax
from jax.experimental import pallas as pl
from jax.experimental.pallas import tpu as pltpu
from jax.sharding import Mesh
from jax.sharding import PartitionSpec as P

BF = jnp.bfloat16
F32 = jnp.float32
I32 = jnp.int32

NX, NZ, NC, NY = 4, 8, 2, 4
ROWS, SLOTS, SIDE = 256, 28, 128
HEIGHT, QUARTER = 4, 7
SLABS = ROWS // HEIGHT
PEERS = NX * NC * NY
HELD = 32
ENTRIES = PEERS * HELD
PIECE = SIDE * SIDE // PEERS
WIDE = SIDE // NY
TARGETS = NX * NC
CAP_Z = 124
ROWS_Z = 128
CAP_X = 120
ORDER_Z = (4, 3, 5, 2, 6, 1, 7)
ORDER_Y = (2, 1, 3)
ORDER_X = ((2, 0), (2, 1), (1, 0), (3, 0), (1, 1), (3, 1), (0, 1))
GROUP = 8
FAR_GROUP = 3
STEPS_AT_ONCE = 8
HEIGHT_2 = NC * HEIGHT
OUT_COLS = 72
ZERO_BLOCK = NY * HEIGHT * QUARTER
VMEM_LIMIT = 48 * 1024 * 1024
ROW_AXES = ("x", "z", "core")


def vmem():
    return pl.BlockSpec(memory_space=pltpu.VMEM)


def smem():
    return pl.BlockSpec(memory_space=pltpu.SMEM)


def params():
    return pltpu.CompilerParams(vmem_limit_bytes=VMEM_LIMIT)


def cost(flops, moved):
    return pl.CostEstimate(flops=flops, bytes_accessed=moved, transcendentals=0)


def prepare_kernel(position_ref, keep_ref, blocks_ref, cuts_ref, rows_ref):
    x, core, part = position_ref[0], position_ref[2], position_ref[3]
    lanes = iota((8, ENTRIES), 1) - ((part * NX + x) * NC + core) * HELD
    flags = jnp.zeros((8, ENTRIES), F32)
    for row in range(HEIGHT):
        for slot in range(QUARTER):
            number = row * QUARTER + slot
            keep = keep_ref[row, slot] != 0
            flags = jnp.where((lanes == number) & keep, 1.0, flags)
            block = blocks_ref[row, slot].astype(F32)
            rows_ref[number] = jnp.where(keep, block, jnp.zeros_like(block)).T
    for part_of in range(NY):
        for extra in range(HELD - SLOTS):
            at = extra * PIECE + part_of * SIDE
            value = flags[:, at : at + SIDE] if extra < 2 else jnp.zeros((8, SIDE), F32)
            for quarter in range(NY):
                begin = quarter * WIDE + part_of * TARGETS
                rows_ref[SLOTS + extra, begin : begin + TARGETS] = value
    for quarter in range(NY):
        peers = slice(quarter * TARGETS, (quarter + 1) * TARGETS)
        for part_of in range(NY):
            begin = quarter * WIDE + part_of * TARGETS
            for half in range(0, HELD, 16):
                rows = rows_ref[half : half + 16, begin : begin + TARGETS]
                cuts_ref[peers, half : half + 16, part_of * SIDE : (part_of + 1) * SIDE] = (
                    jnp.swapaxes(rows, 0, 1).astype(BF)
                )


def prepare(position, nonzero, blocks):
    return pl.pallas_call(
        prepare_kernel,
        out_shape=jax.ShapeDtypeStruct((PEERS, HELD, PIECE), BF),
        in_specs=[smem(), smem(), vmem()],
        out_specs=vmem(),
        scratch_shapes=[pltpu.VMEM((HELD, SIDE, SIDE), F32)],
        compiler_params=params(),
        name="prepare",
    )(position, nonzero, blocks)


def turn_kernel(keep_ref, blocks_ref, out_ref):
    for row in range(HEIGHT):
        for slot in range(QUARTER):
            block = blocks_ref[row, slot]
            out_ref[row, slot] = jnp.where(
                keep_ref[row, slot] != 0, block, jnp.zeros_like(block)
            ).T


def turn(nonzero, blocks):
    return pl.pallas_call(
        turn_kernel,
        out_shape=jax.ShapeDtypeStruct((HEIGHT, QUARTER, SIDE, SIDE), BF),
        in_specs=[smem(), vmem()],
        out_specs=vmem(),
        compiler_params=params(),
        cost_estimate=cost(2 * SLOTS * SIDE**3, 4 * SLOTS * SIDE**2),
        name="turn",
    )(nonzero, blocks)


def own_block(whole_ref, place, rows):
    value = whole_ref[jnp.minimum(place, ZERO_BLOCK - 1), rows, :]
    return jnp.where(place < ZERO_BLOCK, value, jnp.zeros_like(value))


def out_place(place):
    return (place // QUARTER) % HEIGHT, place // (QUARTER * HEIGHT) * QUARTER + place % QUARTER


def own_kernel(
    plan_ref,
    whole_ref,
    out_ref,
    total,
    panel,
    near,
):
    first = pl.multiple_of(plan_ref[15, 0] * WIDE, WIDE)
    for inner in range(HEIGHT):
        for member in range(HEIGHT):
            panel[pl.ds(inner * SIDE, SIDE), pl.ds(member * SIDE, SIDE)] = own_block(
                whole_ref, plan_ref[9 + member, inner], pl.ds(0, SIDE)
            )

    def step(group, carry):
        for at in range(GROUP):
            for inner in range(HEIGHT):
                near[pl.ds(at * WIDE, WIDE), pl.ds(inner * SIDE, SIDE)] = own_block(
                    whole_ref, plan_ref[4 + inner, group * GROUP + at], pl.ds(first, WIDE)
                )
        value = jnp.dot(near[...], panel[...], preferred_element_type=F32)
        total[pl.ds(group * GROUP, GROUP)] = value.reshape(GROUP, WIDE, HEIGHT * SIDE)
        return carry

    lax.fori_loop(0, plan_ref[15, 1], step, 0)
    for place in range(ZERO_BLOCK):
        member, slot = out_place(place)
        column = plan_ref[8, member * (128 // HEIGHT) + slot]
        out_ref[place] = total[column, :, pl.ds(member * SIDE, SIDE)]


def own_sums(lists, whole):
    flops = 2 * 32 * WIDE * (HEIGHT * SIDE) ** 2
    return pl.pallas_call(
        own_kernel,
        out_shape=jax.ShapeDtypeStruct((ZERO_BLOCK, WIDE, SIDE), F32),
        in_specs=[smem(), vmem()],
        out_specs=vmem(),
        scratch_shapes=[
            pltpu.VMEM((OUT_COLS, WIDE, HEIGHT * SIDE), F32),
            pltpu.VMEM((HEIGHT * SIDE, HEIGHT * SIDE), BF),
            pltpu.VMEM((GROUP * WIDE, HEIGHT * SIDE), BF),
        ],
        compiler_params=params(),
        cost_estimate=cost(flops, 3 * ZERO_BLOCK * SIDE * SIDE),
        name="own_sums",
    )(lists, whole)


def far_kernel(
    own_ref,
    plan_ref,
    whole_ref,
    near_ref,
    position_ref,
    *refs,
):
    *out_refs, low, high, pieces_ref = refs[TARGETS:]
    halves = (low, high)
    for (along_x, across), far_ref in zip(((0, 0),) + ORDER_X, refs):
        sender = ((position_ref[0] - along_x) & (NX - 1)) * NC + ((position_ref[2] + across) & 1)
        rows = pl.ds(pl.multiple_of(sender * CAP_X, 8), CAP_X)
        for part in range(NY):
            lanes = slice(part * SIDE, (part + 1) * SIDE)
            pieces_ref[part, rows, :] = far_ref[:, lanes].astype(F32)

    def clear(group, carry):
        for total in halves:
            total[pl.ds(group * GROUP, GROUP)] = jnp.zeros((GROUP, WIDE, 2 * SIDE), F32)
        return carry

    lax.fori_loop(0, own_ref[15, 1], clear, 0)

    def add_product(step):
        begin = plan_ref[2, step]
        length = plan_ref[3, step]
        pieces, columns = [], []
        for at in range(FAR_GROUP):
            place = jnp.minimum(begin + at, CAP_X - 1)
            rows = pl.ds(plan_ref[0, place], TARGETS, stride=CAP_X)
            for part in range(NY):
                pieces.append(pieces_ref[part, rows, :])
            columns.append(jnp.where(at < length, plan_ref[1, place], OUT_COLS))
        left = jnp.concatenate(pieces, axis=0).astype(BF)
        for half, total in enumerate(halves):
            right = jnp.concatenate(
                [
                    own_block(whole_ref, plan_ref[4 + 2 * half + at, step], pl.ds(0, SIDE))
                    for at in range(2)
                ],
                axis=1,
            )
            value = jnp.dot(left, right, preferred_element_type=F32)
            before = [total[column] for column in columns]
            for at, column in enumerate(columns):
                total[column] = before[at] + value[at * WIDE : (at + 1) * WIDE]

    def steps(number, carry):
        for at in range(STEPS_AT_ONCE):
            add_product(number * STEPS_AT_ONCE + at)
        return carry

    lax.fori_loop(0, (plan_ref[8, 0] + STEPS_AT_ONCE - 1) // STEPS_AT_ONCE, steps, 0)

    for step, out_ref in enumerate(out_refs):
        part = (own_ref[15, 0] + step) & (NY - 1)
        for place in range(HEIGHT * QUARTER):
            member, slot = place // QUARTER, part * QUARTER + place % QUARTER
            column = own_ref[8, member * (128 // HEIGHT) + slot]
            value = halves[member // 2][column, :, pl.ds(member % 2 * SIDE, SIDE)]
            value = value + near_ref[part * (HEIGHT * QUARTER) + place]
            out_ref[place] = value.astype(BF)


def far_sums(own_lists, far_lists, whole, near, position, far):
    return pl.pallas_call(
        far_kernel,
        out_shape=[jax.ShapeDtypeStruct((HEIGHT * QUARTER, WIDE, SIDE), BF)] * NY,
        in_specs=[smem(), smem(), vmem(), vmem(), smem()] + [vmem()] * TARGETS,
        out_specs=[vmem()] * NY,
        scratch_shapes=[
            pltpu.VMEM((OUT_COLS + 1, WIDE, 2 * SIDE), F32),
            pltpu.VMEM((OUT_COLS + 1, WIDE, 2 * SIDE), F32),
            pltpu.VMEM((NY, TARGETS * CAP_X, SIDE), F32),
        ],
        compiler_params=params(),
        name="far_sums",
    )(own_lists, far_lists, whole, near, position, *far)


def finish_kernel(position_ref, *refs):
    *cut_refs, out_ref = refs
    at = dict(zip((0,) + ORDER_Y, cut_refs))
    for part in range(NY):

        @pl.when(position_ref[3] == part)
        def _():
            order = [at[(part - sender) % NY] for sender in range(NY)]
            for row in range(HEIGHT):
                for slot in range(QUARTER):
                    cuts = [ref[row * QUARTER + slot] for ref in order]
                    out_ref[row, slot] = jnp.concatenate(cuts, axis=0).T


def finish(position, cuts):
    return pl.pallas_call(
        finish_kernel,
        out_shape=jax.ShapeDtypeStruct((HEIGHT, QUARTER, SIDE, SIDE), BF),
        in_specs=[smem()] + [vmem()] * NY,
        out_specs=vmem(),
        compiler_params=params(),
        name="finish",
    )(position, *cuts)


def iota(shape, axis):
    return lax.broadcasted_iota(I32, shape, axis)


def dot(a, b):
    return jnp.dot(a.astype(BF), b.astype(BF), preferred_element_type=F32)


def dot_rows(a, b):
    return lax.dot_general(
        a.astype(BF), b.astype(BF), (((1,), (1,)), ((), ())), preferred_element_type=F32
    )


def earlier(size):
    return (iota((size, size), 0) < iota((size, size), 1)).astype(F32)


def places(need):
    order = earlier(SIDE)
    parts = []
    before = jnp.zeros((need.shape[0], 1), F32)
    for begin in range(0, need.shape[1], SIDE):
        part = need[:, begin : begin + SIDE]
        parts.append(dot(part, order) + before)
        before = before + jnp.sum(part, axis=1, keepdims=True)
    return jnp.concatenate(parts, axis=1)


def codes(need, capacity):
    place = places(need)
    return jnp.where((need > 0) & (place < capacity), place, -1.0)


def one_hot(code, rows):
    number = iota((rows, code.shape[1]), 0).astype(F32).astype(BF)
    return jnp.where(number == code.astype(BF), jnp.ones((), BF), jnp.zeros((), BF))


def quarter_of(slot):
    return sum((slot >= bound * QUARTER).astype(I32) for bound in range(1, NY))


def pattern_kernel(position_ref, columns_ref, entries_ref, slots_ref, union_ref, need_ref, kq_ref):
    step = 64
    for begin in range(0, ROWS, step):
        column = iota((step, ROWS), 1)
        found = jnp.full((step, ROWS), -1, I32)
        for slot in range(SLOTS):
            at = columns_ref[begin : begin + step, slot : slot + 1]
            found = jnp.where(at == column, slot, found)
        slots_ref[begin : begin + step, :] = found
    names = (slots_ref[...] >= 0).astype(F32)
    mine = iota((128, ROWS), 1) // HEIGHT == iota((128, ROWS), 0)
    union = (dot(mine.astype(F32), names) > 0).astype(F32)
    union_ref[...] = union

    entry = iota((1, ENTRIES), 1)
    peer, number = entry // HELD, entry % HELD
    x, core = (peer // NC) % NX, peer % NC
    row = ((x * NZ + position_ref[1]) * NC + core) * HEIGHT + quarter_of(number)
    column = entries_ref[...]
    every = iota((ROWS, ENTRIES), 0)
    named = dot(jnp.where(mine, 0.0, union), (every == row).astype(F32))
    need_ref[...] = named * dot(union, (every == column).astype(F32))
    kind = iota((8, ENTRIES), 0)
    both = jnp.where(kind == 1, jnp.maximum(column, 0), 0)
    kq_ref[...] = jnp.where(kind == 0, row, both).astype(F32)


def pattern(position, columns, entries):
    return pl.pallas_call(
        pattern_kernel,
        out_shape=(
            jax.ShapeDtypeStruct((ROWS, ROWS), I32),
            jax.ShapeDtypeStruct((128, ROWS), F32),
            jax.ShapeDtypeStruct((128, ENTRIES), F32),
            jax.ShapeDtypeStruct((8, ENTRIES), F32),
        ),
        in_specs=[smem(), vmem(), vmem()],
        out_specs=(vmem(), vmem(), vmem(), vmem()),
        compiler_params=params(),
        cost_estimate=cost(2 * SLOTS * ROWS**3 // 4, 8 * ROWS**2),
        name="pattern",
    )(position, columns, entries)


def send_kernel(position_ref, need_ref, kq_ref, near_ref, *refs):
    *out_refs, chosen_ref = refs
    z = position_ref[1]
    near = near_ref[...]
    kind = iota((8, ENTRIES), 0)
    pick = (iota((8, ENTRIES), 1) % HELD == SLOTS + kind) & (kind < 2)
    flags = dot(pick.astype(F32), near)
    flags = jnp.concatenate([flags[0:1], flags[1:2]], axis=1)
    need = need_ref[...] * flags
    slab = iota((8, 128), 1)
    plane = (slab // NC) % NZ == (iota((8, 128), 0) + z) & (NZ - 1)
    wanted = (dot(plane.astype(F32), need) > 0).astype(F32)
    code = codes(wanted, CAP_Z)
    most = jnp.max(jnp.sum(wanted, axis=1, keepdims=True), axis=0, keepdims=True)
    most = jnp.broadcast_to(jnp.minimum(most, 250.0), (1, 128))
    totals = jnp.minimum(dot_rows(jnp.ones((8, ENTRIES), F32), need)[0:1], 250.0)
    for to in range(NZ):
        chosen_ref[to * ROWS_Z : (to + 1) * ROWS_Z, :] = one_hot(code[to : to + 1], ROWS_Z)
    packed = jnp.dot(chosen_ref[...], near, preferred_element_type=F32)
    kq = kq_ref[...]
    line = iota((128, ENTRIES), 0)
    facts = jnp.where(line == SLABS, kq[0:1], jnp.where(line == SLABS + 1, kq[1:2], need))
    facts = jnp.dot(chosen_ref[...], facts.T.astype(BF), preferred_element_type=F32)
    tail = iota((16, PIECE), 0)
    slab = iota((16, 128), 1)
    target = iota((16, 128), 0)
    for to in range(NZ):
        choice = (target // NC * NZ + ((z + to) & (NZ - 1))) * NC + target % NC
        choice = slab == jnp.where(target < TARGETS, choice, SLABS - TARGETS + target)
        notes = dot_rows(choice, facts[to * ROWS_Z : (to + 1) * ROWS_Z])
        first = jnp.concatenate([notes[i : i + 1] for i in range(4)], axis=1)
        second = jnp.concatenate([notes[i : i + 1] for i in range(4, 8)], axis=1)
        third = jnp.concatenate([notes[8:9], notes[9:10], totals, most], axis=1)
        begin = to * ROWS_Z
        out_refs[to][0 : ROWS_Z - 16] = packed[begin : begin + ROWS_Z - 16].astype(BF)
        value = packed[begin + ROWS_Z - 16 : begin + ROWS_Z]
        value = jnp.where(tail == 12, first, value)
        value = jnp.where(tail == 13, second, value)
        value = jnp.where(tail == 14, third, value)
        out_refs[to][ROWS_Z - 16 : ROWS_Z] = value.astype(BF)


def send(position, need, kq, near):
    return pl.pallas_call(
        send_kernel,
        out_shape=[jax.ShapeDtypeStruct((ROWS_Z, PIECE), BF)] * NZ,
        in_specs=[smem()] + [vmem()] * 3,
        out_specs=[vmem()] * NZ,
        scratch_shapes=[pltpu.VMEM((NZ * ROWS_Z, ENTRIES), BF)],
        compiler_params=params(),
        name="send",
    )(position, need, kq, near)


def notes_of(along_refs):
    asked, third = [], []
    for along_ref in along_refs:
        notes = along_ref[ROWS_Z - 16 : ROWS_Z].astype(F32)
        asked.append(
            jnp.concatenate(
                [
                    notes[12 + i // 4 : 13 + i // 4, i % 4 * SIDE : (i % 4 + 1) * SIDE]
                    for i in range(TARGETS)
                ],
                axis=0,
            )
        )
        third.append(notes[14:15])
    return jnp.concatenate(asked, axis=1), third


def route_kernel(position_ref, *refs):
    along_refs, out_refs = refs[:NZ], refs[NZ : NZ + TARGETS]
    chosen_ref, along_ref = refs[NZ + TARGETS :]
    asked, _ = notes_of(along_refs)
    line = iota(asked.shape, 0)
    ordered = []
    for along_x, across in ((0, 0),) + ORDER_X:
        to = ((position_ref[0] + along_x) & (NX - 1)) * NC + ((position_ref[2] + across) & 1)
        ordered.append(jnp.sum(jnp.where(line == to, asked, 0.0), axis=0, keepdims=True))
    asked = jnp.concatenate(ordered, axis=0)
    for number, ref in enumerate(along_refs):
        along_ref[number * ROWS_Z : (number + 1) * ROWS_Z] = ref[...]
    code = codes(asked, CAP_X)
    for to in range(TARGETS):
        chosen_ref[to * SIDE : (to + 1) * SIDE, :] = one_hot(code[to : to + 1], SIDE)
    packed = jnp.dot(chosen_ref[...], along_ref[...], preferred_element_type=F32)
    for to in range(TARGETS):
        out_refs[to][...] = packed[to * SIDE : to * SIDE + CAP_X].astype(BF)


def route(position, along):
    return pl.pallas_call(
        route_kernel,
        out_shape=[jax.ShapeDtypeStruct((CAP_X, PIECE), BF)] * TARGETS,
        in_specs=[smem()] + [vmem()] * NZ,
        out_specs=[vmem()] * TARGETS,
        scratch_shapes=[
            pltpu.VMEM((TARGETS * SIDE, NZ * ROWS_Z), BF),
            pltpu.VMEM((NZ * ROWS_Z, PIECE), BF),
        ],
        compiler_params=params(),
        name="route",
    )(position, *along)


def own_places(position_ref, slots_ref):
    chip = position_ref[0] * NZ + position_ref[1]
    both = slots_ref[pl.ds(pl.multiple_of(chip * HEIGHT_2, HEIGHT_2), HEIGHT_2), :]
    swapped = jnp.concatenate([both[HEIGHT:], both[:HEIGHT]], axis=0)
    slot = jnp.where(position_ref[2] == 0, both, swapped)
    quarter = quarter_of(slot)
    held = (quarter * HEIGHT + iota(slot.shape, 0)) * QUARTER + slot - quarter * QUARTER
    return slot, jnp.where(slot >= 0, held - ZERO_BLOCK, 0).astype(F32)


def own_plan_kernel(position_ref, slots_ref, union_ref, out_ref):
    x, z, core, part = (position_ref[i] for i in range(4))
    slab = (x * NZ + z) * NC + core
    order = earlier(ROWS)
    out_ref[...] = jnp.zeros_like(out_ref)
    mine = union_ref[pl.ds(slab, 1), :]
    rank = dot(jnp.broadcast_to(mine, (8, ROWS)), order)

    slot, held = own_places(position_ref, slots_ref)
    number = iota((OUT_COLS, ROWS), 0).astype(F32)
    chosen = ((rank[0:1] == number) & (mine > 0)).astype(F32)
    out_ref[4:8, 0:OUT_COLS] = dot_rows(held, chosen)[0:HEIGHT].astype(I32) + ZERO_BLOCK
    wide = 128 // HEIGHT
    chosen = jnp.concatenate(
        [slot[i : i + 1] == iota((wide, ROWS), 0) for i in range(HEIGHT)], axis=0
    )
    out_ref[8:9, 0:128] = dot_rows(rank, chosen.astype(F32))[0:1].astype(I32)
    chosen = (iota((8, ROWS), 1) == iota((8, ROWS), 0) + slab * HEIGHT).astype(F32)
    out_ref[9:13, 0:8] = dot_rows(held, chosen)[0:HEIGHT].astype(I32) + ZERO_BLOCK
    groups = ((jnp.sum(mine) + (GROUP - 1)) * (1.0 / GROUP)).astype(I32)
    lane = iota((1, 128), 1)
    scalars = jnp.where(lane == 0, part, 0)
    out_ref[15:16, :] = jnp.where(lane == 1, groups, scalars)


def own_plan(position, slots, union):
    return pl.pallas_call(
        own_plan_kernel,
        out_shape=jax.ShapeDtypeStruct((16, 128), I32),
        in_specs=[smem(), vmem(), vmem()],
        out_specs=vmem(),
        compiler_params=params(),
        cost_estimate=cost(ROWS**3, 4 * ROWS**2),
        name="own_plan",
    )(position, slots, union)


def far_plan_kernel(position_ref, slots_ref, union_ref, *refs):
    *along_refs, out_ref = refs
    x, z, core = (position_ref[i] for i in range(3))
    slab = (x * NZ + z) * NC + core
    out_ref[...] = jnp.zeros_like(out_ref)
    asked, third = notes_of(along_refs)
    mine = iota(asked.shape, 0) == x * NC + core
    asked = jnp.sum(jnp.where(mine, asked, 0.0), axis=0, keepdims=True)
    number = jnp.sum(asked).astype(I32)
    code = codes(jnp.broadcast_to(asked, (8, asked.shape[1])), CAP_X)[0:1]
    chosen = one_hot(code, SIDE).astype(F32)
    row = jnp.concatenate([part[:, :SIDE] for part in third], axis=1)
    column = jnp.concatenate([part[:, SIDE : 2 * SIDE] for part in third], axis=1)
    row_down = jnp.sum(chosen * row, axis=1, keepdims=True).astype(I32)
    column_down = jnp.sum(chosen * column, axis=1, keepdims=True).astype(I32)
    row_along = dot_rows(jnp.broadcast_to(row, (8, row.shape[1])), chosen)[0:1].astype(I32)

    down, along = iota((SIDE, SIDE), 0), iota((SIDE, SIDE), 1)
    less = (row_down < row_along) | ((row_down == row_along) & (down < along))
    order = jnp.sum((less & (down < number)).astype(F32), axis=0, keepdims=True)
    ordered = ((order == down.astype(F32)) & (along < number)).astype(F32)
    position = iota((8, SIDE), 1).astype(F32)
    out_ref[0:1, 0:SIDE] = dot_rows(position, ordered)[0:1].astype(I32)
    names = union_ref[pl.ds(slab, 1), :]
    order = earlier(ROWS)
    rank = dot(jnp.broadcast_to(names, (8, ROWS)), order)
    every = iota((SIDE, ROWS), 1)
    rank = dot_rows(rank, (every == column_down).astype(F32))
    out_ref[1:2, 0:SIDE] = dot_rows(rank, ordered)[0:1].astype(I32)

    valid = iota((SIDE, ROWS), 0) < number
    count = dot(jnp.ones((8, SIDE), F32), ((every == row_down) & valid).astype(F32))
    start = jnp.minimum(dot(count, order), 250.0)[0:1]
    _, held = own_places(position_ref, slots_ref)
    needed = ((count + (FAR_GROUP - 1)) * (1.0 / FAR_GROUP)).astype(I32).astype(F32)
    first = dot(needed, order)[0:1]
    number = iota((SIDE, ROWS), 0).astype(F32)
    chosen = ((first <= number) & (number < first + needed[0:1])).astype(F32)
    kind = iota((8, ROWS), 0)
    values = jnp.where(kind == 0, start, jnp.where(kind == 1, first, count))
    values = dot_rows(values, chosen).astype(I32)
    done = (iota((1, SIDE), 1) - values[1:2]) * FAR_GROUP
    steps = jnp.sum(needed[0:1]).astype(I32)
    valid = iota((1, SIDE), 1) < steps
    out_ref[2:3, :] = jnp.where(valid, values[0:1] + done, 0)
    out_ref[3:4, :] = jnp.where(valid, values[2:3] - done, 0)
    out_ref[4:8, :] = dot_rows(held, chosen)[0:HEIGHT].astype(I32) + ZERO_BLOCK
    out_ref[8:9, :] = jnp.zeros((1, SIDE), I32) + jnp.minimum(steps, SIDE)

    third = functools.reduce(jnp.maximum, third), functools.reduce(jnp.add, third)
    most_z = jnp.max(third[0][:, 3 * SIDE :])
    most_x = jnp.max(third[1][:, 2 * SIDE : 3 * SIDE])
    fits = (most_x <= CAP_X) & (most_z <= CAP_Z)
    out_ref[9:10, :] = jnp.zeros((1, SIDE), I32) + fits.astype(I32)


def far_plan(position, slots, union, along):
    return pl.pallas_call(
        far_plan_kernel,
        out_shape=jax.ShapeDtypeStruct((16, 128), I32),
        in_specs=[smem()] + [vmem()] * (2 + NZ),
        out_specs=vmem(),
        compiler_params=params(),
        cost_estimate=cost(2 * 20 * ROWS**3, 8 * ROWS**2),
        name="far_plan",
    )(position, slots, union, *along)


def dense(blocks, nonzero, columns):
    slab = lax.axis_index(ROW_AXES)
    part = lax.axis_index("col")
    masked = blocks * nonzero[:, :, None, None].astype(BF)
    slab_ids = jnp.arange(SLABS, dtype=I32)
    local_rows = jnp.arange(HEIGHT, dtype=I32)
    grouped = columns.reshape(SLABS, HEIGHT * SLOTS)
    targets = slab * HEIGHT + local_rows
    wanted = jnp.any(grouped[:, :, None] == targets[None, None, :], axis=1)
    wanted = wanted & (slab_ids != slab)[:, None]
    picked = jnp.sum(jnp.where(wanted, local_rows, 0), axis=1)
    filled = jnp.any(wanted, axis=1)
    outgoing = jnp.where(filled[:, None, None, None], masked[picked], jnp.zeros((), BF))
    incoming = lax.all_to_all(outgoing, ROW_AXES, split_axis=0, concat_axis=0, tiled=True)
    row_table = jnp.concatenate([incoming, masked], axis=0)
    own_cols = lax.dynamic_slice_in_dim(columns, slab * HEIGHT, HEIGHT, 0)
    source = own_cols // HEIGHT
    row_index = jnp.where(source == slab, SLABS + own_cols % HEIGHT, source)
    far_cols = columns[own_cols]
    far_quarter = lax.dynamic_slice_in_dim(far_cols, part * QUARTER, QUARTER, 2)
    whole = lax.all_gather(masked, "col", axis=1, tiled=True)
    results = []
    for member in range(HEIGHT):
        match = far_quarter[member][:, :, None] == own_cols[member][None, None, :]
        products = jnp.einsum(
            "tab,tubc->tuac", whole[member], row_table[row_index[member]],
            preferred_element_type=F32,
        )
        summed = lax.dot_general(
            match.astype(F32).reshape(SLOTS * QUARTER, SLOTS),
            products.reshape(SLOTS * QUARTER, SIDE * SIDE),
            (((0,), (0,)), ((), ())),
            precision=lax.Precision.HIGHEST,
            preferred_element_type=F32,
        )
        results.append(summed.reshape(SLOTS, SIDE, SIDE))
    square = lax.psum_scatter(jnp.stack(results), "col", scatter_dimension=1, tiled=True)
    return square.astype(BF)


def plane_columns(columns):
    split = columns.reshape(NX, NZ, NC, HEIGHT, NY, QUARTER)
    mine = lax.dynamic_index_in_dim(split, lax.axis_index("z"), 1, keepdims=False)
    mine = mine.transpose(3, 0, 1, 2, 4).reshape(PEERS, SLOTS)
    return jnp.pad(mine, ((0, 0), (0, HELD - SLOTS)), constant_values=-1).reshape(1, ENTRIES)


def shards(blocks, nonzero, columns):
    position = jnp.stack([lax.axis_index(name) for name in ROW_AXES + ("col",)])
    cuts = prepare(position, nonzero, blocks)
    cuts, names, same = lax.optimization_barrier((cuts, columns, blocks))
    turned = turn(nonzero, same)
    slots, union, need, kq = pattern(position, names, plane_columns(columns))
    near = lax.all_to_all(cuts, ("col", "x", "core"), split_axis=0, concat_axis=0, tiled=True)
    near, turned, need = lax.optimization_barrier((near, turned, need))
    whole = lax.all_gather(turned, "col", axis=0, tiled=False)
    whole = whole.reshape(ZERO_BLOCK, SIDE, SIDE)
    packed = send(position, need, kq, near.reshape(ENTRIES, PIECE))
    packed, slots = lax.optimization_barrier((packed, slots))
    along = [packed[0]] + [
        lax.ppermute(packed[step], "z", [(i, (i + step) % NZ) for i in range(NZ)])
        for step in ORDER_Z
    ]
    own_lists = own_plan(position, slots, union)
    along, own_lists = lax.optimization_barrier((along, own_lists))
    packed, notes = lax.optimization_barrier((route(position, along), along))
    far = [packed[0]]
    for number, (along_x, across) in enumerate(ORDER_X):
        pairs = [
            (i, ((i // NC + along_x) % NX) * NC + (i + across) % NC) for i in range(TARGETS)
        ]
        far.append(lax.ppermute(packed[1 + number], ("x", "core"), pairs))
    far_lists = far_plan(position, slots, union, notes)
    own = own_sums(own_lists, whole)
    far, fits, own = lax.optimization_barrier((far, far_lists[9, 0] != 0, own))
    result = far_sums(own_lists, far_lists, whole, own, position, far)
    cuts = [result[0]]
    for step in ORDER_Y:
        pairs = [(i, (i + step) % NY) for i in range(NY)]
        cuts.append(lax.ppermute(result[step], "col", pairs))
    square = finish(position, cuts)
    return lax.cond(
        fits,
        lambda value, *_: value,
        lambda _, *inputs: dense(*inputs),
        square,
        blocks,
        nonzero,
        columns,
    )


def solution(mesh):
    fine = Mesh(mesh.devices.reshape(NX, NZ, NC, NY), ROW_AXES + ("col",))
    spec = P(ROW_AXES, "col", None, None)
    return jax.shard_map(
        shards,
        mesh=fine,
        in_specs=(spec, P(ROW_AXES, "col"), P()),
        out_specs=spec,
        check_vma=False,
    )
```

```python
import functools

import jax
import jax.numpy as jnp
from jax import lax
from jax.experimental import pallas as pl
from jax.experimental.pallas import tpu as pltpu
from jax.sharding import Mesh
from jax.sharding import PartitionSpec as P

BF = jnp.bfloat16
F32 = jnp.float32
I32 = jnp.int32

NX, NZ, NC, NY = 4, 8, 2, 4
ROWS, SLOTS, SIDE = 256, 28, 128
HEIGHT, QUARTER = 4, 7
SLABS = ROWS // HEIGHT
PEERS = NX * NC * NY
HELD = 32
ENTRIES = PEERS * HELD
PIECE = SIDE * SIDE // PEERS
WIDE = SIDE // NY
TARGETS = NX * NC
CAP_Z = 124
ROWS_Z = 128
CAP_X = 120
ORDER_Z = (4, 3, 5, 2, 6, 1, 7)
ORDER_Y = (2, 1, 3)
ORDER_X = ((2, 0), (2, 1), (1, 0), (3, 0), (1, 1), (3, 1), (0, 1))
GROUP = 8
FAR_GROUP = 3
STEPS_AT_ONCE = 8
HEIGHT_2 = NC * HEIGHT
OUT_COLS = 72
ZERO_BLOCK = NY * HEIGHT * QUARTER
VMEM_LIMIT = 48 * 1024 * 1024
ROW_AXES = ("x", "z", "core")


def vmem():
    return pl.BlockSpec(memory_space=pltpu.VMEM)


def smem():
    return pl.BlockSpec(memory_space=pltpu.SMEM)


def params():
    return pltpu.CompilerParams(vmem_limit_bytes=VMEM_LIMIT)


def cost(flops, moved):
    return pl.CostEstimate(flops=flops, bytes_accessed=moved, transcendentals=0)


def prepare_kernel(position_ref, keep_ref, blocks_ref, cuts_ref, rows_ref):
    x, core, part = position_ref[0], position_ref[2], position_ref[3]
    lanes = iota((8, ENTRIES), 1) - ((part * NX + x) * NC + core) * HELD
    flags = jnp.zeros((8, ENTRIES), F32)
    for row in range(HEIGHT):
        for slot in range(QUARTER):
            number = row * QUARTER + slot
            keep = keep_ref[row, slot] != 0
            flags = jnp.where((lanes == number) & keep, 1.0, flags)
            block = blocks_ref[row, slot].astype(F32)
            rows_ref[number] = jnp.where(keep, block, jnp.zeros_like(block)).T
    for part_of in range(NY):
        for extra in range(HELD - SLOTS):
            at = extra * PIECE + part_of * SIDE
            value = flags[:, at : at + SIDE] if extra < 2 else jnp.zeros((8, SIDE), F32)
            for quarter in range(NY):
                begin = quarter * WIDE + part_of * TARGETS
                rows_ref[SLOTS + extra, begin : begin + TARGETS] = value
    for quarter in range(NY):
        peers = slice(quarter * TARGETS, (quarter + 1) * TARGETS)
        for part_of in range(NY):
            begin = quarter * WIDE + part_of * TARGETS
            for half in range(0, HELD, 16):
                rows = rows_ref[half : half + 16, begin : begin + TARGETS]
                cuts_ref[peers, half : half + 16, part_of * SIDE : (part_of + 1) * SIDE] = (
                    jnp.swapaxes(rows, 0, 1).astype(BF)
                )


def prepare(position, nonzero, blocks):
    return pl.pallas_call(
        prepare_kernel,
        out_shape=jax.ShapeDtypeStruct((PEERS, HELD, PIECE), BF),
        in_specs=[smem(), smem(), vmem()],
        out_specs=vmem(),
        scratch_shapes=[pltpu.VMEM((HELD, SIDE, SIDE), F32)],
        compiler_params=params(),
        name="prepare",
    )(position, nonzero, blocks)


def turn_kernel(keep_ref, blocks_ref, out_ref):
    for row in range(HEIGHT):
        for slot in range(QUARTER):
            block = blocks_ref[row, slot]
            out_ref[row, slot] = jnp.where(
                keep_ref[row, slot] != 0, block, jnp.zeros_like(block)
            ).T


def turn(nonzero, blocks):
    return pl.pallas_call(
        turn_kernel,
        out_shape=jax.ShapeDtypeStruct((HEIGHT, QUARTER, SIDE, SIDE), BF),
        in_specs=[smem(), vmem()],
        out_specs=vmem(),
        compiler_params=params(),
        cost_estimate=cost(2 * SLOTS * SIDE**3, 4 * SLOTS * SIDE**2),
        name="turn",
    )(nonzero, blocks)


def own_block(whole_ref, place, rows):
    value = whole_ref[jnp.minimum(place, ZERO_BLOCK - 1), rows, :]
    return jnp.where(place < ZERO_BLOCK, value, jnp.zeros_like(value))


def out_place(place):
    return (place // QUARTER) % HEIGHT, place // (QUARTER * HEIGHT) * QUARTER + place % QUARTER


def own_kernel(
    plan_ref,
    whole_ref,
    out_ref,
    total,
    panel,
    near,
):
    first = pl.multiple_of(plan_ref[15, 0] * WIDE, WIDE)
    for inner in range(HEIGHT):
        for member in range(HEIGHT):
            panel[pl.ds(inner * SIDE, SIDE), pl.ds(member * SIDE, SIDE)] = own_block(
                whole_ref, plan_ref[9 + member, inner], pl.ds(0, SIDE)
            )

    def step(group, carry):
        for at in range(GROUP):
            for inner in range(HEIGHT):
                near[pl.ds(at * WIDE, WIDE), pl.ds(inner * SIDE, SIDE)] = own_block(
                    whole_ref, plan_ref[4 + inner, group * GROUP + at], pl.ds(first, WIDE)
                )
        value = jnp.dot(near[...], panel[...], preferred_element_type=F32)
        total[pl.ds(group * GROUP, GROUP)] = value.reshape(GROUP, WIDE, HEIGHT * SIDE)
        return carry

    lax.fori_loop(0, plan_ref[15, 1], step, 0)
    for place in range(ZERO_BLOCK):
        member, slot = out_place(place)
        column = plan_ref[8, member * (128 // HEIGHT) + slot]
        out_ref[place] = total[column, :, pl.ds(member * SIDE, SIDE)]


def own_sums(lists, whole):
    flops = 2 * 32 * WIDE * (HEIGHT * SIDE) ** 2
    return pl.pallas_call(
        own_kernel,
        out_shape=jax.ShapeDtypeStruct((ZERO_BLOCK, WIDE, SIDE), F32),
        in_specs=[smem(), vmem()],
        out_specs=vmem(),
        scratch_shapes=[
            pltpu.VMEM((OUT_COLS, WIDE, HEIGHT * SIDE), F32),
            pltpu.VMEM((HEIGHT * SIDE, HEIGHT * SIDE), BF),
            pltpu.VMEM((GROUP * WIDE, HEIGHT * SIDE), BF),
        ],
        compiler_params=params(),
        cost_estimate=cost(flops, 3 * ZERO_BLOCK * SIDE * SIDE),
        name="own_sums",
    )(lists, whole)


def far_kernel(
    own_ref,
    plan_ref,
    whole_ref,
    near_ref,
    position_ref,
    *refs,
):
    *out_refs, low, high, pieces_ref = refs[TARGETS:]
    halves = (low, high)
    for (along_x, across), far_ref in zip(((0, 0),) + ORDER_X, refs):
        sender = ((position_ref[0] - along_x) & (NX - 1)) * NC + ((position_ref[2] + across) & 1)
        rows = pl.ds(pl.multiple_of(sender * CAP_X, 8), CAP_X)
        for part in range(NY):
            lanes = slice(part * SIDE, (part + 1) * SIDE)
            pieces_ref[part, rows, :] = far_ref[:, lanes].astype(F32)

    def clear(group, carry):
        for total in halves:
            total[pl.ds(group * GROUP, GROUP)] = jnp.zeros((GROUP, WIDE, 2 * SIDE), F32)
        return carry

    lax.fori_loop(0, own_ref[15, 1], clear, 0)

    def add_product(step):
        begin = plan_ref[2, step]
        length = plan_ref[3, step]
        pieces, columns = [], []
        for at in range(FAR_GROUP):
            place = jnp.minimum(begin + at, CAP_X - 1)
            rows = pl.ds(plan_ref[0, place], TARGETS, stride=CAP_X)
            for part in range(NY):
                pieces.append(pieces_ref[part, rows, :])
            columns.append(jnp.where(at < length, plan_ref[1, place], OUT_COLS))
        left = jnp.concatenate(pieces, axis=0).astype(BF)
        for half, total in enumerate(halves):
            right = jnp.concatenate(
                [
                    own_block(whole_ref, plan_ref[4 + 2 * half + at, step], pl.ds(0, SIDE))
                    for at in range(2)
                ],
                axis=1,
            )
            value = jnp.dot(left, right, preferred_element_type=F32)
            before = [total[column] for column in columns]
            for at, column in enumerate(columns):
                total[column] = before[at] + value[at * WIDE : (at + 1) * WIDE]

    def steps(number, carry):
        for at in range(STEPS_AT_ONCE):
            add_product(number * STEPS_AT_ONCE + at)
        return carry

    lax.fori_loop(0, (plan_ref[8, 0] + STEPS_AT_ONCE - 1) // STEPS_AT_ONCE, steps, 0)

    for step, out_ref in enumerate(out_refs):
        part = (own_ref[15, 0] + step) & (NY - 1)
        for place in range(HEIGHT * QUARTER):
            member, slot = place // QUARTER, part * QUARTER + place % QUARTER
            column = own_ref[8, member * (128 // HEIGHT) + slot]
            value = halves[member // 2][column, :, pl.ds(member % 2 * SIDE, SIDE)]
            value = value + near_ref[part * (HEIGHT * QUARTER) + place]
            out_ref[place] = value.astype(BF)


def far_sums(own_lists, far_lists, whole, near, position, far):
    return pl.pallas_call(
        far_kernel,
        out_shape=[jax.ShapeDtypeStruct((HEIGHT * QUARTER, WIDE, SIDE), BF)] * NY,
        in_specs=[smem(), smem(), vmem(), vmem(), smem()] + [vmem()] * TARGETS,
        out_specs=[vmem()] * NY,
        scratch_shapes=[
            pltpu.VMEM((OUT_COLS + 1, WIDE, 2 * SIDE), F32),
            pltpu.VMEM((OUT_COLS + 1, WIDE, 2 * SIDE), F32),
            pltpu.VMEM((NY, TARGETS * CAP_X, SIDE), F32),
        ],
        compiler_params=params(),
        name="far_sums",
    )(own_lists, far_lists, whole, near, position, *far)


def finish_kernel(position_ref, *refs):
    *cut_refs, out_ref = refs
    at = dict(zip((0,) + ORDER_Y, cut_refs))
    for part in range(NY):

        @pl.when(position_ref[3] == part)
        def _():
            order = [at[(part - sender) % NY] for sender in range(NY)]
            for row in range(HEIGHT):
                for slot in range(QUARTER):
                    cuts = [ref[row * QUARTER + slot] for ref in order]
                    out_ref[row, slot] = jnp.concatenate(cuts, axis=0).T


def finish(position, cuts):
    return pl.pallas_call(
        finish_kernel,
        out_shape=jax.ShapeDtypeStruct((HEIGHT, QUARTER, SIDE, SIDE), BF),
        in_specs=[smem()] + [vmem()] * NY,
        out_specs=vmem(),
        compiler_params=params(),
        name="finish",
    )(position, *cuts)


def iota(shape, axis):
    return lax.broadcasted_iota(I32, shape, axis)


def dot(a, b):
    return jnp.dot(a.astype(BF), b.astype(BF), preferred_element_type=F32)


def dot_rows(a, b):
    return lax.dot_general(
        a.astype(BF), b.astype(BF), (((1,), (1,)), ((), ())), preferred_element_type=F32
    )


def earlier(size):
    return (iota((size, size), 0) < iota((size, size), 1)).astype(F32)


def places(need):
    order = earlier(SIDE)
    parts = []
    before = jnp.zeros((need.shape[0], 1), F32)
    for begin in range(0, need.shape[1], SIDE):
        part = need[:, begin : begin + SIDE]
        parts.append(dot(part, order) + before)
        before = before + jnp.sum(part, axis=1, keepdims=True)
    return jnp.concatenate(parts, axis=1)


def codes(need, capacity):
    place = places(need)
    return jnp.where((need > 0) & (place < capacity), place, -1.0)


def one_hot(code, rows):
    number = iota((rows, code.shape[1]), 0).astype(F32).astype(BF)
    return jnp.where(number == code.astype(BF), jnp.ones((), BF), jnp.zeros((), BF))


def quarter_of(slot):
    return sum((slot >= bound * QUARTER).astype(I32) for bound in range(1, NY))


def pattern_kernel(position_ref, columns_ref, entries_ref, slots_ref, union_ref, need_ref, kq_ref):
    step = 64
    for begin in range(0, ROWS, step):
        column = iota((step, ROWS), 1)
        found = jnp.full((step, ROWS), -1, I32)
        for slot in range(SLOTS):
            at = columns_ref[begin : begin + step, slot : slot + 1]
            found = jnp.where(at == column, slot, found)
        slots_ref[begin : begin + step, :] = found
    names = (slots_ref[...] >= 0).astype(F32)
    mine = iota((128, ROWS), 1) // HEIGHT == iota((128, ROWS), 0)
    union = (dot(mine.astype(F32), names) > 0).astype(F32)
    union_ref[...] = union

    entry = iota((1, ENTRIES), 1)
    peer, number = entry // HELD, entry % HELD
    x, core = (peer // NC) % NX, peer % NC
    row = ((x * NZ + position_ref[1]) * NC + core) * HEIGHT + quarter_of(number)
    column = entries_ref[...]
    every = iota((ROWS, ENTRIES), 0)
    named = dot(jnp.where(mine, 0.0, union), (every == row).astype(F32))
    need_ref[...] = named * dot(union, (every == column).astype(F32))
    kind = iota((8, ENTRIES), 0)
    both = jnp.where(kind == 1, jnp.maximum(column, 0), 0)
    kq_ref[...] = jnp.where(kind == 0, row, both).astype(F32)


def pattern(position, columns, entries):
    return pl.pallas_call(
        pattern_kernel,
        out_shape=(
            jax.ShapeDtypeStruct((ROWS, ROWS), I32),
            jax.ShapeDtypeStruct((128, ROWS), F32),
            jax.ShapeDtypeStruct((128, ENTRIES), F32),
            jax.ShapeDtypeStruct((8, ENTRIES), F32),
        ),
        in_specs=[smem(), vmem(), vmem()],
        out_specs=(vmem(), vmem(), vmem(), vmem()),
        compiler_params=params(),
        cost_estimate=cost(2 * SLOTS * ROWS**3 // 4, 8 * ROWS**2),
        name="pattern",
    )(position, columns, entries)


def send_kernel(position_ref, need_ref, kq_ref, near_ref, *refs):
    *out_refs, chosen_ref = refs
    z = position_ref[1]
    near = near_ref[...]
    kind = iota((8, ENTRIES), 0)
    pick = (iota((8, ENTRIES), 1) % HELD == SLOTS + kind) & (kind < 2)
    flags = dot(pick.astype(F32), near)
    flags = jnp.concatenate([flags[0:1], flags[1:2]], axis=1)
    need = need_ref[...] * flags
    slab = iota((8, 128), 1)
    plane = (slab // NC) % NZ == (iota((8, 128), 0) + z) & (NZ - 1)
    wanted = (dot(plane.astype(F32), need) > 0).astype(F32)
    code = codes(wanted, CAP_Z)
    most = jnp.max(jnp.sum(wanted, axis=1, keepdims=True), axis=0, keepdims=True)
    most = jnp.broadcast_to(jnp.minimum(most, 250.0), (1, 128))
    totals = jnp.minimum(dot_rows(jnp.ones((8, ENTRIES), F32), need)[0:1], 250.0)
    for to in range(NZ):
        chosen_ref[to * ROWS_Z : (to + 1) * ROWS_Z, :] = one_hot(code[to : to + 1], ROWS_Z)
    packed = jnp.dot(chosen_ref[...], near, preferred_element_type=F32)
    kq = kq_ref[...]
    line = iota((128, ENTRIES), 0)
    facts = jnp.where(line == SLABS, kq[0:1], jnp.where(line == SLABS + 1, kq[1:2], need))
    facts = jnp.dot(chosen_ref[...], facts.T.astype(BF), preferred_element_type=F32)
    tail = iota((16, PIECE), 0)
    slab = iota((16, 128), 1)
    target = iota((16, 128), 0)
    for to in range(NZ):
        choice = (target // NC * NZ + ((z + to) & (NZ - 1))) * NC + target % NC
        choice = slab == jnp.where(target < TARGETS, choice, SLABS - TARGETS + target)
        notes = dot_rows(choice, facts[to * ROWS_Z : (to + 1) * ROWS_Z])
        first = jnp.concatenate([notes[i : i + 1] for i in range(4)], axis=1)
        second = jnp.concatenate([notes[i : i + 1] for i in range(4, 8)], axis=1)
        third = jnp.concatenate([notes[8:9], notes[9:10], totals, most], axis=1)
        begin = to * ROWS_Z
        out_refs[to][0 : ROWS_Z - 16] = packed[begin : begin + ROWS_Z - 16].astype(BF)
        value = packed[begin + ROWS_Z - 16 : begin + ROWS_Z]
        value = jnp.where(tail == 12, first, value)
        value = jnp.where(tail == 13, second, value)
        value = jnp.where(tail == 14, third, value)
        out_refs[to][ROWS_Z - 16 : ROWS_Z] = value.astype(BF)


def send(position, need, kq, near):
    return pl.pallas_call(
        send_kernel,
        out_shape=[jax.ShapeDtypeStruct((ROWS_Z, PIECE), BF)] * NZ,
        in_specs=[smem()] + [vmem()] * 3,
        out_specs=[vmem()] * NZ,
        scratch_shapes=[pltpu.VMEM((NZ * ROWS_Z, ENTRIES), BF)],
        compiler_params=params(),
        name="send",
    )(position, need, kq, near)


def notes_of(along_refs):
    asked, third = [], []
    for along_ref in along_refs:
        notes = along_ref[ROWS_Z - 16 : ROWS_Z].astype(F32)
        asked.append(
            jnp.concatenate(
                [
                    notes[12 + i // 4 : 13 + i // 4, i % 4 * SIDE : (i % 4 + 1) * SIDE]
                    for i in range(TARGETS)
                ],
                axis=0,
            )
        )
        third.append(notes[14:15])
    return jnp.concatenate(asked, axis=1), third


def route_kernel(position_ref, *refs):
    along_refs, out_refs = refs[:NZ], refs[NZ : NZ + TARGETS]
    chosen_ref, along_ref = refs[NZ + TARGETS :]
    asked, _ = notes_of(along_refs)
    line = iota(asked.shape, 0)
    ordered = []
    for along_x, across in ((0, 0),) + ORDER_X:
        to = ((position_ref[0] + along_x) & (NX - 1)) * NC + ((position_ref[2] + across) & 1)
        ordered.append(jnp.sum(jnp.where(line == to, asked, 0.0), axis=0, keepdims=True))
    asked = jnp.concatenate(ordered, axis=0)
    for number, ref in enumerate(along_refs):
        along_ref[number * ROWS_Z : (number + 1) * ROWS_Z] = ref[...]
    code = codes(asked, CAP_X)
    for to in range(TARGETS):
        chosen_ref[to * SIDE : (to + 1) * SIDE, :] = one_hot(code[to : to + 1], SIDE)
    packed = jnp.dot(chosen_ref[...], along_ref[...], preferred_element_type=F32)
    for to in range(TARGETS):
        out_refs[to][...] = packed[to * SIDE : to * SIDE + CAP_X].astype(BF)


def route(position, along):
    return pl.pallas_call(
        route_kernel,
        out_shape=[jax.ShapeDtypeStruct((CAP_X, PIECE), BF)] * TARGETS,
        in_specs=[smem()] + [vmem()] * NZ,
        out_specs=[vmem()] * TARGETS,
        scratch_shapes=[
            pltpu.VMEM((TARGETS * SIDE, NZ * ROWS_Z), BF),
            pltpu.VMEM((NZ * ROWS_Z, PIECE), BF),
        ],
        compiler_params=params(),
        name="route",
    )(position, *along)


def own_places(position_ref, slots_ref):
    chip = position_ref[0] * NZ + position_ref[1]
    both = slots_ref[pl.ds(pl.multiple_of(chip * HEIGHT_2, HEIGHT_2), HEIGHT_2), :]
    swapped = jnp.concatenate([both[HEIGHT:], both[:HEIGHT]], axis=0)
    slot = jnp.where(position_ref[2] == 0, both, swapped)
    quarter = quarter_of(slot)
    held = (quarter * HEIGHT + iota(slot.shape, 0)) * QUARTER + slot - quarter * QUARTER
    return slot, jnp.where(slot >= 0, held - ZERO_BLOCK, 0).astype(F32)


def own_plan_kernel(position_ref, slots_ref, union_ref, out_ref):
    x, z, core, part = (position_ref[i] for i in range(4))
    slab = (x * NZ + z) * NC + core
    order = earlier(ROWS)
    out_ref[...] = jnp.zeros_like(out_ref)
    mine = union_ref[pl.ds(slab, 1), :]
    rank = dot(jnp.broadcast_to(mine, (8, ROWS)), order)

    slot, held = own_places(position_ref, slots_ref)
    number = iota((OUT_COLS, ROWS), 0).astype(F32)
    chosen = ((rank[0:1] == number) & (mine > 0)).astype(F32)
    out_ref[4:8, 0:OUT_COLS] = dot_rows(held, chosen)[0:HEIGHT].astype(I32) + ZERO_BLOCK
    wide = 128 // HEIGHT
    chosen = jnp.concatenate(
        [slot[i : i + 1] == iota((wide, ROWS), 0) for i in range(HEIGHT)], axis=0
    )
    out_ref[8:9, 0:128] = dot_rows(rank, chosen.astype(F32))[0:1].astype(I32)
    chosen = (iota((8, ROWS), 1) == iota((8, ROWS), 0) + slab * HEIGHT).astype(F32)
    out_ref[9:13, 0:8] = dot_rows(held, chosen)[0:HEIGHT].astype(I32) + ZERO_BLOCK
    groups = ((jnp.sum(mine) + (GROUP - 1)) * (1.0 / GROUP)).astype(I32)
    lane = iota((1, 128), 1)
    scalars = jnp.where(lane == 0, part, 0)
    out_ref[15:16, :] = jnp.where(lane == 1, groups, scalars)


def own_plan(position, slots, union):
    return pl.pallas_call(
        own_plan_kernel,
        out_shape=jax.ShapeDtypeStruct((16, 128), I32),
        in_specs=[smem(), vmem(), vmem()],
        out_specs=vmem(),
        compiler_params=params(),
        cost_estimate=cost(ROWS**3, 4 * ROWS**2),
        name="own_plan",
    )(position, slots, union)


def far_plan_kernel(position_ref, slots_ref, union_ref, *refs):
    *along_refs, out_ref = refs
    x, z, core = (position_ref[i] for i in range(3))
    slab = (x * NZ + z) * NC + core
    out_ref[...] = jnp.zeros_like(out_ref)
    asked, third = notes_of(along_refs)
    mine = iota(asked.shape, 0) == x * NC + core
    asked = jnp.sum(jnp.where(mine, asked, 0.0), axis=0, keepdims=True)
    number = jnp.sum(asked).astype(I32)
    code = codes(jnp.broadcast_to(asked, (8, asked.shape[1])), CAP_X)[0:1]
    chosen = one_hot(code, SIDE).astype(F32)
    row = jnp.concatenate([part[:, :SIDE] for part in third], axis=1)
    column = jnp.concatenate([part[:, SIDE : 2 * SIDE] for part in third], axis=1)
    row_down = jnp.sum(chosen * row, axis=1, keepdims=True).astype(I32)
    column_down = jnp.sum(chosen * column, axis=1, keepdims=True).astype(I32)
    row_along = dot_rows(jnp.broadcast_to(row, (8, row.shape[1])), chosen)[0:1].astype(I32)

    down, along = iota((SIDE, SIDE), 0), iota((SIDE, SIDE), 1)
    less = (row_down < row_along) | ((row_down == row_along) & (down < along))
    order = jnp.sum((less & (down < number)).astype(F32), axis=0, keepdims=True)
    ordered = ((order == down.astype(F32)) & (along < number)).astype(F32)
    position = iota((8, SIDE), 1).astype(F32)
    out_ref[0:1, 0:SIDE] = dot_rows(position, ordered)[0:1].astype(I32)
    names = union_ref[pl.ds(slab, 1), :]
    order = earlier(ROWS)
    rank = dot(jnp.broadcast_to(names, (8, ROWS)), order)
    every = iota((SIDE, ROWS), 1)
    rank = dot_rows(rank, (every == column_down).astype(F32))
    out_ref[1:2, 0:SIDE] = dot_rows(rank, ordered)[0:1].astype(I32)

    valid = iota((SIDE, ROWS), 0) < number
    count = dot(jnp.ones((8, SIDE), F32), ((every == row_down) & valid).astype(F32))
    start = jnp.minimum(dot(count, order), 250.0)[0:1]
    _, held = own_places(position_ref, slots_ref)
    needed = ((count + (FAR_GROUP - 1)) * (1.0 / FAR_GROUP)).astype(I32).astype(F32)
    first = dot(needed, order)[0:1]
    number = iota((SIDE, ROWS), 0).astype(F32)
    chosen = ((first <= number) & (number < first + needed[0:1])).astype(F32)
    kind = iota((8, ROWS), 0)
    values = jnp.where(kind == 0, start, jnp.where(kind == 1, first, count))
    values = dot_rows(values, chosen).astype(I32)
    done = (iota((1, SIDE), 1) - values[1:2]) * FAR_GROUP
    steps = jnp.sum(needed[0:1]).astype(I32)
    valid = iota((1, SIDE), 1) < steps
    out_ref[2:3, :] = jnp.where(valid, values[0:1] + done, 0)
    out_ref[3:4, :] = jnp.where(valid, values[2:3] - done, 0)
    out_ref[4:8, :] = dot_rows(held, chosen)[0:HEIGHT].astype(I32) + ZERO_BLOCK
    out_ref[8:9, :] = jnp.zeros((1, SIDE), I32) + jnp.minimum(steps, SIDE)

    third = functools.reduce(jnp.maximum, third), functools.reduce(jnp.add, third)
    most_z = jnp.max(third[0][:, 3 * SIDE :])
    most_x = jnp.max(third[1][:, 2 * SIDE : 3 * SIDE])
    fits = (most_x <= CAP_X) & (most_z <= CAP_Z)
    out_ref[9:10, :] = jnp.zeros((1, SIDE), I32) + fits.astype(I32)


def far_plan(position, slots, union, along):
    return pl.pallas_call(
        far_plan_kernel,
        out_shape=jax.ShapeDtypeStruct((16, 128), I32),
        in_specs=[smem()] + [vmem()] * (2 + NZ),
        out_specs=vmem(),
        compiler_params=params(),
        cost_estimate=cost(2 * 20 * ROWS**3, 8 * ROWS**2),
        name="far_plan",
    )(position, slots, union, *along)


def dense(blocks, nonzero, columns):
    slab = lax.axis_index(ROW_AXES)
    part = lax.axis_index("col")
    masked = blocks * nonzero[:, :, None, None].astype(BF)
    slab_ids = jnp.arange(SLABS, dtype=I32)
    local_rows = jnp.arange(HEIGHT, dtype=I32)
    grouped = columns.reshape(SLABS, HEIGHT * SLOTS)
    targets = slab * HEIGHT + local_rows
    wanted = jnp.any(grouped[:, :, None] == targets[None, None, :], axis=1)
    wanted = wanted & (slab_ids != slab)[:, None]
    picked = jnp.sum(jnp.where(wanted, local_rows, 0), axis=1)
    filled = jnp.any(wanted, axis=1)
    outgoing = jnp.where(filled[:, None, None, None], masked[picked], jnp.zeros((), BF))
    incoming = lax.all_to_all(outgoing, ROW_AXES, split_axis=0, concat_axis=0, tiled=True)
    row_table = jnp.concatenate([incoming, masked], axis=0)
    own_cols = lax.dynamic_slice_in_dim(columns, slab * HEIGHT, HEIGHT, 0)
    source = own_cols // HEIGHT
    row_index = jnp.where(source == slab, SLABS + own_cols % HEIGHT, source)
    far_cols = columns[own_cols]
    far_quarter = lax.dynamic_slice_in_dim(far_cols, part * QUARTER, QUARTER, 2)
    whole = lax.all_gather(masked, "col", axis=1, tiled=True)
    results = []
    for member in range(HEIGHT):
        match = far_quarter[member][:, :, None] == own_cols[member][None, None, :]
        products = jnp.einsum(
            "tab,tubc->tuac", whole[member], row_table[row_index[member]],
            preferred_element_type=F32,
        )
        summed = lax.dot_general(
            match.astype(F32).reshape(SLOTS * QUARTER, SLOTS),
            products.reshape(SLOTS * QUARTER, SIDE * SIDE),
            (((0,), (0,)), ((), ())),
            precision=lax.Precision.HIGHEST,
            preferred_element_type=F32,
        )
        results.append(summed.reshape(SLOTS, SIDE, SIDE))
    square = lax.psum_scatter(jnp.stack(results), "col", scatter_dimension=1, tiled=True)
    return square.astype(BF)


def plane_columns(columns):
    split = columns.reshape(NX, NZ, NC, HEIGHT, NY, QUARTER)
    mine = lax.dynamic_index_in_dim(split, lax.axis_index("z"), 1, keepdims=False)
    mine = mine.transpose(3, 0, 1, 2, 4).reshape(PEERS, SLOTS)
    return jnp.pad(mine, ((0, 0), (0, HELD - SLOTS)), constant_values=-1).reshape(1, ENTRIES)


def shards(blocks, nonzero, columns):
    position = jnp.stack([lax.axis_index(name) for name in ROW_AXES + ("col",)])
    cuts = prepare(position, nonzero, blocks)
    cuts, names, same = lax.optimization_barrier((cuts, columns, blocks))
    turned = turn(nonzero, same)
    slots, union, need, kq = pattern(position, names, plane_columns(columns))
    near = lax.all_to_all(cuts, ("col", "x", "core"), split_axis=0, concat_axis=0, tiled=True)
    turned, need = lax.optimization_barrier((turned, need))
    whole = lax.all_gather(turned, "col", axis=0, tiled=False)
    whole = whole.reshape(ZERO_BLOCK, SIDE, SIDE)
    packed = send(position, need, kq, near.reshape(ENTRIES, PIECE))
    packed, slots = lax.optimization_barrier((packed, slots))
    along = [packed[0]] + [
        lax.ppermute(packed[step], "z", [(i, (i + step) % NZ) for i in range(NZ)])
        for step in ORDER_Z
    ]
    own_lists = own_plan(position, slots, union)
    along, own_lists = lax.optimization_barrier((along, own_lists))
    packed, notes = lax.optimization_barrier((route(position, along), along))
    far = [packed[0]]
    for number, (along_x, across) in enumerate(ORDER_X):
        pairs = [
            (i, ((i // NC + along_x) % NX) * NC + (i + across) % NC) for i in range(TARGETS)
        ]
        far.append(lax.ppermute(packed[1 + number], ("x", "core"), pairs))
    far_lists = far_plan(position, slots, union, notes)
    own = own_sums(own_lists, whole)
    far, own = lax.optimization_barrier((far, own))
    result = far_sums(own_lists, far_lists, whole, own, position, far)
    cuts = [result[0]]
    for step in ORDER_Y:
        pairs = [(i, (i + step) % NY) for i in range(NY)]
        cuts.append(lax.ppermute(result[step], "col", pairs))
    square = finish(position, cuts)
    return lax.cond(
        far_lists[9, 0] != 0,
        lambda value, *_: value,
        lambda _, *inputs: dense(*inputs),
        square,
        blocks,
        nonzero,
        columns,
    )


def solution(mesh):
    fine = Mesh(mesh.devices.reshape(NX, NZ, NC, NY), ROW_AXES + ("col",))
    spec = P(ROW_AXES, "col", None, None)
    return jax.shard_map(
        shards,
        mesh=fine,
        in_specs=(spec, P(ROW_AXES, "col"), P()),
        out_specs=spec,
        check_vma=False,
    )
```

```python
import functools

import jax
import jax.numpy as jnp
from jax import lax
from jax.experimental import pallas as pl
from jax.experimental.pallas import tpu as pltpu
from jax.sharding import Mesh
from jax.sharding import PartitionSpec as P

BF = jnp.bfloat16
F32 = jnp.float32
I32 = jnp.int32

NX, NZ, NC, NY = 4, 8, 2, 4
ROWS, SLOTS, SIDE = 256, 28, 128
HEIGHT, QUARTER = 4, 7
SLABS = ROWS // HEIGHT
PEERS = NX * NC * NY
HELD = 32
ENTRIES = PEERS * HELD
PIECE = SIDE * SIDE // PEERS
WIDE = SIDE // NY
TARGETS = NX * NC
CAP_Z = 124
ROWS_Z = 128
CAP_X = 120
ORDER_Z = (4, 3, 5, 2, 6, 1, 7)
ORDER_Y = (2, 1, 3)
ORDER_X = ((2, 0), (2, 1), (1, 0), (3, 0), (1, 1), (3, 1), (0, 1))
GROUP = 8
FAR_GROUP = 3
STEPS_AT_ONCE = 8
HEIGHT_2 = NC * HEIGHT
OUT_COLS = 72
ZERO_BLOCK = NY * HEIGHT * QUARTER
VMEM_LIMIT = 48 * 1024 * 1024
ROW_AXES = ("x", "z", "core")


def vmem():
    return pl.BlockSpec(memory_space=pltpu.VMEM)


def smem():
    return pl.BlockSpec(memory_space=pltpu.SMEM)


def params():
    return pltpu.CompilerParams(vmem_limit_bytes=VMEM_LIMIT)


def cost(flops, moved):
    return pl.CostEstimate(flops=flops, bytes_accessed=moved, transcendentals=0)


def prepare_kernel(position_ref, keep_ref, blocks_ref, cuts_ref, rows_ref):
    x, core, part = position_ref[0], position_ref[2], position_ref[3]
    lanes = iota((8, ENTRIES), 1) - ((part * NX + x) * NC + core) * HELD
    flags = jnp.zeros((8, ENTRIES), F32)
    for row in range(HEIGHT):
        for slot in range(QUARTER):
            number = row * QUARTER + slot
            keep = keep_ref[row, slot] != 0
            flags = jnp.where((lanes == number) & keep, 1.0, flags)
            block = blocks_ref[row, slot].astype(F32)
            rows_ref[number] = jnp.where(keep, block, jnp.zeros_like(block)).T
    for part_of in range(NY):
        for extra in range(HELD - SLOTS):
            at = extra * PIECE + part_of * SIDE
            value = flags[:, at : at + SIDE] if extra < 2 else jnp.zeros((8, SIDE), F32)
            for quarter in range(NY):
                begin = quarter * WIDE + part_of * TARGETS
                rows_ref[SLOTS + extra, begin : begin + TARGETS] = value
    for quarter in range(NY):
        peers = slice(quarter * TARGETS, (quarter + 1) * TARGETS)
        for part_of in range(NY):
            begin = quarter * WIDE + part_of * TARGETS
            for half in range(0, HELD, 16):
                rows = rows_ref[half : half + 16, begin : begin + TARGETS]
                cuts_ref[peers, half : half + 16, part_of * SIDE : (part_of + 1) * SIDE] = (
                    jnp.swapaxes(rows, 0, 1).astype(BF)
                )


def prepare(position, nonzero, blocks):
    return pl.pallas_call(
        prepare_kernel,
        out_shape=jax.ShapeDtypeStruct((PEERS, HELD, PIECE), BF),
        in_specs=[smem(), smem(), vmem()],
        out_specs=vmem(),
        scratch_shapes=[pltpu.VMEM((HELD, SIDE, SIDE), F32)],
        compiler_params=params(),
        name="prepare",
    )(position, nonzero, blocks)


def turn_kernel(keep_ref, blocks_ref, out_ref):
    for row in range(HEIGHT):
        for slot in range(QUARTER):
            block = blocks_ref[row, slot]
            out_ref[row, slot] = jnp.where(
                keep_ref[row, slot] != 0, block, jnp.zeros_like(block)
            ).T


def turn(nonzero, blocks):
    return pl.pallas_call(
        turn_kernel,
        out_shape=jax.ShapeDtypeStruct((HEIGHT, QUARTER, SIDE, SIDE), BF),
        in_specs=[smem(), vmem()],
        out_specs=vmem(),
        compiler_params=params(),
        cost_estimate=cost(2 * SLOTS * SIDE**3, 4 * SLOTS * SIDE**2),
        name="turn",
    )(nonzero, blocks)


def own_block(whole_ref, place, rows):
    value = whole_ref[jnp.minimum(place, ZERO_BLOCK - 1), rows, :]
    return jnp.where(place < ZERO_BLOCK, value, jnp.zeros_like(value))


def out_place(place):
    return (place // QUARTER) % HEIGHT, place // (QUARTER * HEIGHT) * QUARTER + place % QUARTER


def own_kernel(
    plan_ref,
    whole_ref,
    out_ref,
    total,
    panel,
    near,
):
    first = pl.multiple_of(plan_ref[15, 0] * WIDE, WIDE)
    for inner in range(HEIGHT):
        for member in range(HEIGHT):
            panel[pl.ds(inner * SIDE, SIDE), pl.ds(member * SIDE, SIDE)] = own_block(
                whole_ref, plan_ref[9 + member, inner], pl.ds(0, SIDE)
            )

    def step(group, carry):
        for at in range(GROUP):
            for inner in range(HEIGHT):
                near[pl.ds(at * WIDE, WIDE), pl.ds(inner * SIDE, SIDE)] = own_block(
                    whole_ref, plan_ref[4 + inner, group * GROUP + at], pl.ds(first, WIDE)
                )
        value = jnp.dot(near[...], panel[...], preferred_element_type=F32)
        total[pl.ds(group * GROUP, GROUP)] = value.reshape(GROUP, WIDE, HEIGHT * SIDE)
        return carry

    lax.fori_loop(0, plan_ref[15, 1], step, 0)
    for place in range(ZERO_BLOCK):
        member, slot = out_place(place)
        column = plan_ref[8, member * (128 // HEIGHT) + slot]
        out_ref[place] = total[column, :, pl.ds(member * SIDE, SIDE)]


def own_sums(lists, whole):
    flops = 2 * 32 * WIDE * (HEIGHT * SIDE) ** 2
    return pl.pallas_call(
        own_kernel,
        out_shape=jax.ShapeDtypeStruct((ZERO_BLOCK, WIDE, SIDE), F32),
        in_specs=[smem(), vmem()],
        out_specs=vmem(),
        scratch_shapes=[
            pltpu.VMEM((OUT_COLS, WIDE, HEIGHT * SIDE), F32),
            pltpu.VMEM((HEIGHT * SIDE, HEIGHT * SIDE), BF),
            pltpu.VMEM((GROUP * WIDE, HEIGHT * SIDE), BF),
        ],
        compiler_params=params(),
        cost_estimate=cost(flops, 3 * ZERO_BLOCK * SIDE * SIDE),
        name="own_sums",
    )(lists, whole)


def far_kernel(
    own_ref,
    plan_ref,
    whole_ref,
    near_ref,
    position_ref,
    *refs,
):
    *out_refs, low, high, pieces_ref = refs[TARGETS:]
    halves = (low, high)
    for (along_x, across), far_ref in zip(((0, 0),) + ORDER_X, refs):
        sender = ((position_ref[0] - along_x) & (NX - 1)) * NC + ((position_ref[2] + across) & 1)
        rows = pl.ds(pl.multiple_of(sender * CAP_X, 8), CAP_X)
        for part in range(NY):
            lanes = slice(part * SIDE, (part + 1) * SIDE)
            pieces_ref[part, rows, :] = far_ref[:, lanes].astype(F32)

    def clear(group, carry):
        for total in halves:
            total[pl.ds(group * GROUP, GROUP)] = jnp.zeros((GROUP, WIDE, 2 * SIDE), F32)
        return carry

    lax.fori_loop(0, own_ref[15, 1], clear, 0)

    def add_product(step):
        begin = plan_ref[2, step]
        length = plan_ref[3, step]
        pieces, columns = [], []
        for at in range(FAR_GROUP):
            place = jnp.minimum(begin + at, CAP_X - 1)
            rows = pl.ds(plan_ref[0, place], TARGETS, stride=CAP_X)
            for part in range(NY):
                pieces.append(pieces_ref[part, rows, :])
            columns.append(jnp.where(at < length, plan_ref[1, place], OUT_COLS))
        left = jnp.concatenate(pieces, axis=0).astype(BF)
        for half, total in enumerate(halves):
            right = jnp.concatenate(
                [
                    own_block(whole_ref, plan_ref[4 + 2 * half + at, step], pl.ds(0, SIDE))
                    for at in range(2)
                ],
                axis=1,
            )
            value = jnp.dot(left, right, preferred_element_type=F32)
            before = [total[column] for column in columns]
            for at, column in enumerate(columns):
                total[column] = before[at] + value[at * WIDE : (at + 1) * WIDE]

    def steps(number, carry):
        for at in range(STEPS_AT_ONCE):
            add_product(number * STEPS_AT_ONCE + at)
        return carry

    lax.fori_loop(0, (plan_ref[8, 0] + STEPS_AT_ONCE - 1) // STEPS_AT_ONCE, steps, 0)

    for step, out_ref in enumerate(out_refs):
        part = (own_ref[15, 0] + step) & (NY - 1)
        for place in range(HEIGHT * QUARTER):
            member, slot = place // QUARTER, part * QUARTER + place % QUARTER
            column = own_ref[8, member * (128 // HEIGHT) + slot]
            value = halves[member // 2][column, :, pl.ds(member % 2 * SIDE, SIDE)]
            value = value + near_ref[part * (HEIGHT * QUARTER) + place]
            out_ref[place] = value.astype(BF)


def far_sums(own_lists, far_lists, whole, near, position, far):
    return pl.pallas_call(
        far_kernel,
        out_shape=[jax.ShapeDtypeStruct((HEIGHT * QUARTER, WIDE, SIDE), BF)] * NY,
        in_specs=[smem(), smem(), vmem(), vmem(), smem()] + [vmem()] * TARGETS,
        out_specs=[vmem()] * NY,
        scratch_shapes=[
            pltpu.VMEM((OUT_COLS + 1, WIDE, 2 * SIDE), F32),
            pltpu.VMEM((OUT_COLS + 1, WIDE, 2 * SIDE), F32),
            pltpu.VMEM((NY, TARGETS * CAP_X, SIDE), F32),
        ],
        compiler_params=params(),
        name="far_sums",
    )(own_lists, far_lists, whole, near, position, *far)


def finish_kernel(position_ref, *refs):
    *cut_refs, out_ref = refs
    at = dict(zip((0,) + ORDER_Y, cut_refs))
    for part in range(NY):

        @pl.when(position_ref[3] == part)
        def _():
            order = [at[(part - sender) % NY] for sender in range(NY)]
            for row in range(HEIGHT):
                for slot in range(QUARTER):
                    cuts = [ref[row * QUARTER + slot] for ref in order]
                    out_ref[row, slot] = jnp.concatenate(cuts, axis=0).T


def finish(position, cuts):
    return pl.pallas_call(
        finish_kernel,
        out_shape=jax.ShapeDtypeStruct((HEIGHT, QUARTER, SIDE, SIDE), BF),
        in_specs=[smem()] + [vmem()] * NY,
        out_specs=vmem(),
        compiler_params=params(),
        name="finish",
    )(position, *cuts)


def iota(shape, axis):
    return lax.broadcasted_iota(I32, shape, axis)


def dot(a, b):
    return jnp.dot(a.astype(BF), b.astype(BF), preferred_element_type=F32)


def dot_rows(a, b):
    return lax.dot_general(
        a.astype(BF), b.astype(BF), (((1,), (1,)), ((), ())), preferred_element_type=F32
    )


def earlier(size):
    return (iota((size, size), 0) < iota((size, size), 1)).astype(F32)


def places(need):
    order = earlier(SIDE)
    parts = []
    before = jnp.zeros((need.shape[0], 1), F32)
    for begin in range(0, need.shape[1], SIDE):
        part = need[:, begin : begin + SIDE]
        parts.append(dot(part, order) + before)
        before = before + jnp.sum(part, axis=1, keepdims=True)
    return jnp.concatenate(parts, axis=1)


def codes(need, capacity):
    place = places(need)
    return jnp.where((need > 0) & (place < capacity), place, -1.0)


def one_hot(code, rows):
    number = iota((rows, code.shape[1]), 0).astype(F32).astype(BF)
    return jnp.where(number == code.astype(BF), jnp.ones((), BF), jnp.zeros((), BF))


def quarter_of(slot):
    return sum((slot >= bound * QUARTER).astype(I32) for bound in range(1, NY))


def pattern_kernel(position_ref, columns_ref, entries_ref, slots_ref, union_ref, need_ref, kq_ref):
    step = 64
    for begin in range(0, ROWS, step):
        column = iota((step, ROWS), 1)
        found = jnp.full((step, ROWS), -1, I32)
        for slot in range(SLOTS):
            at = columns_ref[begin : begin + step, slot : slot + 1]
            found = jnp.where(at == column, slot, found)
        slots_ref[begin : begin + step, :] = found
    names = (slots_ref[...] >= 0).astype(F32)
    mine = iota((128, ROWS), 1) // HEIGHT == iota((128, ROWS), 0)
    union = (dot(mine.astype(F32), names) > 0).astype(F32)
    union_ref[...] = union

    entry = iota((1, ENTRIES), 1)
    peer, number = entry // HELD, entry % HELD
    x, core = (peer // NC) % NX, peer % NC
    row = ((x * NZ + position_ref[1]) * NC + core) * HEIGHT + quarter_of(number)
    column = entries_ref[...]
    every = iota((ROWS, ENTRIES), 0)
    named = dot(jnp.where(mine, 0.0, union), (every == row).astype(F32))
    need_ref[...] = named * dot(union, (every == column).astype(F32))
    kind = iota((8, ENTRIES), 0)
    both = jnp.where(kind == 1, jnp.maximum(column, 0), 0)
    kq_ref[...] = jnp.where(kind == 0, row, both).astype(F32)


def pattern(position, columns, entries):
    return pl.pallas_call(
        pattern_kernel,
        out_shape=(
            jax.ShapeDtypeStruct((ROWS, ROWS), I32),
            jax.ShapeDtypeStruct((128, ROWS), F32),
            jax.ShapeDtypeStruct((128, ENTRIES), F32),
            jax.ShapeDtypeStruct((8, ENTRIES), F32),
        ),
        in_specs=[smem(), vmem(), vmem()],
        out_specs=(vmem(), vmem(), vmem(), vmem()),
        compiler_params=params(),
        cost_estimate=cost(2 * SLOTS * ROWS**3 // 4, 8 * ROWS**2),
        name="pattern",
    )(position, columns, entries)


def send_kernel(position_ref, need_ref, kq_ref, near_ref, *refs):
    *out_refs, chosen_ref = refs
    z = position_ref[1]
    near = near_ref[...]
    kind = iota((8, ENTRIES), 0)
    pick = (iota((8, ENTRIES), 1) % HELD == SLOTS + kind) & (kind < 2)
    flags = dot(pick.astype(F32), near)
    flags = jnp.concatenate([flags[0:1], flags[1:2]], axis=1)
    need = need_ref[...] * flags
    slab = iota((8, 128), 1)
    plane = (slab // NC) % NZ == (iota((8, 128), 0) + z) & (NZ - 1)
    wanted = (dot(plane.astype(F32), need) > 0).astype(F32)
    code = codes(wanted, CAP_Z)
    most = jnp.max(jnp.sum(wanted, axis=1, keepdims=True), axis=0, keepdims=True)
    most = jnp.broadcast_to(jnp.minimum(most, 250.0), (1, 128))
    totals = jnp.minimum(dot_rows(jnp.ones((8, ENTRIES), F32), need)[0:1], 250.0)
    for to in range(NZ):
        chosen_ref[to * ROWS_Z : (to + 1) * ROWS_Z, :] = one_hot(code[to : to + 1], ROWS_Z)
    packed = jnp.dot(chosen_ref[...], near, preferred_element_type=F32)
    kq = kq_ref[...]
    line = iota((128, ENTRIES), 0)
    facts = jnp.where(line == SLABS, kq[0:1], jnp.where(line == SLABS + 1, kq[1:2], need))
    facts = jnp.dot(chosen_ref[...], facts.T.astype(BF), preferred_element_type=F32)
    tail = iota((16, PIECE), 0)
    slab = iota((16, 128), 1)
    target = iota((16, 128), 0)
    for to in range(NZ):
        choice = (target // NC * NZ + ((z + to) & (NZ - 1))) * NC + target % NC
        choice = slab == jnp.where(target < TARGETS, choice, SLABS - TARGETS + target)
        notes = dot_rows(choice, facts[to * ROWS_Z : (to + 1) * ROWS_Z])
        first = jnp.concatenate([notes[i : i + 1] for i in range(4)], axis=1)
        second = jnp.concatenate([notes[i : i + 1] for i in range(4, 8)], axis=1)
        third = jnp.concatenate([notes[8:9], notes[9:10], totals, most], axis=1)
        begin = to * ROWS_Z
        out_refs[to][0 : ROWS_Z - 16] = packed[begin : begin + ROWS_Z - 16].astype(BF)
        value = packed[begin + ROWS_Z - 16 : begin + ROWS_Z]
        value = jnp.where(tail == 12, first, value)
        value = jnp.where(tail == 13, second, value)
        value = jnp.where(tail == 14, third, value)
        out_refs[to][ROWS_Z - 16 : ROWS_Z] = value.astype(BF)


def send(position, need, kq, near):
    return pl.pallas_call(
        send_kernel,
        out_shape=[jax.ShapeDtypeStruct((ROWS_Z, PIECE), BF)] * NZ,
        in_specs=[smem()] + [vmem()] * 3,
        out_specs=[vmem()] * NZ,
        scratch_shapes=[pltpu.VMEM((NZ * ROWS_Z, ENTRIES), BF)],
        compiler_params=params(),
        name="send",
    )(position, need, kq, near)


def notes_of(along_refs):
    asked, third = [], []
    for along_ref in along_refs:
        notes = along_ref[ROWS_Z - 16 : ROWS_Z].astype(F32)
        asked.append(
            jnp.concatenate(
                [
                    notes[12 + i // 4 : 13 + i // 4, i % 4 * SIDE : (i % 4 + 1) * SIDE]
                    for i in range(TARGETS)
                ],
                axis=0,
            )
        )
        third.append(notes[14:15])
    return jnp.concatenate(asked, axis=1), third


def route_kernel(position_ref, *refs):
    along_refs, out_refs = refs[:NZ], refs[NZ : NZ + TARGETS]
    chosen_ref, along_ref = refs[NZ + TARGETS :]
    asked, _ = notes_of(along_refs)
    line = iota(asked.shape, 0)
    ordered = []
    for along_x, across in ((0, 0),) + ORDER_X:
        to = ((position_ref[0] + along_x) & (NX - 1)) * NC + ((position_ref[2] + across) & 1)
        ordered.append(jnp.sum(jnp.where(line == to, asked, 0.0), axis=0, keepdims=True))
    asked = jnp.concatenate(ordered, axis=0)
    for number, ref in enumerate(along_refs):
        along_ref[number * ROWS_Z : (number + 1) * ROWS_Z] = ref[...]
    code = codes(asked, CAP_X)
    for to in range(TARGETS):
        chosen_ref[to * SIDE : (to + 1) * SIDE, :] = one_hot(code[to : to + 1], SIDE)
    packed = jnp.dot(chosen_ref[...], along_ref[...], preferred_element_type=F32)
    for to in range(TARGETS):
        out_refs[to][...] = packed[to * SIDE : to * SIDE + CAP_X].astype(BF)


def route(position, along):
    return pl.pallas_call(
        route_kernel,
        out_shape=[jax.ShapeDtypeStruct((CAP_X, PIECE), BF)] * TARGETS,
        in_specs=[smem()] + [vmem()] * NZ,
        out_specs=[vmem()] * TARGETS,
        scratch_shapes=[
            pltpu.VMEM((TARGETS * SIDE, NZ * ROWS_Z), BF),
            pltpu.VMEM((NZ * ROWS_Z, PIECE), BF),
        ],
        compiler_params=params(),
        name="route",
    )(position, *along)


def own_places(position_ref, slots_ref):
    chip = position_ref[0] * NZ + position_ref[1]
    both = slots_ref[pl.ds(pl.multiple_of(chip * HEIGHT_2, HEIGHT_2), HEIGHT_2), :]
    swapped = jnp.concatenate([both[HEIGHT:], both[:HEIGHT]], axis=0)
    slot = jnp.where(position_ref[2] == 0, both, swapped)
    quarter = quarter_of(slot)
    held = (quarter * HEIGHT + iota(slot.shape, 0)) * QUARTER + slot - quarter * QUARTER
    return slot, jnp.where(slot >= 0, held - ZERO_BLOCK, 0).astype(F32)


def own_plan_kernel(position_ref, slots_ref, union_ref, out_ref):
    x, z, core, part = (position_ref[i] for i in range(4))
    slab = (x * NZ + z) * NC + core
    order = earlier(ROWS)
    out_ref[...] = jnp.zeros_like(out_ref)
    mine = union_ref[pl.ds(slab, 1), :]
    rank = dot(jnp.broadcast_to(mine, (8, ROWS)), order)

    slot, held = own_places(position_ref, slots_ref)
    number = iota((OUT_COLS, ROWS), 0).astype(F32)
    chosen = ((rank[0:1] == number) & (mine > 0)).astype(F32)
    out_ref[4:8, 0:OUT_COLS] = dot_rows(held, chosen)[0:HEIGHT].astype(I32) + ZERO_BLOCK
    wide = 128 // HEIGHT
    chosen = jnp.concatenate(
        [slot[i : i + 1] == iota((wide, ROWS), 0) for i in range(HEIGHT)], axis=0
    )
    out_ref[8:9, 0:128] = dot_rows(rank, chosen.astype(F32))[0:1].astype(I32)
    chosen = (iota((8, ROWS), 1) == iota((8, ROWS), 0) + slab * HEIGHT).astype(F32)
    out_ref[9:13, 0:8] = dot_rows(held, chosen)[0:HEIGHT].astype(I32) + ZERO_BLOCK
    groups = ((jnp.sum(mine) + (GROUP - 1)) * (1.0 / GROUP)).astype(I32)
    lane = iota((1, 128), 1)
    scalars = jnp.where(lane == 0, part, 0)
    out_ref[15:16, :] = jnp.where(lane == 1, groups, scalars)


def own_plan(position, slots, union):
    return pl.pallas_call(
        own_plan_kernel,
        out_shape=jax.ShapeDtypeStruct((16, 128), I32),
        in_specs=[smem(), vmem(), vmem()],
        out_specs=vmem(),
        compiler_params=params(),
        cost_estimate=cost(ROWS**3, 4 * ROWS**2),
        name="own_plan",
    )(position, slots, union)


def far_plan_kernel(position_ref, slots_ref, union_ref, *refs):
    *along_refs, out_ref = refs
    x, z, core = (position_ref[i] for i in range(3))
    slab = (x * NZ + z) * NC + core
    out_ref[...] = jnp.zeros_like(out_ref)
    asked, third = notes_of(along_refs)
    mine = iota(asked.shape, 0) == x * NC + core
    asked = jnp.sum(jnp.where(mine, asked, 0.0), axis=0, keepdims=True)
    number = jnp.sum(asked).astype(I32)
    code = codes(jnp.broadcast_to(asked, (8, asked.shape[1])), CAP_X)[0:1]
    chosen = one_hot(code, SIDE).astype(F32)
    row = jnp.concatenate([part[:, :SIDE] for part in third], axis=1)
    column = jnp.concatenate([part[:, SIDE : 2 * SIDE] for part in third], axis=1)
    row_down = jnp.sum(chosen * row, axis=1, keepdims=True).astype(I32)
    column_down = jnp.sum(chosen * column, axis=1, keepdims=True).astype(I32)
    row_along = dot_rows(jnp.broadcast_to(row, (8, row.shape[1])), chosen)[0:1].astype(I32)

    down, along = iota((SIDE, SIDE), 0), iota((SIDE, SIDE), 1)
    less = (row_down < row_along) | ((row_down == row_along) & (down < along))
    order = jnp.sum((less & (down < number)).astype(F32), axis=0, keepdims=True)
    ordered = ((order == down.astype(F32)) & (along < number)).astype(F32)
    position = iota((8, SIDE), 1).astype(F32)
    out_ref[0:1, 0:SIDE] = dot_rows(position, ordered)[0:1].astype(I32)
    names = union_ref[pl.ds(slab, 1), :]
    order = earlier(ROWS)
    rank = dot(jnp.broadcast_to(names, (8, ROWS)), order)
    every = iota((SIDE, ROWS), 1)
    rank = dot_rows(rank, (every == column_down).astype(F32))
    out_ref[1:2, 0:SIDE] = dot_rows(rank, ordered)[0:1].astype(I32)

    valid = iota((SIDE, ROWS), 0) < number
    count = dot(jnp.ones((8, SIDE), F32), ((every == row_down) & valid).astype(F32))
    start = jnp.minimum(dot(count, order), 250.0)[0:1]
    _, held = own_places(position_ref, slots_ref)
    needed = ((count + (FAR_GROUP - 1)) * (1.0 / FAR_GROUP)).astype(I32).astype(F32)
    first = dot(needed, order)[0:1]
    number = iota((SIDE, ROWS), 0).astype(F32)
    chosen = ((first <= number) & (number < first + needed[0:1])).astype(F32)
    kind = iota((8, ROWS), 0)
    values = jnp.where(kind == 0, start, jnp.where(kind == 1, first, count))
    values = dot_rows(values, chosen).astype(I32)
    done = (iota((1, SIDE), 1) - values[1:2]) * FAR_GROUP
    steps = jnp.sum(needed[0:1]).astype(I32)
    valid = iota((1, SIDE), 1) < steps
    out_ref[2:3, :] = jnp.where(valid, values[0:1] + done, 0)
    out_ref[3:4, :] = jnp.where(valid, values[2:3] - done, 0)
    out_ref[4:8, :] = dot_rows(held, chosen)[0:HEIGHT].astype(I32) + ZERO_BLOCK
    out_ref[8:9, :] = jnp.zeros((1, SIDE), I32) + jnp.minimum(steps, SIDE)

    third = functools.reduce(jnp.maximum, third), functools.reduce(jnp.add, third)
    most_z = jnp.max(third[0][:, 3 * SIDE :])
    most_x = jnp.max(third[1][:, 2 * SIDE : 3 * SIDE])
    fits = (most_x <= CAP_X) & (most_z <= CAP_Z)
    out_ref[9:10, :] = jnp.zeros((1, SIDE), I32) + fits.astype(I32)


def far_plan(position, slots, union, along):
    return pl.pallas_call(
        far_plan_kernel,
        out_shape=jax.ShapeDtypeStruct((16, 128), I32),
        in_specs=[smem()] + [vmem()] * (2 + NZ),
        out_specs=vmem(),
        compiler_params=params(),
        cost_estimate=cost(2 * 20 * ROWS**3, 8 * ROWS**2),
        name="far_plan",
    )(position, slots, union, *along)


def dense(blocks, nonzero, columns):
    slab = lax.axis_index(ROW_AXES)
    part = lax.axis_index("col")
    masked = blocks * nonzero[:, :, None, None].astype(BF)
    slab_ids = jnp.arange(SLABS, dtype=I32)
    local_rows = jnp.arange(HEIGHT, dtype=I32)
    grouped = columns.reshape(SLABS, HEIGHT * SLOTS)
    targets = slab * HEIGHT + local_rows
    wanted = jnp.any(grouped[:, :, None] == targets[None, None, :], axis=1)
    wanted = wanted & (slab_ids != slab)[:, None]
    picked = jnp.sum(jnp.where(wanted, local_rows, 0), axis=1)
    filled = jnp.any(wanted, axis=1)
    outgoing = jnp.where(filled[:, None, None, None], masked[picked], jnp.zeros((), BF))
    incoming = lax.all_to_all(outgoing, ROW_AXES, split_axis=0, concat_axis=0, tiled=True)
    row_table = jnp.concatenate([incoming, masked], axis=0)
    own_cols = lax.dynamic_slice_in_dim(columns, slab * HEIGHT, HEIGHT, 0)
    source = own_cols // HEIGHT
    row_index = jnp.where(source == slab, SLABS + own_cols % HEIGHT, source)
    far_cols = columns[own_cols]
    far_quarter = lax.dynamic_slice_in_dim(far_cols, part * QUARTER, QUARTER, 2)
    whole = lax.all_gather(masked, "col", axis=1, tiled=True)
    results = []
    for member in range(HEIGHT):
        match = far_quarter[member][:, :, None] == own_cols[member][None, None, :]
        products = jnp.einsum(
            "tab,tubc->tuac", whole[member], row_table[row_index[member]],
            preferred_element_type=F32,
        )
        summed = lax.dot_general(
            match.astype(F32).reshape(SLOTS * QUARTER, SLOTS),
            products.reshape(SLOTS * QUARTER, SIDE * SIDE),
            (((0,), (0,)), ((), ())),
            precision=lax.Precision.HIGHEST,
            preferred_element_type=F32,
        )
        results.append(summed.reshape(SLOTS, SIDE, SIDE))
    square = lax.psum_scatter(jnp.stack(results), "col", scatter_dimension=1, tiled=True)
    return square.astype(BF)


def plane_columns(columns):
    split = columns.reshape(NX, NZ, NC, HEIGHT, NY, QUARTER)
    mine = lax.dynamic_index_in_dim(split, lax.axis_index("z"), 1, keepdims=False)
    mine = mine.transpose(3, 0, 1, 2, 4).reshape(PEERS, SLOTS)
    return jnp.pad(mine, ((0, 0), (0, HELD - SLOTS)), constant_values=-1).reshape(1, ENTRIES)


def shards(blocks, nonzero, columns):
    position = jnp.stack([lax.axis_index(name) for name in ROW_AXES + ("col",)])
    cuts = prepare(position, nonzero, blocks)
    cuts, names, same = lax.optimization_barrier((cuts, columns, blocks))
    turned = turn(nonzero, same)
    slots, union, need, kq = pattern(position, names, plane_columns(columns))
    near = lax.all_to_all(cuts, ("col", "x", "core"), split_axis=0, concat_axis=0, tiled=True)
    near, turned, need = lax.optimization_barrier((near, turned, need))
    whole = lax.all_gather(turned, "col", axis=0, tiled=False)
    whole = whole.reshape(ZERO_BLOCK, SIDE, SIDE)
    packed = send(position, need, kq, near.reshape(ENTRIES, PIECE))
    packed, slots = lax.optimization_barrier((packed, slots))
    along = [packed[0]] + [
        lax.ppermute(packed[step], "z", [(i, (i + step) % NZ) for i in range(NZ)])
        for step in ORDER_Z
    ]
    own_lists = own_plan(position, slots, union)
    along, own_lists = lax.optimization_barrier((along, own_lists))
    packed, notes = lax.optimization_barrier((route(position, along), along))
    far = [packed[0]]
    for number, (along_x, across) in enumerate(ORDER_X):
        pairs = [
            (i, ((i // NC + along_x) % NX) * NC + (i + across) % NC) for i in range(TARGETS)
        ]
        far.append(lax.ppermute(packed[1 + number], ("x", "core"), pairs))
    notes, whole = lax.optimization_barrier((notes, whole))
    far_lists = far_plan(position, slots, union, notes)
    own = own_sums(own_lists, whole)
    far, own = lax.optimization_barrier((far, own))
    result = far_sums(own_lists, far_lists, whole, own, position, far)
    cuts = [result[0]]
    for step in ORDER_Y:
        pairs = [(i, (i + step) % NY) for i in range(NY)]
        cuts.append(lax.ppermute(result[step], "col", pairs))
    square = finish(position, cuts)
    return lax.cond(
        far_lists[9, 0] != 0,
        lambda value, *_: value,
        lambda _, *inputs: dense(*inputs),
        square,
        blocks,
        nonzero,
        columns,
    )


def solution(mesh):
    fine = Mesh(mesh.devices.reshape(NX, NZ, NC, NY), ROW_AXES + ("col",))
    spec = P(ROW_AXES, "col", None, None)
    return jax.shard_map(
        shards,
        mesh=fine,
        in_specs=(spec, P(ROW_AXES, "col"), P()),
        out_specs=spec,
        check_vma=False,
    )
```

```python
import functools

import jax
import jax.numpy as jnp
from jax import lax
from jax.experimental import pallas as pl
from jax.experimental.pallas import tpu as pltpu
from jax.sharding import Mesh
from jax.sharding import PartitionSpec as P

BF = jnp.bfloat16
F32 = jnp.float32
I32 = jnp.int32

NX, NZ, NC, NY = 4, 8, 2, 4
ROWS, SLOTS, SIDE = 256, 28, 128
HEIGHT, QUARTER = 4, 7
SLABS = ROWS // HEIGHT
PEERS = NX * NC * NY
HELD = 32
ENTRIES = PEERS * HELD
PIECE = SIDE * SIDE // PEERS
WIDE = SIDE // NY
TARGETS = NX * NC
CAP_Z = 124
ROWS_Z = 128
CAP_X = 120
ORDER_Z = (4, 3, 5, 2, 6, 1, 7)
ORDER_Y = (2, 1, 3)
ORDER_X = ((2, 0), (2, 1), (1, 0), (3, 0), (1, 1), (3, 1), (0, 1))
GROUP = 8
FAR_GROUP = 3
STEPS_AT_ONCE = 8
HEIGHT_2 = NC * HEIGHT
OUT_COLS = 72
ZERO_BLOCK = NY * HEIGHT * QUARTER
VMEM_LIMIT = 48 * 1024 * 1024
ROW_AXES = ("x", "z", "core")


def vmem():
    return pl.BlockSpec(memory_space=pltpu.VMEM)


def smem():
    return pl.BlockSpec(memory_space=pltpu.SMEM)


def params():
    return pltpu.CompilerParams(vmem_limit_bytes=VMEM_LIMIT)


def cost(flops, moved):
    return pl.CostEstimate(flops=flops, bytes_accessed=moved, transcendentals=0)


def prepare_kernel(position_ref, keep_ref, blocks_ref, cuts_ref, rows_ref):
    x, core, part = position_ref[0], position_ref[2], position_ref[3]
    lanes = iota((8, ENTRIES), 1) - ((part * NX + x) * NC + core) * HELD
    flags = jnp.zeros((8, ENTRIES), F32)
    for row in range(HEIGHT):
        for slot in range(QUARTER):
            number = row * QUARTER + slot
            keep = keep_ref[row, slot] != 0
            flags = jnp.where((lanes == number) & keep, 1.0, flags)
            block = blocks_ref[row, slot].astype(F32)
            rows_ref[number] = jnp.where(keep, block, jnp.zeros_like(block)).T
    for part_of in range(NY):
        for extra in range(HELD - SLOTS):
            at = extra * PIECE + part_of * SIDE
            value = flags[:, at : at + SIDE] if extra < 2 else jnp.zeros((8, SIDE), F32)
            for quarter in range(NY):
                begin = quarter * WIDE + part_of * TARGETS
                rows_ref[SLOTS + extra, begin : begin + TARGETS] = value
    for quarter in range(NY):
        peers = slice(quarter * TARGETS, (quarter + 1) * TARGETS)
        for part_of in range(NY):
            begin = quarter * WIDE + part_of * TARGETS
            for half in range(0, HELD, 16):
                rows = rows_ref[half : half + 16, begin : begin + TARGETS]
                cuts_ref[peers, half : half + 16, part_of * SIDE : (part_of + 1) * SIDE] = (
                    jnp.swapaxes(rows, 0, 1).astype(BF)
                )


def prepare(position, nonzero, blocks):
    return pl.pallas_call(
        prepare_kernel,
        out_shape=jax.ShapeDtypeStruct((PEERS, HELD, PIECE), BF),
        in_specs=[smem(), smem(), vmem()],
        out_specs=vmem(),
        scratch_shapes=[pltpu.VMEM((HELD, SIDE, SIDE), F32)],
        compiler_params=params(),
        name="prepare",
    )(position, nonzero, blocks)


def turn_kernel(keep_ref, blocks_ref, out_ref):
    for row in range(HEIGHT):
        for slot in range(QUARTER):
            block = blocks_ref[row, slot]
            out_ref[row, slot] = jnp.where(
                keep_ref[row, slot] != 0, block, jnp.zeros_like(block)
            ).T


def turn(nonzero, blocks):
    return pl.pallas_call(
        turn_kernel,
        out_shape=jax.ShapeDtypeStruct((HEIGHT, QUARTER, SIDE, SIDE), BF),
        in_specs=[smem(), vmem()],
        out_specs=vmem(),
        compiler_params=params(),
        cost_estimate=cost(2 * SLOTS * SIDE**3, 4 * SLOTS * SIDE**2),
        name="turn",
    )(nonzero, blocks)


def own_block(whole_ref, place, rows):
    value = whole_ref[jnp.minimum(place, ZERO_BLOCK - 1), rows, :]
    return jnp.where(place < ZERO_BLOCK, value, jnp.zeros_like(value))


def out_place(place):
    return (place // QUARTER) % HEIGHT, place // (QUARTER * HEIGHT) * QUARTER + place % QUARTER


def own_kernel(
    plan_ref,
    whole_ref,
    out_ref,
    total,
    panel,
    near,
):
    first = pl.multiple_of(plan_ref[15, 0] * WIDE, WIDE)
    for inner in range(HEIGHT):
        for member in range(HEIGHT):
            panel[pl.ds(inner * SIDE, SIDE), pl.ds(member * SIDE, SIDE)] = own_block(
                whole_ref, plan_ref[9 + member, inner], pl.ds(0, SIDE)
            )

    def step(group, carry):
        for at in range(GROUP):
            for inner in range(HEIGHT):
                near[pl.ds(at * WIDE, WIDE), pl.ds(inner * SIDE, SIDE)] = own_block(
                    whole_ref, plan_ref[4 + inner, group * GROUP + at], pl.ds(first, WIDE)
                )
        value = jnp.dot(near[...], panel[...], preferred_element_type=F32)
        total[pl.ds(group * GROUP, GROUP)] = value.reshape(GROUP, WIDE, HEIGHT * SIDE)
        return carry

    lax.fori_loop(0, plan_ref[15, 1], step, 0)
    for place in range(ZERO_BLOCK):
        member, slot = out_place(place)
        column = plan_ref[8, member * (128 // HEIGHT) + slot]
        out_ref[place] = total[column, :, pl.ds(member * SIDE, SIDE)]


def own_sums(lists, whole):
    flops = 2 * 32 * WIDE * (HEIGHT * SIDE) ** 2
    return pl.pallas_call(
        own_kernel,
        out_shape=jax.ShapeDtypeStruct((ZERO_BLOCK, WIDE, SIDE), F32),
        in_specs=[smem(), vmem()],
        out_specs=vmem(),
        scratch_shapes=[
            pltpu.VMEM((OUT_COLS, WIDE, HEIGHT * SIDE), F32),
            pltpu.VMEM((HEIGHT * SIDE, HEIGHT * SIDE), BF),
            pltpu.VMEM((GROUP * WIDE, HEIGHT * SIDE), BF),
        ],
        compiler_params=params(),
        cost_estimate=cost(flops, 3 * ZERO_BLOCK * SIDE * SIDE),
        name="own_sums",
    )(lists, whole)


def far_kernel(
    own_ref,
    plan_ref,
    whole_ref,
    near_ref,
    position_ref,
    *refs,
):
    *out_refs, low, high, pieces_ref = refs[TARGETS:]
    halves = (low, high)
    for (along_x, across), far_ref in zip(((0, 0),) + ORDER_X, refs):
        sender = ((position_ref[0] - along_x) & (NX - 1)) * NC + ((position_ref[2] + across) & 1)
        rows = pl.ds(pl.multiple_of(sender * CAP_X, 8), CAP_X)
        for part in range(NY):
            lanes = slice(part * SIDE, (part + 1) * SIDE)
            pieces_ref[part, rows, :] = far_ref[:, lanes].astype(F32)

    def clear(group, carry):
        for total in halves:
            total[pl.ds(group * GROUP, GROUP)] = jnp.zeros((GROUP, WIDE, 2 * SIDE), F32)
        return carry

    lax.fori_loop(0, own_ref[15, 1], clear, 0)

    def add_product(step):
        begin = plan_ref[2, step]
        length = plan_ref[3, step]
        pieces, columns = [], []
        for at in range(FAR_GROUP):
            place = jnp.minimum(begin + at, CAP_X - 1)
            rows = pl.ds(plan_ref[0, place], TARGETS, stride=CAP_X)
            for part in range(NY):
                pieces.append(pieces_ref[part, rows, :])
            columns.append(jnp.where(at < length, plan_ref[1, place], OUT_COLS))
        left = jnp.concatenate(pieces, axis=0).astype(BF)
        for half, total in enumerate(halves):
            right = jnp.concatenate(
                [
                    own_block(whole_ref, plan_ref[4 + 2 * half + at, step], pl.ds(0, SIDE))
                    for at in range(2)
                ],
                axis=1,
            )
            value = jnp.dot(left, right, preferred_element_type=F32)
            before = [total[column] for column in columns]
            for at, column in enumerate(columns):
                total[column] = before[at] + value[at * WIDE : (at + 1) * WIDE]

    def steps(number, carry):
        for at in range(STEPS_AT_ONCE):
            add_product(number * STEPS_AT_ONCE + at)
        return carry

    lax.fori_loop(0, (plan_ref[8, 0] + STEPS_AT_ONCE - 1) // STEPS_AT_ONCE, steps, 0)

    for step, out_ref in enumerate(out_refs):
        part = (own_ref[15, 0] + step) & (NY - 1)
        for place in range(HEIGHT * QUARTER):
            member, slot = place // QUARTER, part * QUARTER + place % QUARTER
            column = own_ref[8, member * (128 // HEIGHT) + slot]
            value = halves[member // 2][column, :, pl.ds(member % 2 * SIDE, SIDE)]
            value = value + near_ref[part * (HEIGHT * QUARTER) + place]
            out_ref[place] = value.astype(BF)


def far_sums(own_lists, far_lists, whole, near, position, far):
    return pl.pallas_call(
        far_kernel,
        out_shape=[jax.ShapeDtypeStruct((HEIGHT * QUARTER, WIDE, SIDE), BF)] * NY,
        in_specs=[smem(), smem(), vmem(), vmem(), smem()] + [vmem()] * TARGETS,
        out_specs=[vmem()] * NY,
        scratch_shapes=[
            pltpu.VMEM((OUT_COLS + 1, WIDE, 2 * SIDE), F32),
            pltpu.VMEM((OUT_COLS + 1, WIDE, 2 * SIDE), F32),
            pltpu.VMEM((NY, TARGETS * CAP_X, SIDE), F32),
        ],
        compiler_params=params(),
        name="far_sums",
    )(own_lists, far_lists, whole, near, position, *far)


def finish_kernel(position_ref, *refs):
    *cut_refs, out_ref = refs
    at = dict(zip((0,) + ORDER_Y, cut_refs))
    for part in range(NY):

        @pl.when(position_ref[3] == part)
        def _():
            order = [at[(part - sender) % NY] for sender in range(NY)]
            for row in range(HEIGHT):
                for slot in range(QUARTER):
                    cuts = [ref[row * QUARTER + slot] for ref in order]
                    out_ref[row, slot] = jnp.concatenate(cuts, axis=0).T


def finish(position, cuts):
    return pl.pallas_call(
        finish_kernel,
        out_shape=jax.ShapeDtypeStruct((HEIGHT, QUARTER, SIDE, SIDE), BF),
        in_specs=[smem()] + [vmem()] * NY,
        out_specs=vmem(),
        compiler_params=params(),
        name="finish",
    )(position, *cuts)


def iota(shape, axis):
    return lax.broadcasted_iota(I32, shape, axis)


def dot(a, b):
    return jnp.dot(a.astype(BF), b.astype(BF), preferred_element_type=F32)


def dot_rows(a, b):
    return lax.dot_general(
        a.astype(BF), b.astype(BF), (((1,), (1,)), ((), ())), preferred_element_type=F32
    )


def earlier(size):
    return (iota((size, size), 0) < iota((size, size), 1)).astype(F32)


def places(need):
    order = earlier(SIDE)
    parts = []
    before = jnp.zeros((need.shape[0], 1), F32)
    for begin in range(0, need.shape[1], SIDE):
        part = need[:, begin : begin + SIDE]
        parts.append(dot(part, order) + before)
        before = before + jnp.sum(part, axis=1, keepdims=True)
    return jnp.concatenate(parts, axis=1)


def codes(need, capacity):
    place = places(need)
    return jnp.where((need > 0) & (place < capacity), place, -1.0)


def one_hot(code, rows):
    number = iota((rows, code.shape[1]), 0).astype(F32).astype(BF)
    return jnp.where(number == code.astype(BF), jnp.ones((), BF), jnp.zeros((), BF))


def quarter_of(slot):
    return sum((slot >= bound * QUARTER).astype(I32) for bound in range(1, NY))


def pattern_kernel(position_ref, columns_ref, entries_ref, slots_ref, union_ref, need_ref, kq_ref):
    step = 64
    for begin in range(0, ROWS, step):
        column = iota((step, ROWS), 1)
        found = jnp.full((step, ROWS), -1, I32)
        for slot in range(SLOTS):
            at = columns_ref[begin : begin + step, slot : slot + 1]
            found = jnp.where(at == column, slot, found)
        slots_ref[begin : begin + step, :] = found
    names = (slots_ref[...] >= 0).astype(F32)
    mine = iota((128, ROWS), 1) // HEIGHT == iota((128, ROWS), 0)
    union = (dot(mine.astype(F32), names) > 0).astype(F32)
    union_ref[...] = union

    entry = iota((1, ENTRIES), 1)
    peer, number = entry // HELD, entry % HELD
    x, core = (peer // NC) % NX, peer % NC
    row = ((x * NZ + position_ref[1]) * NC + core) * HEIGHT + quarter_of(number)
    column = entries_ref[...]
    every = iota((ROWS, ENTRIES), 0)
    named = dot(jnp.where(mine, 0.0, union), (every == row).astype(F32))
    need_ref[...] = named * dot(union, (every == column).astype(F32))
    kind = iota((8, ENTRIES), 0)
    both = jnp.where(kind == 1, jnp.maximum(column, 0), 0)
    kq_ref[...] = jnp.where(kind == 0, row, both).astype(F32)


def pattern(position, columns, entries):
    return pl.pallas_call(
        pattern_kernel,
        out_shape=(
            jax.ShapeDtypeStruct((ROWS, ROWS), I32),
            jax.ShapeDtypeStruct((128, ROWS), F32),
            jax.ShapeDtypeStruct((128, ENTRIES), F32),
            jax.ShapeDtypeStruct((8, ENTRIES), F32),
        ),
        in_specs=[smem(), vmem(), vmem()],
        out_specs=(vmem(), vmem(), vmem(), vmem()),
        compiler_params=params(),
        cost_estimate=cost(2 * SLOTS * ROWS**3 // 4, 8 * ROWS**2),
        name="pattern",
    )(position, columns, entries)


def send_kernel(position_ref, need_ref, kq_ref, near_ref, *refs):
    *out_refs, chosen_ref = refs
    z = position_ref[1]
    near = near_ref[...]
    kind = iota((8, ENTRIES), 0)
    pick = (iota((8, ENTRIES), 1) % HELD == SLOTS + kind) & (kind < 2)
    flags = dot(pick.astype(F32), near)
    flags = jnp.concatenate([flags[0:1], flags[1:2]], axis=1)
    need = need_ref[...] * flags
    slab = iota((8, 128), 1)
    plane = (slab // NC) % NZ == (iota((8, 128), 0) + z) & (NZ - 1)
    wanted = (dot(plane.astype(F32), need) > 0).astype(F32)
    code = codes(wanted, CAP_Z)
    most = jnp.max(jnp.sum(wanted, axis=1, keepdims=True), axis=0, keepdims=True)
    most = jnp.broadcast_to(jnp.minimum(most, 250.0), (1, 128))
    totals = jnp.minimum(dot_rows(jnp.ones((8, ENTRIES), F32), need)[0:1], 250.0)
    for to in range(NZ):
        chosen_ref[to * ROWS_Z : (to + 1) * ROWS_Z, :] = one_hot(code[to : to + 1], ROWS_Z)
    packed = jnp.dot(chosen_ref[...], near, preferred_element_type=F32)
    kq = kq_ref[...]
    line = iota((128, ENTRIES), 0)
    facts = jnp.where(line == SLABS, kq[0:1], jnp.where(line == SLABS + 1, kq[1:2], need))
    facts = jnp.dot(chosen_ref[...], facts.T.astype(BF), preferred_element_type=F32)
    tail = iota((16, PIECE), 0)
    slab = iota((16, 128), 1)
    target = iota((16, 128), 0)
    for to in range(NZ):
        choice = (target // NC * NZ + ((z + to) & (NZ - 1))) * NC + target % NC
        choice = slab == jnp.where(target < TARGETS, choice, SLABS - TARGETS + target)
        notes = dot_rows(choice, facts[to * ROWS_Z : (to + 1) * ROWS_Z])
        first = jnp.concatenate([notes[i : i + 1] for i in range(4)], axis=1)
        second = jnp.concatenate([notes[i : i + 1] for i in range(4, 8)], axis=1)
        third = jnp.concatenate([notes[8:9], notes[9:10], totals, most], axis=1)
        begin = to * ROWS_Z
        out_refs[to][0 : ROWS_Z - 16] = packed[begin : begin + ROWS_Z - 16].astype(BF)
        value = packed[begin + ROWS_Z - 16 : begin + ROWS_Z]
        value = jnp.where(tail == 12, first, value)
        value = jnp.where(tail == 13, second, value)
        value = jnp.where(tail == 14, third, value)
        out_refs[to][ROWS_Z - 16 : ROWS_Z] = value.astype(BF)


def send(position, need, kq, near):
    return pl.pallas_call(
        send_kernel,
        out_shape=[jax.ShapeDtypeStruct((ROWS_Z, PIECE), BF)] * NZ,
        in_specs=[smem()] + [vmem()] * 3,
        out_specs=[vmem()] * NZ,
        scratch_shapes=[pltpu.VMEM((NZ * ROWS_Z, ENTRIES), BF)],
        compiler_params=params(),
        name="send",
    )(position, need, kq, near)


def notes_of(along_refs):
    asked, third = [], []
    for along_ref in along_refs:
        notes = along_ref[ROWS_Z - 16 : ROWS_Z].astype(F32)
        asked.append(
            jnp.concatenate(
                [
                    notes[12 + i // 4 : 13 + i // 4, i % 4 * SIDE : (i % 4 + 1) * SIDE]
                    for i in range(TARGETS)
                ],
                axis=0,
            )
        )
        third.append(notes[14:15])
    return jnp.concatenate(asked, axis=1), third


def route_kernel(position_ref, *refs):
    along_refs, out_refs = refs[:NZ], refs[NZ : NZ + TARGETS]
    chosen_ref, along_ref = refs[NZ + TARGETS :]
    asked, _ = notes_of(along_refs)
    line = iota(asked.shape, 0)
    ordered = []
    for along_x, across in ((0, 0),) + ORDER_X:
        to = ((position_ref[0] + along_x) & (NX - 1)) * NC + ((position_ref[2] + across) & 1)
        ordered.append(jnp.sum(jnp.where(line == to, asked, 0.0), axis=0, keepdims=True))
    asked = jnp.concatenate(ordered, axis=0)
    for number, ref in enumerate(along_refs):
        along_ref[number * ROWS_Z : (number + 1) * ROWS_Z] = ref[...]
    code = codes(asked, CAP_X)
    for to in range(TARGETS):
        chosen_ref[to * SIDE : (to + 1) * SIDE, :] = one_hot(code[to : to + 1], SIDE)
    packed = jnp.dot(chosen_ref[...], along_ref[...], preferred_element_type=F32)
    for to in range(TARGETS):
        out_refs[to][...] = packed[to * SIDE : to * SIDE + CAP_X].astype(BF)


def route(position, along):
    return pl.pallas_call(
        route_kernel,
        out_shape=[jax.ShapeDtypeStruct((CAP_X, PIECE), BF)] * TARGETS,
        in_specs=[smem()] + [vmem()] * NZ,
        out_specs=[vmem()] * TARGETS,
        scratch_shapes=[
            pltpu.VMEM((TARGETS * SIDE, NZ * ROWS_Z), BF),
            pltpu.VMEM((NZ * ROWS_Z, PIECE), BF),
        ],
        compiler_params=params(),
        name="route",
    )(position, *along)


def own_places(position_ref, slots_ref):
    chip = position_ref[0] * NZ + position_ref[1]
    both = slots_ref[pl.ds(pl.multiple_of(chip * HEIGHT_2, HEIGHT_2), HEIGHT_2), :]
    swapped = jnp.concatenate([both[HEIGHT:], both[:HEIGHT]], axis=0)
    slot = jnp.where(position_ref[2] == 0, both, swapped)
    quarter = quarter_of(slot)
    held = (quarter * HEIGHT + iota(slot.shape, 0)) * QUARTER + slot - quarter * QUARTER
    return slot, jnp.where(slot >= 0, held - ZERO_BLOCK, 0).astype(F32)


def own_plan_kernel(position_ref, slots_ref, union_ref, out_ref):
    x, z, core, part = (position_ref[i] for i in range(4))
    slab = (x * NZ + z) * NC + core
    order = earlier(ROWS)
    out_ref[...] = jnp.zeros_like(out_ref)
    mine = union_ref[pl.ds(slab, 1), :]
    rank = dot(jnp.broadcast_to(mine, (8, ROWS)), order)

    slot, held = own_places(position_ref, slots_ref)
    number = iota((OUT_COLS, ROWS), 0).astype(F32)
    chosen = ((rank[0:1] == number) & (mine > 0)).astype(F32)
    out_ref[4:8, 0:OUT_COLS] = dot_rows(held, chosen)[0:HEIGHT].astype(I32) + ZERO_BLOCK
    wide = 128 // HEIGHT
    chosen = jnp.concatenate(
        [slot[i : i + 1] == iota((wide, ROWS), 0) for i in range(HEIGHT)], axis=0
    )
    out_ref[8:9, 0:128] = dot_rows(rank, chosen.astype(F32))[0:1].astype(I32)
    chosen = (iota((8, ROWS), 1) == iota((8, ROWS), 0) + slab * HEIGHT).astype(F32)
    out_ref[9:13, 0:8] = dot_rows(held, chosen)[0:HEIGHT].astype(I32) + ZERO_BLOCK
    groups = ((jnp.sum(mine) + (GROUP - 1)) * (1.0 / GROUP)).astype(I32)
    lane = iota((1, 128), 1)
    scalars = jnp.where(lane == 0, part, 0)
    out_ref[15:16, :] = jnp.where(lane == 1, groups, scalars)


def own_plan(position, slots, union):
    return pl.pallas_call(
        own_plan_kernel,
        out_shape=jax.ShapeDtypeStruct((16, 128), I32),
        in_specs=[smem(), vmem(), vmem()],
        out_specs=vmem(),
        compiler_params=params(),
        cost_estimate=cost(ROWS**3, 4 * ROWS**2),
        name="own_plan",
    )(position, slots, union)


def far_plan_kernel(position_ref, slots_ref, union_ref, *refs):
    *along_refs, out_ref = refs
    x, z, core = (position_ref[i] for i in range(3))
    slab = (x * NZ + z) * NC + core
    out_ref[...] = jnp.zeros_like(out_ref)
    asked, third = notes_of(along_refs)
    mine = iota(asked.shape, 0) == x * NC + core
    asked = jnp.sum(jnp.where(mine, asked, 0.0), axis=0, keepdims=True)
    number = jnp.sum(asked).astype(I32)
    code = codes(jnp.broadcast_to(asked, (8, asked.shape[1])), CAP_X)[0:1]
    chosen = one_hot(code, SIDE).astype(F32)
    row = jnp.concatenate([part[:, :SIDE] for part in third], axis=1)
    column = jnp.concatenate([part[:, SIDE : 2 * SIDE] for part in third], axis=1)
    row_down = jnp.sum(chosen * row, axis=1, keepdims=True).astype(I32)
    column_down = jnp.sum(chosen * column, axis=1, keepdims=True).astype(I32)
    row_along = dot_rows(jnp.broadcast_to(row, (8, row.shape[1])), chosen)[0:1].astype(I32)

    down, along = iota((SIDE, SIDE), 0), iota((SIDE, SIDE), 1)
    less = (row_down < row_along) | ((row_down == row_along) & (down < along))
    order = jnp.sum((less & (down < number)).astype(F32), axis=0, keepdims=True)
    ordered = ((order == down.astype(F32)) & (along < number)).astype(F32)
    position = iota((8, SIDE), 1).astype(F32)
    out_ref[0:1, 0:SIDE] = dot_rows(position, ordered)[0:1].astype(I32)
    names = union_ref[pl.ds(slab, 1), :]
    order = earlier(ROWS)
    rank = dot(jnp.broadcast_to(names, (8, ROWS)), order)
    every = iota((SIDE, ROWS), 1)
    rank = dot_rows(rank, (every == column_down).astype(F32))
    out_ref[1:2, 0:SIDE] = dot_rows(rank, ordered)[0:1].astype(I32)

    valid = iota((SIDE, ROWS), 0) < number
    count = dot(jnp.ones((8, SIDE), F32), ((every == row_down) & valid).astype(F32))
    start = jnp.minimum(dot(count, order), 250.0)[0:1]
    _, held = own_places(position_ref, slots_ref)
    needed = ((count + (FAR_GROUP - 1)) * (1.0 / FAR_GROUP)).astype(I32).astype(F32)
    first = dot(needed, order)[0:1]
    number = iota((SIDE, ROWS), 0).astype(F32)
    chosen = ((first <= number) & (number < first + needed[0:1])).astype(F32)
    kind = iota((8, ROWS), 0)
    values = jnp.where(kind == 0, start, jnp.where(kind == 1, first, count))
    values = dot_rows(values, chosen).astype(I32)
    done = (iota((1, SIDE), 1) - values[1:2]) * FAR_GROUP
    steps = jnp.sum(needed[0:1]).astype(I32)
    valid = iota((1, SIDE), 1) < steps
    out_ref[2:3, :] = jnp.where(valid, values[0:1] + done, 0)
    out_ref[3:4, :] = jnp.where(valid, values[2:3] - done, 0)
    out_ref[4:8, :] = dot_rows(held, chosen)[0:HEIGHT].astype(I32) + ZERO_BLOCK
    out_ref[8:9, :] = jnp.zeros((1, SIDE), I32) + jnp.minimum(steps, SIDE)

    third = functools.reduce(jnp.maximum, third), functools.reduce(jnp.add, third)
    most_z = jnp.max(third[0][:, 3 * SIDE :])
    most_x = jnp.max(third[1][:, 2 * SIDE : 3 * SIDE])
    fits = (most_x <= CAP_X) & (most_z <= CAP_Z)
    out_ref[9:10, :] = jnp.zeros((1, SIDE), I32) + fits.astype(I32)


def far_plan(position, slots, union, along):
    return pl.pallas_call(
        far_plan_kernel,
        out_shape=jax.ShapeDtypeStruct((16, 128), I32),
        in_specs=[smem()] + [vmem()] * (2 + NZ),
        out_specs=vmem(),
        compiler_params=params(),
        cost_estimate=cost(2 * 20 * ROWS**3, 8 * ROWS**2),
        name="far_plan",
    )(position, slots, union, *along)


def dense(blocks, nonzero, columns):
    slab = lax.axis_index(ROW_AXES)
    part = lax.axis_index("col")
    masked = blocks * nonzero[:, :, None, None].astype(BF)
    slab_ids = jnp.arange(SLABS, dtype=I32)
    local_rows = jnp.arange(HEIGHT, dtype=I32)
    grouped = columns.reshape(SLABS, HEIGHT * SLOTS)
    targets = slab * HEIGHT + local_rows
    wanted = jnp.any(grouped[:, :, None] == targets[None, None, :], axis=1)
    wanted = wanted & (slab_ids != slab)[:, None]
    picked = jnp.sum(jnp.where(wanted, local_rows, 0), axis=1)
    filled = jnp.any(wanted, axis=1)
    outgoing = jnp.where(filled[:, None, None, None], masked[picked], jnp.zeros((), BF))
    incoming = lax.all_to_all(outgoing, ROW_AXES, split_axis=0, concat_axis=0, tiled=True)
    row_table = jnp.concatenate([incoming, masked], axis=0)
    own_cols = lax.dynamic_slice_in_dim(columns, slab * HEIGHT, HEIGHT, 0)
    source = own_cols // HEIGHT
    row_index = jnp.where(source == slab, SLABS + own_cols % HEIGHT, source)
    far_cols = columns[own_cols]
    far_quarter = lax.dynamic_slice_in_dim(far_cols, part * QUARTER, QUARTER, 2)
    whole = lax.all_gather(masked, "col", axis=1, tiled=True)
    results = []
    for member in range(HEIGHT):
        match = far_quarter[member][:, :, None] == own_cols[member][None, None, :]
        products = jnp.einsum(
            "tab,tubc->tuac", whole[member], row_table[row_index[member]],
            preferred_element_type=F32,
        )
        summed = lax.dot_general(
            match.astype(F32).reshape(SLOTS * QUARTER, SLOTS),
            products.reshape(SLOTS * QUARTER, SIDE * SIDE),
            (((0,), (0,)), ((), ())),
            precision=lax.Precision.HIGHEST,
            preferred_element_type=F32,
        )
        results.append(summed.reshape(SLOTS, SIDE, SIDE))
    square = lax.psum_scatter(jnp.stack(results), "col", scatter_dimension=1, tiled=True)
    return square.astype(BF)


def plane_columns(columns):
    split = columns.reshape(NX, NZ, NC, HEIGHT, NY, QUARTER)
    mine = lax.dynamic_index_in_dim(split, lax.axis_index("z"), 1, keepdims=False)
    mine = mine.transpose(3, 0, 1, 2, 4).reshape(PEERS, SLOTS)
    return jnp.pad(mine, ((0, 0), (0, HELD - SLOTS)), constant_values=-1).reshape(1, ENTRIES)


def shards(blocks, nonzero, columns):
    position = jnp.stack([lax.axis_index(name) for name in ROW_AXES + ("col",)])
    cuts = prepare(position, nonzero, blocks)
    cuts, names, same = lax.optimization_barrier((cuts, columns, blocks))
    turned = turn(nonzero, same)
    slots, union, need, kq = pattern(position, names, plane_columns(columns))
    near = lax.all_to_all(cuts, ("col", "x", "core"), split_axis=0, concat_axis=0, tiled=True)
    near, turned, need = lax.optimization_barrier((near, turned, need))
    whole = lax.all_gather(turned, "col", axis=0, tiled=False)
    whole = whole.reshape(ZERO_BLOCK, SIDE, SIDE)
    packed = send(position, need, kq, near.reshape(ENTRIES, PIECE))
    packed, slots = lax.optimization_barrier((packed, slots))
    along = [packed[0]] + [
        lax.ppermute(packed[step], "z", [(i, (i + step) % NZ) for i in range(NZ)])
        for step in ORDER_Z
    ]
    own_lists = own_plan(position, slots, union)
    along, own_lists = lax.optimization_barrier((along, own_lists))
    packed, notes = lax.optimization_barrier((route(position, along), along))
    far = [packed[0]]
    for number, (along_x, across) in enumerate(ORDER_X):
        pairs = [
            (i, ((i // NC + along_x) % NX) * NC + (i + across) % NC) for i in range(TARGETS)
        ]
        far.append(lax.ppermute(packed[1 + number], ("x", "core"), pairs))
    notes, whole = lax.optimization_barrier((notes, whole))
    far_lists = far_plan(position, slots, union, notes)
    own_lists, far_lists = lax.optimization_barrier((own_lists, far_lists))
    own = own_sums(own_lists, whole)
    far, own = lax.optimization_barrier((far, own))
    result = far_sums(own_lists, far_lists, whole, own, position, far)
    cuts = [result[0]]
    for step in ORDER_Y:
        pairs = [(i, (i + step) % NY) for i in range(NY)]
        cuts.append(lax.ppermute(result[step], "col", pairs))
    square = finish(position, cuts)
    return lax.cond(
        far_lists[9, 0] != 0,
        lambda value, *_: value,
        lambda _, *inputs: dense(*inputs),
        square,
        blocks,
        nonzero,
        columns,
    )


def solution(mesh):
    fine = Mesh(mesh.devices.reshape(NX, NZ, NC, NY), ROW_AXES + ("col",))
    spec = P(ROW_AXES, "col", None, None)
    return jax.shard_map(
        shards,
        mesh=fine,
        in_specs=(spec, P(ROW_AXES, "col"), P()),
        out_specs=spec,
        check_vma=False,
    )
```
